32 devices in a mesh: beam: 4 (over y, x), ma: 8 (over z, core).
Axes of the slice: x: 2, y: 2, z: 4, core: 2. Of those that a mesh axis runs over, the one named last changes fastest.
Arguments:
- sky_harmonics: float32 [16, 2, 2048], P('ma'), may hold values from -6 to 6
- beam_harmonics: float32 [32, 2, 2048], P('beam'), may hold values from -6 to 6
- wigner: bfloat16 [32, 16, 16, 2048], P('beam', 'ma'), may hold values from -0.125 to 0.125
- order_map: int32 [16], replicated, may hold values from 0 to 2047, as said below
- block_owner: int32 [1024, 1], P('ma'), may hold values from 0 to 7; in each aligned block of 128 rows (0 to 127, 128 to 255, ...) at most 32 rows name the same one
- block_local: int32 [1024], P('ma'), may hold values from 0 to 63
- cell_offset: int32 [131072], P('ma'), may hold values from 0 to 126
- cell_fraction: float32 [131072], P('ma'), may hold values from 0 to 1
- beam_angle: float32 [131072], P('ma'), may hold values from -3.140625 to 3.140625
- sample_count: int32 [8], P('ma'), may hold values from 1 to 16384, 98304 in all
- noise_weight: float32 [128, 128], replicated, may hold values from -0.2 to 2, as said below
Outputs:
- sky_gradient: float32 [16, 2, 2048], P('ma', None, 'beam')
The draws below stay inside these ranges and needn't reach their ends.
Inputs may be any that keep to these rules, and one draw needn't show every extreme that they name: `order_map`: 16 distinct azimuthal orders. `block_owner`: among the 128 sample blocks of one device, at most 32 name the same owner, and in some device some owner is named exactly 32 times. `noise_weight`: diagonal entries lie in 1 to 2, the others within 0.2 in magnitude.
All inputs are finite; a program needn't handle non-finite values. No bound on the sum of `sample_count` on one device may be relied on, other than what follows from the above.
Results may differ from the reference program's by a relative error of at most 0.017.
Values may be sent and summed in bfloat16 or wider, within the bound.
No kernel may reach another device: no remote copies, remote signals or barrier semaphores. Data moves between devices by JAX's collectives and lax.ppermute only.
A program may use at most 128 MiB of HBM per device.

```python
import math
import jax
import jax.numpy as jnp
import numpy as np
from jax import lax

L = 2048
PHI = 4096
CELLS = 128
NSB = 128
K = 32
M = 16
R = 16
BLK_DEV = 64
S_DEV = 16384
SB_ALL = 1024
S_ALL = 131072
CAP = 32
N_MA = 8


def draw_order_map(key, part):
    return jax.random.permutation(key, L)[:M].astype(jnp.int32)


def draw_noise_weight(key, part):
    first_key, second_key = jax.random.split(jax.random.fold_in(key, 17))
    diagonal = jax.random.uniform(first_key, (CELLS,), jnp.float32, 1.0, 2.0)
    spread_part = jax.random.normal(second_key, (CELLS, CELLS), jnp.float32) * (0.5 / jnp.sqrt(CELLS * 1.0))
    spread_part = jnp.clip(spread_part, -0.2, 0.2)
    eye_mask = jnp.eye(CELLS, dtype=jnp.float32)
    return (jnp.diag(diagonal) + spread_part * (1.0 - eye_mask)).astype(jnp.float32)


def plant(entries, rng, least, high):
    longest = entries.shape.index(max(entries.shape))
    spots = []
    for shift in (0, 1):
        where = [jax.random.randint(jax.random.fold_in(rng, axis), (), 0, length) for axis, length in enumerate(entries.shape)]
        where[longest] = (where[longest] + shift) % entries.shape[longest]
        spots.append(tuple(where))
    return entries.at[spots[0]].set(least).at[spots[1]].set(high)


def steps_of(rng, shape, shards, low, largest):
    gain = 1.0
    for dim, parts in shards:
        heights = jax.random.uniform(jax.random.fold_in(jax.random.fold_in(rng, 6), dim), (parts,), jnp.float32, low / len(shards), largest / len(shards))
        gain = gain * jnp.repeat(jnp.exp(heights), shape[dim] // parts).reshape((-1,) + (1,) * (len(shape) - 1 - dim))
    return gain


def length_profile(number_of, total, most, skew):
    weights = [(1 << 20) // math.isqrt(rank ** skew) + 1 for rank in range(2, number_of + 1)]
    surplus, given = total - most - (number_of - 1), [1] * (number_of - 1)
    while surplus > 0:
        free = [i for i in range(number_of - 1) if given[i] < most]
        pool, budget = sum([weights[i] for i in free]), surplus
        for i in free:
            addition = min(most - given[i], max(1, budget * weights[i] // pool), surplus)
            given[i] = given[i] + addition
            surplus = surplus - addition
    return np.array([most] + given)


def ragged_sizes(rng, number_of, total, bound, lean):
    if number_of == 2:
        one = jax.random.randint(rng, (), max(1, total - bound), min(bound, total - 1) + 1)
        return jnp.stack([one, total - one])
    tallies = jnp.asarray(length_profile(number_of, total, bound, lean), jnp.int32)
    couples = (number_of - 1) // 2
    source_of, taker = tallies[1:1 + 2 * couples:2], tallies[2:2 + 2 * couples:2]
    slack = jnp.minimum(source_of - 1, bound - taker)
    moved = jax.random.randint(jax.random.fold_in(rng, 1), (couples,), 0, 1 << 20) % (slack + 1)
    tallies = tallies.at[1:1 + 2 * couples:2].set(source_of - moved).at[2:2 + 2 * couples:2].set(taker + moved)
    return tallies[jax.random.permutation(jax.random.fold_in(rng, 2), number_of)]


def routed_block(own_key, own, number, rows, amount, top, bound, slope):
    ranking = jax.random.permutation(own_key, amount)
    heavy_load, ordinary = load_shares(amount, rows * top, bound, slope, True), load_shares(amount, rows * top, bound, slope, False)
    places = jnp.arange(amount)

    def named(sizes, offset_by):
        used = int((sizes > 0).sum())
        fixed = max(1, used // 4)
        shifted = fixed + (places - fixed + offset_by * (used - fixed)) % max(1, amount - fixed)
        return jnp.zeros((amount,), jnp.int32).at[ranking[jnp.where(places < fixed, places, shifted)]].set(jnp.asarray(sizes, jnp.int32))

    sizes = jnp.where(number % 4 == 0, named(heavy_load, number // 4), named(ordinary, number - number // 4 - 1))
    mixed = jax.random.permutation(jax.random.fold_in(own, 3), amount)
    giver, sink = mixed[0:amount // 2 * 2:2], mixed[1:amount // 2 * 2:2]
    slack = jnp.minimum(sizes[giver] - 1, bound - sizes[sink]) // 2
    slack = jnp.where((giver == ranking[0]) | (sink == ranking[0]) | (sizes[sink] == 0), 0, jnp.maximum(slack, 0))
    shifted = jax.random.randint(jax.random.fold_in(own, 4), (amount // 2,), 0, 1 << 20) % (slack + 1)
    sizes = sizes.at[giver].add(-shifted).at[sink].add(shifted)
    items = jnp.searchsorted(jnp.cumsum(sizes), jnp.arange(rows * top), side="right").astype(jnp.int32)
    table = items.reshape(top, rows).T
    table = table[jax.random.permutation(jax.random.fold_in(own, 1), rows)]
    offset_by = jax.random.randint(jax.random.fold_in(own, 2), (rows, 1), 0, top)
    return jnp.take_along_axis(table, (jnp.arange(top)[None, :] + offset_by) % top, axis=1)


def load_shares(count, total, bound, lean, full):
    weights = [(1 << 20) // math.isqrt(grade ** lean) + 1 for grade in range(1, count + 1)]
    largest = bound if full else min(bound, max(-(-total // count), total * weights[0] // sum(weights)))
    least = 1 if total - largest >= count - 1 else 0
    given, surplus = [largest] + [least] * (count - 1), total - largest - least * (count - 1)
    while surplus > 0:
        candidates = [i for i in range(1, count) if given[i] < largest] or [i for i in range(1, count) if given[i] < bound]
        pool, remaining = sum([weights[i] for i in candidates]), surplus
        for i in candidates:
            addition = min(bound - given[i], max(1, remaining * weights[i] // pool), surplus)
            given[i] = given[i] + addition
            surplus = surplus - addition
    return np.array(given)


def scatter_about(key, dims, scale, limit, pieces=(), kind=jnp.bfloat16):
    entries = jax.random.normal(key, dims, jnp.float32) * scale
    if len(pieces) > 0:
        entries = steps_of(key, dims, pieces, -0.22, 0.18) * entries
    return jnp.clip(entries, min=-limit, max=limit).astype(kind)


def setup_inputs(seed: int = 0) -> dict:
    splits = jax.random.split(jax.random.key(seed), 12)
    sky_harmonics = scatter_about(splits[0], (M, 2, L), 1.0, 6.0, ((0, 8),), jnp.float32)
    beam_harmonics = scatter_about(splits[1], (K, 2, L), 1.0, 6.0, ((0, 4),), jnp.float32)
    wigner = scatter_about(splits[2], (K, M, R, L), L ** -0.5, 0.125, ((0, 4), (1, 8)))
    order_map = draw_order_map(jax.random.fold_in(splits[11], 71), 0)
    block_owner_keys = jax.random.split(jax.random.fold_in(splits[4], 1), SB_ALL // NSB)
    block_owner_turns = jax.random.permutation(jax.random.fold_in(splits[4], 3), SB_ALL // NSB)
    block_owner = jax.vmap(lambda own, number: routed_block(jax.random.fold_in(splits[4], 2), own, number, NSB, N_MA, 1, CAP, 2))(block_owner_keys, block_owner_turns).reshape((SB_ALL, 1))
    block_local = plant(jax.random.randint(splits[5], (SB_ALL,), 0, BLK_DEV), jax.random.fold_in(splits[5], 1), 0, BLK_DEV - 1).astype(jnp.int32)
    cell_offset = plant(jax.random.randint(splits[6], (S_ALL,), 0, CELLS - 1), jax.random.fold_in(splits[6], 1), 0, (CELLS - 1) - 1).astype(jnp.int32)
    cell_fraction = jnp.clip(1.0 * jax.random.uniform(splits[7], (S_ALL,), jnp.float32) ** steps_of(splits[7], (S_ALL,), ((0, 8),), -0.2, 0.2), 0.0, 1.0)
    beam_angle = jnp.clip(jax.random.uniform(splits[8], (S_ALL,), jnp.float32, -3.140625, 3.140625), -3.140625, 3.140625)
    sample_count = ragged_sizes(splits[9], N_MA, N_MA * S_DEV * 3 // 4, S_DEV, 2).astype(jnp.int32)
    noise_weight = draw_noise_weight(jax.random.fold_in(splits[11], 71), 0)
    return dict(sky_harmonics=sky_harmonics, beam_harmonics=beam_harmonics, wigner=wigner, order_map=order_map, block_owner=block_owner, block_local=block_local, cell_offset=cell_offset, cell_fraction=cell_fraction, beam_angle=beam_angle, sample_count=sample_count, noise_weight=noise_weight)


def cycle_phases(order_map, cycle_cells):
    stepped = jnp.arange(cycle_cells, dtype=jnp.int32)
    phase_turns = order_map[:, None] * stepped[None, :] % cycle_cells
    angles = phase_turns.astype(jnp.float32) * (2.0 * math.pi / cycle_cells)
    scaling = 1.0 / math.sqrt(order_map.shape[0])
    return jnp.stack([jnp.cos(angles), -jnp.sin(angles)], axis=1) * scaling

def rotation(beam_order, beam_angle, total_orders):
    spin_order = ((beam_order + 1) // 2).astype(jnp.float32)
    angles = spin_order * beam_angle
    return jnp.where(beam_order % 2 == 0, jnp.cos(angles), jnp.sin(angles)) / math.sqrt(total_orders)

def harmonic_product(sky_harmonics, beam_harmonics):
    sky_real = sky_harmonics[None, :, 0]
    sky_imag = sky_harmonics[None, :, 1]
    beam_real = beam_harmonics[:, None, 0]
    beam_imag = beam_harmonics[:, None, 1]
    first = sky_real * beam_real - sky_imag * beam_imag
    second = sky_real * beam_imag + sky_imag * beam_real
    return jnp.stack([first, second], axis=2).astype(jnp.bfloat16)

def gradient_terms(grad_harmonics, beam_harmonics):
    grad_real = grad_harmonics[:, :, 0]
    grad_imag = grad_harmonics[:, :, 1]
    beam_real = beam_harmonics[:, None, 0]
    beam_imag = beam_harmonics[:, None, 1]
    first = lax.optimization_barrier(jnp.sum(grad_real * beam_real + grad_imag * beam_imag, axis=0))
    second = lax.optimization_barrier(jnp.sum(grad_imag * beam_real - grad_real * beam_imag, axis=0))
    return jnp.stack([first, second], axis=1)

def reference(sky_harmonics, beam_harmonics, wigner, order_map, block_owner, block_local, cell_offset, cell_fraction, beam_angle, sample_count, noise_weight):
    highest = lax.Precision.HIGHEST
    total_orders = beam_harmonics.shape[0]
    phase_table = cycle_phases(order_map, PHI)
    block_index = block_owner[:, 0] * BLK_DEV + block_local
    cell_low = jnp.repeat(block_index, CELLS) * CELLS + cell_offset
    cell_high = cell_low + 1
    stamps = jnp.arange(cell_offset.shape[0], dtype=jnp.int32)
    valid_mask = (stamps % S_DEV < sample_count[stamps // S_DEV]).astype(jnp.float32)

    def forward_step(beam_order, signal):
        beam_order = jnp.asarray(beam_order).astype(jnp.int32)
        beam_row = lax.dynamic_slice_in_dim(beam_harmonics, beam_order, 1, 0)
        table_row = lax.dynamic_index_in_dim(wigner, beam_order, 0, keepdims=False).astype(jnp.float32)
        product = harmonic_product(sky_harmonics, beam_row)[0].astype(jnp.float32)
        cycle_modes = jnp.einsum('mcl,mrl->mcr', product, table_row, precision=highest)
        cube_flat = jnp.einsum('mcr,mcp->rp', cycle_modes, phase_table, precision=highest).reshape(-1)
        values = (1.0 - cell_fraction) * cube_flat[cell_low] + cell_fraction * cube_flat[cell_high]
        return signal + rotation(beam_order, beam_angle, total_orders) * values
    signal = lax.fori_loop(0, total_orders, forward_step, jnp.zeros(cell_offset.shape, jnp.float32))
    signal = signal * valid_mask
    filtered = jnp.einsum('bu,tu->bt', signal.reshape(-1, CELLS), noise_weight, precision=highest).reshape(-1) * valid_mask

    def adjoint_step(beam_order, gradient):
        beam_order = jnp.asarray(beam_order).astype(jnp.int32)
        beam_row = lax.dynamic_slice_in_dim(beam_harmonics, beam_order, 1, 0)
        table_row = lax.dynamic_index_in_dim(wigner, beam_order, 0, keepdims=False).astype(jnp.float32)
        weighted = rotation(beam_order, beam_angle, total_orders) * filtered
        cube_grad = jnp.zeros((R * PHI,), jnp.float32)
        cube_grad = cube_grad.at[cell_low].add((1.0 - cell_fraction) * weighted)
        cube_grad = cube_grad.at[cell_high].add(cell_fraction * weighted)
        grad_modes = jnp.einsum('rp,mcp->mcr', cube_grad.reshape(R, PHI), phase_table, precision=highest).astype(jnp.bfloat16)
        grad_harmonics = jnp.einsum('mcr,mrl->mcl', grad_modes.astype(jnp.float32), table_row, precision=highest)
        return gradient + gradient_terms(grad_harmonics[None], beam_row)
    return lax.fori_loop(0, total_orders, adjoint_step, jnp.zeros(sky_harmonics.shape, jnp.float32))
```

```python
import functools
import math

import jax
import jax.numpy as jnp
from jax import lax
from jax.experimental import pallas as pl
from jax.experimental.pallas import tpu as pltpu
from jax.sharding import PartitionSpec as P

PHI = 4096
CELLS = 128
CYCLE_BLOCKS = PHI // CELLS
F32 = jnp.float32
BF16 = jnp.bfloat16
LAST_LAST = (((1,), (1,)), ((), ()))


def iota(shape, axis):
    return lax.broadcasted_iota(jnp.int32, shape, axis)


def vmem(count):
    return [pl.BlockSpec(memory_space=pltpu.VMEM)] * count


def smem(count):
    return [pl.BlockSpec(memory_space=pltpu.SMEM)] * count


def own_block(orders, cycles):
    shape = (orders, orders * cycles)
    return iota(shape, 1) // cycles == iota(shape, 0)


def modes_kernel(sky, beam, wigner, out):
    orders, sky_orders, cycles, degrees = wigner.shape
    beam_real, beam_imag = beam[:, 0, :], beam[:, 1, :]
    diagonal = own_block(orders, cycles)
    rows = [None] * (2 * sky_orders)
    for m in range(sky_orders):
        sky_real, sky_imag = sky[m, 0:1, :], sky[m, 1:2, :]
        first = sky_real * beam_real - sky_imag * beam_imag
        second = sky_real * beam_imag + sky_imag * beam_real
        product = jnp.concatenate([first, second], axis=0).astype(BF16)
        table = wigner[:, m].reshape(orders * cycles, degrees)
        modes = lax.dot_general(product, table, LAST_LAST, preferred_element_type=F32)
        for c in range(2):
            part = jnp.where(diagonal, modes[c * orders : (c + 1) * orders], 0.0)
            rows[c * sky_orders + m] = jnp.sum(part, axis=0, keepdims=True)
    block = jnp.concatenate(rows, axis=0).astype(out.dtype)
    for d in range(out.shape[0]):
        out[d] = block


def tables_kernel(
    blocks_local, order_map, owners, locals_, offsets, fractions, angles,
    phi, turn, own, step_real, step_imag, wide,
):
    orders = order_map.shape[0]
    blocks = offsets.shape[0]
    total = turn.shape[0] // blocks
    local_orders = own.shape[0] // blocks
    order = jnp.zeros((orders, CELLS), jnp.int32)
    row = iota((orders, CELLS), 0)
    lane = iota((orders, CELLS), 1)
    for m in range(orders):
        order = jnp.where(row == m, order_map[m], order)
    unit = 2.0 * math.pi / PHI

    def phase(turns):
        angle = (turns % PHI).astype(F32) * unit
        return jnp.cos(angle), -jnp.sin(angle)

    scaling = 1.0 / math.sqrt(orders)
    cell_real, cell_imag = phase(order * lane)
    cell_real, cell_imag = cell_real * scaling, cell_imag * scaling
    next_real, next_imag = phase(order)
    next_real = next_real - 1.0
    first_real, first_imag = phase((order * CELLS) % PHI * lane)
    for j in range(CYCLE_BLOCKS):
        step_real[j] = jnp.broadcast_to(first_real[:, j : j + 1], (orders, CELLS))
        step_imag[j] = jnp.broadcast_to(first_imag[:, j : j + 1], (orders, CELLS))

    def block_phases(s):
        place = (owners[s] * blocks_local + locals_[s]) % CYCLE_BLOCKS
        offset = jnp.broadcast_to(offsets[pl.ds(s, 1), :], (orders, CELLS))
        fraction = jnp.broadcast_to(fractions[pl.ds(s, 1), :], (orders, CELLS))
        real = jnp.take_along_axis(cell_real, offset, axis=1, mode="promise_in_bounds")
        imag = jnp.take_along_axis(cell_imag, offset, axis=1, mode="promise_in_bounds")
        base_real, base_imag = step_real[place], step_imag[place]
        left_real = real * base_real - imag * base_imag
        left_imag = real * base_imag + imag * base_real
        mix_real = 1.0 + fraction * next_real
        mix_imag = fraction * next_imag
        both = jnp.concatenate(
            [left_real * mix_real - left_imag * mix_imag, left_real * mix_imag + left_imag * mix_real],
            axis=0,
        )
        start = pl.multiple_of(s * 2 * orders, 2 * orders)
        phi[pl.ds(start, 2 * orders), :] = both.astype(BF16)

    @pl.loop(0, blocks // 8)
    def _(group):
        for j in range(8):
            block_phases(group * 8 + j)

    scale = 1.0 / math.sqrt(total)
    one_real, one_imag = jnp.cos(angles[...]), jnp.sin(angles[...])
    power_real, power_imag = one_real * scale, one_imag * scale
    wide[pl.ds(0, blocks, stride=total), :] = jnp.full((blocks, CELLS), scale, F32)
    for q in range(1, total // 2 + 1):
        wide[pl.ds(2 * q - 1, blocks, stride=total), :] = power_imag
        if 2 * q < total:
            wide[pl.ds(2 * q, blocks, stride=total), :] = power_real
        power_real, power_imag = (
            power_real * one_real - power_imag * one_imag,
            power_real * one_imag + power_imag * one_real,
        )
    mine = lax.axis_index("beam") * local_orders

    @pl.loop(0, blocks // 8)
    def _(group):
        for j in range(8):
            s = group * 8 + j
            start = pl.multiple_of(s * total, total)
            turn[pl.ds(start, total), :] = wide[pl.ds(start, total), :].astype(BF16)
            from_row = pl.multiple_of(start + mine, local_orders)
            to_row = pl.multiple_of(s * local_orders, local_orders)
            own[pl.ds(to_row, local_orders), :] = wide[pl.ds(from_row, local_orders), :]


def samples_kernel(
    blocks_local, owners, locals_, count, arrived, phi, turn, own, noise,
    out, stacked, modes_rows, modes, partial, filtered, totals, ordered,
):
    beams, sky_devices, rows, lanes = arrived.shape
    sky_orders = rows // 2
    all_sky = sky_devices * sky_orders
    parts = 2 * all_sky
    blocks = partial.shape[0] // 8
    total = turn.shape[0] // blocks
    orders = total // beams
    cycles = lanes // orders

    def cycle_of(s):
        return (owners[s] * blocks_local + locals_[s]) // CYCLE_BLOCKS

    for b in range(beams):
        for a in range(sky_devices):
            for c in range(2):
                piece = arrived[b, a, c * sky_orders : (c + 1) * sky_orders, :].astype(F32)
                start = c * all_sky + a * sky_orders
                stacked[b, start : start + sky_orders, :] = piece
        modes_rows[b * lanes : (b + 1) * lanes, :] = stacked[b].T
    for r in range(cycles):
        modes[r] = modes_rows[pl.ds(r, total, stride=cycles), :].astype(BF16)

    @pl.loop(0, blocks // 8)
    def _(group):
        for j in range(8):
            s = group * 8 + j
            table = phi[pl.ds(pl.multiple_of(s * parts, parts), parts), :]
            cells = jnp.dot(modes[cycle_of(s)], table, preferred_element_type=F32)
            turned = cells * turn[pl.ds(pl.multiple_of(s * total, total), total), :].astype(F32)
            kept = jnp.sum(turned.reshape(total // 8, 8, CELLS), axis=0)
            partial[pl.ds(pl.multiple_of(s * 8, 8), 8), :] = kept

    signal = partial[pl.ds(0, blocks, stride=8), :]
    for i in range(1, 8):
        signal = signal + partial[pl.ds(i, blocks, stride=8), :]
    valid = iota((blocks, CELLS), 0) * CELLS + iota((blocks, CELLS), 1) < count[0]
    signal = jnp.where(valid, signal, 0.0)
    clean = lax.dot_general(
        signal, noise[...], LAST_LAST, precision=lax.Precision.HIGHEST, preferred_element_type=F32
    )
    filtered[...] = jnp.where(valid, clean, 0.0)

    together = len(totals)
    for one in totals:
        one[...] = jnp.zeros_like(one)

    def spread(first):
        weighted = []
        for j in range(together):
            s = first + j
            rotation = own[pl.ds(pl.multiple_of(s * orders, orders), orders), :]
            weighted.append(rotation * filtered[pl.ds(s, 1), :])
        weighted = jnp.concatenate(weighted, axis=0).astype(BF16)
        start = pl.multiple_of(first * parts, together * parts)
        tables = phi[pl.ds(start, together * parts), :]
        terms = lax.dot_general(weighted, tables, LAST_LAST, preferred_element_type=F32)
        for j in range(together):
            row = pl.multiple_of(cycle_of(first + j) * orders, orders)
            here = totals[j]
            here[pl.ds(row, orders), :] += terms[j * orders : (j + 1) * orders]

    unroll = max(1, 8 // together)

    @pl.loop(0, blocks // (together * unroll))
    def _(group):
        for i in range(unroll):
            spread((group * unroll + i) * together)

    gathered = totals[0][...]
    which = iota(gathered.shape, 1) // parts
    for j in range(1, together):
        gathered = jnp.where(which == j, totals[j][...], gathered)
    modes_rows_of = ordered
    totals[0][...] = gathered
    for k in range(orders):
        modes_rows_of[k * cycles : (k + 1) * cycles, :] = totals[0][pl.ds(k, cycles, stride=orders), :]
    turned = ordered[...].T
    summed = turned[0:parts]
    for j in range(1, together):
        summed = summed + turned[j * parts : (j + 1) * parts]
    summed = summed.astype(out.dtype)
    for a in range(sky_devices):
        for c in range(2):
            start = c * all_sky + a * sky_orders
            out[a, c * sky_orders : (c + 1) * sky_orders, :] = summed[start : start + sky_orders]


def gradient_kernel(arrived, beam, wigner, out):
    orders, sky_orders, cycles, degrees = wigner.shape
    beam_real, beam_imag = beam[:, 0, :], beam[:, 1, :]
    diagonal = own_block(orders, cycles)
    modes = jnp.sum(arrived[...].astype(F32), axis=0).astype(BF16).astype(F32)
    width = out.shape[2]
    for m in range(sky_orders):
        spreads = []
        for c in range(2):
            row = modes[c * sky_orders + m : c * sky_orders + m + 1]
            spreads.append(jnp.where(diagonal, row, 0.0))
        left = jnp.concatenate(spreads, axis=0).astype(BF16)
        table = wigner[:, m].reshape(orders * cycles, degrees)
        harmonics = jnp.dot(left, table, preferred_element_type=F32)
        real, imag = harmonics[:orders], harmonics[orders:]
        first = jnp.sum(real * beam_real + imag * beam_imag, axis=0, keepdims=True)
        second = jnp.sum(imag * beam_real - real * beam_imag, axis=0, keepdims=True)
        both = jnp.concatenate([first, second], axis=0).astype(out.dtype)
        for d in range(out.shape[0]):
            out[d, 2 * m : 2 * m + 2, :] = both[:, d * width : (d + 1) * width]


def local(
    sky_harmonics,
    beam_harmonics,
    wigner,
    order_map,
    block_owner,
    block_local,
    cell_offset,
    cell_fraction,
    beam_angle,
    sample_count,
    noise_weight,
):
    beams, sky_devices = lax.axis_size("beam"), lax.axis_size("ma")
    orders, sky_orders, cycles, degrees = wigner.shape
    total = orders * beams
    all_sky = sky_orders * sky_devices
    parts = 2 * all_sky
    blocks = block_local.shape[0]
    blocks_local = cycles // sky_devices * CYCLE_BLOCKS
    lanes = orders * cycles
    rows = 2 * sky_orders
    together = max(1, CELLS // parts)
    owners = block_owner.reshape(blocks)
    limit = pltpu.CompilerParams(vmem_limit_bytes=40 * 1024 * 1024)

    sent = pl.pallas_call(
        modes_kernel,
        out_shape=jax.ShapeDtypeStruct((beams * sky_devices, rows, lanes), F32),
        in_specs=vmem(3),
        out_specs=vmem(1)[0],
        compiler_params=limit,
        name="modes",
    )(sky_harmonics, beam_harmonics, wigner)
    arrived = lax.all_to_all(sent, ("beam", "ma"), split_axis=0, concat_axis=0, tiled=True)

    phi, turn, own = pl.pallas_call(
        functools.partial(tables_kernel, blocks_local),
        out_shape=[
            jax.ShapeDtypeStruct((blocks * parts, CELLS), BF16),
            jax.ShapeDtypeStruct((blocks * total, CELLS), BF16),
            jax.ShapeDtypeStruct((blocks * orders, CELLS), F32),
        ],
        in_specs=smem(3) + vmem(3),
        out_specs=vmem(3),
        scratch_shapes=[
            pltpu.VMEM((CYCLE_BLOCKS, all_sky, CELLS), F32),
            pltpu.VMEM((CYCLE_BLOCKS, all_sky, CELLS), F32),
            pltpu.VMEM((blocks * total, CELLS), F32),
        ],
        compiler_params=limit,
        cost_estimate=pl.CostEstimate(flops=100_000_000, bytes_accessed=4_000_000, transcendentals=100_000),
        name="tables",
    )(
        order_map, owners, block_local,
        cell_offset.reshape(blocks, CELLS),
        cell_fraction.reshape(blocks, CELLS),
        beam_angle.reshape(blocks, CELLS),
    )

    grads = pl.pallas_call(
        functools.partial(samples_kernel, blocks_local),
        out_shape=jax.ShapeDtypeStruct((sky_devices, rows, lanes), F32),
        in_specs=smem(3) + vmem(5),
        out_specs=vmem(1)[0],
        scratch_shapes=[
            pltpu.VMEM((beams, parts, lanes), F32),
            pltpu.VMEM((beams * lanes, parts), F32),
            pltpu.VMEM((cycles, total, parts), BF16),
            pltpu.VMEM((blocks * 8, CELLS), F32),
            pltpu.VMEM((blocks, CELLS), F32),
            [pltpu.VMEM((lanes, together * parts), F32) for _ in range(together)],
            pltpu.VMEM((lanes, together * parts), F32),
        ],
        compiler_params=limit,
        name="samples",
    )(
        owners, block_local, sample_count,
        arrived.reshape(beams, sky_devices, rows, lanes),
        phi, turn, own, noise_weight,
    )
    grads = lax.all_to_all(grads, "ma", split_axis=0, concat_axis=0, tiled=True)

    shares = pl.pallas_call(
        gradient_kernel,
        out_shape=jax.ShapeDtypeStruct((beams, rows, degrees // beams), BF16),
        in_specs=vmem(3),
        out_specs=vmem(1)[0],
        compiler_params=limit,
        name="gradient",
    )(grads, beam_harmonics, wigner)
    shares = lax.all_to_all(shares, "beam", split_axis=0, concat_axis=0, tiled=True)
    result = jnp.sum(shares.astype(F32), axis=0)
    return result.reshape(sky_orders, 2, degrees // beams)


def solution(mesh):
    return jax.shard_map(
        local,
        mesh=mesh,
        in_specs=(
            P("ma", None, None),
            P("beam", None, None),
            P("beam", "ma", None, None),
            P(),
            P("ma", None),
            P("ma"),
            P("ma"),
            P("ma"),
            P("ma"),
            P("ma"),
            P(),
        ),
        out_specs=P("ma", None, "beam"),
        check_vma=False,
    )
```

```python
import functools
import math

import jax
import jax.numpy as jnp
from jax import lax
from jax.experimental import pallas as pl
from jax.experimental.pallas import tpu as pltpu
from jax.sharding import PartitionSpec as P

PHI = 4096
CELLS = 128
CYCLE_BLOCKS = PHI // CELLS
F32 = jnp.float32
BF16 = jnp.bfloat16
LAST_LAST = (((1,), (1,)), ((), ()))


def iota(shape, axis):
    return lax.broadcasted_iota(jnp.int32, shape, axis)


def vmem(count):
    return [pl.BlockSpec(memory_space=pltpu.VMEM)] * count


def smem(count):
    return [pl.BlockSpec(memory_space=pltpu.SMEM)] * count


def own_block(orders, cycles):
    shape = (orders, orders * cycles)
    return iota(shape, 1) // cycles == iota(shape, 0)


def modes_kernel(sky, beam, wigner, out):
    orders, sky_orders, cycles, degrees = wigner.shape
    beam_real, beam_imag = beam[:, 0, :], beam[:, 1, :]
    diagonal = own_block(orders, cycles)
    rows = [None] * (2 * sky_orders)
    for m in range(sky_orders):
        sky_real, sky_imag = sky[m, 0:1, :], sky[m, 1:2, :]
        first = sky_real * beam_real - sky_imag * beam_imag
        second = sky_real * beam_imag + sky_imag * beam_real
        product = jnp.concatenate([first, second], axis=0).astype(BF16)
        table = wigner[:, m].reshape(orders * cycles, degrees)
        modes = lax.dot_general(product, table, LAST_LAST, preferred_element_type=F32)
        for c in range(2):
            part = jnp.where(diagonal, modes[c * orders : (c + 1) * orders], 0.0)
            rows[c * sky_orders + m] = jnp.sum(part, axis=0, keepdims=True)
    block = jnp.concatenate(rows, axis=0).astype(out.dtype)
    for d in range(out.shape[0]):
        out[d] = block


def tables_kernel(
    blocks_local, order_map, owners, locals_, offsets, fractions, angles,
    phi, turn, own, step_real, step_imag, wide,
):
    orders = order_map.shape[0]
    blocks = offsets.shape[0]
    total = turn.shape[0] // blocks
    local_orders = own.shape[0] // blocks
    order = jnp.zeros((orders, CELLS), jnp.int32)
    row = iota((orders, CELLS), 0)
    lane = iota((orders, CELLS), 1)
    for m in range(orders):
        order = jnp.where(row == m, order_map[m], order)
    unit = 2.0 * math.pi / PHI

    def phase(turns):
        angle = (turns % PHI).astype(F32) * unit
        return jnp.cos(angle), -jnp.sin(angle)

    scaling = 1.0 / math.sqrt(orders)
    cell_real, cell_imag = phase(order * lane)
    cell_real, cell_imag = cell_real * scaling, cell_imag * scaling
    next_real, next_imag = phase(order)
    next_real = next_real - 1.0
    first_real, first_imag = phase((order * CELLS) % PHI * lane)
    for j in range(CYCLE_BLOCKS):
        step_real[j] = jnp.broadcast_to(first_real[:, j : j + 1], (orders, CELLS))
        step_imag[j] = jnp.broadcast_to(first_imag[:, j : j + 1], (orders, CELLS))

    def block_phases(s):
        place = (owners[s] * blocks_local + locals_[s]) % CYCLE_BLOCKS
        offset = jnp.broadcast_to(offsets[pl.ds(s, 1), :], (orders, CELLS))
        fraction = jnp.broadcast_to(fractions[pl.ds(s, 1), :], (orders, CELLS))
        real = jnp.take_along_axis(cell_real, offset, axis=1, mode="promise_in_bounds")
        imag = jnp.take_along_axis(cell_imag, offset, axis=1, mode="promise_in_bounds")
        base_real, base_imag = step_real[place], step_imag[place]
        left_real = real * base_real - imag * base_imag
        left_imag = real * base_imag + imag * base_real
        mix_real = 1.0 + fraction * next_real
        mix_imag = fraction * next_imag
        both = jnp.concatenate(
            [left_real * mix_real - left_imag * mix_imag, left_real * mix_imag + left_imag * mix_real],
            axis=0,
        )
        start = pl.multiple_of(s * 2 * orders, 2 * orders)
        phi[pl.ds(start, 2 * orders), :] = both.astype(BF16)

    @pl.loop(0, blocks // 8)
    def _(group):
        for j in range(8):
            block_phases(group * 8 + j)

    scale = 1.0 / math.sqrt(total)
    one_real, one_imag = jnp.cos(angles[...]), jnp.sin(angles[...])
    power_real, power_imag = one_real * scale, one_imag * scale
    wide[pl.ds(0, blocks, stride=total), :] = jnp.full((blocks, CELLS), scale, F32)
    for q in range(1, total // 2 + 1):
        wide[pl.ds(2 * q - 1, blocks, stride=total), :] = power_imag
        if 2 * q < total:
            wide[pl.ds(2 * q, blocks, stride=total), :] = power_real
        power_real, power_imag = (
            power_real * one_real - power_imag * one_imag,
            power_real * one_imag + power_imag * one_real,
        )
    mine = lax.axis_index("beam") * local_orders

    @pl.loop(0, blocks // 8)
    def _(group):
        for j in range(8):
            s = group * 8 + j
            start = pl.multiple_of(s * total, total)
            turn[pl.ds(start, total), :] = wide[pl.ds(start, total), :].astype(BF16)
            from_row = pl.multiple_of(start + mine, local_orders)
            to_row = pl.multiple_of(s * local_orders, local_orders)
            own[pl.ds(to_row, local_orders), :] = wide[pl.ds(from_row, local_orders), :]


def samples_kernel(
    blocks_local, owners, locals_, count, arrived, phi, turn, own, noise,
    outs, stacked, modes_rows, modes, partial, filtered, totals, ordered, pieces,
):
    beams, sky_devices, rows, lanes = arrived.shape
    sky_orders = rows // 2
    all_sky = sky_devices * sky_orders
    parts = 2 * all_sky
    blocks = partial.shape[0] // 8
    total = turn.shape[0] // blocks
    orders = total // beams
    cycles = lanes // orders

    def cycle_of(s):
        return (owners[s] * blocks_local + locals_[s]) // CYCLE_BLOCKS

    for b in range(beams):
        for a in range(sky_devices):
            for c in range(2):
                piece = arrived[b, a, c * sky_orders : (c + 1) * sky_orders, :].astype(F32)
                start = c * all_sky + a * sky_orders
                stacked[b, start : start + sky_orders, :] = piece
        modes_rows[b * lanes : (b + 1) * lanes, :] = stacked[b].T
    for r in range(cycles):
        modes[r] = modes_rows[pl.ds(r, total, stride=cycles), :].astype(BF16)

    @pl.loop(0, blocks // 8)
    def _(group):
        for j in range(8):
            s = group * 8 + j
            table = phi[pl.ds(pl.multiple_of(s * parts, parts), parts), :]
            cells = jnp.dot(modes[cycle_of(s)], table, preferred_element_type=F32)
            turned = cells * turn[pl.ds(pl.multiple_of(s * total, total), total), :].astype(F32)
            kept = jnp.sum(turned.reshape(total // 8, 8, CELLS), axis=0)
            partial[pl.ds(pl.multiple_of(s * 8, 8), 8), :] = kept

    signal = partial[pl.ds(0, blocks, stride=8), :]
    for i in range(1, 8):
        signal = signal + partial[pl.ds(i, blocks, stride=8), :]
    valid = iota((blocks, CELLS), 0) * CELLS + iota((blocks, CELLS), 1) < count[0]
    signal = jnp.where(valid, signal, 0.0)
    clean = lax.dot_general(
        signal, noise[...], LAST_LAST, precision=lax.Precision.HIGHEST, preferred_element_type=F32
    )
    filtered[...] = jnp.where(valid, clean, 0.0)

    together = len(totals)
    for one in totals:
        one[...] = jnp.zeros_like(one)

    def spread(first):
        weighted = []
        for j in range(together):
            s = first + j
            rotation = own[pl.ds(pl.multiple_of(s * orders, orders), orders), :]
            weighted.append(rotation * filtered[pl.ds(s, 1), :])
        weighted = jnp.concatenate(weighted, axis=0).astype(BF16)
        start = pl.multiple_of(first * parts, together * parts)
        tables = phi[pl.ds(start, together * parts), :]
        terms = lax.dot_general(weighted, tables, LAST_LAST, preferred_element_type=F32)
        for j in range(together):
            row = pl.multiple_of(cycle_of(first + j) * orders, orders)
            here = totals[j]
            here[pl.ds(row, orders), :] += terms[j * orders : (j + 1) * orders]

    unroll = max(1, 8 // together)

    @pl.loop(0, blocks // (together * unroll))
    def _(group):
        for i in range(unroll):
            spread((group * unroll + i) * together)

    gathered = totals[0][...]
    which = iota(gathered.shape, 1) // parts
    for j in range(1, together):
        gathered = jnp.where(which == j, totals[j][...], gathered)
    modes_rows_of = ordered
    totals[0][...] = gathered
    for k in range(orders):
        modes_rows_of[k * cycles : (k + 1) * cycles, :] = totals[0][pl.ds(k, cycles, stride=orders), :]
    turned = ordered[...].T
    summed = turned[0:parts]
    for j in range(1, together):
        summed = summed + turned[j * parts : (j + 1) * parts]
    me = lax.axis_index("ma")
    for a in range(sky_devices):
        for c in range(2):
            start = c * all_sky + a * sky_orders
            pieces[a ^ me, c * sky_orders : (c + 1) * sky_orders, :] = summed[start : start + sky_orders]
    for j, out in enumerate(outs):
        out[...] = pieces[j].astype(out.dtype)


def gradient_kernel(arrived, beam, wigner, outs, pieces):
    me = lax.axis_index("beam")
    orders, sky_orders, cycles, degrees = wigner.shape
    beam_real, beam_imag = beam[:, 0, :], beam[:, 1, :]
    diagonal = own_block(orders, cycles)
    modes = arrived[0][...].astype(F32)
    for one in arrived[1:]:
        modes = modes + one[...].astype(F32)
    modes = modes.astype(BF16).astype(F32)
    width = pieces.shape[3]
    for m in range(sky_orders):
        spreads = []
        for c in range(2):
            row = modes[c * sky_orders + m : c * sky_orders + m + 1]
            spreads.append(jnp.where(diagonal, row, 0.0))
        left = jnp.concatenate(spreads, axis=0).astype(BF16)
        table = wigner[:, m].reshape(orders * cycles, degrees)
        harmonics = jnp.dot(left, table, preferred_element_type=F32)
        real, imag = harmonics[:orders], harmonics[orders:]
        first = jnp.sum(real * beam_real + imag * beam_imag, axis=0, keepdims=True)
        second = jnp.sum(imag * beam_real - real * beam_imag, axis=0, keepdims=True)
        both = jnp.concatenate([first, second], axis=0)
        for d in range(len(outs)):
            pieces[d ^ me, m] = both[:, d * width : (d + 1) * width]
    for j, out in enumerate(outs):
        out[...] = pieces[j].astype(out.dtype)


def exchange(pieces, axis):
    count = lax.axis_size(axis)
    return [pieces[0]] + [
        lax.ppermute(pieces[j], axis, [(i, i ^ j) for i in range(count)]) for j in range(1, count)
    ]


def local(
    sky_harmonics,
    beam_harmonics,
    wigner,
    order_map,
    block_owner,
    block_local,
    cell_offset,
    cell_fraction,
    beam_angle,
    sample_count,
    noise_weight,
):
    beams, sky_devices = lax.axis_size("beam"), lax.axis_size("ma")
    orders, sky_orders, cycles, degrees = wigner.shape
    total = orders * beams
    all_sky = sky_orders * sky_devices
    parts = 2 * all_sky
    blocks = block_local.shape[0]
    blocks_local = cycles // sky_devices * CYCLE_BLOCKS
    lanes = orders * cycles
    rows = 2 * sky_orders
    together = max(1, CELLS // parts)
    owners = block_owner.reshape(blocks)
    limit = pltpu.CompilerParams(vmem_limit_bytes=40 * 1024 * 1024)

    sent = pl.pallas_call(
        modes_kernel,
        out_shape=jax.ShapeDtypeStruct((beams * sky_devices, rows, lanes), F32),
        in_specs=vmem(3),
        out_specs=vmem(1)[0],
        compiler_params=limit,
        name="modes",
    )(sky_harmonics, beam_harmonics, wigner)
    arrived = lax.all_to_all(sent, ("beam", "ma"), split_axis=0, concat_axis=0, tiled=True)

    phi, turn, own = pl.pallas_call(
        functools.partial(tables_kernel, blocks_local),
        out_shape=[
            jax.ShapeDtypeStruct((blocks * parts, CELLS), BF16),
            jax.ShapeDtypeStruct((blocks * total, CELLS), BF16),
            jax.ShapeDtypeStruct((blocks * orders, CELLS), F32),
        ],
        in_specs=smem(3) + vmem(3),
        out_specs=vmem(3),
        scratch_shapes=[
            pltpu.VMEM((CYCLE_BLOCKS, all_sky, CELLS), F32),
            pltpu.VMEM((CYCLE_BLOCKS, all_sky, CELLS), F32),
            pltpu.VMEM((blocks * total, CELLS), F32),
        ],
        compiler_params=limit,
        cost_estimate=pl.CostEstimate(flops=100_000_000, bytes_accessed=4_000_000, transcendentals=100_000),
        name="tables",
    )(
        order_map, owners, block_local,
        cell_offset.reshape(blocks, CELLS),
        cell_fraction.reshape(blocks, CELLS),
        beam_angle.reshape(blocks, CELLS),
    )

    grads = pl.pallas_call(
        functools.partial(samples_kernel, blocks_local),
        out_shape=([jax.ShapeDtypeStruct((rows, lanes), F32)] * sky_devices,),
        in_specs=smem(3) + vmem(5),
        out_specs=(vmem(sky_devices),),
        scratch_shapes=[
            pltpu.VMEM((beams, parts, lanes), F32),
            pltpu.VMEM((beams * lanes, parts), F32),
            pltpu.VMEM((cycles, total, parts), BF16),
            pltpu.VMEM((blocks * 8, CELLS), F32),
            pltpu.VMEM((blocks, CELLS), F32),
            [pltpu.VMEM((lanes, together * parts), F32) for _ in range(together)],
            pltpu.VMEM((lanes, together * parts), F32),
            pltpu.VMEM((sky_devices, rows, lanes), F32),
        ],
        compiler_params=limit,
        name="samples",
    )(
        owners, block_local, sample_count,
        arrived.reshape(beams, sky_devices, rows, lanes),
        phi, turn, own, noise_weight,
    )
    grads = exchange(grads[0], "ma")

    width = degrees // beams
    shares = pl.pallas_call(
        gradient_kernel,
        out_shape=([jax.ShapeDtypeStruct((sky_orders, 2, width), BF16)] * beams,),
        in_specs=[vmem(sky_devices)] + vmem(2),
        out_specs=(vmem(beams),),
        scratch_shapes=[pltpu.VMEM((beams, sky_orders, 2, width), F32)],
        compiler_params=limit,
        name="gradient",
    )(grads, beam_harmonics, wigner)
    return sum(share.astype(F32) for share in exchange(shares[0], "beam"))


def solution(mesh):
    return jax.shard_map(
        local,
        mesh=mesh,
        in_specs=(
            P("ma", None, None),
            P("beam", None, None),
            P("beam", "ma", None, None),
            P(),
            P("ma", None),
            P("ma"),
            P("ma"),
            P("ma"),
            P("ma"),
            P("ma"),
            P(),
        ),
        out_specs=P("ma", None, "beam"),
        check_vma=False,
    )
```

```python
import functools
import math

import jax
import jax.numpy as jnp
from jax import lax
from jax.experimental import pallas as pl
from jax.experimental.pallas import tpu as pltpu
from jax.sharding import PartitionSpec as P

PHI = 4096
CELLS = 128
CYCLE_BLOCKS = PHI // CELLS
F32 = jnp.float32
BF16 = jnp.bfloat16
LAST_LAST = (((1,), (1,)), ((), ()))


def iota(shape, axis):
    return lax.broadcasted_iota(jnp.int32, shape, axis)


def vmem(count):
    return [pl.BlockSpec(memory_space=pltpu.VMEM)] * count


def smem(count):
    return [pl.BlockSpec(memory_space=pltpu.SMEM)] * count


def hbm(count):
    return [pl.BlockSpec(memory_space=pltpu.HBM)] * count


def sine_turns(z):
    square = z * z
    value = 39.53670603 * square - 76.54978229
    value = value * square + 81.60100407
    value = value * square - 41.34165503
    value = value * square + 6.28318516
    return value * z


def cosine_steps(steps):
    centred = ((steps + PHI // 2) & (PHI - 1)) - PHI // 2
    return sine_turns(0.25 - jnp.abs(centred).astype(F32) * (1.0 / PHI))


def own_block(orders, cycles):
    shape = (orders, orders * cycles)
    return iota(shape, 1) // cycles == iota(shape, 0)


def modes_kernel(sky_hbm, beam_hbm, wigner_hbm, out, sky, beam, wigner, arrivals):
    sky_orders, orders, cycles, degrees = wigner.shape
    small = [
        pltpu.make_async_copy(sky_hbm, sky, arrivals.at[0]),
        pltpu.make_async_copy(beam_hbm, beam, arrivals.at[1]),
    ]
    large = [
        pltpu.make_async_copy(wigner_hbm.at[:, m], wigner.at[m], arrivals.at[2 + m])
        for m in range(sky_orders)
    ]
    for copy in small + large:
        copy.start()
    for copy in small:
        copy.wait()
    beam_real, beam_imag = beam[:, 0, :], beam[:, 1, :]
    diagonal = own_block(orders, cycles)
    rows = [None] * (2 * sky_orders)
    for m in range(sky_orders):
        sky_real, sky_imag = sky[m, 0:1, :], sky[m, 1:2, :]
        first = sky_real * beam_real - sky_imag * beam_imag
        second = sky_real * beam_imag + sky_imag * beam_real
        product = jnp.concatenate([first, second], axis=0).astype(BF16)
        large[m].wait()
        table = wigner[m].reshape(orders * cycles, degrees)
        modes = lax.dot_general(product, table, LAST_LAST, preferred_element_type=F32)
        for c in range(2):
            part = jnp.where(diagonal, modes[c * orders : (c + 1) * orders], 0.0)
            rows[c * sky_orders + m] = jnp.sum(part, axis=0, keepdims=True)
    out[...] = jnp.concatenate(rows, axis=0)


def tables_kernel(
    blocks_local, angles_hbm, order_hbm, owners_hbm, locals_hbm, offsets_hbm, fractions_hbm,
    phi_hbm, turn_hbm, angles, order_map, owners, locals_, offsets, fractions, phi, turn,
    arrivals, departures, step_real, step_imag, cosines, sines,
):
    sources = (angles_hbm, order_hbm, owners_hbm, locals_hbm, offsets_hbm, fractions_hbm)
    places = (angles, order_map, owners, locals_, offsets, fractions)
    copies = [
        pltpu.make_async_copy(source, place, arrivals.at[i])
        for i, (source, place) in enumerate(zip(sources, places))
    ]
    for copy in copies:
        copy.start()
    copies.pop(0).wait()
    orders = order_map.shape[0]
    blocks = offsets.shape[0]
    half = turn.shape[0] // blocks // 2

    part = angles[...] * (0.5 / math.pi)
    part = part - jnp.round(part)
    cosines[...] = sine_turns(0.25 - jnp.abs(part))
    folded = jnp.where(part > 0.25, 0.5 - part, jnp.where(part < -0.25, -0.5 - part, part))
    sines[...] = sine_turns(folded)

    for copy in copies:
        copy.wait()
    order = jnp.zeros((orders, CELLS), jnp.int32)
    row = iota((orders, CELLS), 0)
    lane = iota((orders, CELLS), 1)
    for m in range(orders):
        order = jnp.where(row == m, order_map[m], order)

    def phase(steps):
        return cosine_steps(steps), cosine_steps(steps + PHI // 4)

    scaling = 1.0 / math.sqrt(orders)
    cell_real, cell_imag = phase(order * lane)
    cell_real, cell_imag = cell_real * scaling, cell_imag * scaling
    next_real, next_imag = phase(order)
    next_real = next_real - 1.0
    first_real, first_imag = phase(((order * CELLS) & (PHI - 1)) * lane)
    for j in range(CYCLE_BLOCKS):
        step_real[j] = jnp.broadcast_to(first_real[:, j : j + 1], (orders, CELLS))
        step_imag[j] = jnp.broadcast_to(first_imag[:, j : j + 1], (orders, CELLS))

    def block_phases(s):
        place = (owners[s] * blocks_local + locals_[s]) & (CYCLE_BLOCKS - 1)
        offset = jnp.broadcast_to(offsets[pl.ds(s, 1), :], (orders, CELLS))
        fraction = jnp.broadcast_to(fractions[pl.ds(s, 1), :], (orders, CELLS))
        real = jnp.take_along_axis(cell_real, offset, axis=1, mode="promise_in_bounds")
        imag = jnp.take_along_axis(cell_imag, offset, axis=1, mode="promise_in_bounds")
        base_real, base_imag = step_real[place], step_imag[place]
        left_real = real * base_real - imag * base_imag
        left_imag = real * base_imag + imag * base_real
        mix_real = 1.0 + fraction * next_real
        mix_imag = fraction * next_imag
        both = jnp.concatenate(
            [left_real * mix_real - left_imag * mix_imag, left_real * mix_imag + left_imag * mix_real],
            axis=0,
        )
        start = pl.multiple_of(s * 2 * orders, 2 * orders)
        phi[pl.ds(start, 2 * orders), :] = both.astype(BF16)

    scale = 1.0 / math.sqrt(2 * half)
    power = iota((8, CELLS), 0)

    def block_turns(s):
        one_real = jnp.broadcast_to(cosines[pl.ds(s, 1), :], (8, CELLS))
        one_imag = jnp.broadcast_to(sines[pl.ds(s, 1), :], (8, CELLS))
        step = (one_real, one_imag)
        odd = power & 1 == 1
        real, imag = jnp.where(odd, one_real * scale, scale), jnp.where(odd, one_imag * scale, 0.0)
        for bit in (2, 4):
            step = (step[0] * step[0] - step[1] * step[1], 2.0 * step[0] * step[1])
            taken = power & bit == bit
            by_real, by_imag = jnp.where(taken, step[0], 1.0), jnp.where(taken, step[1], 0.0)
            real, imag = real * by_real - imag * by_imag, real * by_imag + imag * by_real
        step = (step[0] * step[0] - step[1] * step[1], 2.0 * step[0] * step[1])
        start = pl.multiple_of(s * 2 * half, 2 * half)
        for j in range(half // 8):
            if j:
                real, imag = real * step[0] - imag * step[1], real * step[1] + imag * step[0]
            turn[pl.ds(start + 8 * j, 8), :] = real
            turn[pl.ds(start + half + 8 * j, 8), :] = real * one_imag + imag * one_real

    def leave(first, count):
        phi_rows = pl.ds(pl.multiple_of(first * 2 * orders, 8 * 2 * orders), count * 2 * orders)
        turn_rows = pl.ds(pl.multiple_of(first * 2 * half, 8 * 2 * half), count * 2 * half)
        return [
            pltpu.make_async_copy(phi.at[phi_rows], phi_hbm.at[phi_rows], departures.at[0]),
            pltpu.make_async_copy(turn.at[turn_rows], turn_hbm.at[turn_rows], departures.at[1]),
        ]

    @pl.loop(0, blocks // 8)
    def _(group):
        for j in range(8):
            block_phases(group * 8 + j)
            block_turns(group * 8 + j)
        for copy in leave(group * 8, 8):
            copy.start()

    for copy in leave(0, blocks):
        copy.wait()


def samples_kernel(
    blocks_local, arrived_hbm, owners_hbm, locals_hbm, count_hbm, noise_hbm, phi_hbm, turn_hbm,
    out, arrived, owners, locals_, count, noise, phi, turn, arrivals, table_arrivals,
    stacked, modes_rows, modes, partial, filtered, totals, ordered,
):
    sources = (arrived_hbm, owners_hbm, locals_hbm, count_hbm, noise_hbm)
    places = (arrived, owners, locals_, count, noise)
    copies = [
        pltpu.make_async_copy(source, place, arrivals.at[i])
        for i, (source, place) in enumerate(zip(sources, places))
    ]
    for copy in copies:
        copy.start()
    beams, sky_devices, rows, lanes = arrived.shape
    sky_orders = rows // 2
    all_sky = sky_devices * sky_orders
    parts = 2 * all_sky
    blocks = partial.shape[0] // 8
    total = turn.shape[0] // blocks
    orders = total // beams
    cycles = lanes // orders
    together = len(totals)
    unroll = max(1, 16 // together)

    steps = blocks // (together * unroll)

    def table_copies(step):
        phi_count, turn_count = phi.shape[0] // steps, turn.shape[0] // steps
        phi_rows = pl.ds(pl.multiple_of(step * phi_count, phi_count), phi_count)
        turn_rows = pl.ds(pl.multiple_of(step * turn_count, turn_count), turn_count)
        return [
            pltpu.make_async_copy(phi_hbm.at[phi_rows], phi.at[phi_rows], table_arrivals.at[step, 0]),
            pltpu.make_async_copy(turn_hbm.at[turn_rows], turn.at[turn_rows], table_arrivals.at[step, 1]),
        ]

    for step in range(steps):
        for copy in table_copies(step):
            copy.start()

    def cycle_of(s):
        return (owners[s] * blocks_local + locals_[s]) // CYCLE_BLOCKS

    width = together * parts
    if width > parts:
        stacked[...] = jnp.zeros_like(stacked)
    copies.pop(0).wait()
    for b in range(beams):
        for a in range(sky_devices):
            for c in range(2):
                piece = arrived[b, a, c * sky_orders : (c + 1) * sky_orders, :]
                start = c * all_sky + a * sky_orders
                stacked[b, start : start + sky_orders, :] = piece
        modes_rows[b * lanes : (b + 1) * lanes, :] = stacked[b].T
    for r in range(cycles):
        halves = [
            modes_rows[pl.ds(r + parity * cycles, total // 2, stride=2 * cycles), :]
            for parity in range(2)
        ]
        values = jnp.concatenate(halves, axis=0)
        for j in range(together):
            moved = pltpu.roll(values, j * parts, 1) if j else values
            modes[r, j] = moved.astype(BF16)
    for copy in copies:
        copy.wait()

    def gather(first):
        left = jnp.concatenate([modes[cycle_of(first + j), j] for j in range(together)], axis=0)
        table = phi[pl.ds(pl.multiple_of(first * parts, width), width), :]
        cells = jnp.dot(left, table, preferred_element_type=F32)
        rotation = turn[pl.ds(pl.multiple_of(first * total, together * total), together * total), :]
        turned = (cells * rotation).reshape(together, total // 8, 8, CELLS)
        kept = jnp.sum(turned, axis=1).reshape(together * 8, CELLS)
        partial[pl.ds(pl.multiple_of(first * 8, together * 8), together * 8), :] = kept

    @pl.loop(0, steps)
    def _(step):
        for copy in table_copies(step):
            copy.wait()
        for i in range(unroll):
            gather((step * unroll + i) * together)

    signal = partial[pl.ds(0, blocks, stride=8), :]
    for i in range(1, 8):
        signal = signal + partial[pl.ds(i, blocks, stride=8), :]
    valid = iota((blocks, CELLS), 0) * CELLS + iota((blocks, CELLS), 1) < count[0]
    signal = jnp.where(valid, signal, 0.0)
    clean = lax.dot_general(
        signal, noise[...], LAST_LAST, precision=lax.Precision.HIGHEST, preferred_element_type=F32
    )
    filtered[...] = jnp.where(valid, clean, 0.0)

    for one in totals:
        one[...] = jnp.zeros_like(one)
    half = orders // 2
    mine = lax.axis_index("beam") * half

    def spread(first):
        weighted = []
        for j in range(together):
            s = first + j
            rotation = jnp.concatenate(
                [turn[pl.ds(s * total + p * (total // 2) + mine, half), :] for p in range(2)], axis=0
            )
            weighted.append(rotation * filtered[pl.ds(s, 1), :])
        weighted = jnp.concatenate(weighted, axis=0).astype(BF16)
        table = phi[pl.ds(pl.multiple_of(first * parts, width), width), :]
        terms = lax.dot_general(weighted, table, LAST_LAST, preferred_element_type=F32)
        for j in range(together):
            row = pl.multiple_of(cycle_of(first + j) * orders, orders)
            here = totals[j]
            here[pl.ds(row, orders), :] += terms[j * orders : (j + 1) * orders]

    @pl.loop(0, steps)
    def _(step):
        for i in range(unroll):
            spread((step * unroll + i) * together)

    gathered = totals[0][...]
    which = iota(gathered.shape, 1) // parts
    for j in range(1, together):
        gathered = jnp.where(which == j, totals[j][...], gathered)
    totals[0][...] = gathered
    for k in range(orders):
        place = k // 2 + (k % 2) * half
        ordered[k * cycles : (k + 1) * cycles, :] = totals[0][pl.ds(place, cycles, stride=orders), :]
    turned = ordered[...].T
    summed = turned[0:parts]
    for j in range(1, together):
        summed = summed + turned[j * parts : (j + 1) * parts]
    for a in range(sky_devices):
        for c in range(2):
            start = c * all_sky + a * sky_orders
            out[a, c * sky_orders : (c + 1) * sky_orders, :] = summed[start : start + sky_orders]


def gradient_kernel(arrived, beam, wigner, outs, pieces):
    me = lax.axis_index("beam")
    orders, sky_orders, cycles, degrees = wigner.shape
    beam_real, beam_imag = beam[:, 0, :], beam[:, 1, :]
    diagonal = own_block(orders, cycles)
    modes = jnp.sum(arrived[...], axis=0).astype(BF16).astype(F32)
    width = pieces.shape[3]
    for m in range(sky_orders):
        spreads = []
        for c in range(2):
            row = modes[c * sky_orders + m : c * sky_orders + m + 1]
            spreads.append(jnp.where(diagonal, row, 0.0))
        left = jnp.concatenate(spreads, axis=0).astype(BF16)
        table = wigner[:, m].reshape(orders * cycles, degrees)
        harmonics = jnp.dot(left, table, preferred_element_type=F32)
        real, imag = harmonics[:orders], harmonics[orders:]
        first = jnp.sum(real * beam_real + imag * beam_imag, axis=0, keepdims=True)
        second = jnp.sum(imag * beam_real - real * beam_imag, axis=0, keepdims=True)
        both = jnp.concatenate([first, second], axis=0)
        for d in range(len(outs)):
            pieces[d ^ me, m] = both[:, d * width : (d + 1) * width]
    for j, out in enumerate(outs):
        out[...] = pieces[j].astype(out.dtype)


def exchange(pieces, axis):
    count = lax.axis_size(axis)
    return [pieces[0]] + [
        lax.ppermute(pieces[j], axis, [(i, i ^ j) for i in range(count)]) for j in range(1, count)
    ]


def local(
    sky_harmonics,
    beam_harmonics,
    wigner,
    order_map,
    block_owner,
    block_local,
    cell_offset,
    cell_fraction,
    beam_angle,
    sample_count,
    noise_weight,
):
    beams, sky_devices = lax.axis_size("beam"), lax.axis_size("ma")
    orders, sky_orders, cycles, degrees = wigner.shape
    total = orders * beams
    all_sky = sky_orders * sky_devices
    parts = 2 * all_sky
    blocks = block_local.shape[0]
    blocks_local = cycles // sky_devices * CYCLE_BLOCKS
    lanes = orders * cycles
    rows = 2 * sky_orders
    together = max(1, CELLS // parts)
    owners = block_owner.reshape(blocks)
    whole = pltpu.CompilerParams(vmem_limit_bytes=64 * 1024 * 1024)
    together_blocks = max(1, 16 // together) * together
    integers = [
        pltpu.SMEM((blocks,), jnp.int32),
        pltpu.SMEM((blocks,), jnp.int32),
    ]

    sent = pl.pallas_call(
        modes_kernel,
        out_shape=jax.ShapeDtypeStruct((rows, lanes), F32),
        in_specs=hbm(3),
        out_specs=vmem(1)[0],
        scratch_shapes=[
            pltpu.VMEM(sky_harmonics.shape, F32),
            pltpu.VMEM(beam_harmonics.shape, F32),
            pltpu.VMEM((sky_orders, orders, cycles, degrees), BF16),
            pltpu.SemaphoreType.DMA((2 + sky_orders,)),
        ],
        compiler_params=whole,
        name="modes",
    )(sky_harmonics, beam_harmonics, wigner)
    arrived = lax.all_gather(sent, ("beam", "ma"))

    tables = [
        jax.ShapeDtypeStruct((blocks * parts, CELLS), BF16),
        jax.ShapeDtypeStruct((blocks * total, CELLS), F32),
    ]
    samples = pltpu.VMEM((blocks, CELLS), F32)
    phi, turn = pl.pallas_call(
        functools.partial(tables_kernel, blocks_local),
        out_shape=tables,
        in_specs=hbm(6),
        out_specs=hbm(2),
        scratch_shapes=[
            samples,
            pltpu.SMEM((all_sky,), jnp.int32),
            *integers,
            pltpu.VMEM((blocks, CELLS), jnp.int32),
            samples,
            *[pltpu.VMEM(table.shape, table.dtype) for table in tables],
            pltpu.SemaphoreType.DMA((6,)),
            pltpu.SemaphoreType.DMA((2,)),
            pltpu.VMEM((CYCLE_BLOCKS, all_sky, CELLS), F32),
            pltpu.VMEM((CYCLE_BLOCKS, all_sky, CELLS), F32),
            samples,
            samples,
        ],
        compiler_params=whole,
        cost_estimate=pl.CostEstimate(flops=100_000_000, bytes_accessed=4_000_000, transcendentals=0),
        name="tables",
    )(
        beam_angle.reshape(blocks, CELLS),
        order_map, owners, block_local,
        cell_offset.reshape(blocks, CELLS),
        cell_fraction.reshape(blocks, CELLS),
    )

    grads = pl.pallas_call(
        functools.partial(samples_kernel, blocks_local),
        out_shape=jax.ShapeDtypeStruct((sky_devices, rows, lanes), F32),
        in_specs=hbm(7),
        out_specs=vmem(1)[0],
        scratch_shapes=[
            pltpu.VMEM((beams, sky_devices, rows, lanes), F32),
            *integers,
            pltpu.SMEM((1,), jnp.int32),
            pltpu.VMEM((CELLS, CELLS), F32),
            *[pltpu.VMEM(table.shape, table.dtype) for table in tables],
            pltpu.SemaphoreType.DMA((5,)),
            pltpu.SemaphoreType.DMA((blocks // together_blocks, 2)),
            pltpu.VMEM((beams, together * parts, lanes), F32),
            pltpu.VMEM((beams * lanes, together * parts), F32),
            pltpu.VMEM((cycles, together, total, together * parts), BF16),
            pltpu.VMEM((blocks * 8, CELLS), F32),
            samples,
            [pltpu.VMEM((lanes, together * parts), F32) for _ in range(together)],
            pltpu.VMEM((lanes, together * parts), F32),
        ],
        compiler_params=whole,
        name="samples",
    )(
        arrived.reshape(beams, sky_devices, rows, lanes),
        owners, block_local, sample_count, noise_weight, phi, turn,
    )
    grads = lax.all_to_all(grads, "ma", split_axis=0, concat_axis=0, tiled=True)

    width = degrees // beams
    shares = pl.pallas_call(
        gradient_kernel,
        out_shape=([jax.ShapeDtypeStruct((sky_orders, 2, width), BF16)] * beams,),
        in_specs=vmem(3),
        out_specs=(vmem(beams),),
        scratch_shapes=[pltpu.VMEM((beams, sky_orders, 2, width), F32)],
        name="gradient",
    )(grads, beam_harmonics, wigner)
    return sum(share.astype(F32) for share in exchange(shares[0], "beam"))


def solution(mesh):
    return jax.shard_map(
        local,
        mesh=mesh,
        in_specs=(
            P("ma", None, None),
            P("beam", None, None),
            P("beam", "ma", None, None),
            P(),
            P("ma", None),
            P("ma"),
            P("ma"),
            P("ma"),
            P("ma"),
            P("ma"),
            P(),
        ),
        out_specs=P("ma", None, "beam"),
        check_vma=False,
    )
```

```python
import functools
import math

import jax
import jax.numpy as jnp
from jax import lax
from jax.experimental import pallas as pl
from jax.experimental.pallas import tpu as pltpu
from jax.sharding import PartitionSpec as P

PHI = 4096
CELLS = 128
CYCLE_BLOCKS = PHI // CELLS
F32 = jnp.float32
BF16 = jnp.bfloat16
LAST_LAST = (((1,), (1,)), ((), ()))


def iota(shape, axis):
    return lax.broadcasted_iota(jnp.int32, shape, axis)


def vmem(count):
    return [pl.BlockSpec(memory_space=pltpu.VMEM)] * count


def smem(count):
    return [pl.BlockSpec(memory_space=pltpu.SMEM)] * count


def hbm(count):
    return [pl.BlockSpec(memory_space=pltpu.HBM)] * count


def sine_turns(z):
    square = z * z
    value = 39.53670603 * square - 76.54978229
    value = value * square + 81.60100407
    value = value * square - 41.34165503
    value = value * square + 6.28318516
    return value * z


def cosine_steps(steps):
    centred = ((steps + PHI // 2) & (PHI - 1)) - PHI // 2
    return sine_turns(0.25 - jnp.abs(centred).astype(F32) * (1.0 / PHI))


def every(ref, first, count, step):
    if ref.shape[1] == CELLS:
        return ref[pl.ds(first, count, stride=step), :]
    return jnp.concatenate([ref[first + i * step][None] for i in range(count)], axis=0)


def own_block(orders, cycles):
    shape = (orders, orders * cycles)
    return iota(shape, 1) // cycles == iota(shape, 0)


def modes_kernel(sky_hbm, beam_hbm, wigner_hbm, *refs):
    others = (len(refs) - 5) // 2
    out, beam, wigner = refs[others : others + 3]
    sky, arrivals = refs[-2:]
    sky_orders, orders, cycles, degrees = wigner.shape
    small = [
        pltpu.make_async_copy(sky_hbm, sky, arrivals.at[0]),
        pltpu.make_async_copy(beam_hbm, beam, arrivals.at[1]),
    ]
    large = [
        pltpu.make_async_copy(wigner_hbm.at[:, m], wigner.at[m], arrivals.at[2 + m])
        for m in range(sky_orders)
    ]
    later = [
        pltpu.make_async_copy(source, place, arrivals.at[2 + sky_orders + i])
        for i, (source, place) in enumerate(zip(refs[:others], refs[others + 3 : -2]))
    ]
    for copy in small + large + later:
        copy.start()
    for copy in small:
        copy.wait()
    beam_real, beam_imag = beam[:, 0, :], beam[:, 1, :]
    diagonal = own_block(orders, cycles)
    rows = [None] * (2 * sky_orders)
    for m in range(sky_orders):
        sky_real, sky_imag = sky[m, 0:1, :], sky[m, 1:2, :]
        first = sky_real * beam_real - sky_imag * beam_imag
        second = sky_real * beam_imag + sky_imag * beam_real
        product = jnp.concatenate([first, second], axis=0).astype(BF16)
        large[m].wait()
        table = wigner[m].reshape(orders * cycles, degrees)
        modes = lax.dot_general(product, table, LAST_LAST, preferred_element_type=F32)
        for c in range(2):
            part = jnp.where(diagonal, modes[c * orders : (c + 1) * orders], 0.0)
            rows[c * sky_orders + m] = jnp.sum(part, axis=0, keepdims=True)
    block = jnp.concatenate(rows, axis=0)
    for d in range(out.shape[0]):
        out[d] = block
    for copy in later:
        copy.wait()


def tables_kernel(
    blocks_local, sky_devices, order_hbm, owners_hbm, locals_hbm, angles, offsets, fractions,
    phi, turn, order_map, owners, locals_, arrivals, step_real, step_imag, cosines, sines,
):
    sources = (order_hbm, owners_hbm, locals_hbm)
    places = (order_map, owners, locals_)
    copies = [
        pltpu.make_async_copy(source, place, arrivals.at[i])
        for i, (source, place) in enumerate(zip(sources, places))
    ]
    for copy in copies:
        copy.start()
    orders = order_map.shape[0]
    blocks = offsets.shape[0]
    half = turn.shape[0] // blocks // 2

    part = angles[...] * (0.5 / math.pi)
    part = part - jnp.round(part)
    cosines[...] = sine_turns(0.25 - jnp.abs(part))
    folded = jnp.where(part > 0.25, 0.5 - part, jnp.where(part < -0.25, -0.5 - part, part))
    sines[...] = sine_turns(folded)

    for copy in copies:
        copy.wait()
    order = jnp.zeros((orders, CELLS), jnp.int32)
    row = iota((orders, CELLS), 0)
    lane = iota((orders, CELLS), 1)
    for m in range(orders):
        place = m % (orders // sky_devices) * sky_devices + m // (orders // sky_devices)
        order = jnp.where(row == place, order_map[m], order)

    def phase(steps):
        return cosine_steps(steps), cosine_steps(steps + PHI // 4)

    scaling = 1.0 / math.sqrt(orders)
    cell_real, cell_imag = phase(order * lane)
    cell_real, cell_imag = cell_real * scaling, cell_imag * scaling
    next_real, next_imag = phase(order)
    next_real = next_real - 1.0
    first_real, first_imag = phase(((order * CELLS) & (PHI - 1)) * lane)
    for j in range(CYCLE_BLOCKS):
        step_real[j] = jnp.broadcast_to(first_real[:, j : j + 1], (orders, CELLS))
        step_imag[j] = jnp.broadcast_to(first_imag[:, j : j + 1], (orders, CELLS))

    def block_phases(s):
        place = (owners[s] * blocks_local + locals_[s]) & (CYCLE_BLOCKS - 1)
        offset = jnp.broadcast_to(offsets[pl.ds(s, 1), :], (orders, CELLS))
        fraction = jnp.broadcast_to(fractions[pl.ds(s, 1), :], (orders, CELLS))
        real = jnp.take_along_axis(cell_real, offset, axis=1, mode="promise_in_bounds")
        imag = jnp.take_along_axis(cell_imag, offset, axis=1, mode="promise_in_bounds")
        base_real, base_imag = step_real[place], step_imag[place]
        left_real = real * base_real - imag * base_imag
        left_imag = real * base_imag + imag * base_real
        mix_real = 1.0 + fraction * next_real
        mix_imag = fraction * next_imag
        both = jnp.concatenate(
            [left_real * mix_real - left_imag * mix_imag, left_real * mix_imag + left_imag * mix_real],
            axis=0,
        )
        start = pl.multiple_of(s * 2 * orders, 2 * orders)
        phi[pl.ds(start, 2 * orders), :] = both.astype(BF16)

    scale = 1.0 / math.sqrt(2 * half)
    power = iota((8, CELLS), 0)

    def block_turns(s):
        one_real = jnp.broadcast_to(cosines[pl.ds(s, 1), :], (8, CELLS))
        one_imag = jnp.broadcast_to(sines[pl.ds(s, 1), :], (8, CELLS))
        step = (one_real, one_imag)
        odd = power & 1 == 1
        real, imag = jnp.where(odd, one_real * scale, scale), jnp.where(odd, one_imag * scale, 0.0)
        for bit in (2, 4):
            step = (step[0] * step[0] - step[1] * step[1], 2.0 * step[0] * step[1])
            taken = power & bit == bit
            by_real, by_imag = jnp.where(taken, step[0], 1.0), jnp.where(taken, step[1], 0.0)
            real, imag = real * by_real - imag * by_imag, real * by_imag + imag * by_real
        step = (step[0] * step[0] - step[1] * step[1], 2.0 * step[0] * step[1])
        start = pl.multiple_of(s * 2 * half, 2 * half)
        for j in range(half // 8):
            if j:
                real, imag = real * step[0] - imag * step[1], real * step[1] + imag * step[0]
            turn[pl.ds(start + 8 * j, 8), :] = real
            turn[pl.ds(start + half + 8 * j, 8), :] = real * one_imag + imag * one_real

    @pl.loop(0, blocks // 8)
    def _(group):
        for j in range(8):
            block_phases(group * 8 + j)
            block_turns(group * 8 + j)


def samples_kernel(
    blocks_local, owners_hbm, locals_hbm, count, arrived, noise, phi, turn,
    out, owners, locals_, arrivals,
    stacked, modes_rows, modes, partial, filtered, totals, ordered,
):
    sources = (owners_hbm, locals_hbm)
    places = (owners, locals_)
    copies = [
        pltpu.make_async_copy(source, place, arrivals.at[i])
        for i, (source, place) in enumerate(zip(sources, places))
    ]
    for copy in copies:
        copy.start()
    sky_devices, rows, lanes = out.shape
    parts = sky_devices * rows
    beams = arrived.shape[0] // parts
    blocks = partial.shape[0] // 8
    total = turn.shape[0] // blocks
    orders = total // beams
    cycles = lanes // orders
    together = len(totals)
    unroll = 16

    steps = blocks // (together * unroll)

    def cycle_of(s):
        return (owners[s] * blocks_local + locals_[s]) // CYCLE_BLOCKS

    width = together * parts
    for b in range(beams):
        for row in range(rows):
            some = every(arrived, b * parts + row, sky_devices, rows)
            for j in range(together):
                start = j * parts + row * sky_devices
                stacked[b, start : start + sky_devices, :] = some
        modes_rows[b * lanes : (b + 1) * lanes, :] = stacked[b].T
    lane_group = iota((total, width), 1) // parts
    for r in range(cycles):
        halves = [
            modes_rows[pl.ds(r + parity * cycles, total // 2, stride=2 * cycles), :]
            for parity in range(2)
        ]
        values = jnp.concatenate(halves, axis=0)
        for j in range(together):
            modes[r, j] = jnp.where(lane_group == j, values, 0.0).astype(BF16)
    for copy in copies:
        copy.wait()

    def gather(first):
        left = jnp.concatenate([modes[cycle_of(first + j), j] for j in range(together)], axis=0)
        table = phi[pl.ds(pl.multiple_of(first * parts, width), width), :]
        cells = jnp.dot(left, table, preferred_element_type=F32)
        rotation = turn[pl.ds(pl.multiple_of(first * total, together * total), together * total), :]
        turned = (cells * rotation).reshape(together, total // 8, 8, CELLS)
        kept = jnp.sum(turned, axis=1).reshape(together * 8, CELLS)
        partial[pl.ds(pl.multiple_of(first * 8, together * 8), together * 8), :] = kept

    @pl.loop(0, steps)
    def _(step):
        for i in range(unroll):
            gather((step * unroll + i) * together)

    signal = partial[pl.ds(0, blocks, stride=8), :]
    for i in range(1, 8):
        signal = signal + partial[pl.ds(i, blocks, stride=8), :]
    valid = iota((blocks, CELLS), 0) * CELLS + iota((blocks, CELLS), 1) < count[0]
    signal = jnp.where(valid, signal, 0.0)
    clean = lax.dot_general(
        signal.astype(BF16), noise[...].astype(BF16), LAST_LAST, preferred_element_type=F32
    )
    filtered[...] = jnp.where(valid, clean, 0.0)

    for one in totals:
        one[...] = jnp.zeros_like(one)
    half = orders // 2
    mine = lax.axis_index("beam") * half

    def spread(first):
        weighted = []
        for j in range(together):
            s = first + j
            rotation = jnp.concatenate(
                [turn[pl.ds(s * total + p * (total // 2) + mine, half), :] for p in range(2)], axis=0
            )
            weighted.append(rotation * filtered[pl.ds(s, 1), :])
        weighted = jnp.concatenate(weighted, axis=0).astype(BF16)
        table = phi[pl.ds(pl.multiple_of(first * parts, width), width), :]
        terms = lax.dot_general(weighted, table, LAST_LAST, preferred_element_type=F32)
        for j in range(together):
            row = pl.multiple_of(cycle_of(first + j) * orders, orders)
            here = totals[j]
            here[pl.ds(row, orders), :] += terms[j * orders : (j + 1) * orders]

    @pl.loop(0, steps)
    def _(step):
        for i in range(unroll):
            spread((step * unroll + i) * together)

    gathered = totals[0][...]
    which = iota(gathered.shape, 1) // parts
    for j in range(1, together):
        gathered = jnp.where(which == j, totals[j][...], gathered)
    totals[0][...] = gathered
    for k in range(orders):
        place = k // 2 + (k % 2) * half
        ordered[k * cycles : (k + 1) * cycles, :] = totals[0][pl.ds(place, cycles, stride=orders), :]
    turned = ordered[...].T
    summed = turned[0:parts]
    for j in range(1, together):
        summed = summed + turned[j * parts : (j + 1) * parts]
    for row in range(rows):
        out[:, row, :] = summed[row * sky_devices : (row + 1) * sky_devices]


def gradient_kernel(arrived, beam, wigner, outs, pieces):
    me = lax.axis_index("beam")
    sky_orders, orders, cycles, degrees = wigner.shape
    beam_real, beam_imag = beam[:, 0, :], beam[:, 1, :]
    diagonal = own_block(orders, cycles)
    modes = jnp.sum(arrived[...], axis=0).astype(BF16).astype(F32)
    width = pieces.shape[3]
    for m in range(sky_orders):
        spreads = []
        for c in range(2):
            row = modes[c * sky_orders + m : c * sky_orders + m + 1]
            spreads.append(jnp.where(diagonal, row, 0.0))
        left = jnp.concatenate(spreads, axis=0).astype(BF16)
        table = wigner[m].reshape(orders * cycles, degrees)
        harmonics = jnp.dot(left, table, preferred_element_type=F32)
        real, imag = harmonics[:orders], harmonics[orders:]
        first = jnp.sum(real * beam_real + imag * beam_imag, axis=0, keepdims=True)
        second = jnp.sum(imag * beam_real - real * beam_imag, axis=0, keepdims=True)
        both = jnp.concatenate([first, second], axis=0)
        for d in range(len(outs)):
            pieces[d ^ me, m] = both[:, d * width : (d + 1) * width]
    for j, out in enumerate(outs):
        out[...] = pieces[j].astype(out.dtype)


def exchange(pieces, axis):
    count = lax.axis_size(axis)
    return [pieces[0]] + [
        lax.ppermute(pieces[j], axis, [(i, i ^ j) for i in range(count)]) for j in range(1, count)
    ]


def local(
    sky_harmonics,
    beam_harmonics,
    wigner,
    order_map,
    block_owner,
    block_local,
    cell_offset,
    cell_fraction,
    beam_angle,
    sample_count,
    noise_weight,
):
    beams, sky_devices = lax.axis_size("beam"), lax.axis_size("ma")
    orders, sky_orders, cycles, degrees = wigner.shape
    total = orders * beams
    all_sky = sky_orders * sky_devices
    parts = 2 * all_sky
    blocks = block_local.shape[0]
    blocks_local = cycles // sky_devices * CYCLE_BLOCKS
    lanes = orders * cycles
    rows = 2 * sky_orders
    together = max(1, CELLS // parts)
    owners = block_owner.reshape(blocks)
    limit = pltpu.CompilerParams(vmem_limit_bytes=40 * 1024 * 1024)
    integers = [
        pltpu.SMEM((blocks,), jnp.int32),
        pltpu.SMEM((blocks,), jnp.int32),
    ]

    later = (
        order_map, owners, block_local,
        beam_angle.reshape(blocks, CELLS),
        cell_offset.reshape(blocks, CELLS),
        cell_fraction.reshape(blocks, CELLS),
        noise_weight,
    )
    sources = [
        pltpu.with_memory_space_constraint(array, pltpu.HBM)
        for array in (sky_harmonics, beam_harmonics, wigner, *later)
    ]
    kept = [
        pltpu.VMEM((beams * sky_devices, rows, lanes), F32),
        pltpu.VMEM(beam_harmonics.shape, F32),
        pltpu.VMEM((sky_orders, orders, cycles, degrees), BF16),
        *[pltpu.VMEM(array.shape, array.dtype) for array in later],
    ]
    sent, beam, table, order_map, owners, places, angles, offsets, fractions, noise = pl.pallas_call(
        modes_kernel,
        out_shape=kept,
        in_specs=hbm(3 + len(later)),
        out_specs=vmem(len(kept)),
        scratch_shapes=[
            pltpu.VMEM(sky_harmonics.shape, F32),
            pltpu.SemaphoreType.DMA((2 + sky_orders + len(later),)),
        ],
        compiler_params=limit,
        name="modes",
    )(*sources)
    arrived = lax.all_to_all(sent, ("beam", "ma"), split_axis=0, concat_axis=0, tiled=True)

    tables = [
        jax.ShapeDtypeStruct((blocks * parts, CELLS), BF16),
        jax.ShapeDtypeStruct((blocks * total, CELLS), F32),
    ]
    samples = pltpu.VMEM((blocks, CELLS), F32)
    phi, turn = pl.pallas_call(
        functools.partial(tables_kernel, blocks_local, sky_devices),
        out_shape=tables,
        in_specs=hbm(3) + vmem(3),
        out_specs=vmem(2),
        scratch_shapes=[
            pltpu.SMEM((all_sky,), jnp.int32),
            *integers,
            pltpu.SemaphoreType.DMA((3,)),
            pltpu.VMEM((CYCLE_BLOCKS, all_sky, CELLS), F32),
            pltpu.VMEM((CYCLE_BLOCKS, all_sky, CELLS), F32),
            samples,
            samples,
        ],
        compiler_params=limit,
        cost_estimate=pl.CostEstimate(flops=100_000_000, bytes_accessed=4_000_000, transcendentals=0),
        name="tables",
    )(
        order_map, owners, places, angles, offsets, fractions,
    )

    grads = pl.pallas_call(
        functools.partial(samples_kernel, blocks_local),
        out_shape=jax.ShapeDtypeStruct((sky_devices, rows, lanes), F32),
        in_specs=hbm(2) + smem(1) + vmem(4),
        out_specs=vmem(1)[0],
        scratch_shapes=[
            *integers,
            pltpu.SemaphoreType.DMA((2,)),
            pltpu.VMEM((beams, together * parts, lanes), F32),
            pltpu.VMEM((beams * lanes, together * parts), F32),
            pltpu.VMEM((cycles, together, total, together * parts), BF16),
            pltpu.VMEM((blocks * 8, CELLS), F32),
            samples,
            [pltpu.VMEM((lanes, together * parts), F32) for _ in range(together)],
            pltpu.VMEM((lanes, together * parts), F32),
        ],
        compiler_params=limit,
        name="samples",
    )(
        owners, places, sample_count,
        arrived.reshape(beams * parts, lanes), noise, phi, turn,
    )
    grads = lax.all_to_all(grads, "ma", split_axis=0, concat_axis=0, tiled=True)

    width = degrees // beams
    shares = pl.pallas_call(
        gradient_kernel,
        out_shape=([jax.ShapeDtypeStruct((sky_orders, 2, width), BF16)] * beams,),
        in_specs=vmem(3),
        out_specs=(vmem(beams),),
        scratch_shapes=[pltpu.VMEM((beams, sky_orders, 2, width), F32)],
        compiler_params=limit,
        name="gradient",
    )(grads, beam, table)
    return sum(share.astype(F32) for share in exchange(shares[0], "beam"))


def solution(mesh):
    return jax.shard_map(
        local,
        mesh=mesh,
        in_specs=(
            P("ma", None, None),
            P("beam", None, None),
            P("beam", "ma", None, None),
            P(),
            P("ma", None),
            P("ma"),
            P("ma"),
            P("ma"),
            P("ma"),
            P("ma"),
            P(),
        ),
        out_specs=P("ma", None, "beam"),
        check_vma=False,
    )
```

```python
import functools
import math

import jax
import jax.numpy as jnp
from jax import lax
from jax.experimental import pallas as pl
from jax.experimental.pallas import tpu as pltpu
from jax.sharding import PartitionSpec as P

PHI = 4096
CELLS = 128
CYCLE_BLOCKS = PHI // CELLS
F32 = jnp.float32
BF16 = jnp.bfloat16
LAST_LAST = (((1,), (1,)), ((), ()))


def iota(shape, axis):
    return lax.broadcasted_iota(jnp.int32, shape, axis)


def vmem(count):
    return [pl.BlockSpec(memory_space=pltpu.VMEM)] * count


def smem(count):
    return [pl.BlockSpec(memory_space=pltpu.SMEM)] * count


def hbm(count):
    return [pl.BlockSpec(memory_space=pltpu.HBM)] * count


def sine_turns(z):
    square = z * z
    value = 39.53670603 * square - 76.54978229
    value = value * square + 81.60100407
    value = value * square - 41.34165503
    value = value * square + 6.28318516
    return value * z


def cosine_steps(steps):
    centred = ((steps + PHI // 2) & (PHI - 1)) - PHI // 2
    return sine_turns(0.25 - jnp.abs(centred).astype(F32) * (1.0 / PHI))


def every(ref, first, count, step):
    if ref.shape[1] == CELLS:
        return ref[pl.ds(first, count, stride=step), :]
    return jnp.concatenate([ref[first + i * step][None] for i in range(count)], axis=0)


def bring(sources, places, semaphores, first):
    copies = [
        pltpu.make_async_copy(source, place, semaphores.at[first + i])
        for i, (source, place) in enumerate(zip(sources, places))
    ]
    for copy in copies:
        copy.start()
    return copies


def own_block(orders, cycles):
    shape = (orders, orders * cycles)
    return iota(shape, 1) // cycles == iota(shape, 0)


def modes_kernel(sky_hbm, beam_hbm, wigner_hbm, out, sky, beam, wigner, arrivals):
    sky_orders, orders, cycles, degrees = wigner.shape
    small = bring((sky_hbm, beam_hbm), (sky, beam), arrivals, 0)
    large = bring([wigner_hbm.at[:, m] for m in range(sky_orders)], [wigner.at[m] for m in range(sky_orders)], arrivals, 2)
    for copy in small:
        copy.wait()
    beam_real, beam_imag = beam[:, 0, :], beam[:, 1, :]
    diagonal = own_block(orders, cycles)
    rows = [None] * (2 * sky_orders)
    for m in range(sky_orders):
        sky_real, sky_imag = sky[m, 0:1, :], sky[m, 1:2, :]
        first = sky_real * beam_real - sky_imag * beam_imag
        second = sky_real * beam_imag + sky_imag * beam_real
        product = jnp.concatenate([first, second], axis=0).astype(BF16)
        large[m].wait()
        table = wigner[m].reshape(orders * cycles, degrees)
        modes = lax.dot_general(product, table, LAST_LAST, preferred_element_type=F32)
        for c in range(2):
            part = jnp.where(diagonal, modes[c * orders : (c + 1) * orders], 0.0)
            rows[c * sky_orders + m] = jnp.sum(part, axis=0, keepdims=True)
    block = jnp.concatenate(rows, axis=0)
    for d in range(out.shape[0]):
        out[d] = block


def tables_kernel(
    blocks_local, sky_devices,
    order_hbm, owners_hbm, locals_hbm, angles_hbm, offsets_hbm, fractions_hbm,
    phi, turn, own, order_map, owners, locals_, angles, offsets, fractions, arrivals,
    step_real, step_imag, cosines, sines, rows_of,
):
    sources = (order_hbm, owners_hbm, locals_hbm, angles_hbm, offsets_hbm, fractions_hbm)
    places = (order_map, owners, locals_, angles, offsets, fractions)
    copies = bring(sources, places, arrivals, 0)
    orders = order_map.shape[0]
    blocks = offsets.shape[0]
    half = turn.shape[0] // blocks // 2
    own_half = own.shape[0] // blocks // 2

    copies[0].wait()
    order = jnp.zeros((orders, CELLS), jnp.int32)
    row = iota((orders, CELLS), 0)
    lane = iota((orders, CELLS), 1)
    for m in range(orders):
        place = m % (orders // sky_devices) * sky_devices + m // (orders // sky_devices)
        order = jnp.where(row == place, order_map[m], order)

    def phase(steps):
        return cosine_steps(steps), cosine_steps(steps + PHI // 4)

    scaling = 1.0 / math.sqrt(orders)
    cell_real, cell_imag = phase(order * lane)
    cell_real, cell_imag = cell_real * scaling, cell_imag * scaling
    next_real, next_imag = phase(order)
    next_real = next_real - 1.0
    first_real, first_imag = phase(((order * CELLS) & (PHI - 1)) * lane)
    for j in range(CYCLE_BLOCKS):
        step_real[j] = jnp.broadcast_to(first_real[:, j : j + 1], (orders, CELLS))
        step_imag[j] = jnp.broadcast_to(first_imag[:, j : j + 1], (orders, CELLS))

    for copy in copies[1:]:
        copy.wait()
    part = angles[...] * (0.5 / math.pi)
    part = part - jnp.round(part)
    cosines[...] = sine_turns(0.25 - jnp.abs(part))
    folded = jnp.where(part > 0.25, 0.5 - part, jnp.where(part < -0.25, -0.5 - part, part))
    sines[...] = sine_turns(folded)

    def block_phases(s):
        place = (owners[s] * blocks_local + locals_[s]) & (CYCLE_BLOCKS - 1)
        offset = jnp.broadcast_to(offsets[pl.ds(s, 1), :], (orders, CELLS))
        fraction = jnp.broadcast_to(fractions[pl.ds(s, 1), :], (orders, CELLS))
        real = jnp.take_along_axis(cell_real, offset, axis=1, mode="promise_in_bounds")
        imag = jnp.take_along_axis(cell_imag, offset, axis=1, mode="promise_in_bounds")
        base_real, base_imag = step_real[place], step_imag[place]
        left_real = real * base_real - imag * base_imag
        left_imag = real * base_imag + imag * base_real
        mix_real = 1.0 + fraction * next_real
        mix_imag = fraction * next_imag
        both = jnp.concatenate(
            [left_real * mix_real - left_imag * mix_imag, left_real * mix_imag + left_imag * mix_real],
            axis=0,
        )
        start = pl.multiple_of(s * 2 * orders, 2 * orders)
        phi[pl.ds(start, 2 * orders), :] = both.astype(BF16)

    scale = 1.0 / math.sqrt(2 * half)
    power = iota((8, CELLS), 0)

    def block_turns(s):
        one_real = jnp.broadcast_to(cosines[pl.ds(s, 1), :], (8, CELLS))
        one_imag = jnp.broadcast_to(sines[pl.ds(s, 1), :], (8, CELLS))
        step = (one_real, one_imag)
        odd = power & 1 == 1
        real, imag = jnp.where(odd, one_real * scale, scale), jnp.where(odd, one_imag * scale, 0.0)
        for bit in (2, 4):
            step = (step[0] * step[0] - step[1] * step[1], 2.0 * step[0] * step[1])
            taken = power & bit == bit
            by_real, by_imag = jnp.where(taken, step[0], 1.0), jnp.where(taken, step[1], 0.0)
            real, imag = real * by_real - imag * by_imag, real * by_imag + imag * by_real
        step = (step[0] * step[0] - step[1] * step[1], 2.0 * step[0] * step[1])
        evens, odds = [], []
        for j in range(half // 8):
            if j:
                real, imag = real * step[0] - imag * step[1], real * step[1] + imag * step[0]
            evens.append(real)
            odds.append(real * one_imag + imag * one_real)
        all_rows = jnp.concatenate(evens + odds, axis=0)
        turn[pl.ds(pl.multiple_of(s * 2 * half, 2 * half), 2 * half), :] = all_rows.astype(BF16)
        rows_of[...] = all_rows
        return [rows_of[pl.ds(p * half + mine, own_half), :] for p in range(2)]

    mine = lax.axis_index("beam") * own_half
    pair = 16 // (2 * own_half)

    @pl.loop(0, blocks // 8)
    def _(group):
        for j in range(0, 8, pair):
            kept = []
            for i in range(pair):
                block_phases(group * 8 + j + i)
                kept += block_turns(group * 8 + j + i)
            start = pl.multiple_of((group * 8 + j) * 2 * own_half, 16)
            own[pl.ds(start, 16), :] = jnp.concatenate(kept, axis=0).astype(BF16)


def samples_kernel(
    blocks_local, owners_hbm, locals_hbm, noise_hbm, count, arrived, phi, turn, own,
    out, owners, locals_, noise, arrivals,
    stacked, modes_rows, modes, partial, filtered, totals, ordered,
):
    copies = bring((owners_hbm, locals_hbm, noise_hbm), (owners, locals_, noise), arrivals, 0)
    sky_devices, rows, lanes = out.shape
    parts = sky_devices * rows
    beams = arrived.shape[0] // parts
    blocks = partial.shape[0] // 8
    total = turn.shape[0] // blocks
    orders = total // beams
    cycles = lanes // orders
    together = len(totals)
    unroll = 16

    steps = blocks // (together * unroll)

    def cycle_of(s):
        return (owners[s] * blocks_local + locals_[s]) // CYCLE_BLOCKS

    width = together * parts
    for b in range(beams):
        for row in range(rows):
            some = every(arrived, b * parts + row, sky_devices, rows)
            for j in range(together):
                start = j * parts + row * sky_devices
                stacked[b, start : start + sky_devices, :] = some
        modes_rows[b * lanes : (b + 1) * lanes, :] = stacked[b].T
    lane_group = iota((total, width), 1) // parts
    for r in range(cycles):
        halves = [
            modes_rows[pl.ds(r + parity * cycles, total // 2, stride=2 * cycles), :]
            for parity in range(2)
        ]
        values = jnp.concatenate(halves, axis=0)
        for j in range(together):
            modes[r, j] = jnp.where(lane_group == j, values, 0.0).astype(BF16)
    for copy in copies:
        copy.wait()

    def gather(first):
        left = jnp.concatenate([modes[cycle_of(first + j), j] for j in range(together)], axis=0)
        table = phi[pl.ds(pl.multiple_of(first * parts, width), width), :]
        cells = jnp.dot(left, table, preferred_element_type=F32)
        rotation = turn[pl.ds(pl.multiple_of(first * total, together * total), together * total), :]
        turned = (cells * rotation.astype(F32)).reshape(together, total // 8, 8, CELLS)
        kept = jnp.sum(turned, axis=1).reshape(together * 8, CELLS)
        partial[pl.ds(pl.multiple_of(first * 8, together * 8), together * 8), :] = kept

    @pl.loop(0, steps)
    def _(step):
        for i in range(unroll):
            gather((step * unroll + i) * together)

    signal = partial[pl.ds(0, blocks, stride=8), :]
    for i in range(1, 8):
        signal = signal + partial[pl.ds(i, blocks, stride=8), :]
    valid = iota((blocks, CELLS), 0) * CELLS + iota((blocks, CELLS), 1) < count[0]
    signal = jnp.where(valid, signal, 0.0)
    clean = lax.dot_general(
        signal.astype(BF16), noise[...].astype(BF16), LAST_LAST, preferred_element_type=F32
    )
    filtered[...] = jnp.where(valid, clean, 0.0)

    for one in totals:
        one[...] = jnp.zeros_like(one)
    half = orders // 2

    def spread(first):
        rotation = own[pl.ds(pl.multiple_of(first * orders, 16), together * orders), :].astype(F32)
        weighted = [
            rotation[j * orders : (j + 1) * orders] * filtered[pl.ds(first + j, 1), :]
            for j in range(together)
        ]
        weighted = jnp.concatenate(weighted, axis=0).astype(BF16)
        table = phi[pl.ds(pl.multiple_of(first * parts, width), width), :]
        terms = lax.dot_general(weighted, table, LAST_LAST, preferred_element_type=F32)
        for j in range(together):
            row = pl.multiple_of(cycle_of(first + j) * orders, orders)
            here = totals[j]
            here[pl.ds(row, orders), :] += terms[j * orders : (j + 1) * orders]

    @pl.loop(0, steps)
    def _(step):
        for i in range(unroll):
            spread((step * unroll + i) * together)

    gathered = totals[0][...]
    which = iota(gathered.shape, 1) // parts
    for j in range(1, together):
        gathered = jnp.where(which == j, totals[j][...], gathered)
    totals[0][...] = gathered
    for k in range(orders):
        place = k // 2 + (k % 2) * half
        ordered[k * cycles : (k + 1) * cycles, :] = totals[0][pl.ds(place, cycles, stride=orders), :]
    turned = ordered[...].T
    summed = turned[0:parts]
    for j in range(1, together):
        summed = summed + turned[j * parts : (j + 1) * parts]
    for row in range(rows):
        out[:, row, :] = summed[row * sky_devices : (row + 1) * sky_devices]


def gradient_kernel(arrived, beam, wigner, outs, pieces):
    me = lax.axis_index("beam")
    orders, sky_orders, cycles, degrees = wigner.shape
    beam_real, beam_imag = beam[:, 0, :], beam[:, 1, :]
    diagonal = own_block(orders, cycles)
    modes = jnp.sum(arrived[...], axis=0).astype(BF16).astype(F32)
    width = pieces.shape[3]
    for m in range(sky_orders):
        spreads = []
        for c in range(2):
            row = modes[c * sky_orders + m : c * sky_orders + m + 1]
            spreads.append(jnp.where(diagonal, row, 0.0))
        left = jnp.concatenate(spreads, axis=0).astype(BF16)
        table = wigner[:, m].reshape(orders * cycles, degrees)
        harmonics = jnp.dot(left, table, preferred_element_type=F32)
        real, imag = harmonics[:orders], harmonics[orders:]
        first = jnp.sum(real * beam_real + imag * beam_imag, axis=0, keepdims=True)
        second = jnp.sum(imag * beam_real - real * beam_imag, axis=0, keepdims=True)
        both = jnp.concatenate([first, second], axis=0)
        for d in range(len(outs)):
            pieces[d ^ me, m] = both[:, d * width : (d + 1) * width]
    for j, out in enumerate(outs):
        out[...] = pieces[j].astype(out.dtype)


def exchange(pieces, axis):
    count = lax.axis_size(axis)
    return [pieces[0]] + [
        lax.ppermute(pieces[j], axis, [(i, i ^ j) for i in range(count)]) for j in range(1, count)
    ]


def local(
    sky_harmonics,
    beam_harmonics,
    wigner,
    order_map,
    block_owner,
    block_local,
    cell_offset,
    cell_fraction,
    beam_angle,
    sample_count,
    noise_weight,
):
    beams, sky_devices = lax.axis_size("beam"), lax.axis_size("ma")
    orders, sky_orders, cycles, degrees = wigner.shape
    total = orders * beams
    all_sky = sky_orders * sky_devices
    parts = 2 * all_sky
    blocks = block_local.shape[0]
    blocks_local = cycles // sky_devices * CYCLE_BLOCKS
    lanes = orders * cycles
    rows = 2 * sky_orders
    together = max(1, CELLS // parts)
    owners = block_owner.reshape(blocks)
    limit = pltpu.CompilerParams(vmem_limit_bytes=32 * 1024 * 1024)
    integers = [
        pltpu.SMEM((blocks,), jnp.int32),
        pltpu.SMEM((blocks,), jnp.int32),
    ]

    def pinned(*arrays):
        return [pltpu.with_memory_space_constraint(array, pltpu.HBM) for array in arrays]

    sent = pl.pallas_call(
        modes_kernel,
        out_shape=jax.ShapeDtypeStruct((beams * sky_devices, rows, lanes), F32),
        in_specs=hbm(3),
        out_specs=vmem(1)[0],
        scratch_shapes=[
            pltpu.VMEM(sky_harmonics.shape, F32),
            pltpu.VMEM(beam_harmonics.shape, F32),
            pltpu.VMEM((sky_orders, orders, cycles, degrees), BF16),
            pltpu.SemaphoreType.DMA((2 + sky_orders,)),
        ],
        compiler_params=limit,
        name="modes",
    )(*pinned(sky_harmonics, beam_harmonics, wigner))
    arrived = lax.all_to_all(sent, ("beam", "ma"), split_axis=0, concat_axis=0, tiled=True)

    samples = pltpu.VMEM((blocks, CELLS), F32)
    phi, turn, own = pl.pallas_call(
        functools.partial(tables_kernel, blocks_local, sky_devices),
        out_shape=[
            pltpu.VMEM((blocks * parts, CELLS), BF16),
            pltpu.VMEM((blocks * total, CELLS), BF16),
            pltpu.VMEM((blocks * orders, CELLS), BF16),
        ],
        in_specs=hbm(6),
        out_specs=vmem(3),
        scratch_shapes=[
            pltpu.SMEM((all_sky,), jnp.int32),
            *integers,
            samples,
            pltpu.VMEM((blocks, CELLS), jnp.int32),
            samples,
            pltpu.SemaphoreType.DMA((6,)),
            pltpu.VMEM((CYCLE_BLOCKS, all_sky, CELLS), F32),
            pltpu.VMEM((CYCLE_BLOCKS, all_sky, CELLS), F32),
            samples,
            samples,
            pltpu.VMEM((total, CELLS), F32),
        ],
        compiler_params=limit,
        cost_estimate=pl.CostEstimate(flops=100_000_000, bytes_accessed=4_000_000, transcendentals=0),
        name="tables",
    )(
        *pinned(
            order_map, owners, block_local,
            beam_angle.reshape(blocks, CELLS),
            cell_offset.reshape(blocks, CELLS),
            cell_fraction.reshape(blocks, CELLS),
        )
    )

    grads = pl.pallas_call(
        functools.partial(samples_kernel, blocks_local),
        out_shape=jax.ShapeDtypeStruct((sky_devices, rows, lanes), F32),
        in_specs=hbm(3) + smem(1) + vmem(4),
        out_specs=vmem(1)[0],
        scratch_shapes=[
            *integers,
            pltpu.VMEM((CELLS, CELLS), F32),
            pltpu.SemaphoreType.DMA((3,)),
            pltpu.VMEM((beams, together * parts, lanes), F32),
            pltpu.VMEM((beams * lanes, together * parts), F32),
            pltpu.VMEM((cycles, together, total, together * parts), BF16),
            pltpu.VMEM((blocks * 8, CELLS), F32),
            samples,
            [pltpu.VMEM((lanes, together * parts), F32) for _ in range(together)],
            pltpu.VMEM((lanes, together * parts), F32),
        ],
        compiler_params=limit,
        name="samples",
    )(
        *pinned(owners, block_local, noise_weight),
        sample_count, arrived.reshape(beams * parts, lanes), phi, turn, own,
    )
    grads = lax.all_to_all(grads, "ma", split_axis=0, concat_axis=0, tiled=True)

    width = degrees // beams
    shares = pl.pallas_call(
        gradient_kernel,
        out_shape=([jax.ShapeDtypeStruct((sky_orders, 2, width), BF16)] * beams,),
        in_specs=vmem(3),
        out_specs=(vmem(beams),),
        scratch_shapes=[pltpu.VMEM((beams, sky_orders, 2, width), F32)],
        compiler_params=limit,
        name="gradient",
    )(grads, beam_harmonics, wigner)
    return sum(share.astype(F32) for share in exchange(shares[0], "beam"))


def solution(mesh):
    return jax.shard_map(
        local,
        mesh=mesh,
        in_specs=(
            P("ma", None, None),
            P("beam", None, None),
            P("beam", "ma", None, None),
            P(),
            P("ma", None),
            P("ma"),
            P("ma"),
            P("ma"),
            P("ma"),
            P("ma"),
            P(),
        ),
        out_specs=P("ma", None, "beam"),
        check_vma=False,
    )
```

```python
import functools
import math

import jax
import jax.numpy as jnp
from jax import lax
from jax.experimental import pallas as pl
from jax.experimental.pallas import tpu as pltpu
from jax.sharding import PartitionSpec as P

PHI = 4096
CELLS = 128
CYCLE_BLOCKS = PHI // CELLS
F32 = jnp.float32
BF16 = jnp.bfloat16
LAST_LAST = (((1,), (1,)), ((), ()))


def iota(shape, axis):
    return lax.broadcasted_iota(jnp.int32, shape, axis)


def vmem(count):
    return [pl.BlockSpec(memory_space=pltpu.VMEM)] * count


def smem(count):
    return [pl.BlockSpec(memory_space=pltpu.SMEM)] * count


def hbm(count):
    return [pl.BlockSpec(memory_space=pltpu.HBM)] * count


def sine_turns(z):
    square = z * z
    value = 39.53670603 * square - 76.54978229
    value = value * square + 81.60100407
    value = value * square - 41.34165503
    value = value * square + 6.28318516
    return value * z


def cosine_steps(steps):
    centred = ((steps + PHI // 2) & (PHI - 1)) - PHI // 2
    return sine_turns(0.25 - jnp.abs(centred).astype(F32) * (1.0 / PHI))


def every(ref, first, count, step):
    if ref.shape[1] == CELLS:
        return ref[pl.ds(first, count, stride=step), :]
    return jnp.concatenate([ref[first + i * step][None] for i in range(count)], axis=0)


def bring(sources, places, semaphores, first):
    copies = [
        pltpu.make_async_copy(source, place, semaphores.at[first + i])
        for i, (source, place) in enumerate(zip(sources, places))
    ]
    for copy in copies:
        copy.start()
    return copies


def own_block(orders, cycles):
    shape = (orders, orders * cycles)
    return iota(shape, 1) // cycles == iota(shape, 0)


def modes_kernel(sky_hbm, beam_hbm, wigner_hbm, out, sky, beam, wigner, arrivals):
    sky_orders, orders, cycles, degrees = wigner.shape
    small = bring((sky_hbm, beam_hbm), (sky, beam), arrivals, 0)
    large = bring([wigner_hbm.at[:, m] for m in range(sky_orders)], [wigner.at[m] for m in range(sky_orders)], arrivals, 2)
    for copy in small:
        copy.wait()
    beam_real, beam_imag = beam[:, 0, :], beam[:, 1, :]
    diagonal = own_block(orders, cycles)
    rows = [None] * (2 * sky_orders)
    for m in range(sky_orders):
        sky_real, sky_imag = sky[m, 0:1, :], sky[m, 1:2, :]
        first = sky_real * beam_real - sky_imag * beam_imag
        second = sky_real * beam_imag + sky_imag * beam_real
        product = jnp.concatenate([first, second], axis=0).astype(BF16)
        large[m].wait()
        table = wigner[m].reshape(orders * cycles, degrees)
        modes = lax.dot_general(table, product, LAST_LAST, preferred_element_type=F32).T
        for c in range(2):
            part = jnp.where(diagonal, modes[c * orders : (c + 1) * orders], 0.0)
            rows[c * sky_orders + m] = jnp.sum(part, axis=0, keepdims=True)
    block = jnp.concatenate(rows, axis=0).astype(BF16)
    for d in range(out.shape[0]):
        out[d] = block


def tables_kernel(
    blocks_local, sky_devices,
    order_hbm, owners_hbm, locals_hbm, angles_hbm, offsets_hbm, fractions_hbm,
    phi, turn, own, order_map, owners, locals_, angles, offsets, fractions, arrivals,
    step_real, step_imag, cosines, sines, rows_of,
):
    sources = (order_hbm, owners_hbm, locals_hbm, angles_hbm, offsets_hbm, fractions_hbm)
    places = (order_map, owners, locals_, angles, offsets, fractions)
    copies = bring(sources, places, arrivals, 0)
    orders = order_map.shape[0]
    blocks = offsets.shape[0]
    half = turn.shape[0] // blocks // 2
    own_half = own.shape[0] // blocks // 2

    copies[0].wait()
    order = jnp.zeros((orders, CELLS), jnp.int32)
    row = iota((orders, CELLS), 0)
    lane = iota((orders, CELLS), 1)
    for m in range(orders):
        place = m % (orders // sky_devices) * sky_devices + m // (orders // sky_devices)
        order = jnp.where(row == place, order_map[m], order)

    def phase(steps):
        return cosine_steps(steps), cosine_steps(steps + PHI // 4)

    scaling = 1.0 / math.sqrt(orders)
    cell_real, cell_imag = phase(order * lane)
    cell_real, cell_imag = cell_real * scaling, cell_imag * scaling
    next_real, next_imag = phase(order)
    next_real = next_real - 1.0
    first_real, first_imag = phase(((order * CELLS) & (PHI - 1)) * lane)
    for j in range(CYCLE_BLOCKS):
        step_real[j] = jnp.broadcast_to(first_real[:, j : j + 1], (orders, CELLS))
        step_imag[j] = jnp.broadcast_to(first_imag[:, j : j + 1], (orders, CELLS))

    for copy in copies[1:]:
        copy.wait()
    part = angles[...] * (0.5 / math.pi)
    part = part - jnp.round(part)
    cosines[...] = sine_turns(0.25 - jnp.abs(part))
    folded = jnp.where(part > 0.25, 0.5 - part, jnp.where(part < -0.25, -0.5 - part, part))
    sines[...] = sine_turns(folded)

    def block_phases(s):
        place = (owners[s] * blocks_local + locals_[s]) & (CYCLE_BLOCKS - 1)
        offset = jnp.broadcast_to(offsets[pl.ds(s, 1), :], (orders, CELLS))
        fraction = jnp.broadcast_to(fractions[pl.ds(s, 1), :], (orders, CELLS))
        real = jnp.take_along_axis(cell_real, offset, axis=1, mode="promise_in_bounds")
        imag = jnp.take_along_axis(cell_imag, offset, axis=1, mode="promise_in_bounds")
        base_real, base_imag = step_real[place], step_imag[place]
        left_real = real * base_real - imag * base_imag
        left_imag = real * base_imag + imag * base_real
        mix_real = 1.0 + fraction * next_real
        mix_imag = fraction * next_imag
        both = jnp.concatenate(
            [left_real * mix_real - left_imag * mix_imag, left_real * mix_imag + left_imag * mix_real],
            axis=0,
        )
        start = pl.multiple_of(s * 2 * orders, 2 * orders)
        phi[pl.ds(start, 2 * orders), :] = both.astype(BF16)

    scale = 1.0 / math.sqrt(2 * half)
    power = iota((8, CELLS), 0)

    def block_turns(s):
        one_real = jnp.broadcast_to(cosines[pl.ds(s, 1), :], (8, CELLS))
        one_imag = jnp.broadcast_to(sines[pl.ds(s, 1), :], (8, CELLS))
        step = (one_real, one_imag)
        odd = power & 1 == 1
        real, imag = jnp.where(odd, one_real * scale, scale), jnp.where(odd, one_imag * scale, 0.0)
        for bit in (2, 4):
            step = (step[0] * step[0] - step[1] * step[1], 2.0 * step[0] * step[1])
            taken = power & bit == bit
            by_real, by_imag = jnp.where(taken, step[0], 1.0), jnp.where(taken, step[1], 0.0)
            real, imag = real * by_real - imag * by_imag, real * by_imag + imag * by_real
        step = (step[0] * step[0] - step[1] * step[1], 2.0 * step[0] * step[1])
        evens, odds = [], []
        for j in range(half // 8):
            if j:
                real, imag = real * step[0] - imag * step[1], real * step[1] + imag * step[0]
            evens.append(real)
            odds.append(real * one_imag + imag * one_real)
        all_rows = jnp.concatenate(evens + odds, axis=0)
        turn[pl.ds(pl.multiple_of(s * 2 * half, 2 * half), 2 * half), :] = all_rows.astype(BF16)
        rows_of[...] = all_rows
        return [rows_of[pl.ds(p * half + mine, own_half), :] for p in range(2)]

    mine = lax.axis_index("beam") * own_half
    pair = 16 // (2 * own_half)

    @pl.loop(0, blocks // 8)
    def _(group):
        for j in range(0, 8, pair):
            kept = []
            for i in range(pair):
                block_phases(group * 8 + j + i)
                kept += block_turns(group * 8 + j + i)
            start = pl.multiple_of((group * 8 + j) * 2 * own_half, 16)
            own[pl.ds(start, 16), :] = jnp.concatenate(kept, axis=0).astype(BF16)


def samples_kernel(
    blocks_local, owners_hbm, locals_hbm, noise_hbm, count, arrived, phi, turn, own,
    out, owners, locals_, noise, arrivals, widened,
    stacked, modes_rows, modes, partial, filtered, totals, ordered,
):
    copies = bring((owners_hbm, locals_hbm, noise_hbm), (owners, locals_, noise), arrivals, 0)
    widened[...] = arrived[...].astype(F32)
    sky_devices, rows, lanes = out.shape
    parts = sky_devices * rows
    beams = arrived.shape[0] // parts
    blocks = partial.shape[0] // 8
    total = turn.shape[0] // blocks
    orders = total // beams
    cycles = lanes // orders
    together = len(totals)
    unroll = 32

    steps = max(1, blocks // (together * unroll))

    def cycle_of(s):
        return (owners[s] * blocks_local + locals_[s]) // CYCLE_BLOCKS

    width = together * parts
    for b in range(beams):
        for row in range(rows):
            some = every(widened, b * parts + row, sky_devices, rows)
            for j in range(together):
                start = j * parts + row * sky_devices
                stacked[b, start : start + sky_devices, :] = some
        modes_rows[b * lanes : (b + 1) * lanes, :] = stacked[b].T
    lane_group = iota((total, width), 1) // parts
    for r in range(cycles):
        halves = [
            modes_rows[pl.ds(r + parity * cycles, total // 2, stride=2 * cycles), :]
            for parity in range(2)
        ]
        values = jnp.concatenate(halves, axis=0)
        for j in range(together):
            modes[r, j] = jnp.where(lane_group == j, values, 0.0).astype(BF16)
    for copy in copies:
        copy.wait()

    def gather(first):
        left = jnp.concatenate([modes[cycle_of(first + j), j] for j in range(together)], axis=0)
        table = phi[pl.ds(pl.multiple_of(first * parts, width), width), :]
        cells = jnp.dot(left, table, preferred_element_type=F32)
        rotation = turn[pl.ds(pl.multiple_of(first * total, together * total), together * total), :]
        turned = (cells * rotation.astype(F32)).reshape(together, total // 8, 8, CELLS)
        kept = jnp.sum(turned, axis=1).reshape(together * 8, CELLS)
        partial[pl.ds(pl.multiple_of(first * 8, together * 8), together * 8), :] = kept

    @pl.loop(0, steps)
    def _(step):
        for i in range(unroll):
            gather((step * unroll + i) * together)

    signal = partial[pl.ds(0, blocks, stride=8), :]
    for i in range(1, 8):
        signal = signal + partial[pl.ds(i, blocks, stride=8), :]
    valid = iota((blocks, CELLS), 0) * CELLS + iota((blocks, CELLS), 1) < count[0]
    signal = jnp.where(valid, signal, 0.0)
    clean = lax.dot_general(
        signal.astype(BF16), noise[...].astype(BF16), LAST_LAST, preferred_element_type=F32
    )
    filtered[...] = jnp.where(valid, clean, 0.0)

    for one in totals:
        one[...] = jnp.zeros_like(one)
    half = orders // 2

    def spread(first):
        rotation = own[pl.ds(pl.multiple_of(first * orders, 16), together * orders), :].astype(F32)
        weighted = [
            rotation[j * orders : (j + 1) * orders] * filtered[pl.ds(first + j, 1), :]
            for j in range(together)
        ]
        weighted = jnp.concatenate(weighted, axis=0).astype(BF16)
        table = phi[pl.ds(pl.multiple_of(first * parts, width), width), :]
        terms = lax.dot_general(weighted, table, LAST_LAST, preferred_element_type=F32)
        for j in range(together):
            row = pl.multiple_of(cycle_of(first + j) * orders, orders)
            here = totals[j]
            here[pl.ds(row, orders), :] += terms[j * orders : (j + 1) * orders]

    @pl.loop(0, steps)
    def _(step):
        for i in range(unroll):
            spread((step * unroll + i) * together)

    gathered = totals[0][...]
    which = iota(gathered.shape, 1) // parts
    for j in range(1, together):
        gathered = jnp.where(which == j, totals[j][...], gathered)
    totals[0][...] = gathered
    for k in range(orders):
        place = k // 2 + (k % 2) * half
        ordered[k * cycles : (k + 1) * cycles, :] = totals[0][pl.ds(place, cycles, stride=orders), :]
    turned = ordered[...].T
    summed = turned[0:parts]
    for j in range(1, together):
        summed = summed + turned[j * parts : (j + 1) * parts]
    for row in range(rows):
        out[:, row, :] = summed[row * sky_devices : (row + 1) * sky_devices]


def gradient_kernel(arrived, beam, wigner, kept, sent, pieces):
    me = lax.axis_index("beam")
    orders, sky_orders, cycles, degrees = wigner.shape
    beam_real, beam_imag = beam[:, 0, :], beam[:, 1, :]
    diagonal = own_block(orders, cycles)
    modes = jnp.sum(arrived[...], axis=0).astype(BF16).astype(F32)
    width = pieces.shape[3]
    for m in range(sky_orders):
        spreads = []
        for c in range(2):
            row = modes[c * sky_orders + m : c * sky_orders + m + 1]
            spreads.append(jnp.where(diagonal, row, 0.0))
        left = jnp.concatenate(spreads, axis=0).astype(BF16)
        table = wigner[:, m].reshape(orders * cycles, degrees)
        harmonics = jnp.dot(left, table, preferred_element_type=F32)
        real, imag = harmonics[:orders], harmonics[orders:]
        first = jnp.sum(real * beam_real + imag * beam_imag, axis=0, keepdims=True)
        second = jnp.sum(imag * beam_real - real * beam_imag, axis=0, keepdims=True)
        both = jnp.concatenate([first, second], axis=0)
        for d in range(pieces.shape[0]):
            pieces[d ^ me, m] = both[:, d * width : (d + 1) * width]
    kept[...] = pieces[: kept.shape[0]]
    sent[...] = pieces[kept.shape[0] :].astype(BF16)


def scatter_sum(kept, sent, axis):
    while True:
        step = kept.shape[0]
        pairs = [(i, i ^ step) for i in range(lax.axis_size(axis))]
        summed = kept + lax.ppermute(sent, axis, pairs).astype(F32)
        if step == 1:
            return summed[0]
        kept, sent = summed[: step // 2], summed[step // 2 :]


def local(
    sky_harmonics,
    beam_harmonics,
    wigner,
    order_map,
    block_owner,
    block_local,
    cell_offset,
    cell_fraction,
    beam_angle,
    sample_count,
    noise_weight,
):
    beams, sky_devices = lax.axis_size("beam"), lax.axis_size("ma")
    orders, sky_orders, cycles, degrees = wigner.shape
    total = orders * beams
    all_sky = sky_orders * sky_devices
    parts = 2 * all_sky
    blocks = block_local.shape[0]
    blocks_local = cycles // sky_devices * CYCLE_BLOCKS
    lanes = orders * cycles
    rows = 2 * sky_orders
    together = max(1, CELLS // parts)
    owners = block_owner.reshape(blocks)
    limit = pltpu.CompilerParams(vmem_limit_bytes=32 * 1024 * 1024)
    integers = [
        pltpu.SMEM((blocks,), jnp.int32),
        pltpu.SMEM((blocks,), jnp.int32),
    ]

    def pinned(*arrays):
        return [pltpu.with_memory_space_constraint(array, pltpu.HBM) for array in arrays]

    sent = pl.pallas_call(
        modes_kernel,
        out_shape=pltpu.VMEM((beams * sky_devices, rows, lanes), BF16),
        in_specs=hbm(3),
        out_specs=vmem(1)[0],
        scratch_shapes=[
            pltpu.VMEM(sky_harmonics.shape, F32),
            pltpu.VMEM(beam_harmonics.shape, F32),
            pltpu.VMEM((sky_orders, orders, cycles, degrees), BF16),
            pltpu.SemaphoreType.DMA((2 + sky_orders,)),
        ],
        compiler_params=limit,
        name="modes",
    )(*pinned(sky_harmonics, beam_harmonics, wigner))
    arrived = lax.all_to_all(sent, ("beam", "ma"), split_axis=0, concat_axis=0, tiled=True)

    samples = pltpu.VMEM((blocks, CELLS), F32)
    phi, turn, own = pl.pallas_call(
        functools.partial(tables_kernel, blocks_local, sky_devices),
        out_shape=[
            pltpu.VMEM((blocks * parts, CELLS), BF16),
            pltpu.VMEM((blocks * total, CELLS), BF16),
            pltpu.VMEM((blocks * orders, CELLS), BF16),
        ],
        in_specs=hbm(6),
        out_specs=vmem(3),
        scratch_shapes=[
            pltpu.SMEM((all_sky,), jnp.int32),
            *integers,
            samples,
            pltpu.VMEM((blocks, CELLS), jnp.int32),
            samples,
            pltpu.SemaphoreType.DMA((6,)),
            pltpu.VMEM((CYCLE_BLOCKS, all_sky, CELLS), F32),
            pltpu.VMEM((CYCLE_BLOCKS, all_sky, CELLS), F32),
            samples,
            samples,
            pltpu.VMEM((total, CELLS), F32),
        ],
        compiler_params=limit,
        cost_estimate=pl.CostEstimate(flops=100_000_000, bytes_accessed=4_000_000, transcendentals=0),
        name="tables",
    )(
        *pinned(
            order_map, owners, block_local,
            beam_angle.reshape(blocks, CELLS),
            cell_offset.reshape(blocks, CELLS),
            cell_fraction.reshape(blocks, CELLS),
        )
    )

    grads = pl.pallas_call(
        functools.partial(samples_kernel, blocks_local),
        out_shape=jax.ShapeDtypeStruct((sky_devices, rows, lanes), F32),
        in_specs=hbm(3) + smem(1) + vmem(4),
        out_specs=vmem(1)[0],
        scratch_shapes=[
            *integers,
            pltpu.VMEM((CELLS, CELLS), F32),
            pltpu.SemaphoreType.DMA((3,)),
            pltpu.VMEM((beams * parts, lanes), F32),
            pltpu.VMEM((beams, together * parts, lanes), F32),
            pltpu.VMEM((beams * lanes, together * parts), F32),
            pltpu.VMEM((cycles, together, total, together * parts), BF16),
            pltpu.VMEM((blocks * 8, CELLS), F32),
            samples,
            [pltpu.VMEM((lanes, together * parts), F32) for _ in range(together)],
            pltpu.VMEM((lanes, together * parts), F32),
        ],
        compiler_params=limit,
        name="samples",
    )(
        *pinned(owners, block_local, noise_weight),
        sample_count,
        arrived.reshape(beams * parts, lanes), phi, turn, own,
    )
    grads = lax.all_to_all(grads, "ma", split_axis=0, concat_axis=0, tiled=True)

    width = degrees // beams
    half = (beams // 2, sky_orders, 2, width)
    kept, sent = pl.pallas_call(
        gradient_kernel,
        out_shape=[jax.ShapeDtypeStruct(half, F32), jax.ShapeDtypeStruct(half, BF16)],
        in_specs=vmem(3),
        out_specs=vmem(2),
        scratch_shapes=[pltpu.VMEM((beams, sky_orders, 2, width), F32)],
        compiler_params=limit,
        name="gradient",
    )(grads, beam_harmonics, wigner)
    return scatter_sum(kept, sent, "beam")


def solution(mesh):
    return jax.shard_map(
        local,
        mesh=mesh,
        in_specs=(
            P("ma", None, None),
            P("beam", None, None),
            P("beam", "ma", None, None),
            P(),
            P("ma", None),
            P("ma"),
            P("ma"),
            P("ma"),
            P("ma"),
            P("ma"),
            P(),
        ),
        out_specs=P("ma", None, "beam"),
        check_vma=False,
    )
```

```python
import functools
import math

import jax
import jax.numpy as jnp
from jax import lax
from jax.experimental import pallas as pl
from jax.experimental.pallas import tpu as pltpu
from jax.sharding import PartitionSpec as P

PHI = 4096
CELLS = 128
CYCLE_BLOCKS = PHI // CELLS
F32 = jnp.float32
BF16 = jnp.bfloat16
SWAP = [(0, 1), (1, 0)]
LAST_LAST = (((1,), (1,)), ((), ()))


def iota(shape, axis):
    return lax.broadcasted_iota(jnp.int32, shape, axis)


def vmem(count):
    return [pl.BlockSpec(memory_space=pltpu.VMEM)] * count


def smem(count):
    return [pl.BlockSpec(memory_space=pltpu.SMEM)] * count


def hbm(count):
    return [pl.BlockSpec(memory_space=pltpu.HBM)] * count


def sine_turns(z):
    square = z * z
    value = 39.53670603 * square - 76.54978229
    value = value * square + 81.60100407
    value = value * square - 41.34165503
    value = value * square + 6.28318516
    return value * z


def cosine_steps(steps):
    centred = ((steps + PHI // 2) & (PHI - 1)) - PHI // 2
    return sine_turns(0.25 - jnp.abs(centred).astype(F32) * (1.0 / PHI))


def every(ref, first, count, step):
    if ref.shape[1] == CELLS:
        return ref[pl.ds(first, count, stride=step), :]
    return jnp.concatenate([ref[first + i * step][None] for i in range(count)], axis=0)


def bring(sources, places, semaphores, first):
    copies = [
        pltpu.make_async_copy(source, place, semaphores.at[first + i])
        for i, (source, place) in enumerate(zip(sources, places))
    ]
    for copy in copies:
        copy.start()
    return copies


def own_block(orders, cycles):
    shape = (orders, orders * cycles)
    return iota(shape, 1) // cycles == iota(shape, 0)


def modes_kernel(sky_hbm, beam_hbm, wigner_hbm, out, sky, beam, wigner, arrivals):
    chunks, orders, sky_orders, cycles, width = wigner.shape
    small = bring((sky_hbm, beam_hbm), (sky, beam), arrivals, 0)
    spans = [pl.ds(i * width, width) for i in range(chunks)]
    large = bring([wigner_hbm.at[:, :, :, span] for span in spans], [wigner.at[i] for i in range(chunks)], arrivals, 2)
    for copy in small:
        copy.wait()
    beam_real, beam_imag = beam[:, 0, :], beam[:, 1, :]
    diagonal = own_block(orders, cycles)
    products = []
    for m in range(sky_orders):
        sky_real, sky_imag = sky[m, 0:1, :], sky[m, 1:2, :]
        first = sky_real * beam_real - sky_imag * beam_imag
        second = sky_real * beam_imag + sky_imag * beam_real
        products.append(jnp.concatenate([first, second], axis=0).astype(BF16))
    sums = [0.0] * sky_orders
    for i in range(chunks):
        large[i].wait()
        for m in range(sky_orders):
            table = wigner[i, :, m].reshape(orders * cycles, width)
            left = products[m][:, i * width : (i + 1) * width]
            sums[m] += lax.dot_general(table, left, LAST_LAST, preferred_element_type=F32)
    rows = [None] * (2 * sky_orders)
    for m in range(sky_orders):
        modes = sums[m].T
        for c in range(2):
            part = jnp.where(diagonal, modes[c * orders : (c + 1) * orders], 0.0)
            rows[c * sky_orders + m] = jnp.sum(part, axis=0, keepdims=True)
    block = jnp.concatenate(rows, axis=0).astype(BF16)
    for d in range(out.shape[0]):
        out[d] = block


def tables_kernel(
    blocks_local, sky_devices,
    order_hbm, owners_hbm, locals_hbm, angles_hbm, offsets_hbm, fractions_hbm,
    phi, turn, own, order_map, owners, locals_, angles, offsets, fractions, arrivals,
    step_real, step_imag, cosines, sines, rows_of,
):
    sources = (order_hbm, owners_hbm, locals_hbm, angles_hbm, offsets_hbm, fractions_hbm)
    places = (order_map, owners, locals_, angles, offsets, fractions)
    copies = bring(sources, places, arrivals, 0)
    orders = order_map.shape[0]
    blocks = offsets.shape[0]
    half = turn.shape[0] // blocks // 2
    own_half = own.shape[0] // blocks // 2

    copies[0].wait()
    order = jnp.zeros((orders, CELLS), jnp.int32)
    row = iota((orders, CELLS), 0)
    lane = iota((orders, CELLS), 1)
    for m in range(orders):
        device, inner = divmod(m, orders // sky_devices)
        place = inner * sky_devices + device % 2 * (sky_devices // 2) + device // 2
        order = jnp.where(row == place, order_map[m], order)

    def phase(steps):
        return cosine_steps(steps), cosine_steps(steps + PHI // 4)

    scaling = 1.0 / math.sqrt(orders)
    cell_real, cell_imag = phase(order * lane)
    cell_real, cell_imag = cell_real * scaling, cell_imag * scaling
    next_real, next_imag = phase(order)
    next_real = next_real - 1.0
    first_real, first_imag = phase(((order * CELLS) & (PHI - 1)) * lane)
    for j in range(CYCLE_BLOCKS):
        step_real[j] = jnp.broadcast_to(first_real[:, j : j + 1], (orders, CELLS))
        step_imag[j] = jnp.broadcast_to(first_imag[:, j : j + 1], (orders, CELLS))

    for copy in copies[1:]:
        copy.wait()
    part = angles[...] * (0.5 / math.pi)
    part = part - jnp.round(part)
    cosines[...] = sine_turns(0.25 - jnp.abs(part))
    folded = jnp.where(part > 0.25, 0.5 - part, jnp.where(part < -0.25, -0.5 - part, part))
    sines[...] = sine_turns(folded)

    def block_phases(s):
        place = (owners[s] * blocks_local + locals_[s]) & (CYCLE_BLOCKS - 1)
        offset = jnp.broadcast_to(offsets[pl.ds(s, 1), :], (orders, CELLS))
        fraction = jnp.broadcast_to(fractions[pl.ds(s, 1), :], (orders, CELLS))
        real = jnp.take_along_axis(cell_real, offset, axis=1, mode="promise_in_bounds")
        imag = jnp.take_along_axis(cell_imag, offset, axis=1, mode="promise_in_bounds")
        base_real, base_imag = step_real[place], step_imag[place]
        left_real = real * base_real - imag * base_imag
        left_imag = real * base_imag + imag * base_real
        mix_real = 1.0 + fraction * next_real
        mix_imag = fraction * next_imag
        both = jnp.concatenate(
            [left_real * mix_real - left_imag * mix_imag, left_real * mix_imag + left_imag * mix_real],
            axis=0,
        )
        start = pl.multiple_of(s * 2 * orders, 2 * orders)
        phi[pl.ds(start, 2 * orders), :] = both.astype(BF16)

    scale = 1.0 / math.sqrt(2 * half)
    power = iota((8, CELLS), 0)

    def block_turns(s):
        one_real = jnp.broadcast_to(cosines[pl.ds(s, 1), :], (8, CELLS))
        one_imag = jnp.broadcast_to(sines[pl.ds(s, 1), :], (8, CELLS))
        step = (one_real, one_imag)
        odd = power & 1 == 1
        real, imag = jnp.where(odd, one_real * scale, scale), jnp.where(odd, one_imag * scale, 0.0)
        for bit in (2, 4):
            step = (step[0] * step[0] - step[1] * step[1], 2.0 * step[0] * step[1])
            taken = power & bit == bit
            by_real, by_imag = jnp.where(taken, step[0], 1.0), jnp.where(taken, step[1], 0.0)
            real, imag = real * by_real - imag * by_imag, real * by_imag + imag * by_real
        step = (step[0] * step[0] - step[1] * step[1], 2.0 * step[0] * step[1])
        evens, odds = [], []
        for j in range(half // 8):
            if j:
                real, imag = real * step[0] - imag * step[1], real * step[1] + imag * step[0]
            evens.append(real)
            odds.append(real * one_imag + imag * one_real)
        all_rows = jnp.concatenate(evens + odds, axis=0)
        turn[pl.ds(pl.multiple_of(s * 2 * half, 2 * half), 2 * half), :] = all_rows.astype(BF16)
        rows_of[...] = all_rows
        return [rows_of[pl.ds(p * half + mine, own_half), :] for p in range(2)]

    mine = lax.axis_index("beam") * own_half
    pair = 16 // (2 * own_half)

    @pl.loop(0, blocks // 8)
    def _(group):
        for j in range(0, 8, pair):
            kept = []
            for i in range(pair):
                block_phases(group * 8 + j + i)
                kept += block_turns(group * 8 + j + i)
            start = pl.multiple_of((group * 8 + j) * 2 * own_half, 16)
            own[pl.ds(start, 16), :] = jnp.concatenate(kept, axis=0).astype(BF16)


def samples_kernel(
    blocks_local, owners_hbm, locals_hbm, noise_hbm, count, arrived, others, phi, turn, own,
    kept, given, owners, locals_, noise, arrivals, widened,
    stacked, modes_rows, modes, partial, filtered, totals, ordered,
):
    copies = bring((owners_hbm, locals_hbm, noise_hbm), (owners, locals_, noise), arrivals, 0)
    core = lax.axis_index("core")
    widened[core] = arrived[...].astype(F32)
    widened[1 - core] = others[...].astype(F32)
    levels, rows, lanes = kept.shape
    parts = 2 * levels * rows
    beams = arrived.shape[0] // (levels * rows)
    blocks = partial.shape[0] // 8
    total = turn.shape[0] // blocks
    orders = total // beams
    cycles = lanes // orders
    together = len(totals)
    unroll = 32

    steps = max(1, blocks // (together * unroll))

    def cycle_of(s):
        return (owners[s] * blocks_local + locals_[s]) // CYCLE_BLOCKS

    width = together * parts
    for b in range(beams):
        for row in range(rows):
            for c in range(2):
                some = every(widened.at[c], b * levels * rows + row, levels, rows)
                for j in range(together):
                    start = j * parts + (2 * row + c) * levels
                    stacked[b, start : start + levels, :] = some
        modes_rows[b * lanes : (b + 1) * lanes, :] = stacked[b].T
    lane_group = iota((total, width), 1) // parts
    for r in range(cycles):
        halves = [
            modes_rows[pl.ds(r + parity * cycles, total // 2, stride=2 * cycles), :]
            for parity in range(2)
        ]
        values = jnp.concatenate(halves, axis=0)
        for j in range(together):
            modes[r, j] = jnp.where(lane_group == j, values, 0.0).astype(BF16)
    for copy in copies:
        copy.wait()

    def gather(first):
        left = jnp.concatenate([modes[cycle_of(first + j), j] for j in range(together)], axis=0)
        table = phi[pl.ds(pl.multiple_of(first * parts, width), width), :]
        cells = jnp.dot(left, table, preferred_element_type=F32)
        rotation = turn[pl.ds(pl.multiple_of(first * total, together * total), together * total), :]
        turned = (cells * rotation.astype(F32)).reshape(together, total // 8, 8, CELLS)
        kept = jnp.sum(turned, axis=1).reshape(together * 8, CELLS)
        partial[pl.ds(pl.multiple_of(first * 8, together * 8), together * 8), :] = kept

    @pl.loop(0, steps)
    def _(step):
        for i in range(unroll):
            gather((step * unroll + i) * together)

    signal = partial[pl.ds(0, blocks, stride=8), :]
    for i in range(1, 8):
        signal = signal + partial[pl.ds(i, blocks, stride=8), :]
    valid = iota((blocks, CELLS), 0) * CELLS + iota((blocks, CELLS), 1) < count[0]
    signal = jnp.where(valid, signal, 0.0)
    clean = lax.dot_general(
        signal.astype(BF16), noise[...].astype(BF16), LAST_LAST, preferred_element_type=F32
    )
    filtered[...] = jnp.where(valid, clean, 0.0)

    for one in totals:
        one[...] = jnp.zeros_like(one)
    half = orders // 2

    def spread(first):
        rotation = own[pl.ds(pl.multiple_of(first * orders, 16), together * orders), :].astype(F32)
        weighted = [
            rotation[j * orders : (j + 1) * orders] * filtered[pl.ds(first + j, 1), :]
            for j in range(together)
        ]
        weighted = jnp.concatenate(weighted, axis=0).astype(BF16)
        table = phi[pl.ds(pl.multiple_of(first * parts, width), width), :]
        terms = lax.dot_general(weighted, table, LAST_LAST, preferred_element_type=F32)
        for j in range(together):
            row = pl.multiple_of(cycle_of(first + j) * orders, orders)
            here = totals[j]
            here[pl.ds(row, orders), :] += terms[j * orders : (j + 1) * orders]

    @pl.loop(0, steps)
    def _(step):
        for i in range(unroll):
            spread((step * unroll + i) * together)

    gathered = totals[0][...]
    which = iota(gathered.shape, 1) // parts
    for j in range(1, together):
        gathered = jnp.where(which == j, totals[j][...], gathered)
    totals[0][...] = gathered
    for k in range(orders):
        place = k // 2 + (k % 2) * half
        ordered[k * cycles : (k + 1) * cycles, 0:width] = totals[0][pl.ds(place, cycles, stride=orders), :]
    turned = ordered[0:lanes, 0:width].T
    summed = turned[0:parts]
    for j in range(1, together):
        summed = summed + turned[j * parts : (j + 1) * parts]
    ordered[0:parts, 0:lanes] = summed
    for row in range(rows):
        kept[:, row, :] = ordered[pl.ds((2 * row + core) * levels, levels), 0:lanes]
        given[:, row, :] = ordered[pl.ds((2 * row + 1 - core) * levels, levels), 0:lanes]


def gradient_kernel(duties, arrived, beam, wigner, own, kept, given, pieces):
    me = lax.axis_index("beam")
    orders, sky_orders, cycles, degrees = wigner.shape
    beam_real, beam_imag = beam[:, 0, :], beam[:, 1, :]
    diagonal = own_block(orders, cycles)
    modes = jnp.sum(arrived[...], axis=0).astype(BF16).astype(F32)
    width = pieces.shape[3]
    for m in range(sky_orders):
        spreads = []
        for c in range(2):
            row = modes[c * sky_orders + m : c * sky_orders + m + 1]
            spreads.append(jnp.where(diagonal, row, 0.0))
        left = jnp.concatenate(spreads, axis=0).astype(BF16)
        table = wigner[:, m].reshape(orders * cycles, degrees)
        harmonics = jnp.dot(left, table, preferred_element_type=F32)
        real, imag = harmonics[:orders], harmonics[orders:]
        first = jnp.sum(real * beam_real + imag * beam_imag, axis=0, keepdims=True)
        second = jnp.sum(imag * beam_real - real * beam_imag, axis=0, keepdims=True)
        both = jnp.concatenate([first, second], axis=0)
        for d in range(pieces.shape[0]):
            pieces[d ^ me, m] = both[:, d * width : (d + 1) * width]
    own[...] = pieces[0]
    first = lax.axis_index("core") == 0
    for i, (ours, theirs) in enumerate(zip(*duties)):
        kept[i] = pieces[jnp.where(first, ours, theirs)].astype(BF16)
        given[i] = pieces[jnp.where(first, theirs, ours)].astype(BF16)


def scatter_sum(duties, own, kept, given):
    beams = lax.axis_size("beam")
    swapped = lax.ppermute(given, "core", SWAP)
    here, there = own, 0.0
    for i, turns in enumerate(zip(*duties)):
        pairs = [
            (2 * b + core, 2 * (b ^ j) + core)
            for b in range(beams)
            for core, j in enumerate(turns)
            if j
        ]
        term = lax.ppermute(jnp.stack([kept[i], swapped[i]]), ("beam", "core"), pairs).astype(F32)
        here, there = here + term[0], there + term[1]
    return here + lax.ppermute(there, "core", SWAP)


def local(
    sky_harmonics,
    beam_harmonics,
    wigner,
    order_map,
    block_owner,
    block_local,
    cell_offset,
    cell_fraction,
    beam_angle,
    sample_count,
    noise_weight,
):
    beams, levels, cores = lax.axis_size("beam"), lax.axis_size("z"), lax.axis_size("core")
    sky_devices = levels * cores
    orders, sky_orders, cycles, degrees = wigner.shape
    total = orders * beams
    all_sky = sky_orders * sky_devices
    parts = 2 * all_sky
    blocks = block_local.shape[0]
    blocks_local = cycles // sky_devices * CYCLE_BLOCKS
    lanes = orders * cycles
    rows = 2 * sky_orders
    together = max(1, CELLS // parts)
    owners = block_owner.reshape(blocks)
    chunks = 4
    limit = pltpu.CompilerParams(vmem_limit_bytes=32 * 1024 * 1024)
    integers = [
        pltpu.SMEM((blocks,), jnp.int32),
        pltpu.SMEM((blocks,), jnp.int32),
    ]

    def pinned(*arrays):
        return [pltpu.with_memory_space_constraint(array, pltpu.HBM) for array in arrays]

    sent = pl.pallas_call(
        modes_kernel,
        out_shape=jax.ShapeDtypeStruct((beams * levels, rows, lanes), BF16),
        in_specs=hbm(3),
        out_specs=vmem(1)[0],
        scratch_shapes=[
            pltpu.VMEM(sky_harmonics.shape, F32),
            pltpu.VMEM(beam_harmonics.shape, F32),
            pltpu.VMEM((chunks, orders, sky_orders, cycles, degrees // chunks), BF16),
            pltpu.SemaphoreType.DMA((2 + chunks,)),
        ],
        compiler_params=limit,
        name="modes",
    )(*pinned(sky_harmonics, beam_harmonics, wigner))
    arrived = lax.all_to_all(sent, ("beam", "z"), split_axis=0, concat_axis=0, tiled=True)
    arrived = arrived.reshape(beams * levels * rows, lanes)

    samples = pltpu.VMEM((blocks, CELLS), F32)
    phi, turn, own = pl.pallas_call(
        functools.partial(tables_kernel, blocks_local, sky_devices),
        out_shape=[
            pltpu.VMEM((blocks * parts, CELLS), BF16),
            pltpu.VMEM((blocks * total, CELLS), BF16),
            pltpu.VMEM((blocks * orders, CELLS), BF16),
        ],
        in_specs=hbm(6),
        out_specs=vmem(3),
        scratch_shapes=[
            pltpu.SMEM((all_sky,), jnp.int32),
            *integers,
            samples,
            pltpu.VMEM((blocks, CELLS), jnp.int32),
            samples,
            pltpu.SemaphoreType.DMA((6,)),
            pltpu.VMEM((CYCLE_BLOCKS, all_sky, CELLS), F32),
            pltpu.VMEM((CYCLE_BLOCKS, all_sky, CELLS), F32),
            samples,
            samples,
            pltpu.VMEM((total, CELLS), F32),
        ],
        compiler_params=limit,
        cost_estimate=pl.CostEstimate(flops=100_000_000, bytes_accessed=4_000_000, transcendentals=0),
        name="tables",
    )(
        *pinned(
            order_map, owners, block_local,
            beam_angle.reshape(blocks, CELLS),
            cell_offset.reshape(blocks, CELLS),
            cell_fraction.reshape(blocks, CELLS),
        )
    )

    arrived, phi, turn, own = lax.optimization_barrier((arrived, phi, turn, own))
    others = lax.ppermute(arrived, "core", SWAP)
    kept, given = pl.pallas_call(
        functools.partial(samples_kernel, blocks_local),
        out_shape=[jax.ShapeDtypeStruct((levels, rows, lanes), F32)] * 2,
        in_specs=hbm(3) + smem(1) + vmem(5),
        out_specs=vmem(2),
        scratch_shapes=[
            *integers,
            pltpu.VMEM((CELLS, CELLS), F32),
            pltpu.SemaphoreType.DMA((3,)),
            pltpu.VMEM((2, beams * levels * rows, lanes), F32),
            pltpu.VMEM((beams, together * parts, lanes), F32),
            pltpu.VMEM((beams * lanes, together * parts), F32),
            pltpu.VMEM((cycles, together, total, together * parts), BF16),
            pltpu.VMEM((blocks * 8, CELLS), F32),
            samples,
            [pltpu.VMEM((lanes, together * parts), F32) for _ in range(together)],
            pltpu.VMEM((max(parts, lanes), max(lanes, together * parts)), F32),
        ],
        compiler_params=limit,
        name="samples",
    )(
        *pinned(owners, block_local, noise_weight),
        sample_count,
        arrived, others, phi, turn, own,
    )
    grads = kept + lax.ppermute(given, "core", SWAP)
    grads = lax.all_to_all(grads, "z", split_axis=0, concat_axis=0, tiled=True)

    width = degrees // beams
    duties = (list(range(2, beams, 2)) + [0], list(range(1, beams, 2)))
    piece = (sky_orders, 2, width)
    several = jax.ShapeDtypeStruct((len(duties[0]), *piece), BF16)
    own, kept, given = pl.pallas_call(
        functools.partial(gradient_kernel, duties),
        out_shape=[jax.ShapeDtypeStruct(piece, F32), several, several],
        in_specs=vmem(3),
        out_specs=vmem(3),
        scratch_shapes=[pltpu.VMEM((beams, *piece), F32)],
        compiler_params=limit,
        name="gradient",
    )(grads, beam_harmonics, wigner)
    return scatter_sum(duties, own, kept, given)


def solution(mesh):
    beams, sky_devices = mesh.shape["beam"], mesh.shape["ma"]
    devices = mesh.devices.reshape(beams, sky_devices // 2, 2)
    ma = ("z", "core")
    return jax.shard_map(
        local,
        mesh=jax.sharding.Mesh(devices, ("beam", *ma)),
        in_specs=(
            P(ma, None, None),
            P("beam", None, None),
            P("beam", ma, None, None),
            P(),
            P(ma, None),
            P(ma),
            P(ma),
            P(ma),
            P(ma),
            P(ma),
            P(),
        ),
        out_specs=P(ma, None, "beam"),
        check_vma=False,
    )
```

```python
import functools
import math

import jax
import jax.numpy as jnp
from jax import lax
from jax.experimental import pallas as pl
from jax.experimental.pallas import tpu as pltpu
from jax.sharding import PartitionSpec as P

PHI = 4096
CELLS = 128
CYCLE_BLOCKS = PHI // CELLS
F32 = jnp.float32
BF16 = jnp.bfloat16
LAST_LAST = (((1,), (1,)), ((), ()))


def iota(shape, axis):
    return lax.broadcasted_iota(jnp.int32, shape, axis)


def vmem(count):
    return [pl.BlockSpec(memory_space=pltpu.VMEM)] * count


def smem(count):
    return [pl.BlockSpec(memory_space=pltpu.SMEM)] * count


def hbm(count):
    return [pl.BlockSpec(memory_space=pltpu.HBM)] * count


def sine_turns(z):
    square = z * z
    value = 39.53670603 * square - 76.54978229
    value = value * square + 81.60100407
    value = value * square - 41.34165503
    value = value * square + 6.28318516
    return value * z


def cosine_steps(steps):
    centred = ((steps + PHI // 2) & (PHI - 1)) - PHI // 2
    return sine_turns(0.25 - jnp.abs(centred).astype(F32) * (1.0 / PHI))


def every(ref, first, count, step):
    if ref.shape[1] == CELLS:
        return ref[pl.ds(first, count, stride=step), :]
    return jnp.concatenate([ref[first + i * step][None] for i in range(count)], axis=0)


def bring(sources, places, semaphores, first):
    copies = [
        pltpu.make_async_copy(source, place, semaphores.at[first + i])
        for i, (source, place) in enumerate(zip(sources, places))
    ]
    for copy in copies:
        copy.start()
    return copies


def own_block(orders, cycles):
    shape = (orders, orders * cycles)
    return iota(shape, 1) // cycles == iota(shape, 0)


def modes_kernel(sky_hbm, beam_hbm, wigner_hbm, out, sky, beam, wigner, arrivals):
    chunks, orders, sky_orders, cycles, width = wigner.shape
    small = bring((sky_hbm, beam_hbm), (sky, beam), arrivals, 0)
    spans = [pl.ds(i * width, width) for i in range(chunks)]
    large = bring([wigner_hbm.at[:, :, :, span] for span in spans], [wigner.at[i] for i in range(chunks)], arrivals, 2)
    for copy in small:
        copy.wait()
    beam_real, beam_imag = beam[:, 0, :], beam[:, 1, :]
    diagonal = own_block(orders, cycles)
    products = []
    for m in range(sky_orders):
        sky_real, sky_imag = sky[m, 0:1, :], sky[m, 1:2, :]
        first = sky_real * beam_real - sky_imag * beam_imag
        second = sky_real * beam_imag + sky_imag * beam_real
        products.append(jnp.concatenate([first, second], axis=0).astype(BF16))
    sums = [0.0] * sky_orders
    for i in range(chunks):
        large[i].wait()
        for m in range(sky_orders):
            table = wigner[i, :, m].reshape(orders * cycles, width)
            left = products[m][:, i * width : (i + 1) * width]
            sums[m] += lax.dot_general(table, left, LAST_LAST, preferred_element_type=F32)
    rows = [None] * (2 * sky_orders)
    for m in range(sky_orders):
        modes = sums[m].T
        for c in range(2):
            part = jnp.where(diagonal, modes[c * orders : (c + 1) * orders], 0.0)
            rows[c * sky_orders + m] = jnp.sum(part, axis=0, keepdims=True)
    block = jnp.concatenate(rows, axis=0).astype(BF16)
    for d in range(out.shape[0]):
        out[d] = block


def tables_kernel(
    blocks_local, sky_devices,
    after, order_hbm, owners_hbm, locals_hbm, angles_hbm, offsets_hbm, fractions_hbm, beam_hbm, wigner_hbm,
    phi, turn, own, pieces, beam, extras, departures, order_map, owners, locals_, angles, offsets, fractions, arrivals,
    step_real, step_imag, cosines, sines, rows_of,
):
    sources = (order_hbm, owners_hbm, locals_hbm, angles_hbm, offsets_hbm, fractions_hbm)
    places = (order_map, owners, locals_, angles, offsets, fractions)
    copies = bring(sources, places, arrivals, 0)
    me = lax.axis_index("beam")
    extra = bring((beam_hbm,), (beam,), arrivals, 6)[0]
    beam_orders, width = beam.shape[0], pieces[0].shape[3]
    spans = [pl.ds(pl.multiple_of((me ^ j) * width, width), width) for j in range(len(pieces))]
    leaving = bring(
        [wigner_hbm.at[:, :, :, span] for span in spans],
        [piece.at[0:beam_orders] for piece in pieces],
        departures, 0,
    )
    orders = order_map.shape[0]
    blocks = offsets.shape[0]
    half = turn.shape[0] // blocks // 2
    own_half = own.shape[0] // blocks // 2

    copies[0].wait()
    order = jnp.zeros((orders, CELLS), jnp.int32)
    row = iota((orders, CELLS), 0)
    lane = iota((orders, CELLS), 1)
    for m in range(orders):
        place = m % (orders // sky_devices) * sky_devices + m // (orders // sky_devices)
        order = jnp.where(row == place, order_map[m], order)

    def phase(steps):
        return cosine_steps(steps), cosine_steps(steps + PHI // 4)

    scaling = 1.0 / math.sqrt(orders)
    cell_real, cell_imag = phase(order * lane)
    cell_real, cell_imag = cell_real * scaling, cell_imag * scaling
    next_real, next_imag = phase(order)
    next_real = next_real - 1.0
    first_real, first_imag = phase(((order * CELLS) & (PHI - 1)) * lane)
    for j in range(CYCLE_BLOCKS):
        step_real[j] = jnp.broadcast_to(first_real[:, j : j + 1], (orders, CELLS))
        step_imag[j] = jnp.broadcast_to(first_imag[:, j : j + 1], (orders, CELLS))

    for copy in copies[1:]:
        copy.wait()
    part = angles[...] * (0.5 / math.pi)
    part = part - jnp.round(part)
    cosines[...] = sine_turns(0.25 - jnp.abs(part))
    folded = jnp.where(part > 0.25, 0.5 - part, jnp.where(part < -0.25, -0.5 - part, part))
    sines[...] = sine_turns(folded)

    def block_phases(s):
        place = (owners[s] * blocks_local + locals_[s]) & (CYCLE_BLOCKS - 1)
        offset = jnp.broadcast_to(offsets[pl.ds(s, 1), :], (orders, CELLS))
        fraction = jnp.broadcast_to(fractions[pl.ds(s, 1), :], (orders, CELLS))
        real = jnp.take_along_axis(cell_real, offset, axis=1, mode="promise_in_bounds")
        imag = jnp.take_along_axis(cell_imag, offset, axis=1, mode="promise_in_bounds")
        base_real, base_imag = step_real[place], step_imag[place]
        left_real = real * base_real - imag * base_imag
        left_imag = real * base_imag + imag * base_real
        mix_real = 1.0 + fraction * next_real
        mix_imag = fraction * next_imag
        both = jnp.concatenate(
            [left_real * mix_real - left_imag * mix_imag, left_real * mix_imag + left_imag * mix_real],
            axis=0,
        )
        start = pl.multiple_of(s * 2 * orders, 2 * orders)
        phi[pl.ds(start, 2 * orders), :] = both.astype(BF16)

    scale = 1.0 / math.sqrt(2 * half)
    power = iota((8, CELLS), 0)

    def block_turns(s):
        one_real = jnp.broadcast_to(cosines[pl.ds(s, 1), :], (8, CELLS))
        one_imag = jnp.broadcast_to(sines[pl.ds(s, 1), :], (8, CELLS))
        step = (one_real, one_imag)
        odd = power & 1 == 1
        real, imag = jnp.where(odd, one_real * scale, scale), jnp.where(odd, one_imag * scale, 0.0)
        for bit in (2, 4):
            step = (step[0] * step[0] - step[1] * step[1], 2.0 * step[0] * step[1])
            taken = power & bit == bit
            by_real, by_imag = jnp.where(taken, step[0], 1.0), jnp.where(taken, step[1], 0.0)
            real, imag = real * by_real - imag * by_imag, real * by_imag + imag * by_real
        step = (step[0] * step[0] - step[1] * step[1], 2.0 * step[0] * step[1])
        evens, odds = [], []
        for j in range(half // 8):
            if j:
                real, imag = real * step[0] - imag * step[1], real * step[1] + imag * step[0]
            evens.append(real)
            odds.append(real * one_imag + imag * one_real)
        all_rows = jnp.concatenate(evens + odds, axis=0)
        turn[pl.ds(pl.multiple_of(s * 2 * half, 2 * half), 2 * half), :] = all_rows.astype(BF16)
        rows_of[...] = all_rows
        return [rows_of[pl.ds(p * half + mine, own_half), :] for p in range(2)]

    extra.wait()
    extras[...] = jnp.zeros_like(extras)
    for c in range(2):
        values = beam[:, c, :]
        high = values.astype(BF16)
        terms = jnp.concatenate([high, (values - high.astype(F32)).astype(BF16)], axis=0)
        for d in range(len(pieces)):
            rows = pl.ds(c * 2 * beam_orders, 2 * beam_orders)
            extras[d ^ me, rows, :] = terms[:, d * width : (d + 1) * width]
    for j, piece in enumerate(pieces):
        _, sky_orders, cycles, _ = piece.shape
        place = piece.at[beam_orders].reshape(sky_orders * cycles, width)
        leaving += bring((extras.at[j],), (place,), departures, len(pieces) + j)

    mine = me * own_half
    pair = 16 // (2 * own_half)

    run = 16

    @pl.loop(0, blocks // run)
    def _(group):
        for j in range(0, run, pair):
            kept = []
            for i in range(pair):
                block_phases(group * run + j + i)
                kept += block_turns(group * run + j + i)
            start = pl.multiple_of((group * run + j) * 2 * own_half, 16)
            own[pl.ds(start, 16), :] = jnp.concatenate(kept, axis=0).astype(BF16)

    for copy in leaving:
        copy.wait()


def samples_kernel(
    blocks_local, owners_hbm, locals_hbm, noise_hbm, count, arrived, phi, turn, own,
    out, owners, locals_, noise, arrivals, widened,
    stacked, modes_rows, modes, partial, filtered, totals, ordered, shares,
):
    copies = bring((owners_hbm, locals_hbm, noise_hbm), (owners, locals_, noise), arrivals, 0)
    widened[...] = arrived[...].astype(F32)
    sky_devices, rows, lanes = shares.shape
    parts = sky_devices * rows
    beams = arrived.shape[0] // parts
    blocks = partial.shape[0] // 8
    total = turn.shape[0] // blocks
    orders = total // beams
    cycles = lanes // orders
    together = len(totals)
    unroll = 32

    steps = max(1, blocks // (together * unroll))

    def cycle_of(s):
        return (owners[s] * blocks_local + locals_[s]) // CYCLE_BLOCKS

    width = together * parts
    for b in range(beams):
        for row in range(rows):
            some = every(widened, b * parts + row, sky_devices, rows)
            for j in range(together):
                start = j * parts + row * sky_devices
                stacked[b, start : start + sky_devices, :] = some
        modes_rows[b * lanes : (b + 1) * lanes, :] = stacked[b].T
    lane_group = iota((total, width), 1) // parts
    for r in range(cycles):
        halves = [
            modes_rows[pl.ds(r + parity * cycles, total // 2, stride=2 * cycles), :]
            for parity in range(2)
        ]
        values = jnp.concatenate(halves, axis=0)
        for j in range(together):
            modes[r, j] = jnp.where(lane_group == j, values, 0.0).astype(BF16)
    for copy in copies:
        copy.wait()

    def gather(first):
        left = jnp.concatenate([modes[cycle_of(first + j), j] for j in range(together)], axis=0)
        table = phi[pl.ds(pl.multiple_of(first * parts, width), width), :]
        cells = jnp.dot(left, table, preferred_element_type=F32)
        rotation = turn[pl.ds(pl.multiple_of(first * total, together * total), together * total), :]
        turned = (cells * rotation.astype(F32)).reshape(together, total // 8, 8, CELLS)
        kept = jnp.sum(turned, axis=1).reshape(together * 8, CELLS)
        partial[pl.ds(pl.multiple_of(first * 8, together * 8), together * 8), :] = kept

    @pl.loop(0, steps)
    def _(step):
        for i in range(unroll):
            gather((step * unroll + i) * together)

    signal = partial[pl.ds(0, blocks, stride=8), :]
    for i in range(1, 8):
        signal = signal + partial[pl.ds(i, blocks, stride=8), :]
    valid = iota((blocks, CELLS), 0) * CELLS + iota((blocks, CELLS), 1) < count[0]
    signal = jnp.where(valid, signal, 0.0)
    clean = lax.dot_general(
        signal.astype(BF16), noise[...].astype(BF16), LAST_LAST, preferred_element_type=F32
    )
    filtered[...] = jnp.where(valid, clean, 0.0)

    for one in totals:
        one[...] = jnp.zeros_like(one)
    half = orders // 2

    def spread(first):
        rotation = own[pl.ds(pl.multiple_of(first * orders, 16), together * orders), :].astype(F32)
        weighted = [
            rotation[j * orders : (j + 1) * orders] * filtered[pl.ds(first + j, 1), :]
            for j in range(together)
        ]
        weighted = jnp.concatenate(weighted, axis=0).astype(BF16)
        table = phi[pl.ds(pl.multiple_of(first * parts, width), width), :]
        terms = lax.dot_general(weighted, table, LAST_LAST, preferred_element_type=F32)
        for j in range(together):
            row = pl.multiple_of(cycle_of(first + j) * orders, orders)
            here = totals[j]
            here[pl.ds(row, orders), :] += terms[j * orders : (j + 1) * orders]

    @pl.loop(0, steps)
    def _(step):
        for i in range(unroll):
            spread((step * unroll + i) * together)

    gathered = totals[0][...]
    which = iota(gathered.shape, 1) // parts
    for j in range(1, together):
        gathered = jnp.where(which == j, totals[j][...], gathered)
    totals[0][...] = gathered
    for k in range(orders):
        place = k // 2 + (k % 2) * half
        ordered[k * cycles : (k + 1) * cycles, :] = totals[0][pl.ds(place, cycles, stride=orders), :]
    turned = ordered[...].T
    summed = turned[0:parts]
    for j in range(1, together):
        summed = summed + turned[j * parts : (j + 1) * parts]
    for row in range(rows):
        shares[:, row, :] = summed[row * sky_devices : (row + 1) * sky_devices]
    for b in range(beams):
        out[b] = shares[...].astype(BF16)


def gradient_kernel(arrived, pieces, out, modes):
    me = lax.axis_index("beam")
    parts, sky_orders, cycles, width = pieces[0].shape
    orders = parts - 1
    diagonal = own_block(orders, cycles)
    for b in range(len(pieces)):
        modes[b] = jnp.sum(arrived[b].astype(F32), axis=0).astype(BF16).astype(F32)
    first, second = [0.0] * sky_orders, [0.0] * sky_orders
    for j, piece in enumerate(pieces):
        terms = piece[orders].reshape(sky_orders * cycles, width).astype(F32)
        beam_real, beam_imag = [
            terms[2 * c * orders : (2 * c + 1) * orders] + terms[(2 * c + 1) * orders : (2 * c + 2) * orders]
            for c in range(2)
        ]
        these = modes[me ^ j]
        for m in range(sky_orders):
            spreads = []
            for c in range(2):
                row = these[c * sky_orders + m : c * sky_orders + m + 1]
                spreads.append(jnp.where(diagonal, row, 0.0))
            left = jnp.concatenate(spreads, axis=0).astype(BF16)
            table = piece[0:orders, m].reshape(orders * cycles, width)
            harmonics = jnp.dot(left, table, preferred_element_type=F32)
            real, imag = harmonics[:orders], harmonics[orders:]
            first[m] += real * beam_real + imag * beam_imag
            second[m] += imag * beam_real - real * beam_imag
    for m in range(sky_orders):
        out[m, 0:1, :] = jnp.sum(first[m], axis=0, keepdims=True)
        out[m, 1:2, :] = jnp.sum(second[m], axis=0, keepdims=True)


def exchange(pieces, axis):
    count = lax.axis_size(axis)
    return [pieces[0]] + [
        lax.ppermute(pieces[j], axis, [(i, i ^ j) for i in range(count)]) for j in range(1, count)
    ]


def local(
    sky_harmonics,
    beam_harmonics,
    wigner,
    order_map,
    block_owner,
    block_local,
    cell_offset,
    cell_fraction,
    beam_angle,
    sample_count,
    noise_weight,
):
    beams, sky_devices = lax.axis_size("beam"), lax.axis_size("ma")
    orders, sky_orders, cycles, degrees = wigner.shape
    total = orders * beams
    all_sky = sky_orders * sky_devices
    parts = 2 * all_sky
    blocks = block_local.shape[0]
    blocks_local = cycles // sky_devices * CYCLE_BLOCKS
    width = degrees // beams
    lanes = orders * cycles
    rows = 2 * sky_orders
    together = max(1, CELLS // parts)
    owners = block_owner.reshape(blocks)
    limit = pltpu.CompilerParams(vmem_limit_bytes=32 * 1024 * 1024)
    integers = [
        pltpu.SMEM((blocks,), jnp.int32),
        pltpu.SMEM((blocks,), jnp.int32),
    ]

    def pinned(*arrays):
        return [pltpu.with_memory_space_constraint(array, pltpu.HBM) for array in arrays]

    sent = pl.pallas_call(
        modes_kernel,
        out_shape=pltpu.VMEM((beams * sky_devices, rows, lanes), BF16),
        in_specs=hbm(3),
        out_specs=vmem(1)[0],
        scratch_shapes=[
            pltpu.VMEM(sky_harmonics.shape, F32),
            pltpu.VMEM(beam_harmonics.shape, F32),
            pltpu.VMEM((beams, orders, sky_orders, cycles, width), BF16),
            pltpu.SemaphoreType.DMA((2 + beams,)),
        ],
        compiler_params=limit,
        name="modes",
    )(*pinned(sky_harmonics, beam_harmonics, wigner))
    arrived = lax.all_to_all(sent, ("beam", "ma"), split_axis=0, concat_axis=0, tiled=True)

    samples = pltpu.VMEM((blocks, CELLS), F32)
    piece = (orders + 1, sky_orders, cycles, width)
    phi, turn, own, pieces = pl.pallas_call(
        functools.partial(tables_kernel, blocks_local, sky_devices),
        out_shape=[
            pltpu.VMEM((blocks * parts, CELLS), BF16),
            pltpu.VMEM((blocks * total, CELLS), BF16),
            pltpu.VMEM((blocks * orders, CELLS), BF16),
            [pltpu.HBM(piece, BF16)] * beams,
        ],
        in_specs=hbm(9),
        out_specs=[*vmem(3), hbm(beams)],
        scratch_shapes=[
            pltpu.VMEM(beam_harmonics.shape, F32),
            pltpu.VMEM((beams, sky_orders * cycles, width), BF16),
            pltpu.SemaphoreType.DMA((2 * beams,)),
            pltpu.SMEM((all_sky,), jnp.int32),
            *integers,
            samples,
            pltpu.VMEM((blocks, CELLS), jnp.int32),
            samples,
            pltpu.SemaphoreType.DMA((7,)),
            pltpu.VMEM((CYCLE_BLOCKS, all_sky, CELLS), F32),
            pltpu.VMEM((CYCLE_BLOCKS, all_sky, CELLS), F32),
            samples,
            samples,
            pltpu.VMEM((total, CELLS), F32),
        ],
        compiler_params=limit,
        cost_estimate=pl.CostEstimate(flops=100_000_000, bytes_accessed=4_000_000, transcendentals=0),
        name="tables",
    )(
        *pinned(
            sent, order_map, owners, block_local,
            beam_angle.reshape(blocks, CELLS),
            cell_offset.reshape(blocks, CELLS),
            cell_fraction.reshape(blocks, CELLS),
            beam_harmonics, wigner,
        )
    )
    pieces = exchange(pieces, "beam")

    grads = pl.pallas_call(
        functools.partial(samples_kernel, blocks_local),
        out_shape=jax.ShapeDtypeStruct((beams, sky_devices, rows, lanes), BF16),
        in_specs=hbm(3) + smem(1) + vmem(4),
        out_specs=vmem(1)[0],
        scratch_shapes=[
            *integers,
            pltpu.VMEM((CELLS, CELLS), F32),
            pltpu.SemaphoreType.DMA((3,)),
            pltpu.VMEM((beams * parts, lanes), F32),
            pltpu.VMEM((beams, together * parts, lanes), F32),
            pltpu.VMEM((beams * lanes, together * parts), F32),
            pltpu.VMEM((cycles, together, total, together * parts), BF16),
            pltpu.VMEM((blocks * 8, CELLS), F32),
            samples,
            [pltpu.VMEM((lanes, together * parts), F32) for _ in range(together)],
            pltpu.VMEM((lanes, together * parts), F32),
            pltpu.VMEM((sky_devices, rows, lanes), F32),
        ],
        compiler_params=limit,
        cost_estimate=pl.CostEstimate(flops=40_000_000_000, bytes_accessed=100_000_000, transcendentals=0),
        name="samples",
    )(
        *pinned(owners, block_local, noise_weight),
        sample_count,
        arrived.reshape(beams * parts, lanes), phi, turn, own,
    )
    grads = grads.reshape(beams * sky_devices, rows, lanes)
    grads = lax.all_to_all(grads, ("beam", "ma"), split_axis=0, concat_axis=0, tiled=True)
    return pl.pallas_call(
        gradient_kernel,
        out_shape=jax.ShapeDtypeStruct((sky_orders, 2, width), F32),
        in_specs=[vmem(1)[0], vmem(beams)],
        out_specs=vmem(1)[0],
        scratch_shapes=[pltpu.VMEM((beams, rows, lanes), F32)],
        compiler_params=limit,
        name="gradient",
    )(grads.reshape(beams, sky_devices, rows, lanes), pieces)


def solution(mesh):
    return jax.shard_map(
        local,
        mesh=mesh,
        in_specs=(
            P("ma", None, None),
            P("beam", None, None),
            P("beam", "ma", None, None),
            P(),
            P("ma", None),
            P("ma"),
            P("ma"),
            P("ma"),
            P("ma"),
            P("ma"),
            P(),
        ),
        out_specs=P("ma", None, "beam"),
        check_vma=False,
    )
```

```python
import functools
import math

import jax
import jax.numpy as jnp
from jax import lax
from jax.experimental import pallas as pl
from jax.experimental.pallas import tpu as pltpu
from jax.sharding import PartitionSpec as P

PHI = 4096
CELLS = 128
CYCLE_BLOCKS = PHI // CELLS
F32 = jnp.float32
BF16 = jnp.bfloat16
LAST_LAST = (((1,), (1,)), ((), ()))


def iota(shape, axis):
    return lax.broadcasted_iota(jnp.int32, shape, axis)


def vmem(count):
    return [pl.BlockSpec(memory_space=pltpu.VMEM)] * count


def smem(count):
    return [pl.BlockSpec(memory_space=pltpu.SMEM)] * count


def hbm(count):
    return [pl.BlockSpec(memory_space=pltpu.HBM)] * count


def sine_turns(z):
    square = z * z
    value = 39.53670603 * square - 76.54978229
    value = value * square + 81.60100407
    value = value * square - 41.34165503
    value = value * square + 6.28318516
    return value * z


def cosine_steps(steps):
    centred = ((steps + PHI // 2) & (PHI - 1)) - PHI // 2
    return sine_turns(0.25 - jnp.abs(centred).astype(F32) * (1.0 / PHI))


def every(ref, first, count, step):
    if ref.shape[1] == CELLS:
        return ref[pl.ds(first, count, stride=step), :]
    return jnp.concatenate([ref[first + i * step][None] for i in range(count)], axis=0)


def bring(sources, places, semaphores, first):
    copies = [
        pltpu.make_async_copy(source, place, semaphores.at[first + i])
        for i, (source, place) in enumerate(zip(sources, places))
    ]
    for copy in copies:
        copy.start()
    return copies


def own_block(orders, cycles):
    shape = (orders, orders * cycles)
    return iota(shape, 1) // cycles == iota(shape, 0)


def modes_kernel(sky_hbm, beam_hbm, wigner_hbm, out, sky, beam, wigner, arrivals):
    chunks, orders, sky_orders, cycles, width = wigner.shape
    small = bring((sky_hbm, beam_hbm), (sky, beam), arrivals, 0)
    spans = [pl.ds(i * width, width) for i in range(chunks)]
    large = bring([wigner_hbm.at[:, :, :, span] for span in spans], [wigner.at[i] for i in range(chunks)], arrivals, 2)
    for copy in small:
        copy.wait()
    beam_real, beam_imag = beam[:, 0, :], beam[:, 1, :]
    diagonal = own_block(orders, cycles)
    products = []
    for m in range(sky_orders):
        sky_real, sky_imag = sky[m, 0:1, :], sky[m, 1:2, :]
        first = sky_real * beam_real - sky_imag * beam_imag
        second = sky_real * beam_imag + sky_imag * beam_real
        products.append(jnp.concatenate([first, second], axis=0).astype(BF16))
    sums = [0.0] * sky_orders
    for i in range(chunks):
        large[i].wait()
        for m in range(sky_orders):
            table = wigner[i, :, m].reshape(orders * cycles, width)
            left = products[m][:, i * width : (i + 1) * width]
            sums[m] += lax.dot_general(table, left, LAST_LAST, preferred_element_type=F32)
    rows = [None] * (2 * sky_orders)
    for m in range(sky_orders):
        modes = sums[m].T
        for c in range(2):
            part = jnp.where(diagonal, modes[c * orders : (c + 1) * orders], 0.0)
            rows[c * sky_orders + m] = jnp.sum(part, axis=0, keepdims=True)
    block = jnp.concatenate(rows, axis=0).astype(BF16)
    for d in range(out.shape[0]):
        out[d] = block


def tables_kernel(
    blocks_local, sky_devices,
    after, order_hbm, owners_hbm, locals_hbm, angles_hbm, offsets_hbm, fractions_hbm, beam_hbm, wigner_hbm,
    phi, turn, own, pieces_hbm, pieces, beam, departures, order_map, owners, locals_, angles, offsets, fractions, arrivals,
    step_real, step_imag, cosines, sines, rows_of,
):
    sources = (order_hbm, owners_hbm, locals_hbm, angles_hbm, offsets_hbm, fractions_hbm)
    places = (order_map, owners, locals_, angles, offsets, fractions)
    copies = bring(sources, places, arrivals, 0)
    me = lax.axis_index("beam")
    extra = bring((beam_hbm,), (beam,), arrivals, 6)[0]
    beams, beam_orders, width = pieces.shape[0], beam.shape[0], pieces.shape[4]
    spans = [pl.ds(pl.multiple_of((me ^ j) * width, width), width) for j in range(beams)]
    arriving = bring(
        [wigner_hbm.at[:, :, :, span] for span in spans],
        [pieces.at[j, 0:beam_orders] for j in range(beams)],
        departures, 0,
    )
    orders = order_map.shape[0]
    blocks = offsets.shape[0]
    half = turn.shape[0] // blocks // 2
    own_half = own.shape[0] // blocks // 2

    copies[0].wait()
    order = jnp.zeros((orders, CELLS), jnp.int32)
    row = iota((orders, CELLS), 0)
    lane = iota((orders, CELLS), 1)
    for m in range(orders):
        place = m % (orders // sky_devices) * sky_devices + m // (orders // sky_devices)
        order = jnp.where(row == place, order_map[m], order)

    def phase(steps):
        return cosine_steps(steps), cosine_steps(steps + PHI // 4)

    scaling = 1.0 / math.sqrt(orders)
    cell_real, cell_imag = phase(order * lane)
    cell_real, cell_imag = cell_real * scaling, cell_imag * scaling
    next_real, next_imag = phase(order)
    next_real = next_real - 1.0
    first_real, first_imag = phase(((order * CELLS) & (PHI - 1)) * lane)
    for j in range(CYCLE_BLOCKS):
        step_real[j] = jnp.broadcast_to(first_real[:, j : j + 1], (orders, CELLS))
        step_imag[j] = jnp.broadcast_to(first_imag[:, j : j + 1], (orders, CELLS))

    for copy in copies[1:]:
        copy.wait()
    part = angles[...] * (0.5 / math.pi)
    part = part - jnp.round(part)
    cosines[...] = sine_turns(0.25 - jnp.abs(part))
    folded = jnp.where(part > 0.25, 0.5 - part, jnp.where(part < -0.25, -0.5 - part, part))
    sines[...] = sine_turns(folded)

    def block_phases(s):
        place = (owners[s] * blocks_local + locals_[s]) & (CYCLE_BLOCKS - 1)
        offset = jnp.broadcast_to(offsets[pl.ds(s, 1), :], (orders, CELLS))
        fraction = jnp.broadcast_to(fractions[pl.ds(s, 1), :], (orders, CELLS))
        real = jnp.take_along_axis(cell_real, offset, axis=1, mode="promise_in_bounds")
        imag = jnp.take_along_axis(cell_imag, offset, axis=1, mode="promise_in_bounds")
        base_real, base_imag = step_real[place], step_imag[place]
        left_real = real * base_real - imag * base_imag
        left_imag = real * base_imag + imag * base_real
        mix_real = 1.0 + fraction * next_real
        mix_imag = fraction * next_imag
        both = jnp.concatenate(
            [left_real * mix_real - left_imag * mix_imag, left_real * mix_imag + left_imag * mix_real],
            axis=0,
        )
        start = pl.multiple_of(s * 2 * orders, 2 * orders)
        phi[pl.ds(start, 2 * orders), :] = both.astype(BF16)

    scale = 1.0 / math.sqrt(2 * half)
    power = iota((8, CELLS), 0)

    def block_turns(s, rows_of):
        one_real = jnp.broadcast_to(cosines[pl.ds(s, 1), :], (8, CELLS))
        one_imag = jnp.broadcast_to(sines[pl.ds(s, 1), :], (8, CELLS))
        step = (one_real, one_imag)
        odd = power & 1 == 1
        real, imag = jnp.where(odd, one_real * scale, scale), jnp.where(odd, one_imag * scale, 0.0)
        for bit in (2, 4):
            step = (step[0] * step[0] - step[1] * step[1], 2.0 * step[0] * step[1])
            taken = power & bit == bit
            by_real, by_imag = jnp.where(taken, step[0], 1.0), jnp.where(taken, step[1], 0.0)
            real, imag = real * by_real - imag * by_imag, real * by_imag + imag * by_real
        step = (step[0] * step[0] - step[1] * step[1], 2.0 * step[0] * step[1])
        evens, odds = [], []
        for j in range(half // 8):
            if j:
                real, imag = real * step[0] - imag * step[1], real * step[1] + imag * step[0]
            evens.append(real)
            odds.append(real * one_imag + imag * one_real)
        all_rows = jnp.concatenate(evens + odds, axis=0)
        turn[pl.ds(pl.multiple_of(s * 2 * half, 2 * half), 2 * half), :] = all_rows.astype(BF16)
        rows_of[...] = all_rows
        return [rows_of[pl.ds(p * half + mine, own_half), :] for p in range(2)]

    extra.wait()
    sky_orders, cycles = pieces.shape[2:4]
    for j, span in enumerate(spans):
        terms = []
        for c in range(2):
            values = beam[:, c, span]
            high = values.astype(BF16)
            terms += [high, (values - high.astype(F32)).astype(BF16)]
        filling = sky_orders * cycles - 4 * beam_orders
        if filling:
            terms.append(jnp.zeros((filling, width), BF16))
        pieces[j, beam_orders] = jnp.concatenate(terms, axis=0).reshape(sky_orders, cycles, width)
    for copy in arriving:
        copy.wait()
    leaving = bring([pieces.at[j] for j in range(beams)], pieces_hbm, departures, beams)

    mine = me * own_half
    pair = 16 // (2 * own_half)

    run = rows_of.shape[0]

    @pl.loop(0, blocks // run)
    def _(group):
        for j in range(0, run, pair):
            kept = []
            for i in range(pair):
                block_phases(group * run + j + i)
                kept += block_turns(group * run + j + i, rows_of.at[j + i])
            start = pl.multiple_of((group * run + j) * 2 * own_half, 16)
            own[pl.ds(start, 16), :] = jnp.concatenate(kept, axis=0).astype(BF16)

    for copy in leaving:
        copy.wait()


def samples_kernel(
    blocks_local, owners_hbm, locals_hbm, noise_hbm, count, arrived, phi, turn, own,
    out, owners, locals_, noise, arrivals, widened,
    stacked, modes_rows, modes, partial, filtered, totals, ordered, shares,
):
    copies = bring((owners_hbm, locals_hbm, noise_hbm), (owners, locals_, noise), arrivals, 0)
    widened[...] = arrived[...].astype(F32)
    sky_devices, rows, lanes = shares.shape
    parts = sky_devices * rows
    beams = arrived.shape[0] // parts
    blocks = partial.shape[0] // 8
    total = turn.shape[0] // blocks
    orders = total // beams
    cycles = lanes // orders
    together = len(totals)
    unroll = 32

    steps = max(1, blocks // (together * unroll))

    def cycle_of(s):
        return (owners[s] * blocks_local + locals_[s]) // CYCLE_BLOCKS

    width = together * parts
    for b in range(beams):
        for row in range(rows):
            some = every(widened, b * parts + row, sky_devices, rows)
            for j in range(together):
                start = j * parts + row * sky_devices
                stacked[b, start : start + sky_devices, :] = some
        modes_rows[b * lanes : (b + 1) * lanes, :] = stacked[b].T
    lane_group = iota((total, width), 1) // parts
    for r in range(cycles):
        halves = [
            modes_rows[pl.ds(r + parity * cycles, total // 2, stride=2 * cycles), :]
            for parity in range(2)
        ]
        values = jnp.concatenate(halves, axis=0)
        for j in range(together):
            modes[r, j] = jnp.where(lane_group == j, values, 0.0).astype(BF16)
    for copy in copies:
        copy.wait()

    def gather(first):
        left = jnp.concatenate([modes[cycle_of(first + j), j] for j in range(together)], axis=0)
        table = phi[pl.ds(pl.multiple_of(first * parts, width), width), :]
        cells = jnp.dot(left, table, preferred_element_type=F32)
        rotation = turn[pl.ds(pl.multiple_of(first * total, together * total), together * total), :]
        turned = (cells * rotation.astype(F32)).reshape(together, total // 8, 8, CELLS)
        kept = jnp.sum(turned, axis=1).reshape(together * 8, CELLS)
        partial[pl.ds(pl.multiple_of(first * 8, together * 8), together * 8), :] = kept

    @pl.loop(0, steps)
    def _(step):
        for i in range(unroll):
            gather((step * unroll + i) * together)

    signal = partial[pl.ds(0, blocks, stride=8), :]
    for i in range(1, 8):
        signal = signal + partial[pl.ds(i, blocks, stride=8), :]
    valid = iota((blocks, CELLS), 0) * CELLS + iota((blocks, CELLS), 1) < count[0]
    signal = jnp.where(valid, signal, 0.0)
    clean = lax.dot_general(
        signal.astype(BF16), noise[...].astype(BF16), LAST_LAST, preferred_element_type=F32
    )
    filtered[...] = jnp.where(valid, clean, 0.0)

    for one in totals:
        one[...] = jnp.zeros_like(one)
    half = orders // 2

    def spread(first):
        rotation = own[pl.ds(pl.multiple_of(first * orders, 16), together * orders), :].astype(F32)
        weighted = [
            rotation[j * orders : (j + 1) * orders] * filtered[pl.ds(first + j, 1), :]
            for j in range(together)
        ]
        weighted = jnp.concatenate(weighted, axis=0).astype(BF16)
        table = phi[pl.ds(pl.multiple_of(first * parts, width), width), :]
        terms = lax.dot_general(weighted, table, LAST_LAST, preferred_element_type=F32)
        for j in range(together):
            row = pl.multiple_of(cycle_of(first + j) * orders, orders)
            here = totals[j]
            here[pl.ds(row, orders), :] += terms[j * orders : (j + 1) * orders]

    @pl.loop(0, steps)
    def _(step):
        for i in range(unroll):
            spread((step * unroll + i) * together)

    gathered = totals[0][...]
    which = iota(gathered.shape, 1) // parts
    for j in range(1, together):
        gathered = jnp.where(which == j, totals[j][...], gathered)
    totals[0][...] = gathered
    for k in range(orders):
        place = k // 2 + (k % 2) * half
        ordered[k * cycles : (k + 1) * cycles, :] = totals[0][pl.ds(place, cycles, stride=orders), :]
    turned = ordered[...].T
    summed = turned[0:parts]
    for j in range(1, together):
        summed = summed + turned[j * parts : (j + 1) * parts]
    for row in range(rows):
        shares[:, row, :] = summed[row * sky_devices : (row + 1) * sky_devices]
    for b in range(beams):
        out[b] = shares[...].astype(BF16)


def gradient_kernel(arrived, pieces, out, modes):
    me = lax.axis_index("beam")
    parts, sky_orders, cycles, width = pieces[0].shape
    orders = parts - 1
    diagonal = own_block(orders, cycles)
    for b in range(len(pieces)):
        modes[b] = jnp.sum(arrived[b].astype(F32), axis=0).astype(BF16).astype(F32)
    first, second = [0.0] * sky_orders, [0.0] * sky_orders
    for j, piece in enumerate(pieces):
        terms = piece[orders].reshape(sky_orders * cycles, width).astype(F32)
        beam_real, beam_imag = [
            terms[2 * c * orders : (2 * c + 1) * orders] + terms[(2 * c + 1) * orders : (2 * c + 2) * orders]
            for c in range(2)
        ]
        these = modes[me ^ j]
        for m in range(sky_orders):
            spreads = []
            for c in range(2):
                row = these[c * sky_orders + m : c * sky_orders + m + 1]
                spreads.append(jnp.where(diagonal, row, 0.0))
            left = jnp.concatenate(spreads, axis=0).astype(BF16)
            table = piece[0:orders, m].reshape(orders * cycles, width)
            harmonics = jnp.dot(left, table, preferred_element_type=F32)
            real, imag = harmonics[:orders], harmonics[orders:]
            first[m] += real * beam_real + imag * beam_imag
            second[m] += imag * beam_real - real * beam_imag
    for m in range(sky_orders):
        out[m, 0:1, :] = jnp.sum(first[m], axis=0, keepdims=True)
        out[m, 1:2, :] = jnp.sum(second[m], axis=0, keepdims=True)


def exchange(pieces, axis):
    count = lax.axis_size(axis)
    return [pieces[0]] + [
        lax.ppermute(pieces[j], axis, [(i, i ^ j) for i in range(count)]) for j in range(1, count)
    ]


def local(
    sky_harmonics,
    beam_harmonics,
    wigner,
    order_map,
    block_owner,
    block_local,
    cell_offset,
    cell_fraction,
    beam_angle,
    sample_count,
    noise_weight,
):
    beams, sky_devices = lax.axis_size("beam"), lax.axis_size("ma")
    orders, sky_orders, cycles, degrees = wigner.shape
    total = orders * beams
    all_sky = sky_orders * sky_devices
    parts = 2 * all_sky
    blocks = block_local.shape[0]
    blocks_local = cycles // sky_devices * CYCLE_BLOCKS
    width = degrees // beams
    lanes = orders * cycles
    rows = 2 * sky_orders
    together = max(1, CELLS // parts)
    owners = block_owner.reshape(blocks)
    limit = pltpu.CompilerParams(vmem_limit_bytes=32 * 1024 * 1024)
    integers = [
        pltpu.SMEM((blocks,), jnp.int32),
        pltpu.SMEM((blocks,), jnp.int32),
    ]

    def pinned(*arrays):
        return [pltpu.with_memory_space_constraint(array, pltpu.HBM) for array in arrays]

    sent = pl.pallas_call(
        modes_kernel,
        out_shape=pltpu.VMEM((beams * sky_devices, rows, lanes), BF16),
        in_specs=hbm(3),
        out_specs=vmem(1)[0],
        scratch_shapes=[
            pltpu.VMEM(sky_harmonics.shape, F32),
            pltpu.VMEM(beam_harmonics.shape, F32),
            pltpu.VMEM((beams, orders, sky_orders, cycles, width), BF16),
            pltpu.SemaphoreType.DMA((2 + beams,)),
        ],
        compiler_params=limit,
        name="modes",
    )(*pinned(sky_harmonics, beam_harmonics, wigner))
    arrived = lax.all_to_all(sent, ("beam", "ma"), split_axis=0, concat_axis=0, tiled=True)

    samples = pltpu.VMEM((blocks, CELLS), F32)
    piece = (orders + 1, sky_orders, cycles, width)
    phi, turn, own, pieces = pl.pallas_call(
        functools.partial(tables_kernel, blocks_local, sky_devices),
        out_shape=[
            pltpu.VMEM((blocks * parts, CELLS), BF16),
            pltpu.VMEM((blocks * total, CELLS), BF16),
            pltpu.VMEM((blocks * orders, CELLS), BF16),
            [pltpu.HBM(piece, BF16)] * beams,
        ],
        in_specs=hbm(9),
        out_specs=[*vmem(3), hbm(beams)],
        scratch_shapes=[
            pltpu.VMEM((beams, *piece), BF16),
            pltpu.VMEM(beam_harmonics.shape, F32),
            pltpu.SemaphoreType.DMA((2 * beams,)),
            pltpu.SMEM((all_sky,), jnp.int32),
            *integers,
            samples,
            pltpu.VMEM((blocks, CELLS), jnp.int32),
            samples,
            pltpu.SemaphoreType.DMA((7,)),
            pltpu.VMEM((CYCLE_BLOCKS, all_sky, CELLS), F32),
            pltpu.VMEM((CYCLE_BLOCKS, all_sky, CELLS), F32),
            samples,
            samples,
            pltpu.VMEM((16, total, CELLS), F32),
        ],
        compiler_params=limit,
        cost_estimate=pl.CostEstimate(flops=100_000_000, bytes_accessed=4_000_000, transcendentals=0),
        name="tables",
    )(
        *pinned(
            sent, order_map, owners, block_local,
            beam_angle.reshape(blocks, CELLS),
            cell_offset.reshape(blocks, CELLS),
            cell_fraction.reshape(blocks, CELLS),
            beam_harmonics, wigner,
        )
    )
    pieces = exchange(pieces, "beam")

    grads = pl.pallas_call(
        functools.partial(samples_kernel, blocks_local),
        out_shape=jax.ShapeDtypeStruct((beams, sky_devices, rows, lanes), BF16),
        in_specs=hbm(3) + smem(1) + vmem(4),
        out_specs=vmem(1)[0],
        scratch_shapes=[
            *integers,
            pltpu.VMEM((CELLS, CELLS), F32),
            pltpu.SemaphoreType.DMA((3,)),
            pltpu.VMEM((beams * parts, lanes), F32),
            pltpu.VMEM((beams, together * parts, lanes), F32),
            pltpu.VMEM((beams * lanes, together * parts), F32),
            pltpu.VMEM((cycles, together, total, together * parts), BF16),
            pltpu.VMEM((blocks * 8, CELLS), F32),
            samples,
            [pltpu.VMEM((lanes, together * parts), F32) for _ in range(together)],
            pltpu.VMEM((lanes, together * parts), F32),
            pltpu.VMEM((sky_devices, rows, lanes), F32),
        ],
        compiler_params=limit,
        cost_estimate=pl.CostEstimate(flops=40_000_000_000, bytes_accessed=100_000_000, transcendentals=0),
        name="samples",
    )(
        *pinned(owners, block_local, noise_weight),
        sample_count,
        arrived.reshape(beams * parts, lanes), phi, turn, own,
    )
    grads = grads.reshape(beams * sky_devices, rows, lanes)
    grads = lax.all_to_all(grads, ("beam", "ma"), split_axis=0, concat_axis=0, tiled=True)
    return pl.pallas_call(
        gradient_kernel,
        out_shape=jax.ShapeDtypeStruct((sky_orders, 2, width), F32),
        in_specs=[vmem(1)[0], vmem(beams)],
        out_specs=vmem(1)[0],
        scratch_shapes=[pltpu.VMEM((beams, rows, lanes), F32)],
        compiler_params=limit,
        name="gradient",
    )(grads.reshape(beams, sky_devices, rows, lanes), pieces)


def solution(mesh):
    return jax.shard_map(
        local,
        mesh=mesh,
        in_specs=(
            P("ma", None, None),
            P("beam", None, None),
            P("beam", "ma", None, None),
            P(),
            P("ma", None),
            P("ma"),
            P("ma"),
            P("ma"),
            P("ma"),
            P("ma"),
            P(),
        ),
        out_specs=P("ma", None, "beam"),
        check_vma=False,
    )
```

```python
import functools
import math

import jax
import jax.numpy as jnp
from jax import lax
from jax.experimental import pallas as pl
from jax.experimental.pallas import tpu as pltpu
from jax.sharding import PartitionSpec as P

PHI = 4096
CELLS = 128
CYCLE_BLOCKS = PHI // CELLS
F32 = jnp.float32
BF16 = jnp.bfloat16
LAST_LAST = (((1,), (1,)), ((), ()))


def iota(shape, axis):
    return lax.broadcasted_iota(jnp.int32, shape, axis)


def vmem(count):
    return [pl.BlockSpec(memory_space=pltpu.VMEM)] * count


def smem(count):
    return [pl.BlockSpec(memory_space=pltpu.SMEM)] * count


def hbm(count):
    return [pl.BlockSpec(memory_space=pltpu.HBM)] * count


def sine_turns(z):
    square = z * z
    value = 39.53670603 * square - 76.54978229
    value = value * square + 81.60100407
    value = value * square - 41.34165503
    value = value * square + 6.28318516
    return value * z


def cosine_steps(steps):
    centred = ((steps + PHI // 2) & (PHI - 1)) - PHI // 2
    return sine_turns(0.25 - jnp.abs(centred).astype(F32) * (1.0 / PHI))


def every(ref, first, count, step):
    if ref.shape[1] == CELLS:
        return ref[pl.ds(first, count, stride=step), :]
    return jnp.concatenate([ref[first + i * step][None] for i in range(count)], axis=0)


def bring(sources, places, semaphores, first):
    copies = [
        pltpu.make_async_copy(source, place, semaphores.at[first + i])
        for i, (source, place) in enumerate(zip(sources, places))
    ]
    for copy in copies:
        copy.start()
    return copies


def own_block(orders, cycles):
    shape = (orders, orders * cycles)
    return iota(shape, 1) // cycles == iota(shape, 0)


def modes_kernel(sky_hbm, beam_hbm, wigner_hbm, later_hbm, out, later, sky, beam, wigner, arrivals):
    chunks, orders, sky_orders, cycles, width = wigner.shape
    small = bring((sky_hbm, beam_hbm), (sky, beam), arrivals, 0)
    spans = [pl.ds(i * width, width) for i in range(chunks)]
    large = bring([wigner_hbm.at[:, :, :, span] for span in spans], [wigner.at[i] for i in range(chunks)], arrivals, 2)
    others = bring(later_hbm, later, arrivals, 2 + chunks)
    for copy in small:
        copy.wait()
    beam_real, beam_imag = beam[:, 0, :], beam[:, 1, :]
    diagonal = own_block(orders, cycles)
    products = []
    for m in range(sky_orders):
        sky_real, sky_imag = sky[m, 0:1, :], sky[m, 1:2, :]
        first = sky_real * beam_real - sky_imag * beam_imag
        second = sky_real * beam_imag + sky_imag * beam_real
        products.append(jnp.concatenate([first, second], axis=0).astype(BF16))
    sums = [0.0] * sky_orders
    for i in range(chunks):
        large[i].wait()
        for m in range(sky_orders):
            table = wigner[i, :, m].reshape(orders * cycles, width)
            left = products[m][:, i * width : (i + 1) * width]
            sums[m] += lax.dot_general(table, left, LAST_LAST, preferred_element_type=F32)
    rows = [None] * (2 * sky_orders)
    for m in range(sky_orders):
        modes = sums[m].T
        for c in range(2):
            part = jnp.where(diagonal, modes[c * orders : (c + 1) * orders], 0.0)
            rows[c * sky_orders + m] = jnp.sum(part, axis=0, keepdims=True)
    block = jnp.concatenate(rows, axis=0).astype(BF16)
    for d in range(out.shape[0]):
        out[d] = block
    for copy in others:
        copy.wait()


def tables_kernel(
    blocks_local, sky_devices,
    order_vmem, owners_vmem, locals_vmem, angles, offsets, fractions, beam_hbm, wigner_hbm,
    phi, turn, own, pieces_hbm, pieces, beam, departures, order_map, owners, locals_, arrivals,
    step_real, step_imag, powers, rows_of,
):
    copies = bring((order_vmem, owners_vmem, locals_vmem), (order_map, owners, locals_), arrivals, 0)
    me = lax.axis_index("beam")
    extra = bring((beam_hbm,), (beam,), arrivals, 3)[0]
    beams, beam_orders, width = pieces.shape[0], beam.shape[0], pieces.shape[4]
    spans = [pl.ds(pl.multiple_of((me ^ j) * width, width), width) for j in range(beams)]
    arriving = bring(
        [wigner_hbm.at[:, :, :, span] for span in spans],
        [pieces.at[j, 0:beam_orders] for j in range(beams)],
        departures, 0,
    )
    orders = order_map.shape[0]
    blocks = offsets.shape[0]
    half = turn.shape[0] // blocks // 2
    own_half = own.shape[0] // blocks // 2

    part = angles[...] * (0.5 / math.pi)
    part = part - jnp.round(part)
    folded = jnp.where(part > 0.25, 0.5 - part, jnp.where(part < -0.25, -0.5 - part, part))
    real, imag = sine_turns(0.25 - jnp.abs(part)), sine_turns(folded)
    for i in range(4):
        if i:
            real, imag = real * real - imag * imag, 2.0 * real * imag
        powers[2 * i], powers[2 * i + 1] = real, imag

    copies[0].wait()
    order = jnp.zeros((orders, CELLS), jnp.int32)
    row = iota((orders, CELLS), 0)
    lane = iota((orders, CELLS), 1)
    for m in range(orders):
        place = m % (orders // sky_devices) * sky_devices + m // (orders // sky_devices)
        order = jnp.where(row == place, order_map[m], order)

    def phase(steps):
        return cosine_steps(steps), cosine_steps(steps + PHI // 4)

    scaling = 1.0 / math.sqrt(orders)
    cell_real, cell_imag = phase(order * lane)
    cell_real, cell_imag = cell_real * scaling, cell_imag * scaling
    next_real, next_imag = phase(order)
    next_real = next_real - 1.0
    first_real, first_imag = phase(((order * CELLS) & (PHI - 1)) * lane)
    for j in range(CYCLE_BLOCKS):
        step_real[j] = jnp.broadcast_to(first_real[:, j : j + 1], (orders, CELLS))
        step_imag[j] = jnp.broadcast_to(first_imag[:, j : j + 1], (orders, CELLS))
    for copy in copies[1:]:
        copy.wait()

    def block_phases(s):
        place = (owners[s] * blocks_local + locals_[s]) & (CYCLE_BLOCKS - 1)
        offset = jnp.broadcast_to(offsets[pl.ds(s, 1), :], (orders, CELLS))
        fraction = jnp.broadcast_to(fractions[pl.ds(s, 1), :], (orders, CELLS))
        real = jnp.take_along_axis(cell_real, offset, axis=1, mode="promise_in_bounds")
        imag = jnp.take_along_axis(cell_imag, offset, axis=1, mode="promise_in_bounds")
        base_real, base_imag = step_real[place], step_imag[place]
        left_real = real * base_real - imag * base_imag
        left_imag = real * base_imag + imag * base_real
        mix_real = 1.0 + fraction * next_real
        mix_imag = fraction * next_imag
        both = jnp.concatenate(
            [left_real * mix_real - left_imag * mix_imag, left_real * mix_imag + left_imag * mix_real],
            axis=0,
        )
        start = pl.multiple_of(s * 2 * orders, 2 * orders)
        phi[pl.ds(start, 2 * orders), :] = both.astype(BF16)

    scale = 1.0 / math.sqrt(2 * half)
    power = iota((8, CELLS), 0)

    def block_turns(s, rows_of):
        steps = [jnp.broadcast_to(powers[i, pl.ds(s, 1), :], (8, CELLS)) for i in range(8)]
        one_real, one_imag = steps[:2]
        step = steps[6:]
        odd = power & 1 == 1
        real, imag = jnp.where(odd, one_real * scale, scale), jnp.where(odd, one_imag * scale, 0.0)
        for bit in (2, 4):
            taken = power & bit == bit
            by_real, by_imag = jnp.where(taken, steps[bit], 1.0), jnp.where(taken, steps[bit + 1], 0.0)
            real, imag = real * by_real - imag * by_imag, real * by_imag + imag * by_real
        evens, odds = [], []
        for j in range(half // 8):
            if j:
                real, imag = real * step[0] - imag * step[1], real * step[1] + imag * step[0]
            evens.append(real)
            odds.append(real * one_imag + imag * one_real)
        all_rows = jnp.concatenate(evens + odds, axis=0)
        turn[pl.ds(pl.multiple_of(s * 2 * half, 2 * half), 2 * half), :] = all_rows.astype(BF16)
        rows_of[...] = all_rows
        return [rows_of[pl.ds(p * half + mine, own_half), :] for p in range(2)]

    extra.wait()
    sky_orders, cycles = pieces.shape[2:4]
    for j, span in enumerate(spans):
        terms = []
        for c in range(2):
            values = beam[:, c, span]
            high = values.astype(BF16)
            terms += [high, (values - high.astype(F32)).astype(BF16)]
        filling = sky_orders * cycles - 4 * beam_orders
        if filling:
            terms.append(jnp.zeros((filling, width), BF16))
        pieces[j, beam_orders] = jnp.concatenate(terms, axis=0).reshape(sky_orders, cycles, width)
    for copy in arriving:
        copy.wait()
    leaving = bring([pieces.at[j] for j in range(beams)], pieces_hbm, departures, beams)

    mine = me * own_half
    pair = 16 // (2 * own_half)

    run = rows_of.shape[0]

    @pl.loop(0, blocks // run)
    def _(group):
        for j in range(0, run, pair):
            kept = []
            for i in range(pair):
                block_phases(group * run + j + i)
                kept += block_turns(group * run + j + i, rows_of.at[j + i])
            start = pl.multiple_of((group * run + j) * 2 * own_half, 16)
            own[pl.ds(start, 16), :] = jnp.concatenate(kept, axis=0).astype(BF16)

    for copy in leaving:
        copy.wait()


def samples_kernel(
    blocks_local, owners_vmem, locals_vmem, count, noise, arrived, phi, turn, own,
    out, owners, locals_, arrivals, widened,
    stacked, modes_rows, modes, partial, filtered, totals, ordered, shares,
):
    copies = bring((owners_vmem, locals_vmem), (owners, locals_), arrivals, 0)
    widened[...] = arrived[...].astype(F32)
    sky_devices, rows, lanes = shares.shape
    parts = sky_devices * rows
    beams = arrived.shape[0] // parts
    blocks = partial.shape[0] // 8
    total = turn.shape[0] // blocks
    orders = total // beams
    cycles = lanes // orders
    together = len(totals)
    unroll = 32

    steps = max(1, blocks // (together * unroll))

    def cycle_of(s):
        return (owners[s] * blocks_local + locals_[s]) // CYCLE_BLOCKS

    width = together * parts
    for b in range(beams):
        for row in range(rows):
            some = every(widened, b * parts + row, sky_devices, rows)
            for j in range(together):
                start = j * parts + row * sky_devices
                stacked[b, start : start + sky_devices, :] = some
        modes_rows[b * lanes : (b + 1) * lanes, :] = stacked[b].T
    lane_group = iota((total, width), 1) // parts
    for r in range(cycles):
        halves = [
            modes_rows[pl.ds(r + parity * cycles, total // 2, stride=2 * cycles), :]
            for parity in range(2)
        ]
        values = jnp.concatenate(halves, axis=0)
        for j in range(together):
            modes[r, j] = jnp.where(lane_group == j, values, 0.0).astype(BF16)
    for copy in copies:
        copy.wait()

    def gather(first):
        left = jnp.concatenate([modes[cycle_of(first + j), j] for j in range(together)], axis=0)
        table = phi[pl.ds(pl.multiple_of(first * parts, width), width), :]
        cells = jnp.dot(left, table, preferred_element_type=F32)
        rotation = turn[pl.ds(pl.multiple_of(first * total, together * total), together * total), :]
        turned = (cells * rotation.astype(F32)).reshape(together, total // 8, 8, CELLS)
        kept = jnp.sum(turned, axis=1).reshape(together * 8, CELLS)
        partial[pl.ds(pl.multiple_of(first * 8, together * 8), together * 8), :] = kept

    @pl.loop(0, steps)
    def _(step):
        for i in range(unroll):
            gather((step * unroll + i) * together)

    signal = partial[pl.ds(0, blocks, stride=8), :]
    for i in range(1, 8):
        signal = signal + partial[pl.ds(i, blocks, stride=8), :]
    valid = iota((blocks, CELLS), 0) * CELLS + iota((blocks, CELLS), 1) < count[0:1, :]
    signal = jnp.where(valid, signal, 0.0)
    clean = lax.dot_general(
        signal.astype(BF16), noise[...].astype(BF16), LAST_LAST, preferred_element_type=F32
    )
    filtered[...] = jnp.where(valid, clean, 0.0)

    for one in totals:
        one[...] = jnp.zeros_like(one)
    half = orders // 2

    def spread(first):
        rotation = own[pl.ds(pl.multiple_of(first * orders, 16), together * orders), :].astype(F32)
        weighted = [
            rotation[j * orders : (j + 1) * orders] * filtered[pl.ds(first + j, 1), :]
            for j in range(together)
        ]
        weighted = jnp.concatenate(weighted, axis=0).astype(BF16)
        table = phi[pl.ds(pl.multiple_of(first * parts, width), width), :]
        terms = lax.dot_general(weighted, table, LAST_LAST, preferred_element_type=F32)
        for j in range(together):
            row = pl.multiple_of(cycle_of(first + j) * orders, orders)
            here = totals[j]
            here[pl.ds(row, orders), :] += terms[j * orders : (j + 1) * orders]

    @pl.loop(0, steps)
    def _(step):
        for i in range(unroll):
            spread((step * unroll + i) * together)

    gathered = totals[0][...]
    which = iota(gathered.shape, 1) // parts
    for j in range(1, together):
        gathered = jnp.where(which == j, totals[j][...], gathered)
    totals[0][...] = gathered
    for k in range(orders):
        place = k // 2 + (k % 2) * half
        ordered[k * cycles : (k + 1) * cycles, :] = totals[0][pl.ds(place, cycles, stride=orders), :]
    turned = ordered[...].T
    summed = turned[0:parts]
    for j in range(1, together):
        summed = summed + turned[j * parts : (j + 1) * parts]
    for row in range(rows):
        shares[:, row, :] = summed[row * sky_devices : (row + 1) * sky_devices]
    for b in range(beams):
        out[b] = shares[...].astype(BF16)


def gradient_kernel(arrived, pieces, out, modes):
    me = lax.axis_index("beam")
    parts, sky_orders, cycles, width = pieces[0].shape
    orders = parts - 1
    diagonal = own_block(orders, cycles)
    for b in range(len(pieces)):
        modes[b] = jnp.sum(arrived[b].astype(F32), axis=0).astype(BF16).astype(F32)
    first, second = [0.0] * sky_orders, [0.0] * sky_orders
    for j, piece in enumerate(pieces):
        terms = piece[orders].reshape(sky_orders * cycles, width).astype(F32)
        beam_real, beam_imag = [
            terms[2 * c * orders : (2 * c + 1) * orders] + terms[(2 * c + 1) * orders : (2 * c + 2) * orders]
            for c in range(2)
        ]
        these = modes[me ^ j]
        for m in range(sky_orders):
            spreads = []
            for c in range(2):
                row = these[c * sky_orders + m : c * sky_orders + m + 1]
                spreads.append(jnp.where(diagonal, row, 0.0))
            left = jnp.concatenate(spreads, axis=0).astype(BF16)
            table = piece[0:orders, m].reshape(orders * cycles, width)
            harmonics = jnp.dot(left, table, preferred_element_type=F32)
            real, imag = harmonics[:orders], harmonics[orders:]
            first[m] += real * beam_real + imag * beam_imag
            second[m] += imag * beam_real - real * beam_imag
    for m in range(sky_orders):
        out[m, 0:1, :] = jnp.sum(first[m], axis=0, keepdims=True)
        out[m, 1:2, :] = jnp.sum(second[m], axis=0, keepdims=True)


def exchange(pieces, axis):
    count = lax.axis_size(axis)
    return [pieces[0]] + [
        lax.ppermute(pieces[j], axis, [(i, i ^ j) for i in range(count)]) for j in range(1, count)
    ]


def local(
    sky_harmonics,
    beam_harmonics,
    wigner,
    order_map,
    block_owner,
    block_local,
    cell_offset,
    cell_fraction,
    beam_angle,
    sample_count,
    noise_weight,
):
    beams, sky_devices = lax.axis_size("beam"), lax.axis_size("ma")
    orders, sky_orders, cycles, degrees = wigner.shape
    total = orders * beams
    all_sky = sky_orders * sky_devices
    parts = 2 * all_sky
    blocks = block_local.shape[0]
    blocks_local = cycles // sky_devices * CYCLE_BLOCKS
    width = degrees // beams
    lanes = orders * cycles
    rows = 2 * sky_orders
    together = max(1, CELLS // parts)
    owners = block_owner.reshape(blocks)
    limit = pltpu.CompilerParams(vmem_limit_bytes=32 * 1024 * 1024)
    integers = [
        pltpu.SMEM((blocks,), jnp.int32),
        pltpu.SMEM((blocks,), jnp.int32),
    ]

    def pinned(*arrays):
        return [pltpu.with_memory_space_constraint(array, pltpu.HBM) for array in arrays]

    later = (
        order_map, owners, block_local,
        beam_angle.reshape(blocks, CELLS),
        cell_offset.reshape(blocks, CELLS),
        cell_fraction.reshape(blocks, CELLS),
        noise_weight,
    )
    sent, (order_map, owners, places, angles, offsets, fractions, noise) = pl.pallas_call(
        modes_kernel,
        out_shape=[
            jax.ShapeDtypeStruct((beams * sky_devices, rows, lanes), BF16),
            [pltpu.VMEM(array.shape, array.dtype) for array in later],
        ],
        in_specs=[*hbm(3), hbm(len(later))],
        out_specs=[vmem(1)[0], vmem(len(later))],
        scratch_shapes=[
            pltpu.VMEM(sky_harmonics.shape, F32),
            pltpu.VMEM(beam_harmonics.shape, F32),
            pltpu.VMEM((beams, orders, sky_orders, cycles, width), BF16),
            pltpu.SemaphoreType.DMA((2 + beams + len(later),)),
        ],
        compiler_params=limit,
        name="modes",
    )(*pinned(sky_harmonics, beam_harmonics, wigner), pinned(*later))
    arrived = lax.all_to_all(sent, ("beam", "ma"), split_axis=0, concat_axis=0, tiled=True)

    samples = pltpu.VMEM((blocks, CELLS), F32)
    piece = (orders + 1, sky_orders, cycles, width)
    phi, turn, own, pieces = pl.pallas_call(
        functools.partial(tables_kernel, blocks_local, sky_devices),
        out_shape=[
            pltpu.VMEM((blocks * parts, CELLS), BF16),
            pltpu.VMEM((blocks * total, CELLS), BF16),
            pltpu.VMEM((blocks * orders, CELLS), BF16),
            [pltpu.HBM(piece, BF16)] * beams,
        ],
        in_specs=vmem(6) + hbm(2),
        out_specs=[*vmem(3), hbm(beams)],
        scratch_shapes=[
            pltpu.VMEM((beams, *piece), BF16),
            pltpu.VMEM(beam_harmonics.shape, F32),
            pltpu.SemaphoreType.DMA((2 * beams,)),
            pltpu.SMEM((all_sky,), jnp.int32),
            *integers,
            pltpu.SemaphoreType.DMA((4,)),
            pltpu.VMEM((CYCLE_BLOCKS, all_sky, CELLS), F32),
            pltpu.VMEM((CYCLE_BLOCKS, all_sky, CELLS), F32),
            pltpu.VMEM((8, blocks, CELLS), F32),
            pltpu.VMEM((16, total, CELLS), F32),
        ],
        compiler_params=limit,
        cost_estimate=pl.CostEstimate(flops=100_000_000, bytes_accessed=4_000_000, transcendentals=0),
        name="tables",
    )(
        order_map, owners, places, angles, offsets, fractions,
        *pinned(beam_harmonics, wigner),
    )
    pieces = exchange(pieces, "beam")

    grads = pl.pallas_call(
        functools.partial(samples_kernel, blocks_local),
        out_shape=jax.ShapeDtypeStruct((beams, sky_devices, rows, lanes), BF16),
        in_specs=vmem(8),
        out_specs=vmem(1)[0],
        scratch_shapes=[
            *integers,
            pltpu.SemaphoreType.DMA((2,)),
            pltpu.VMEM((beams * parts, lanes), F32),
            pltpu.VMEM((beams, together * parts, lanes), F32),
            pltpu.VMEM((beams * lanes, together * parts), F32),
            pltpu.VMEM((cycles, together, total, together * parts), BF16),
            pltpu.VMEM((blocks * 8, CELLS), F32),
            samples,
            [pltpu.VMEM((lanes, together * parts), F32) for _ in range(together)],
            pltpu.VMEM((lanes, together * parts), F32),
            pltpu.VMEM((sky_devices, rows, lanes), F32),
        ],
        compiler_params=limit,
        cost_estimate=pl.CostEstimate(flops=40_000_000_000, bytes_accessed=100_000_000, transcendentals=0),
        name="samples",
    )(
        owners, places, jnp.broadcast_to(sample_count[None, :], (8, CELLS)), noise,
        arrived.reshape(beams * parts, lanes), phi, turn, own,
    )
    grads = grads.reshape(beams * sky_devices, rows, lanes)
    grads = lax.all_to_all(grads, ("beam", "ma"), split_axis=0, concat_axis=0, tiled=True)
    return pl.pallas_call(
        gradient_kernel,
        out_shape=jax.ShapeDtypeStruct((sky_orders, 2, width), F32),
        in_specs=[vmem(1)[0], vmem(beams)],
        out_specs=vmem(1)[0],
        scratch_shapes=[pltpu.VMEM((beams, rows, lanes), F32)],
        compiler_params=limit,
        name="gradient",
    )(grads.reshape(beams, sky_devices, rows, lanes), pieces)


def solution(mesh):
    return jax.shard_map(
        local,
        mesh=mesh,
        in_specs=(
            P("ma", None, None),
            P("beam", None, None),
            P("beam", "ma", None, None),
            P(),
            P("ma", None),
            P("ma"),
            P("ma"),
            P("ma"),
            P("ma"),
            P("ma"),
            P(),
        ),
        out_specs=P("ma", None, "beam"),
        check_vma=False,
    )
```

```python
import functools
import math

import jax
import jax.numpy as jnp
from jax import lax
from jax.experimental import pallas as pl
from jax.experimental.pallas import tpu as pltpu
from jax.sharding import PartitionSpec as P

PHI = 4096
CELLS = 128
CYCLE_BLOCKS = PHI // CELLS
F32 = jnp.float32
BF16 = jnp.bfloat16
LAST_LAST = (((1,), (1,)), ((), ()))


def iota(shape, axis):
    return lax.broadcasted_iota(jnp.int32, shape, axis)


def vmem(count):
    return [pl.BlockSpec(memory_space=pltpu.VMEM)] * count


def smem(count):
    return [pl.BlockSpec(memory_space=pltpu.SMEM)] * count


def hbm(count):
    return [pl.BlockSpec(memory_space=pltpu.HBM)] * count


def sine_turns(z):
    square = z * z
    value = 39.53670603 * square - 76.54978229
    value = value * square + 81.60100407
    value = value * square - 41.34165503
    value = value * square + 6.28318516
    return value * z


def cosine_steps(steps):
    centred = ((steps + PHI // 2) & (PHI - 1)) - PHI // 2
    return sine_turns(0.25 - jnp.abs(centred).astype(F32) * (1.0 / PHI))


def every(ref, first, count, step):
    if ref.shape[1] == CELLS:
        return ref[pl.ds(first, count, stride=step), :]
    return jnp.concatenate([ref[first + i * step][None] for i in range(count)], axis=0)


def bring(sources, places, semaphores, first):
    copies = [
        pltpu.make_async_copy(source, place, semaphores.at[first + i])
        for i, (source, place) in enumerate(zip(sources, places))
    ]
    for copy in copies:
        copy.start()
    return copies


def own_block(orders, cycles):
    shape = (orders, orders * cycles)
    return iota(shape, 1) // cycles == iota(shape, 0)


def modes_kernel(sky_hbm, beam_hbm, wigner_hbm, later_hbm, out, later, sky, beam, wigner, arrivals):
    chunks, orders, sky_orders, cycles, width = wigner.shape
    small = bring((sky_hbm, beam_hbm), (sky, beam), arrivals, 0)
    spans = [pl.ds(i * width, width) for i in range(chunks)]
    large = bring([wigner_hbm.at[:, :, :, span] for span in spans], [wigner.at[i] for i in range(chunks)], arrivals, 2)
    others = bring(later_hbm, later, arrivals, 2 + chunks)
    for copy in small:
        copy.wait()
    beam_real, beam_imag = beam[:, 0, :], beam[:, 1, :]
    diagonal = own_block(orders, cycles)
    products = []
    for m in range(sky_orders):
        sky_real, sky_imag = sky[m, 0:1, :], sky[m, 1:2, :]
        first = sky_real * beam_real - sky_imag * beam_imag
        second = sky_real * beam_imag + sky_imag * beam_real
        products.append(jnp.concatenate([first, second], axis=0).astype(BF16))
    sums = [0.0] * sky_orders
    for i in range(chunks):
        large[i].wait()
        for m in range(sky_orders):
            table = wigner[i, :, m].reshape(orders * cycles, width)
            left = products[m][:, i * width : (i + 1) * width]
            sums[m] += lax.dot_general(table, left, LAST_LAST, preferred_element_type=F32)
    rows = [None] * (2 * sky_orders)
    for m in range(sky_orders):
        modes = sums[m].T
        for c in range(2):
            part = jnp.where(diagonal, modes[c * orders : (c + 1) * orders], 0.0)
            rows[c * sky_orders + m] = jnp.sum(part, axis=0, keepdims=True)
    block = jnp.concatenate(rows + rows, axis=0).astype(BF16)
    for d in range(out.shape[0]):
        out[d] = block
    for copy in others:
        copy.wait()


def tables_kernel(
    blocks_local, sky_devices,
    order_vmem, owners_vmem, locals_vmem, angles, offsets, fractions, beam_hbm, wigner_hbm,
    phi, turn, own, pieces_hbm, pieces, beam, departures, order_map, owners, locals_, arrivals,
    step_real, step_imag, powers, rows_of,
):
    copies = bring((order_vmem, owners_vmem, locals_vmem), (order_map, owners, locals_), arrivals, 0)
    me = lax.axis_index("beam")
    extra = bring((beam_hbm,), (beam,), arrivals, 3)[0]
    beams, beam_orders, width = pieces.shape[0], beam.shape[0], pieces.shape[4]
    spans = [pl.ds(pl.multiple_of((me ^ j) * width, width), width) for j in range(beams)]
    arriving = bring(
        [wigner_hbm.at[:, :, :, span] for span in spans],
        [pieces.at[j, 0:beam_orders] for j in range(beams)],
        departures, 0,
    )
    orders = order_map.shape[0]
    blocks = offsets.shape[0]
    half = turn.shape[0] // blocks // 2
    own_half = own.shape[0] // blocks // 2

    part = angles[...] * (0.5 / math.pi)
    part = part - jnp.round(part)
    folded = jnp.where(part > 0.25, 0.5 - part, jnp.where(part < -0.25, -0.5 - part, part))
    real, imag = sine_turns(0.25 - jnp.abs(part)), sine_turns(folded)
    for i in range(4):
        if i:
            real, imag = real * real - imag * imag, 2.0 * real * imag
        powers[2 * i], powers[2 * i + 1] = real, imag

    copies[0].wait()
    order = jnp.zeros((orders, CELLS), jnp.int32)
    row = iota((orders, CELLS), 0)
    lane = iota((orders, CELLS), 1)
    for m in range(orders):
        place = m % (orders // sky_devices) * sky_devices + m // (orders // sky_devices)
        order = jnp.where(row == place, order_map[m], order)

    def phase(steps):
        return cosine_steps(steps), cosine_steps(steps + PHI // 4)

    scaling = 1.0 / math.sqrt(orders)
    cell_real, cell_imag = phase(order * lane)
    cell_real, cell_imag = cell_real * scaling, cell_imag * scaling
    next_real, next_imag = phase(order)
    next_real = next_real - 1.0
    first_real, first_imag = phase(((order * CELLS) & (PHI - 1)) * lane)
    for j in range(CYCLE_BLOCKS):
        step_real[j] = jnp.broadcast_to(first_real[:, j : j + 1], (orders, CELLS))
        step_imag[j] = jnp.broadcast_to(first_imag[:, j : j + 1], (orders, CELLS))
    for copy in copies[1:]:
        copy.wait()

    def block_phases(s):
        place = (owners[s] * blocks_local + locals_[s]) & (CYCLE_BLOCKS - 1)
        offset = jnp.broadcast_to(offsets[pl.ds(s, 1), :], (orders, CELLS))
        fraction = jnp.broadcast_to(fractions[pl.ds(s, 1), :], (orders, CELLS))
        real = jnp.take_along_axis(cell_real, offset, axis=1, mode="promise_in_bounds")
        imag = jnp.take_along_axis(cell_imag, offset, axis=1, mode="promise_in_bounds")
        base_real, base_imag = step_real[place], step_imag[place]
        left_real = real * base_real - imag * base_imag
        left_imag = real * base_imag + imag * base_real
        mix_real = 1.0 + fraction * next_real
        mix_imag = fraction * next_imag
        both = jnp.concatenate(
            [left_real * mix_real - left_imag * mix_imag, left_real * mix_imag + left_imag * mix_real],
            axis=0,
        )
        start = pl.multiple_of(s * 2 * orders, 2 * orders)
        phi[pl.ds(start, 2 * orders), :] = both.astype(BF16)

    scale = 1.0 / math.sqrt(2 * half)
    power = iota((8, CELLS), 0)

    def block_turns(s, rows_of):
        steps = [jnp.broadcast_to(powers[i, pl.ds(s, 1), :], (8, CELLS)) for i in range(8)]
        one_real, one_imag = steps[:2]
        step = steps[6:]
        odd = power & 1 == 1
        real, imag = jnp.where(odd, one_real * scale, scale), jnp.where(odd, one_imag * scale, 0.0)
        for bit in (2, 4):
            taken = power & bit == bit
            by_real, by_imag = jnp.where(taken, steps[bit], 1.0), jnp.where(taken, steps[bit + 1], 0.0)
            real, imag = real * by_real - imag * by_imag, real * by_imag + imag * by_real
        evens, odds = [], []
        for j in range(half // 8):
            if j:
                real, imag = real * step[0] - imag * step[1], real * step[1] + imag * step[0]
            evens.append(real)
            odds.append(real * one_imag + imag * one_real)
        all_rows = jnp.concatenate(evens + odds, axis=0)
        turn[pl.ds(pl.multiple_of(s * 2 * half, 2 * half), 2 * half), :] = all_rows.astype(BF16)
        rows_of[...] = all_rows
        return [rows_of[pl.ds(p * half + mine, own_half), :] for p in range(2)]

    extra.wait()
    sky_orders, cycles = pieces.shape[2:4]
    for j, span in enumerate(spans):
        terms = []
        for c in range(2):
            values = beam[:, c, span]
            high = values.astype(BF16)
            terms += [high, (values - high.astype(F32)).astype(BF16)]
        filling = sky_orders * cycles - 4 * beam_orders
        if filling:
            terms.append(jnp.zeros((filling, width), BF16))
        pieces[j, beam_orders] = jnp.concatenate(terms, axis=0).reshape(sky_orders, cycles, width)
    mine = me * own_half
    pair = 16 // (2 * own_half)

    run = rows_of.shape[0]

    def one_run(group):
        for j in range(0, run, pair):
            kept = []
            for i in range(pair):
                block_phases(group * run + j + i)
                kept += block_turns(group * run + j + i, rows_of.at[j + i])
            start = pl.multiple_of((group * run + j) * 2 * own_half, 16)
            own[pl.ds(start, 16), :] = jnp.concatenate(kept, axis=0).astype(BF16)

    runs = blocks // run
    pl.loop(0, runs // 2)(one_run)
    for copy in arriving:
        copy.wait()
    leaving = bring([pieces.at[j] for j in range(beams)], pieces_hbm, departures, beams)
    pl.loop(runs // 2, runs)(one_run)
    for copy in leaving:
        copy.wait()


def samples_kernel(
    blocks_local, owners_vmem, locals_vmem, count, noise, arrived, phi, turn, own,
    out, owners, locals_, arrivals, widened,
    stacked, modes_rows, modes, partial, filtered, totals, ordered, shares,
):
    copies = bring((owners_vmem, locals_vmem), (owners, locals_), arrivals, 0)
    widened[...] = arrived[...].astype(F32)
    sky_devices, rows, lanes = shares.shape
    parts = sky_devices * rows
    beams = arrived.shape[0] // parts
    blocks = partial.shape[0] // 8
    total = turn.shape[0] // blocks
    orders = total // beams
    cycles = lanes // orders
    together = len(totals)
    unroll = 32

    steps = max(1, blocks // (together * unroll))

    def cycle_of(s):
        return (owners[s] * blocks_local + locals_[s]) // CYCLE_BLOCKS

    width = together * parts
    for b in range(beams):
        for row in range(rows):
            some = every(widened, b * parts + row, sky_devices, rows)
            for j in range(together):
                start = j * parts + row * sky_devices
                stacked[b, start : start + sky_devices, :] = some
        modes_rows[b * lanes : (b + 1) * lanes, :] = stacked[b].T
    lane_group = iota((total, width), 1) // parts
    for r in range(cycles):
        halves = [
            modes_rows[pl.ds(r + parity * cycles, total // 2, stride=2 * cycles), :]
            for parity in range(2)
        ]
        values = jnp.concatenate(halves, axis=0)
        for j in range(together):
            modes[r, j] = jnp.where(lane_group == j, values, 0.0).astype(BF16)
    for copy in copies:
        copy.wait()

    def gather(first):
        left = jnp.concatenate([modes[cycle_of(first + j), j] for j in range(together)], axis=0)
        table = phi[pl.ds(pl.multiple_of(first * parts, width), width), :]
        cells = jnp.dot(left, table, preferred_element_type=F32)
        rotation = turn[pl.ds(pl.multiple_of(first * total, together * total), together * total), :]
        turned = (cells * rotation.astype(F32)).reshape(together, total // 8, 8, CELLS)
        kept = jnp.sum(turned, axis=1).reshape(together * 8, CELLS)
        partial[pl.ds(pl.multiple_of(first * 8, together * 8), together * 8), :] = kept

    @pl.loop(0, steps)
    def _(step):
        for i in range(unroll):
            gather((step * unroll + i) * together)

    signal = partial[pl.ds(0, blocks, stride=8), :]
    for i in range(1, 8):
        signal = signal + partial[pl.ds(i, blocks, stride=8), :]
    valid = iota((blocks, CELLS), 0) * CELLS + iota((blocks, CELLS), 1) < count[0:1, :]
    signal = jnp.where(valid, signal, 0.0)
    clean = lax.dot_general(
        signal.astype(BF16), noise[...].astype(BF16), LAST_LAST, preferred_element_type=F32
    )
    filtered[...] = jnp.where(valid, clean, 0.0)

    for one in totals:
        one[...] = jnp.zeros_like(one)
    half = orders // 2

    def spread(first):
        rotation = own[pl.ds(pl.multiple_of(first * orders, 16), together * orders), :].astype(F32)
        weighted = [
            rotation[j * orders : (j + 1) * orders] * filtered[pl.ds(first + j, 1), :]
            for j in range(together)
        ]
        weighted = jnp.concatenate(weighted, axis=0).astype(BF16)
        table = phi[pl.ds(pl.multiple_of(first * parts, width), width), :]
        terms = lax.dot_general(weighted, table, LAST_LAST, preferred_element_type=F32)
        for j in range(together):
            row = pl.multiple_of(cycle_of(first + j) * orders, orders)
            here = totals[j]
            here[pl.ds(row, orders), :] += terms[j * orders : (j + 1) * orders]

    @pl.loop(0, steps)
    def _(step):
        for i in range(unroll):
            spread((step * unroll + i) * together)

    gathered = totals[0][...]
    which = iota(gathered.shape, 1) // parts
    for j in range(1, together):
        gathered = jnp.where(which == j, totals[j][...], gathered)
    totals[0][...] = gathered
    for k in range(orders):
        place = k // 2 + (k % 2) * half
        ordered[k * cycles : (k + 1) * cycles, :] = totals[0][pl.ds(place, cycles, stride=orders), :]
    turned = ordered[...].T
    summed = turned[0:parts]
    for j in range(1, together):
        summed = summed + turned[j * parts : (j + 1) * parts]
    for row in range(rows):
        shares[:, row, :] = summed[row * sky_devices : (row + 1) * sky_devices]
    for b in range(beams):
        out[b] = shares[...].astype(BF16)


def gradient_kernel(arrived, pieces, out, modes):
    me = lax.axis_index("beam")
    parts, sky_orders, cycles, width = pieces[0].shape
    orders = parts - 1
    diagonal = own_block(orders, cycles)
    for b in range(len(pieces)):
        modes[b] = jnp.sum(arrived[b].astype(F32), axis=0).astype(BF16).astype(F32)
    first, second = [0.0] * sky_orders, [0.0] * sky_orders
    for j, piece in enumerate(pieces):
        terms = piece[orders].reshape(sky_orders * cycles, width).astype(F32)
        beam_real, beam_imag = [
            terms[2 * c * orders : (2 * c + 1) * orders] + terms[(2 * c + 1) * orders : (2 * c + 2) * orders]
            for c in range(2)
        ]
        these = modes[me ^ j]
        for m in range(sky_orders):
            spreads = []
            for c in range(2):
                row = these[c * sky_orders + m : c * sky_orders + m + 1]
                spreads.append(jnp.where(diagonal, row, 0.0))
            left = jnp.concatenate(spreads, axis=0).astype(BF16)
            table = piece[0:orders, m].reshape(orders * cycles, width)
            harmonics = jnp.dot(left, table, preferred_element_type=F32)
            real, imag = harmonics[:orders], harmonics[orders:]
            first[m] += real * beam_real + imag * beam_imag
            second[m] += imag * beam_real - real * beam_imag
    for m in range(sky_orders):
        out[m, 0:1, :] = jnp.sum(first[m], axis=0, keepdims=True)
        out[m, 1:2, :] = jnp.sum(second[m], axis=0, keepdims=True)


def exchange(pieces, axis):
    count = lax.axis_size(axis)
    return [pieces[0]] + [
        lax.ppermute(pieces[j], axis, [(i, i ^ j) for i in range(count)]) for j in range(1, count)
    ]


def local(
    sky_harmonics,
    beam_harmonics,
    wigner,
    order_map,
    block_owner,
    block_local,
    cell_offset,
    cell_fraction,
    beam_angle,
    sample_count,
    noise_weight,
):
    beams, sky_devices = lax.axis_size("beam"), lax.axis_size("ma")
    orders, sky_orders, cycles, degrees = wigner.shape
    total = orders * beams
    all_sky = sky_orders * sky_devices
    parts = 2 * all_sky
    blocks = block_local.shape[0]
    blocks_local = cycles // sky_devices * CYCLE_BLOCKS
    width = degrees // beams
    lanes = orders * cycles
    rows = 2 * sky_orders
    together = max(1, CELLS // parts)
    owners = block_owner.reshape(blocks)
    limit = pltpu.CompilerParams(vmem_limit_bytes=32 * 1024 * 1024)
    integers = [
        pltpu.SMEM((blocks,), jnp.int32),
        pltpu.SMEM((blocks,), jnp.int32),
    ]

    def pinned(*arrays):
        return [pltpu.with_memory_space_constraint(array, pltpu.HBM) for array in arrays]

    later = (
        order_map, owners, block_local,
        beam_angle.reshape(blocks, CELLS),
        cell_offset.reshape(blocks, CELLS),
        cell_fraction.reshape(blocks, CELLS),
        noise_weight,
    )
    sent, (order_map, owners, places, angles, offsets, fractions, noise) = pl.pallas_call(
        modes_kernel,
        out_shape=[
            jax.ShapeDtypeStruct((beams * sky_devices // 2, 2 * rows, lanes), BF16),
            [pltpu.VMEM(array.shape, array.dtype) for array in later],
        ],
        in_specs=[*hbm(3), hbm(len(later))],
        out_specs=[vmem(1)[0], vmem(len(later))],
        scratch_shapes=[
            pltpu.VMEM(sky_harmonics.shape, F32),
            pltpu.VMEM(beam_harmonics.shape, F32),
            pltpu.VMEM((beams, orders, sky_orders, cycles, width), BF16),
            pltpu.SemaphoreType.DMA((2 + beams + len(later),)),
        ],
        compiler_params=limit,
        name="modes",
    )(*pinned(sky_harmonics, beam_harmonics, wigner), pinned(*later))
    sent = sent.reshape(beams * sky_devices, rows, lanes)
    arrived = lax.all_to_all(sent, ("beam", "ma"), split_axis=0, concat_axis=0, tiled=True)

    samples = pltpu.VMEM((blocks, CELLS), F32)
    piece = (orders + 1, sky_orders, cycles, width)
    phi, turn, own, pieces = pl.pallas_call(
        functools.partial(tables_kernel, blocks_local, sky_devices),
        out_shape=[
            pltpu.VMEM((blocks * parts, CELLS), BF16),
            pltpu.VMEM((blocks * total, CELLS), BF16),
            pltpu.VMEM((blocks * orders, CELLS), BF16),
            [pltpu.HBM(piece, BF16)] * beams,
        ],
        in_specs=vmem(6) + hbm(2),
        out_specs=[*vmem(3), hbm(beams)],
        scratch_shapes=[
            pltpu.VMEM((beams, *piece), BF16),
            pltpu.VMEM(beam_harmonics.shape, F32),
            pltpu.SemaphoreType.DMA((2 * beams,)),
            pltpu.SMEM((all_sky,), jnp.int32),
            *integers,
            pltpu.SemaphoreType.DMA((4,)),
            pltpu.VMEM((CYCLE_BLOCKS, all_sky, CELLS), F32),
            pltpu.VMEM((CYCLE_BLOCKS, all_sky, CELLS), F32),
            pltpu.VMEM((8, blocks, CELLS), F32),
            pltpu.VMEM((16, total, CELLS), F32),
        ],
        compiler_params=limit,
        cost_estimate=pl.CostEstimate(flops=100_000_000, bytes_accessed=4_000_000, transcendentals=0),
        name="tables",
    )(
        order_map, owners, places, angles, offsets, fractions,
        *pinned(beam_harmonics, wigner),
    )
    pieces = exchange(pieces, "beam")

    grads = pl.pallas_call(
        functools.partial(samples_kernel, blocks_local),
        out_shape=jax.ShapeDtypeStruct((beams, sky_devices, rows, lanes), BF16),
        in_specs=vmem(8),
        out_specs=vmem(1)[0],
        scratch_shapes=[
            *integers,
            pltpu.SemaphoreType.DMA((2,)),
            pltpu.VMEM((beams * parts, lanes), F32),
            pltpu.VMEM((beams, together * parts, lanes), F32),
            pltpu.VMEM((beams * lanes, together * parts), F32),
            pltpu.VMEM((cycles, together, total, together * parts), BF16),
            pltpu.VMEM((blocks * 8, CELLS), F32),
            samples,
            [pltpu.VMEM((lanes, together * parts), F32) for _ in range(together)],
            pltpu.VMEM((lanes, together * parts), F32),
            pltpu.VMEM((sky_devices, rows, lanes), F32),
        ],
        compiler_params=limit,
        cost_estimate=pl.CostEstimate(flops=40_000_000_000, bytes_accessed=100_000_000, transcendentals=0),
        name="samples",
    )(
        owners, places, jnp.broadcast_to(sample_count[None, :], (8, CELLS)), noise,
        arrived.reshape(beams * parts, lanes), phi, turn, own,
    )
    grads = grads.reshape(beams * sky_devices, rows, lanes)
    grads = lax.all_to_all(grads, ("beam", "ma"), split_axis=0, concat_axis=0, tiled=True)
    return pl.pallas_call(
        gradient_kernel,
        out_shape=jax.ShapeDtypeStruct((sky_orders, 2, width), F32),
        in_specs=[vmem(1)[0], vmem(beams)],
        out_specs=vmem(1)[0],
        scratch_shapes=[pltpu.VMEM((beams, rows, lanes), F32)],
        compiler_params=limit,
        name="gradient",
    )(grads.reshape(beams, sky_devices, rows, lanes), pieces)


def solution(mesh):
    return jax.shard_map(
        local,
        mesh=mesh,
        in_specs=(
            P("ma", None, None),
            P("beam", None, None),
            P("beam", "ma", None, None),
            P(),
            P("ma", None),
            P("ma"),
            P("ma"),
            P("ma"),
            P("ma"),
            P("ma"),
            P(),
        ),
        out_specs=P("ma", None, "beam"),
        check_vma=False,
    )
```

```python
import functools
import math

import jax
import jax.numpy as jnp
from jax import lax
from jax.experimental import pallas as pl
from jax.experimental.pallas import tpu as pltpu
from jax.sharding import PartitionSpec as P

PHI = 4096
CELLS = 128
CYCLE_BLOCKS = PHI // CELLS
F32 = jnp.float32
BF16 = jnp.bfloat16
NEAREST = 1.5 * 2.0**23
LAST_LAST = (((1,), (1,)), ((), ()))


def iota(shape, axis):
    return lax.broadcasted_iota(jnp.int32, shape, axis)


def vmem(count):
    return [pl.BlockSpec(memory_space=pltpu.VMEM)] * count


def smem(count):
    return [pl.BlockSpec(memory_space=pltpu.SMEM)] * count


def hbm(count):
    return [pl.BlockSpec(memory_space=pltpu.HBM)] * count


def sine_turns(z):
    square = z * z
    value = 39.53670603 * square - 76.54978229
    value = value * square + 81.60100407
    value = value * square - 41.34165503
    value = value * square + 6.28318516
    return value * z


def whole_turns_off(turns):
    return turns - ((turns + NEAREST) - NEAREST)


def phase(turns):
    part = whole_turns_off(turns)
    ahead = part + 0.25
    return sine_turns(0.25 - jnp.abs(part)), sine_turns(0.25 - jnp.minimum(jnp.abs(ahead), 1.0 - ahead))


def every(ref, first, count, step):
    if ref.shape[1] == CELLS:
        return ref[pl.ds(first, count, stride=step), :]
    return jnp.concatenate([ref[first + i * step][None] for i in range(count)], axis=0)


def bring(sources, places, semaphores, first):
    copies = [
        pltpu.make_async_copy(source, place, semaphores.at[first + i])
        for i, (source, place) in enumerate(zip(sources, places))
    ]
    for copy in copies:
        copy.start()
    return copies


def own_block(orders, cycles):
    shape = (orders, orders * cycles)
    return iota(shape, 1) // cycles == iota(shape, 0)


def modes_kernel(sky_hbm, beam_hbm, wigner_hbm, later_hbm, out, later, sky, beam, wigner, arrivals):
    chunks, orders, sky_orders, cycles, width = wigner.shape
    small = bring((sky_hbm, beam_hbm), (sky, beam), arrivals, 0)
    spans = [pl.ds(i * width, width) for i in range(chunks)]
    large = bring([wigner_hbm.at[:, :, :, span] for span in spans], [wigner.at[i] for i in range(chunks)], arrivals, 2)
    others = bring(later_hbm, later, arrivals, 2 + chunks)
    for copy in small:
        copy.wait()
    beam_real, beam_imag = beam[:, 0, :], beam[:, 1, :]
    diagonal = own_block(orders, cycles)
    products = []
    for m in range(sky_orders):
        sky_real, sky_imag = sky[m, 0:1, :], sky[m, 1:2, :]
        first = sky_real * beam_real - sky_imag * beam_imag
        second = sky_real * beam_imag + sky_imag * beam_real
        products.append(jnp.concatenate([first, second], axis=0).astype(BF16))
    sums = [0.0] * sky_orders
    for i in range(chunks):
        large[i].wait()
        for m in range(sky_orders):
            table = wigner[i, :, m].reshape(orders * cycles, width)
            left = products[m][:, i * width : (i + 1) * width]
            sums[m] += lax.dot_general(table, left, LAST_LAST, preferred_element_type=F32)
    rows = [None] * (2 * sky_orders)
    for m in range(sky_orders):
        modes = sums[m].T
        for c in range(2):
            part = jnp.where(diagonal, modes[c * orders : (c + 1) * orders], 0.0)
            rows[c * sky_orders + m] = jnp.sum(part, axis=0, keepdims=True)
    block = jnp.concatenate(rows + rows, axis=0).astype(BF16)
    for d in range(out.shape[0]):
        out[d] = block
    for copy in others:
        copy.wait()


def tables_kernel(
    blocks_local, sky_devices,
    order_vmem, owners_vmem, locals_vmem, angles, offsets, fractions, beam_hbm, wigner_hbm,
    phi, turn, own, pieces_hbm, pieces, beam, departures, order_map, owners, locals_, arrivals,
    positions, powers, rows_of,
):
    copies = bring((order_vmem, owners_vmem, locals_vmem), (order_map, owners, locals_), arrivals, 0)
    positions[...] = offsets[...].astype(F32)
    me = lax.axis_index("beam")
    extra = bring((beam_hbm,), (beam,), arrivals, 3)[0]
    beams, beam_orders, width = pieces.shape[0], beam.shape[0], pieces.shape[4]
    spans = [pl.ds(pl.multiple_of((me ^ j) * width, width), width) for j in range(beams)]
    arriving = bring(
        [wigner_hbm.at[:, :, :, span] for span in spans],
        [pieces.at[j, 0:beam_orders] for j in range(beams)],
        departures, 0,
    )
    orders = order_map.shape[0]
    blocks = offsets.shape[0]
    half = turn.shape[0] // blocks // 2
    own_half = own.shape[0] // blocks // 2

    real, imag = phase(angles[...] * (-0.5 / math.pi))
    for i in range(4):
        if i:
            real, imag = real * real - imag * imag, 2.0 * real * imag
        powers[2 * i], powers[2 * i + 1] = real, imag

    copies[0].wait()
    order = jnp.zeros((orders, CELLS), F32)
    row = iota((orders, CELLS), 0)
    for m in range(orders):
        place = m % (orders // sky_devices) * sky_devices + m // (orders // sky_devices)
        order = jnp.where(row == place, order_map[m].astype(F32), order)
    order = order * (1.0 / PHI)
    scaling = 1.0 / math.sqrt(orders)
    next_real, next_imag = phase(order)
    next_real, next_imag = (next_real - 1.0) * scaling, next_imag * scaling
    for copy in copies[1:]:
        copy.wait()

    def block_phases(s):
        first = ((owners[s] * blocks_local + locals_[s]) & (CYCLE_BLOCKS - 1)) * CELLS
        position = jnp.broadcast_to(positions[pl.ds(s, 1), :] + first.astype(F32), (orders, CELLS))
        fraction = jnp.broadcast_to(fractions[pl.ds(s, 1), :], (orders, CELLS))
        real, imag = phase(order * position)
        mix_real = scaling + fraction * next_real
        mix_imag = fraction * next_imag
        both = jnp.concatenate(
            [real * mix_real - imag * mix_imag, real * mix_imag + imag * mix_real], axis=0
        )
        start = pl.multiple_of(s * 2 * orders, 2 * orders)
        phi[pl.ds(start, 2 * orders), :] = both.astype(BF16)

    scale = 1.0 / math.sqrt(2 * half)
    power = iota((8, CELLS), 0)

    def block_turns(s, rows_of):
        steps = [jnp.broadcast_to(powers[i, pl.ds(s, 1), :], (8, CELLS)) for i in range(8)]
        one_real, one_imag = steps[:2]
        step = steps[6:]
        odd = power & 1 == 1
        real, imag = jnp.where(odd, one_real * scale, scale), jnp.where(odd, one_imag * scale, 0.0)
        for bit in (2, 4):
            taken = power & bit == bit
            by_real, by_imag = jnp.where(taken, steps[bit], 1.0), jnp.where(taken, steps[bit + 1], 0.0)
            real, imag = real * by_real - imag * by_imag, real * by_imag + imag * by_real
        evens, odds = [], []
        for j in range(half // 8):
            if j:
                real, imag = real * step[0] - imag * step[1], real * step[1] + imag * step[0]
            evens.append(real)
            odds.append(real * one_imag + imag * one_real)
        all_rows = jnp.concatenate(evens + odds, axis=0)
        turn[pl.ds(pl.multiple_of(s * 2 * half, 2 * half), 2 * half), :] = all_rows.astype(BF16)
        rows_of[...] = all_rows
        return [rows_of[pl.ds(p * half + mine, own_half), :] for p in range(2)]

    extra.wait()
    sky_orders, cycles = pieces.shape[2:4]
    for j, span in enumerate(spans):
        terms = []
        for c in range(2):
            values = beam[:, c, span]
            high = values.astype(BF16)
            terms += [high, (values - high.astype(F32)).astype(BF16)]
        filling = sky_orders * cycles - 4 * beam_orders
        if filling:
            terms.append(jnp.zeros((filling, width), BF16))
        pieces[j, beam_orders] = jnp.concatenate(terms, axis=0).reshape(sky_orders, cycles, width)
    mine = me * own_half
    pair = 16 // (2 * own_half)

    run = rows_of.shape[0]

    def one_run(group):
        for j in range(0, run, pair):
            kept = []
            for i in range(pair):
                block_phases(group * run + j + i)
                kept += block_turns(group * run + j + i, rows_of.at[j + i])
            start = pl.multiple_of((group * run + j) * 2 * own_half, 16)
            own[pl.ds(start, 16), :] = jnp.concatenate(kept, axis=0).astype(BF16)

    runs = blocks // run
    pl.loop(0, runs // 2)(one_run)
    for copy in arriving:
        copy.wait()
    leaving = bring([pieces.at[j] for j in range(beams)], pieces_hbm, departures, beams)
    pl.loop(runs // 2, runs)(one_run)
    for copy in leaving:
        copy.wait()


def samples_kernel(
    blocks_local, owners_vmem, locals_vmem, count, noise, arrived, phi, turn, own,
    out, owners, locals_, arrivals, widened,
    stacked, modes_rows, modes, partial, filtered, totals, ordered, shares,
):
    copies = bring((owners_vmem, locals_vmem), (owners, locals_), arrivals, 0)
    widened[...] = arrived[...].astype(F32)
    sky_devices, rows, lanes = shares.shape
    parts = sky_devices * rows
    beams = arrived.shape[0] // parts
    blocks = partial.shape[0] // 8
    total = turn.shape[0] // blocks
    orders = total // beams
    cycles = lanes // orders
    together = len(totals)
    unroll = 32

    steps = max(1, blocks // (together * unroll))

    def cycle_of(s):
        return (owners[s] * blocks_local + locals_[s]) // CYCLE_BLOCKS

    width = together * parts
    for b in range(beams):
        for row in range(rows):
            some = every(widened, b * parts + row, sky_devices, rows)
            for j in range(together):
                start = j * parts + row * sky_devices
                stacked[b, start : start + sky_devices, :] = some
        modes_rows[b * lanes : (b + 1) * lanes, :] = stacked[b].T
    lane_group = iota((total, width), 1) // parts
    for r in range(cycles):
        halves = [
            modes_rows[pl.ds(r + parity * cycles, total // 2, stride=2 * cycles), :]
            for parity in range(2)
        ]
        values = jnp.concatenate(halves, axis=0)
        for j in range(together):
            modes[r, j] = jnp.where(lane_group == j, values, 0.0).astype(BF16)
    for copy in copies:
        copy.wait()

    def gather(first):
        left = jnp.concatenate([modes[cycle_of(first + j), j] for j in range(together)], axis=0)
        table = phi[pl.ds(pl.multiple_of(first * parts, width), width), :]
        cells = jnp.dot(left, table, preferred_element_type=F32)
        rotation = turn[pl.ds(pl.multiple_of(first * total, together * total), together * total), :]
        turned = (cells * rotation.astype(F32)).reshape(together, total // 8, 8, CELLS)
        kept = jnp.sum(turned, axis=1).reshape(together * 8, CELLS)
        partial[pl.ds(pl.multiple_of(first * 8, together * 8), together * 8), :] = kept

    @pl.loop(0, steps)
    def _(step):
        for i in range(unroll):
            gather((step * unroll + i) * together)

    signal = partial[pl.ds(0, blocks, stride=8), :]
    for i in range(1, 8):
        signal = signal + partial[pl.ds(i, blocks, stride=8), :]
    valid = iota((blocks, CELLS), 0) * CELLS + iota((blocks, CELLS), 1) < count[0:1, :]
    signal = jnp.where(valid, signal, 0.0)
    clean = lax.dot_general(
        signal.astype(BF16), noise[...].astype(BF16), LAST_LAST, preferred_element_type=F32
    )
    filtered[...] = jnp.where(valid, clean, 0.0)

    for one in totals:
        one[...] = jnp.zeros_like(one)
    half = orders // 2

    def spread(first):
        rotation = own[pl.ds(pl.multiple_of(first * orders, 16), together * orders), :].astype(F32)
        weighted = [
            rotation[j * orders : (j + 1) * orders] * filtered[pl.ds(first + j, 1), :]
            for j in range(together)
        ]
        weighted = jnp.concatenate(weighted, axis=0).astype(BF16)
        table = phi[pl.ds(pl.multiple_of(first * parts, width), width), :]
        terms = lax.dot_general(weighted, table, LAST_LAST, preferred_element_type=F32)
        for j in range(together):
            row = pl.multiple_of(cycle_of(first + j) * orders, orders)
            here = totals[j]
            here[pl.ds(row, orders), :] += terms[j * orders : (j + 1) * orders]

    @pl.loop(0, steps)
    def _(step):
        for i in range(unroll):
            spread((step * unroll + i) * together)

    gathered = totals[0][...]
    which = iota(gathered.shape, 1) // parts
    for j in range(1, together):
        gathered = jnp.where(which == j, totals[j][...], gathered)
    totals[0][...] = gathered
    for k in range(orders):
        place = k // 2 + (k % 2) * half
        ordered[k * cycles : (k + 1) * cycles, :] = totals[0][pl.ds(place, cycles, stride=orders), :]
    turned = ordered[...].T
    summed = turned[0:parts]
    for j in range(1, together):
        summed = summed + turned[j * parts : (j + 1) * parts]
    for row in range(rows):
        shares[:, row, :] = summed[row * sky_devices : (row + 1) * sky_devices]
    for b in range(beams):
        out[b] = shares[...].astype(BF16)


def gradient_kernel(arrived, pieces, out, modes):
    me = lax.axis_index("beam")
    parts, sky_orders, cycles, width = pieces[0].shape
    orders = parts - 1
    diagonal = own_block(orders, cycles)
    for b in range(len(pieces)):
        modes[b] = jnp.sum(arrived[b].astype(F32), axis=0).astype(BF16).astype(F32)
    first, second = [0.0] * sky_orders, [0.0] * sky_orders
    for j, piece in enumerate(pieces):
        terms = piece[orders].reshape(sky_orders * cycles, width).astype(F32)
        beam_real, beam_imag = [
            terms[2 * c * orders : (2 * c + 1) * orders] + terms[(2 * c + 1) * orders : (2 * c + 2) * orders]
            for c in range(2)
        ]
        these = modes[me ^ j]
        for m in range(sky_orders):
            spreads = []
            for c in range(2):
                row = these[c * sky_orders + m : c * sky_orders + m + 1]
                spreads.append(jnp.where(diagonal, row, 0.0))
            left = jnp.concatenate(spreads, axis=0).astype(BF16)
            table = piece[0:orders, m].reshape(orders * cycles, width)
            harmonics = jnp.dot(left, table, preferred_element_type=F32)
            real, imag = harmonics[:orders], harmonics[orders:]
            first[m] += real * beam_real + imag * beam_imag
            second[m] += imag * beam_real - real * beam_imag
    for m in range(sky_orders):
        out[m, 0:1, :] = jnp.sum(first[m], axis=0, keepdims=True)
        out[m, 1:2, :] = jnp.sum(second[m], axis=0, keepdims=True)


def exchange(pieces, axis):
    count = lax.axis_size(axis)
    return [pieces[0]] + [
        lax.ppermute(pieces[j], axis, [(i, i ^ j) for i in range(count)]) for j in range(1, count)
    ]


def local(
    sky_harmonics,
    beam_harmonics,
    wigner,
    order_map,
    block_owner,
    block_local,
    cell_offset,
    cell_fraction,
    beam_angle,
    sample_count,
    noise_weight,
):
    beams, sky_devices = lax.axis_size("beam"), lax.axis_size("ma")
    orders, sky_orders, cycles, degrees = wigner.shape
    total = orders * beams
    all_sky = sky_orders * sky_devices
    parts = 2 * all_sky
    blocks = block_local.shape[0]
    blocks_local = cycles // sky_devices * CYCLE_BLOCKS
    width = degrees // beams
    lanes = orders * cycles
    rows = 2 * sky_orders
    together = max(1, CELLS // parts)
    owners = block_owner.reshape(blocks)
    limit = pltpu.CompilerParams(vmem_limit_bytes=32 * 1024 * 1024)
    integers = [
        pltpu.SMEM((blocks,), jnp.int32),
        pltpu.SMEM((blocks,), jnp.int32),
    ]

    def pinned(*arrays):
        return [pltpu.with_memory_space_constraint(array, pltpu.HBM) for array in arrays]

    later = (
        order_map, owners, block_local,
        beam_angle.reshape(blocks, CELLS),
        cell_offset.reshape(blocks, CELLS),
        cell_fraction.reshape(blocks, CELLS),
        noise_weight,
    )
    sent, (order_map, owners, places, angles, offsets, fractions, noise) = pl.pallas_call(
        modes_kernel,
        out_shape=[
            jax.ShapeDtypeStruct((beams * sky_devices // 2, 2 * rows, lanes), BF16),
            [pltpu.VMEM(array.shape, array.dtype) for array in later],
        ],
        in_specs=[*hbm(3), hbm(len(later))],
        out_specs=[vmem(1)[0], vmem(len(later))],
        scratch_shapes=[
            pltpu.VMEM(sky_harmonics.shape, F32),
            pltpu.VMEM(beam_harmonics.shape, F32),
            pltpu.VMEM((beams, orders, sky_orders, cycles, width), BF16),
            pltpu.SemaphoreType.DMA((2 + beams + len(later),)),
        ],
        compiler_params=limit,
        name="modes",
    )(*pinned(sky_harmonics, beam_harmonics, wigner), pinned(*later))
    sent = sent.reshape(beams * sky_devices, rows, lanes)
    arrived = lax.all_to_all(sent, ("beam", "ma"), split_axis=0, concat_axis=0, tiled=True)

    samples = pltpu.VMEM((blocks, CELLS), F32)
    piece = (orders + 1, sky_orders, cycles, width)
    phi, turn, own, pieces = pl.pallas_call(
        functools.partial(tables_kernel, blocks_local, sky_devices),
        out_shape=[
            pltpu.VMEM((blocks * parts, CELLS), BF16),
            pltpu.VMEM((blocks * total, CELLS), BF16),
            pltpu.VMEM((blocks * orders, CELLS), BF16),
            [pltpu.HBM(piece, BF16)] * beams,
        ],
        in_specs=vmem(6) + hbm(2),
        out_specs=[*vmem(3), hbm(beams)],
        scratch_shapes=[
            pltpu.VMEM((beams, *piece), BF16),
            pltpu.VMEM(beam_harmonics.shape, F32),
            pltpu.SemaphoreType.DMA((2 * beams,)),
            pltpu.SMEM((all_sky,), jnp.int32),
            *integers,
            pltpu.SemaphoreType.DMA((4,)),
            samples,
            pltpu.VMEM((8, blocks, CELLS), F32),
            pltpu.VMEM((16, total, CELLS), F32),
        ],
        compiler_params=limit,
        cost_estimate=pl.CostEstimate(flops=100_000_000, bytes_accessed=4_000_000, transcendentals=0),
        name="tables",
    )(
        order_map, owners, places, angles, offsets, fractions,
        *pinned(beam_harmonics, wigner),
    )
    pieces = exchange(pieces, "beam")

    grads = pl.pallas_call(
        functools.partial(samples_kernel, blocks_local),
        out_shape=jax.ShapeDtypeStruct((beams, sky_devices, rows, lanes), BF16),
        in_specs=vmem(8),
        out_specs=vmem(1)[0],
        scratch_shapes=[
            *integers,
            pltpu.SemaphoreType.DMA((2,)),
            pltpu.VMEM((beams * parts, lanes), F32),
            pltpu.VMEM((beams, together * parts, lanes), F32),
            pltpu.VMEM((beams * lanes, together * parts), F32),
            pltpu.VMEM((cycles, together, total, together * parts), BF16),
            pltpu.VMEM((blocks * 8, CELLS), F32),
            samples,
            [pltpu.VMEM((lanes, together * parts), F32) for _ in range(together)],
            pltpu.VMEM((lanes, together * parts), F32),
            pltpu.VMEM((sky_devices, rows, lanes), F32),
        ],
        compiler_params=limit,
        cost_estimate=pl.CostEstimate(flops=40_000_000_000, bytes_accessed=100_000_000, transcendentals=0),
        name="samples",
    )(
        owners, places, jnp.broadcast_to(sample_count[None, :], (8, CELLS)), noise,
        arrived.reshape(beams * parts, lanes), phi, turn, own,
    )
    grads = grads.reshape(beams * sky_devices, rows, lanes)
    grads = lax.all_to_all(grads, ("beam", "ma"), split_axis=0, concat_axis=0, tiled=True)
    return pl.pallas_call(
        gradient_kernel,
        out_shape=jax.ShapeDtypeStruct((sky_orders, 2, width), F32),
        in_specs=[vmem(1)[0], vmem(beams)],
        out_specs=vmem(1)[0],
        scratch_shapes=[pltpu.VMEM((beams, rows, lanes), F32)],
        compiler_params=limit,
        name="gradient",
    )(grads.reshape(beams, sky_devices, rows, lanes), pieces)


def solution(mesh):
    return jax.shard_map(
        local,
        mesh=mesh,
        in_specs=(
            P("ma", None, None),
            P("beam", None, None),
            P("beam", "ma", None, None),
            P(),
            P("ma", None),
            P("ma"),
            P("ma"),
            P("ma"),
            P("ma"),
            P("ma"),
            P(),
        ),
        out_specs=P("ma", None, "beam"),
        check_vma=False,
    )
```

```python
import functools
import math

import jax
import jax.numpy as jnp
from jax import lax
from jax.experimental import pallas as pl
from jax.experimental.pallas import tpu as pltpu
from jax.sharding import PartitionSpec as P

PHI = 4096
CELLS = 128
CYCLE_BLOCKS = PHI // CELLS
F32 = jnp.float32
BF16 = jnp.bfloat16
LAST_LAST = (((1,), (1,)), ((), ()))


def iota(shape, axis):
    return lax.broadcasted_iota(jnp.int32, shape, axis)


def vmem(count):
    return [pl.BlockSpec(memory_space=pltpu.VMEM)] * count


def smem(count):
    return [pl.BlockSpec(memory_space=pltpu.SMEM)] * count


def hbm(count):
    return [pl.BlockSpec(memory_space=pltpu.HBM)] * count


def sine_turns(z):
    square = z * z
    value = 39.53670603 * square - 76.54978229
    value = value * square + 81.60100407
    value = value * square - 41.34165503
    value = value * square + 6.28318516
    return value * z


def cosine_steps(steps):
    centred = ((steps + PHI // 2) & (PHI - 1)) - PHI // 2
    return sine_turns(0.25 - jnp.abs(centred).astype(F32) * (1.0 / PHI))


def every(ref, first, count, step):
    if ref.shape[1] == CELLS:
        return ref[pl.ds(first, count, stride=step), :]
    return jnp.concatenate([ref[first + i * step][None] for i in range(count)], axis=0)


def bring(sources, places, semaphores, first):
    copies = [
        pltpu.make_async_copy(source, place, semaphores.at[first + i])
        for i, (source, place) in enumerate(zip(sources, places))
    ]
    for copy in copies:
        copy.start()
    return copies


def own_block(orders, cycles):
    shape = (orders, orders * cycles)
    return iota(shape, 1) // cycles == iota(shape, 0)


def modes_kernel(sky_hbm, beam_hbm, wigner_hbm, later_hbm, out, later, sky, beam, wigner, arrivals):
    chunks, orders, sky_orders, cycles, width = wigner.shape
    small = bring((sky_hbm, beam_hbm), (sky, beam), arrivals, 0)
    spans = [pl.ds(i * width, width) for i in range(chunks)]
    large = bring([wigner_hbm.at[:, :, :, span] for span in spans], [wigner.at[i] for i in range(chunks)], arrivals, 2)
    others = bring(later_hbm, later, arrivals, 2 + chunks)
    for copy in small:
        copy.wait()
    beam_real, beam_imag = beam[:, 0, :], beam[:, 1, :]
    diagonal = own_block(orders, cycles)
    products = []
    for m in range(sky_orders):
        sky_real, sky_imag = sky[m, 0:1, :], sky[m, 1:2, :]
        first = sky_real * beam_real - sky_imag * beam_imag
        second = sky_real * beam_imag + sky_imag * beam_real
        products.append(jnp.concatenate([first, second], axis=0).astype(BF16))
    sums = [0.0] * sky_orders
    for i in range(chunks):
        large[i].wait()
        for m in range(sky_orders):
            table = wigner[i, :, m].reshape(orders * cycles, width)
            left = products[m][:, i * width : (i + 1) * width]
            sums[m] += lax.dot_general(table, left, LAST_LAST, preferred_element_type=F32)
    rows = [None] * (2 * sky_orders)
    for m in range(sky_orders):
        modes = sums[m].T
        for c in range(2):
            part = jnp.where(diagonal, modes[c * orders : (c + 1) * orders], 0.0)
            rows[c * sky_orders + m] = jnp.sum(part, axis=0, keepdims=True)
    block = jnp.concatenate(rows + rows, axis=0).astype(BF16)
    for d in range(out.shape[0]):
        out[d] = block
    for copy in others:
        copy.wait()


def tables_kernel(
    blocks_local, sky_devices,
    order_vmem, owners_vmem, locals_vmem, angles, offsets, fractions, beam_hbm, wigner_hbm,
    phi, turn, own, pieces_hbm, pieces, beam, departures, order_map, owners, locals_, arrivals,
    step_real, step_imag, powers,
):
    copies = bring((order_vmem, owners_vmem, locals_vmem), (order_map, owners, locals_), arrivals, 0)
    me = lax.axis_index("beam")
    extra = bring((beam_hbm,), (beam,), arrivals, 3)[0]
    beams, beam_orders, width = pieces.shape[0], beam.shape[0], pieces.shape[4]
    spans = [pl.ds(pl.multiple_of((me ^ j) * width, width), width) for j in range(beams)]
    arriving = bring(
        [wigner_hbm.at[:, :, :, span] for span in spans],
        [pieces.at[j, 0:beam_orders] for j in range(beams)],
        departures, 0,
    )
    orders = order_map.shape[0]
    blocks = offsets.shape[0]
    half = turn.shape[0] // blocks // 2
    own_half = own.shape[0] // blocks // 2

    part = angles[...] * (0.5 / math.pi)
    part = part - jnp.round(part)
    folded = jnp.where(part > 0.25, 0.5 - part, jnp.where(part < -0.25, -0.5 - part, part))
    real, imag = sine_turns(0.25 - jnp.abs(part)), sine_turns(folded)
    for i in range(4):
        if i:
            real, imag = real * real - imag * imag, 2.0 * real * imag
        powers[2 * i], powers[2 * i + 1] = real, imag

    copies[0].wait()
    order = jnp.zeros((orders, CELLS), jnp.int32)
    row = iota((orders, CELLS), 0)
    lane = iota((orders, CELLS), 1)
    for m in range(orders):
        place = m % (orders // sky_devices) * sky_devices + m // (orders // sky_devices)
        order = jnp.where(row == place, order_map[m], order)

    def phase(steps):
        return cosine_steps(steps), cosine_steps(steps + PHI // 4)

    scaling = 1.0 / math.sqrt(orders)
    cell_real, cell_imag = phase(order * lane)
    cell_real, cell_imag = cell_real * scaling, cell_imag * scaling
    next_real, next_imag = phase(order)
    next_real = next_real - 1.0
    first_real, first_imag = phase(((order * CELLS) & (PHI - 1)) * lane)
    for j in range(CYCLE_BLOCKS):
        step_real[j] = jnp.broadcast_to(first_real[:, j : j + 1], (orders, CELLS))
        step_imag[j] = jnp.broadcast_to(first_imag[:, j : j + 1], (orders, CELLS))
    for copy in copies[1:]:
        copy.wait()

    def block_phases(s):
        place = (owners[s] * blocks_local + locals_[s]) & (CYCLE_BLOCKS - 1)
        offset = jnp.broadcast_to(offsets[pl.ds(s, 1), :], (orders, CELLS))
        fraction = jnp.broadcast_to(fractions[pl.ds(s, 1), :], (orders, CELLS))
        real = jnp.take_along_axis(cell_real, offset, axis=1, mode="promise_in_bounds")
        imag = jnp.take_along_axis(cell_imag, offset, axis=1, mode="promise_in_bounds")
        base_real, base_imag = step_real[place], step_imag[place]
        left_real = real * base_real - imag * base_imag
        left_imag = real * base_imag + imag * base_real
        mix_real = 1.0 + fraction * next_real
        mix_imag = fraction * next_imag
        both = jnp.concatenate(
            [left_real * mix_real - left_imag * mix_imag, left_real * mix_imag + left_imag * mix_real],
            axis=0,
        )
        start = pl.multiple_of(s * 2 * orders, 2 * orders)
        phi[pl.ds(start, 2 * orders), :] = both.astype(BF16)

    scale = 1.0 / math.sqrt(2 * half)
    power = iota((8, CELLS), 0)

    def block_turns(s):
        steps = [jnp.broadcast_to(powers[i, pl.ds(s, 1), :], (8, CELLS)) for i in range(8)]
        one_real, one_imag = steps[:2]
        step = steps[6:]
        odd = power & 1 == 1
        real, imag = jnp.where(odd, one_real * scale, scale), jnp.where(odd, one_imag * scale, 0.0)
        for bit in (2, 4):
            taken = power & bit == bit
            by_real, by_imag = jnp.where(taken, steps[bit], 1.0), jnp.where(taken, steps[bit + 1], 0.0)
            real, imag = real * by_real - imag * by_imag, real * by_imag + imag * by_real
        evens, odds = [], []
        for j in range(half // 8):
            if j:
                real, imag = real * step[0] - imag * step[1], real * step[1] + imag * step[0]
            evens.append(real)
            odds.append(real * one_imag + imag * one_real)
        return evens + odds

    extra.wait()
    sky_orders, cycles = pieces.shape[2:4]
    for j, span in enumerate(spans):
        terms = []
        for c in range(2):
            values = beam[:, c, span]
            high = values.astype(BF16)
            terms += [high, (values - high.astype(F32)).astype(BF16)]
        filling = sky_orders * cycles - 4 * beam_orders
        if filling:
            terms.append(jnp.zeros((filling, width), BF16))
        pieces[j, beam_orders] = jnp.concatenate(terms, axis=0).reshape(sky_orders, cycles, width)
    some = max(2, CELLS // (2 * half))
    shape = (some * 2 * own_half, some * 2 * half)
    own_row, turn_row = iota(shape, 0), iota(shape, 1)
    kept = own_row % (2 * own_half)
    source = kept // own_half * half + me * own_half + kept % own_half
    chosen = turn_row == own_row // (2 * own_half) * (2 * half) + source
    chosen = jnp.where(chosen, 1.0, 0.0).astype(BF16)
    run = 16

    def one_run(group):
        for j in range(0, run, some):
            first = group * run + j
            rows = []
            for i in range(some):
                block_phases(first + i)
                rows += block_turns(first + i)
            rows = jnp.concatenate(rows, axis=0).astype(BF16)
            turn[pl.ds(pl.multiple_of(first * 2 * half, shape[1]), shape[1]), :] = rows
            mine = jnp.dot(chosen, rows, preferred_element_type=F32)
            own[pl.ds(pl.multiple_of(first * 2 * own_half, shape[0]), shape[0]), :] = mine.astype(BF16)

    runs = blocks // run
    pl.loop(0, runs // 2)(one_run)
    for copy in arriving:
        copy.wait()
    leaving = bring([pieces.at[j] for j in range(beams)], pieces_hbm, departures, beams)
    pl.loop(runs // 2, runs)(one_run)
    for copy in leaving:
        copy.wait()


def samples_kernel(
    blocks_local, owners_vmem, locals_vmem, count, noise, arrived, phi, turn, own,
    out, owners, locals_, arrivals, widened,
    stacked, modes_rows, modes, partial, filtered, totals, ordered, shares,
):
    copies = bring((owners_vmem, locals_vmem), (owners, locals_), arrivals, 0)
    widened[...] = arrived[...].astype(F32)
    sky_devices, rows, lanes = shares.shape
    parts = sky_devices * rows
    beams = arrived.shape[0] // parts
    blocks = partial.shape[0] // 8
    total = turn.shape[0] // blocks
    orders = total // beams
    cycles = lanes // orders
    together = len(totals)
    unroll = 32

    steps = max(1, blocks // (together * unroll))

    def cycle_of(s):
        return (owners[s] * blocks_local + locals_[s]) // CYCLE_BLOCKS

    width = together * parts
    for b in range(beams):
        for row in range(rows):
            some = every(widened, b * parts + row, sky_devices, rows)
            for j in range(together):
                start = j * parts + row * sky_devices
                stacked[b, start : start + sky_devices, :] = some
        modes_rows[b * lanes : (b + 1) * lanes, :] = stacked[b].T
    lane_group = iota((total, width), 1) // parts
    for r in range(cycles):
        halves = [
            modes_rows[pl.ds(r + parity * cycles, total // 2, stride=2 * cycles), :]
            for parity in range(2)
        ]
        values = jnp.concatenate(halves, axis=0)
        for j in range(together):
            modes[r, j] = jnp.where(lane_group == j, values, 0.0).astype(BF16)
    for copy in copies:
        copy.wait()

    def gather(first):
        left = jnp.concatenate([modes[cycle_of(first + j), j] for j in range(together)], axis=0)
        table = phi[pl.ds(pl.multiple_of(first * parts, width), width), :]
        cells = jnp.dot(left, table, preferred_element_type=F32)
        rotation = turn[pl.ds(pl.multiple_of(first * total, together * total), together * total), :]
        turned = (cells * rotation.astype(F32)).reshape(together, total // 8, 8, CELLS)
        kept = jnp.sum(turned, axis=1).reshape(together * 8, CELLS)
        partial[pl.ds(pl.multiple_of(first * 8, together * 8), together * 8), :] = kept

    @pl.loop(0, steps)
    def _(step):
        for i in range(unroll):
            gather((step * unroll + i) * together)

    signal = partial[pl.ds(0, blocks, stride=8), :]
    for i in range(1, 8):
        signal = signal + partial[pl.ds(i, blocks, stride=8), :]
    valid = iota((blocks, CELLS), 0) * CELLS + iota((blocks, CELLS), 1) < count[0:1, :]
    signal = jnp.where(valid, signal, 0.0)
    clean = lax.dot_general(
        signal.astype(BF16), noise[...].astype(BF16), LAST_LAST, preferred_element_type=F32
    )
    filtered[...] = jnp.where(valid, clean, 0.0)

    for one in totals:
        one[...] = jnp.zeros_like(one)
    half = orders // 2

    def spread(first):
        rotation = own[pl.ds(pl.multiple_of(first * orders, 16), together * orders), :].astype(F32)
        weighted = [
            rotation[j * orders : (j + 1) * orders] * filtered[pl.ds(first + j, 1), :]
            for j in range(together)
        ]
        weighted = jnp.concatenate(weighted, axis=0).astype(BF16)
        table = phi[pl.ds(pl.multiple_of(first * parts, width), width), :]
        terms = lax.dot_general(weighted, table, LAST_LAST, preferred_element_type=F32)
        for j in range(together):
            row = pl.multiple_of(cycle_of(first + j) * orders, orders)
            here = totals[j]
            here[pl.ds(row, orders), :] += terms[j * orders : (j + 1) * orders]

    @pl.loop(0, steps)
    def _(step):
        for i in range(unroll):
            spread((step * unroll + i) * together)

    gathered = totals[0][...]
    which = iota(gathered.shape, 1) // parts
    for j in range(1, together):
        gathered = jnp.where(which == j, totals[j][...], gathered)
    totals[0][...] = gathered
    for k in range(orders):
        place = k // 2 + (k % 2) * half
        ordered[k * cycles : (k + 1) * cycles, :] = totals[0][pl.ds(place, cycles, stride=orders), :]
    turned = ordered[...].T
    summed = turned[0:parts]
    for j in range(1, together):
        summed = summed + turned[j * parts : (j + 1) * parts]
    for row in range(rows):
        shares[:, row, :] = summed[row * sky_devices : (row + 1) * sky_devices]
    for b in range(beams):
        out[b] = shares[...].astype(BF16)


def gradient_kernel(arrived, pieces, out, modes):
    me = lax.axis_index("beam")
    parts, sky_orders, cycles, width = pieces[0].shape
    orders = parts - 1
    diagonal = own_block(orders, cycles)
    for b in range(len(pieces)):
        modes[b] = jnp.sum(arrived[b].astype(F32), axis=0).astype(BF16).astype(F32)
    first, second = [0.0] * sky_orders, [0.0] * sky_orders
    for j, piece in enumerate(pieces):
        terms = piece[orders].reshape(sky_orders * cycles, width).astype(F32)
        beam_real, beam_imag = [
            terms[2 * c * orders : (2 * c + 1) * orders] + terms[(2 * c + 1) * orders : (2 * c + 2) * orders]
            for c in range(2)
        ]
        these = modes[me ^ j]
        for m in range(sky_orders):
            spreads = []
            for c in range(2):
                row = these[c * sky_orders + m : c * sky_orders + m + 1]
                spreads.append(jnp.where(diagonal, row, 0.0))
            left = jnp.concatenate(spreads, axis=0).astype(BF16)
            table = piece[0:orders, m].reshape(orders * cycles, width)
            harmonics = jnp.dot(left, table, preferred_element_type=F32)
            real, imag = harmonics[:orders], harmonics[orders:]
            first[m] += real * beam_real + imag * beam_imag
            second[m] += imag * beam_real - real * beam_imag
    for m in range(sky_orders):
        out[m, 0:1, :] = jnp.sum(first[m], axis=0, keepdims=True)
        out[m, 1:2, :] = jnp.sum(second[m], axis=0, keepdims=True)


def exchange(pieces, axis):
    count = lax.axis_size(axis)
    return [pieces[0]] + [
        lax.ppermute(pieces[j], axis, [(i, i ^ j) for i in range(count)]) for j in range(1, count)
    ]


def local(
    sky_harmonics,
    beam_harmonics,
    wigner,
    order_map,
    block_owner,
    block_local,
    cell_offset,
    cell_fraction,
    beam_angle,
    sample_count,
    noise_weight,
):
    beams, sky_devices = lax.axis_size("beam"), lax.axis_size("ma")
    orders, sky_orders, cycles, degrees = wigner.shape
    total = orders * beams
    all_sky = sky_orders * sky_devices
    parts = 2 * all_sky
    blocks = block_local.shape[0]
    blocks_local = cycles // sky_devices * CYCLE_BLOCKS
    width = degrees // beams
    lanes = orders * cycles
    rows = 2 * sky_orders
    together = max(1, CELLS // parts)
    owners = block_owner.reshape(blocks)
    limit = pltpu.CompilerParams(vmem_limit_bytes=32 * 1024 * 1024)
    integers = [
        pltpu.SMEM((blocks,), jnp.int32),
        pltpu.SMEM((blocks,), jnp.int32),
    ]

    def pinned(*arrays):
        return [pltpu.with_memory_space_constraint(array, pltpu.HBM) for array in arrays]

    later = (
        order_map, owners, block_local,
        beam_angle.reshape(blocks, CELLS),
        cell_offset.reshape(blocks, CELLS),
        cell_fraction.reshape(blocks, CELLS),
        noise_weight,
    )
    sent, (order_map, owners, places, angles, offsets, fractions, noise) = pl.pallas_call(
        modes_kernel,
        out_shape=[
            jax.ShapeDtypeStruct((beams * sky_devices // 2, 2 * rows, lanes), BF16),
            [pltpu.VMEM(array.shape, array.dtype) for array in later],
        ],
        in_specs=[*hbm(3), hbm(len(later))],
        out_specs=[vmem(1)[0], vmem(len(later))],
        scratch_shapes=[
            pltpu.VMEM(sky_harmonics.shape, F32),
            pltpu.VMEM(beam_harmonics.shape, F32),
            pltpu.VMEM((beams, orders, sky_orders, cycles, width), BF16),
            pltpu.SemaphoreType.DMA((2 + beams + len(later),)),
        ],
        compiler_params=limit,
        name="modes",
    )(*pinned(sky_harmonics, beam_harmonics, wigner), pinned(*later))
    sent = sent.reshape(beams * sky_devices, rows, lanes)
    arrived = lax.all_to_all(sent, ("beam", "ma"), split_axis=0, concat_axis=0, tiled=True)

    samples = pltpu.VMEM((blocks, CELLS), F32)
    piece = (orders + 1, sky_orders, cycles, width)
    phi, turn, own, pieces = pl.pallas_call(
        functools.partial(tables_kernel, blocks_local, sky_devices),
        out_shape=[
            pltpu.VMEM((blocks * parts, CELLS), BF16),
            pltpu.VMEM((blocks * total, CELLS), BF16),
            pltpu.VMEM((blocks * orders, CELLS), BF16),
            [pltpu.HBM(piece, BF16)] * beams,
        ],
        in_specs=vmem(6) + hbm(2),
        out_specs=[*vmem(3), hbm(beams)],
        scratch_shapes=[
            pltpu.VMEM((beams, *piece), BF16),
            pltpu.VMEM(beam_harmonics.shape, F32),
            pltpu.SemaphoreType.DMA((2 * beams,)),
            pltpu.SMEM((all_sky,), jnp.int32),
            *integers,
            pltpu.SemaphoreType.DMA((4,)),
            pltpu.VMEM((CYCLE_BLOCKS, all_sky, CELLS), F32),
            pltpu.VMEM((CYCLE_BLOCKS, all_sky, CELLS), F32),
            pltpu.VMEM((8, blocks, CELLS), F32),
        ],
        compiler_params=limit,
        cost_estimate=pl.CostEstimate(flops=100_000_000, bytes_accessed=4_000_000, transcendentals=0),
        name="tables",
    )(
        order_map, owners, places, angles, offsets, fractions,
        *pinned(beam_harmonics, wigner),
    )
    pieces = exchange(pieces, "beam")

    grads = pl.pallas_call(
        functools.partial(samples_kernel, blocks_local),
        out_shape=jax.ShapeDtypeStruct((beams, sky_devices, rows, lanes), BF16),
        in_specs=vmem(8),
        out_specs=vmem(1)[0],
        scratch_shapes=[
            *integers,
            pltpu.SemaphoreType.DMA((2,)),
            pltpu.VMEM((beams * parts, lanes), F32),
            pltpu.VMEM((beams, together * parts, lanes), F32),
            pltpu.VMEM((beams * lanes, together * parts), F32),
            pltpu.VMEM((cycles, together, total, together * parts), BF16),
            pltpu.VMEM((blocks * 8, CELLS), F32),
            samples,
            [pltpu.VMEM((lanes, together * parts), F32) for _ in range(together)],
            pltpu.VMEM((lanes, together * parts), F32),
            pltpu.VMEM((sky_devices, rows, lanes), F32),
        ],
        compiler_params=limit,
        cost_estimate=pl.CostEstimate(flops=40_000_000_000, bytes_accessed=100_000_000, transcendentals=0),
        name="samples",
    )(
        owners, places, jnp.broadcast_to(sample_count[None, :], (8, CELLS)), noise,
        arrived.reshape(beams * parts, lanes), phi, turn, own,
    )
    grads = grads.reshape(beams * sky_devices, rows, lanes)
    grads = lax.all_to_all(grads, ("beam", "ma"), split_axis=0, concat_axis=0, tiled=True)
    return pl.pallas_call(
        gradient_kernel,
        out_shape=jax.ShapeDtypeStruct((sky_orders, 2, width), F32),
        in_specs=[vmem(1)[0], vmem(beams)],
        out_specs=vmem(1)[0],
        scratch_shapes=[pltpu.VMEM((beams, rows, lanes), F32)],
        compiler_params=limit,
        name="gradient",
    )(grads.reshape(beams, sky_devices, rows, lanes), pieces)


def solution(mesh):
    return jax.shard_map(
        local,
        mesh=mesh,
        in_specs=(
            P("ma", None, None),
            P("beam", None, None),
            P("beam", "ma", None, None),
            P(),
            P("ma", None),
            P("ma"),
            P("ma"),
            P("ma"),
            P("ma"),
            P("ma"),
            P(),
        ),
        out_specs=P("ma", None, "beam"),
        check_vma=False,
    )
```

```python
import functools
import math

import jax
import jax.numpy as jnp
from jax import lax
from jax.experimental import pallas as pl
from jax.experimental.pallas import tpu as pltpu
from jax.sharding import PartitionSpec as P

PHI = 4096
CELLS = 128
CYCLE_BLOCKS = PHI // CELLS
F32 = jnp.float32
BF16 = jnp.bfloat16
LAST_LAST = (((1,), (1,)), ((), ()))


def iota(shape, axis):
    return lax.broadcasted_iota(jnp.int32, shape, axis)


def vmem(count):
    return [pl.BlockSpec(memory_space=pltpu.VMEM)] * count


def smem(count):
    return [pl.BlockSpec(memory_space=pltpu.SMEM)] * count


def hbm(count):
    return [pl.BlockSpec(memory_space=pltpu.HBM)] * count


def sine_turns(z):
    square = z * z
    value = 39.53670603 * square - 76.54978229
    value = value * square + 81.60100407
    value = value * square - 41.34165503
    value = value * square + 6.28318516
    return value * z


def cosine_steps(steps):
    centred = ((steps + PHI // 2) & (PHI - 1)) - PHI // 2
    return sine_turns(0.25 - jnp.abs(centred).astype(F32) * (1.0 / PHI))


def every(ref, first, count, step):
    if ref.shape[1] == CELLS:
        return ref[pl.ds(first, count, stride=step), :]
    return jnp.concatenate([ref[first + i * step][None] for i in range(count)], axis=0)


def put_every(ref, first, step, values):
    if ref.shape[1] == CELLS:
        ref[pl.ds(first, values.shape[0], stride=step), :] = values
    else:
        for i in range(values.shape[0]):
            ref[first + i * step, :] = values[i]


def bring(sources, places, semaphores, first):
    copies = [
        pltpu.make_async_copy(source, place, semaphores.at[first + i])
        for i, (source, place) in enumerate(zip(sources, places))
    ]
    for copy in copies:
        copy.start()
    return copies


def own_block(orders, cycles):
    shape = (orders, orders * cycles)
    return iota(shape, 1) // cycles == iota(shape, 0)


def modes_kernel(sky_hbm, beam_hbm, wigner_hbm, later_hbm, out, later, sky, beam, wigner, arrivals):
    chunks, orders, sky_orders, cycles, width = wigner.shape
    small = bring((sky_hbm, beam_hbm), (sky, beam), arrivals, 0)
    spans = [pl.ds(i * width, width) for i in range(chunks)]
    large = bring([wigner_hbm.at[:, :, :, span] for span in spans], [wigner.at[i] for i in range(chunks)], arrivals, 2)
    others = bring(later_hbm, later, arrivals, 2 + chunks)
    for copy in small:
        copy.wait()
    beam_real, beam_imag = beam[:, 0, :], beam[:, 1, :]
    diagonal = own_block(orders, cycles)
    products = []
    for m in range(sky_orders):
        sky_real, sky_imag = sky[m, 0:1, :], sky[m, 1:2, :]
        first = sky_real * beam_real - sky_imag * beam_imag
        second = sky_real * beam_imag + sky_imag * beam_real
        products.append(jnp.concatenate([first, second], axis=0).astype(BF16))
    sums = [0.0] * sky_orders
    for i in range(chunks):
        large[i].wait()
        for m in range(sky_orders):
            table = wigner[i, :, m].reshape(orders * cycles, width)
            left = products[m][:, i * width : (i + 1) * width]
            sums[m] += lax.dot_general(table, left, LAST_LAST, preferred_element_type=F32)
    rows = [None] * (2 * sky_orders)
    for m in range(sky_orders):
        modes = sums[m].T
        for c in range(2):
            part = jnp.where(diagonal, modes[c * orders : (c + 1) * orders], 0.0)
            rows[c * sky_orders + m] = jnp.sum(part, axis=0, keepdims=True)
    block = jnp.concatenate(rows + rows, axis=0).astype(BF16)
    for d in range(out.shape[0]):
        out[d] = block
    for copy in others:
        copy.wait()


def tables_kernel(
    blocks_local, sky_devices,
    order_vmem, owners_vmem, locals_vmem, angles, offsets, fractions, beam_hbm, wigner_hbm,
    phi, turn, own, pieces_hbm, pieces, beam, departures, order_map, owners, locals_, arrivals,
    step_real, step_imag, powers,
):
    copies = bring((order_vmem, owners_vmem, locals_vmem), (order_map, owners, locals_), arrivals, 0)
    me = lax.axis_index("beam")
    extra = bring((beam_hbm,), (beam,), arrivals, 3)[0]
    beams, beam_orders, width = pieces.shape[0], beam.shape[0], pieces.shape[4]
    spans = [pl.ds(pl.multiple_of((me ^ j) * width, width), width) for j in range(beams)]
    arriving = bring(
        [wigner_hbm.at[:, :, :, span] for span in spans],
        [pieces.at[j, 0:beam_orders] for j in range(beams)],
        departures, 0,
    )
    orders = order_map.shape[0]
    blocks = offsets.shape[0]
    half = turn.shape[0] // blocks // 2
    own_half = own.shape[0] // blocks // 2

    part = angles[...] * (0.5 / math.pi)
    part = part - jnp.round(part)
    folded = jnp.where(part > 0.25, 0.5 - part, jnp.where(part < -0.25, -0.5 - part, part))
    real, imag = sine_turns(0.25 - jnp.abs(part)), sine_turns(folded)
    for i in range(4):
        if i:
            real, imag = real * real - imag * imag, 2.0 * real * imag
        powers[2 * i], powers[2 * i + 1] = real, imag

    copies[0].wait()
    order = jnp.zeros((orders, CELLS), jnp.int32)
    row = iota((orders, CELLS), 0)
    lane = iota((orders, CELLS), 1)
    for m in range(orders):
        place = m % (orders // sky_devices) * sky_devices + m // (orders // sky_devices)
        order = jnp.where(row == place, order_map[m], order)

    def phase(steps):
        return cosine_steps(steps), cosine_steps(steps + PHI // 4)

    scaling = 1.0 / math.sqrt(orders)
    cell_real, cell_imag = phase(order * lane)
    cell_real, cell_imag = cell_real * scaling, cell_imag * scaling
    next_real, next_imag = phase(order)
    next_real = next_real - 1.0
    first_real, first_imag = phase(((order * CELLS) & (PHI - 1)) * lane)
    for j in range(CYCLE_BLOCKS):
        step_real[j] = jnp.broadcast_to(first_real[:, j : j + 1], (orders, CELLS))
        step_imag[j] = jnp.broadcast_to(first_imag[:, j : j + 1], (orders, CELLS))
    for copy in copies[1:]:
        copy.wait()

    def block_phases(s):
        place = (owners[s] * blocks_local + locals_[s]) & (CYCLE_BLOCKS - 1)
        offset = jnp.broadcast_to(offsets[pl.ds(s, 1), :], (orders, CELLS))
        fraction = jnp.broadcast_to(fractions[pl.ds(s, 1), :], (orders, CELLS))
        real = jnp.take_along_axis(cell_real, offset, axis=1, mode="promise_in_bounds")
        imag = jnp.take_along_axis(cell_imag, offset, axis=1, mode="promise_in_bounds")
        base_real, base_imag = step_real[place], step_imag[place]
        left_real = real * base_real - imag * base_imag
        left_imag = real * base_imag + imag * base_real
        mix_real = 1.0 + fraction * next_real
        mix_imag = fraction * next_imag
        both = jnp.concatenate(
            [left_real * mix_real - left_imag * mix_imag, left_real * mix_imag + left_imag * mix_real],
            axis=0,
        )
        start = pl.multiple_of(s * 2 * orders, 2 * orders)
        phi[pl.ds(start, 2 * orders), :] = both.astype(BF16)

    scale = 1.0 / math.sqrt(2 * half)
    power = iota((8, CELLS), 0)

    def block_turns(s):
        steps = [jnp.broadcast_to(powers[i, pl.ds(s, 1), :], (8, CELLS)) for i in range(8)]
        one_real, one_imag = steps[:2]
        step = steps[6:]
        odd = power & 1 == 1
        real, imag = jnp.where(odd, one_real * scale, scale), jnp.where(odd, one_imag * scale, 0.0)
        for bit in (2, 4):
            taken = power & bit == bit
            by_real, by_imag = jnp.where(taken, steps[bit], 1.0), jnp.where(taken, steps[bit + 1], 0.0)
            real, imag = real * by_real - imag * by_imag, real * by_imag + imag * by_real
        evens, odds = [], []
        for j in range(half // 8):
            if j:
                real, imag = real * step[0] - imag * step[1], real * step[1] + imag * step[0]
            evens.append(real)
            odds.append(real * one_imag + imag * one_real)
        return evens + odds

    extra.wait()
    sky_orders, cycles = pieces.shape[2:4]
    for j, span in enumerate(spans):
        terms = []
        for c in range(2):
            values = beam[:, c, span]
            high = values.astype(BF16)
            terms += [high, (values - high.astype(F32)).astype(BF16)]
        filling = sky_orders * cycles - 4 * beam_orders
        if filling:
            terms.append(jnp.zeros((filling, width), BF16))
        pieces[j, beam_orders] = jnp.concatenate(terms, axis=0).reshape(sky_orders, cycles, width)
    some = max(2, CELLS // (2 * half))
    shape = (some * 2 * own_half, some * 2 * half)
    own_row, turn_row = iota(shape, 0), iota(shape, 1)
    kept = own_row % (2 * own_half)
    source = kept // own_half * half + me * own_half + kept % own_half
    chosen = turn_row == own_row // (2 * own_half) * (2 * half) + source
    chosen = jnp.where(chosen, 1.0, 0.0).astype(BF16)
    run = 16

    def one_run(group):
        for j in range(0, run, some):
            first = group * run + j
            rows = []
            for i in range(some):
                block_phases(first + i)
                rows += block_turns(first + i)
            rows = jnp.concatenate(rows, axis=0).astype(BF16)
            turn[pl.ds(pl.multiple_of(first * 2 * half, shape[1]), shape[1]), :] = rows
            mine = jnp.dot(chosen, rows, preferred_element_type=F32)
            own[pl.ds(pl.multiple_of(first * 2 * own_half, shape[0]), shape[0]), :] = mine.astype(BF16)

    runs = blocks // run
    early = max(1, runs // 4)
    pl.loop(0, early)(one_run)
    for copy in arriving:
        copy.wait()
    leaving = bring([pieces.at[j] for j in range(beams)], pieces_hbm, departures, beams)
    pl.loop(early, runs)(one_run)
    for copy in leaving:
        copy.wait()


def samples_kernel(
    blocks_local, rows, owners_vmem, locals_vmem, count, noise, arrived, phi, turn, own,
    out, owners, locals_, arrivals, widened,
    stacked, modes_rows, modes, partial, filtered, totals, ordered, shares,
):
    copies = bring((owners_vmem, locals_vmem), (owners, locals_), arrivals, 0)
    widened[...] = arrived[...].astype(F32)
    lanes = shares.shape[1]
    parts = shares.shape[0]
    beams = arrived.shape[0] // parts
    sky_devices = parts // rows
    blocks = partial.shape[0] // 8
    total = turn.shape[0] // blocks
    orders = total // beams
    cycles = lanes // orders
    together = len(totals)
    unroll = 32

    steps = max(1, blocks // (together * unroll))

    def cycle_of(s):
        return (owners[s] * blocks_local + locals_[s]) // CYCLE_BLOCKS

    width = together * parts
    for b in range(beams):
        for row in range(rows):
            some = every(widened, b * parts + row, sky_devices, rows)
            for j in range(together):
                start = j * parts + row * sky_devices
                stacked[b, start : start + sky_devices, :] = some
        modes_rows[b * lanes : (b + 1) * lanes, :] = stacked[b].T
    lane_group = iota((total, width), 1) // parts
    for r in range(cycles):
        halves = [
            modes_rows[pl.ds(r + parity * cycles, total // 2, stride=2 * cycles), :]
            for parity in range(2)
        ]
        values = jnp.concatenate(halves, axis=0)
        for j in range(together):
            modes[r, j] = jnp.where(lane_group == j, values, 0.0).astype(BF16)
    for copy in copies:
        copy.wait()

    def gather(first):
        left = jnp.concatenate([modes[cycle_of(first + j), j] for j in range(together)], axis=0)
        table = phi[pl.ds(pl.multiple_of(first * parts, width), width), :]
        cells = jnp.dot(left, table, preferred_element_type=F32)
        rotation = turn[pl.ds(pl.multiple_of(first * total, together * total), together * total), :]
        turned = (cells * rotation.astype(F32)).reshape(together, total // 8, 8, CELLS)
        kept = jnp.sum(turned, axis=1).reshape(together * 8, CELLS)
        partial[pl.ds(pl.multiple_of(first * 8, together * 8), together * 8), :] = kept

    @pl.loop(0, steps)
    def _(step):
        for i in range(unroll):
            gather((step * unroll + i) * together)

    signal = partial[pl.ds(0, blocks, stride=8), :]
    for i in range(1, 8):
        signal = signal + partial[pl.ds(i, blocks, stride=8), :]
    valid = iota((blocks, CELLS), 0) * CELLS + iota((blocks, CELLS), 1) < count[0:1, :]
    signal = jnp.where(valid, signal, 0.0)
    clean = lax.dot_general(
        signal.astype(BF16), noise[...].astype(BF16), LAST_LAST, preferred_element_type=F32
    )
    filtered[...] = jnp.where(valid, clean, 0.0)

    for one in totals:
        one[...] = jnp.zeros_like(one)
    half = orders // 2

    def spread(first):
        rotation = own[pl.ds(pl.multiple_of(first * orders, 16), together * orders), :].astype(F32)
        weighted = [
            rotation[j * orders : (j + 1) * orders] * filtered[pl.ds(first + j, 1), :]
            for j in range(together)
        ]
        weighted = jnp.concatenate(weighted, axis=0).astype(BF16)
        table = phi[pl.ds(pl.multiple_of(first * parts, width), width), :]
        terms = lax.dot_general(weighted, table, LAST_LAST, preferred_element_type=F32)
        for j in range(together):
            row = pl.multiple_of(cycle_of(first + j) * orders, orders)
            here = totals[j]
            here[pl.ds(row, orders), :] += terms[j * orders : (j + 1) * orders]

    @pl.loop(0, steps)
    def _(step):
        for i in range(unroll):
            spread((step * unroll + i) * together)

    gathered = totals[0][...]
    which = iota(gathered.shape, 1) // parts
    for j in range(1, together):
        gathered = jnp.where(which == j, totals[j][...], gathered)
    totals[0][...] = gathered
    for k in range(orders):
        place = k // 2 + (k % 2) * half
        ordered[k * cycles : (k + 1) * cycles, :] = totals[0][pl.ds(place, cycles, stride=orders), :]
    turned = ordered[...].T
    summed = turned[0:parts]
    for j in range(1, together):
        summed = summed + turned[j * parts : (j + 1) * parts]
    for row in range(rows):
        put_every(shares, row, rows, summed[row * sky_devices : (row + 1) * sky_devices])
    block = shares[...].astype(BF16)
    for b in range(beams):
        out[b] = block


def gradient_kernel(arrived, pieces, out, modes):
    me = lax.axis_index("beam")
    parts, sky_orders, cycles, width = pieces[0].shape
    orders = parts - 1
    diagonal = own_block(orders, cycles)
    for b in range(len(pieces)):
        terms = arrived[b].astype(F32)
        while terms.shape[0] > 2 * sky_orders:
            middle = terms.shape[0] // 2
            terms = terms[:middle] + terms[middle:]
        modes[b] = terms.astype(BF16).astype(F32)
    first, second = [0.0] * sky_orders, [0.0] * sky_orders
    for j, piece in enumerate(pieces):
        terms = piece[orders].reshape(sky_orders * cycles, width).astype(F32)
        beam_real, beam_imag = [
            terms[2 * c * orders : (2 * c + 1) * orders] + terms[(2 * c + 1) * orders : (2 * c + 2) * orders]
            for c in range(2)
        ]
        these = modes[me ^ j]
        for m in range(sky_orders):
            spreads = []
            for c in range(2):
                row = these[c * sky_orders + m : c * sky_orders + m + 1]
                spreads.append(jnp.where(diagonal, row, 0.0))
            left = jnp.concatenate(spreads, axis=0).astype(BF16)
            table = piece[0:orders, m].reshape(orders * cycles, width)
            harmonics = jnp.dot(left, table, preferred_element_type=F32)
            real, imag = harmonics[:orders], harmonics[orders:]
            first[m] += real * beam_real + imag * beam_imag
            second[m] += imag * beam_real - real * beam_imag
    for m in range(sky_orders):
        out[m, 0:1, :] = jnp.sum(first[m], axis=0, keepdims=True)
        out[m, 1:2, :] = jnp.sum(second[m], axis=0, keepdims=True)


def exchange(pieces, axis):
    count = lax.axis_size(axis)
    return [pieces[0]] + [
        lax.ppermute(pieces[j], axis, [(i, i ^ j) for i in range(count)]) for j in range(1, count)
    ]


def local(
    sky_harmonics,
    beam_harmonics,
    wigner,
    order_map,
    block_owner,
    block_local,
    cell_offset,
    cell_fraction,
    beam_angle,
    sample_count,
    noise_weight,
):
    beams, sky_devices = lax.axis_size("beam"), lax.axis_size("ma")
    orders, sky_orders, cycles, degrees = wigner.shape
    total = orders * beams
    all_sky = sky_orders * sky_devices
    parts = 2 * all_sky
    blocks = block_local.shape[0]
    blocks_local = cycles // sky_devices * CYCLE_BLOCKS
    width = degrees // beams
    lanes = orders * cycles
    rows = 2 * sky_orders
    together = max(1, CELLS // parts)
    owners = block_owner.reshape(blocks)
    limit = pltpu.CompilerParams(vmem_limit_bytes=32 * 1024 * 1024)
    integers = [
        pltpu.SMEM((blocks,), jnp.int32),
        pltpu.SMEM((blocks,), jnp.int32),
    ]

    def pinned(*arrays):
        return [pltpu.with_memory_space_constraint(array, pltpu.HBM) for array in arrays]

    later = (
        order_map, owners, block_local,
        beam_angle.reshape(blocks, CELLS),
        cell_offset.reshape(blocks, CELLS),
        cell_fraction.reshape(blocks, CELLS),
        noise_weight,
    )
    sent, (order_map, owners, places, angles, offsets, fractions, noise) = pl.pallas_call(
        modes_kernel,
        out_shape=[
            jax.ShapeDtypeStruct((beams * sky_devices // 2, 2 * rows, lanes), BF16),
            [pltpu.VMEM(array.shape, array.dtype) for array in later],
        ],
        in_specs=[*hbm(3), hbm(len(later))],
        out_specs=[vmem(1)[0], vmem(len(later))],
        scratch_shapes=[
            pltpu.VMEM(sky_harmonics.shape, F32),
            pltpu.VMEM(beam_harmonics.shape, F32),
            pltpu.VMEM((beams, orders, sky_orders, cycles, width), BF16),
            pltpu.SemaphoreType.DMA((2 + beams + len(later),)),
        ],
        compiler_params=limit,
        name="modes",
    )(*pinned(sky_harmonics, beam_harmonics, wigner), pinned(*later))
    sent = sent.reshape(beams * sky_devices, rows, lanes)
    arrived = lax.all_to_all(sent, ("beam", "ma"), split_axis=0, concat_axis=0, tiled=True)

    samples = pltpu.VMEM((blocks, CELLS), F32)
    piece = (orders + 1, sky_orders, cycles, width)
    phi, turn, own, pieces = pl.pallas_call(
        functools.partial(tables_kernel, blocks_local, sky_devices),
        out_shape=[
            pltpu.VMEM((blocks * parts, CELLS), BF16),
            pltpu.VMEM((blocks * total, CELLS), BF16),
            pltpu.VMEM((blocks * orders, CELLS), BF16),
            [pltpu.HBM(piece, BF16)] * beams,
        ],
        in_specs=vmem(6) + hbm(2),
        out_specs=[*vmem(3), hbm(beams)],
        scratch_shapes=[
            pltpu.VMEM((beams, *piece), BF16),
            pltpu.VMEM(beam_harmonics.shape, F32),
            pltpu.SemaphoreType.DMA((2 * beams,)),
            pltpu.SMEM((all_sky,), jnp.int32),
            *integers,
            pltpu.SemaphoreType.DMA((4,)),
            pltpu.VMEM((CYCLE_BLOCKS, all_sky, CELLS), F32),
            pltpu.VMEM((CYCLE_BLOCKS, all_sky, CELLS), F32),
            pltpu.VMEM((8, blocks, CELLS), F32),
        ],
        compiler_params=limit,
        cost_estimate=pl.CostEstimate(flops=100_000_000, bytes_accessed=4_000_000, transcendentals=0),
        name="tables",
    )(
        order_map, owners, places, angles, offsets, fractions,
        *pinned(beam_harmonics, wigner),
    )
    pieces = exchange(pieces, "beam")

    grads = pl.pallas_call(
        functools.partial(samples_kernel, blocks_local, rows),
        out_shape=jax.ShapeDtypeStruct((beams, parts, lanes), BF16),
        in_specs=vmem(8),
        out_specs=vmem(1)[0],
        scratch_shapes=[
            *integers,
            pltpu.SemaphoreType.DMA((2,)),
            pltpu.VMEM((beams * parts, lanes), F32),
            pltpu.VMEM((beams, together * parts, lanes), F32),
            pltpu.VMEM((beams * lanes, together * parts), F32),
            pltpu.VMEM((cycles, together, total, together * parts), BF16),
            pltpu.VMEM((blocks * 8, CELLS), F32),
            samples,
            [pltpu.VMEM((lanes, together * parts), F32) for _ in range(together)],
            pltpu.VMEM((lanes, together * parts), F32),
            pltpu.VMEM((parts, lanes), F32),
        ],
        compiler_params=limit,
        cost_estimate=pl.CostEstimate(flops=40_000_000_000, bytes_accessed=100_000_000, transcendentals=0),
        name="samples",
    )(
        owners, places, jnp.broadcast_to(sample_count[None, :], (8, CELLS)), noise,
        arrived.reshape(beams * parts, lanes), phi, turn, own,
    )
    grads = grads.reshape(beams * sky_devices, rows, lanes)
    grads = lax.all_to_all(grads, ("beam", "ma"), split_axis=0, concat_axis=0, tiled=True)
    return pl.pallas_call(
        gradient_kernel,
        out_shape=jax.ShapeDtypeStruct((sky_orders, 2, width), F32),
        in_specs=[vmem(1)[0], vmem(beams)],
        out_specs=vmem(1)[0],
        scratch_shapes=[pltpu.VMEM((beams, rows, lanes), F32)],
        compiler_params=limit,
        name="gradient",
    )(grads.reshape(beams, parts, lanes), pieces)


def solution(mesh):
    return jax.shard_map(
        local,
        mesh=mesh,
        in_specs=(
            P("ma", None, None),
            P("beam", None, None),
            P("beam", "ma", None, None),
            P(),
            P("ma", None),
            P("ma"),
            P("ma"),
            P("ma"),
            P("ma"),
            P("ma"),
            P(),
        ),
        out_specs=P("ma", None, "beam"),
        check_vma=False,
    )
```

```python
import functools
import math

import jax
import jax.numpy as jnp
from jax import lax
from jax.experimental import pallas as pl
from jax.experimental.pallas import tpu as pltpu
from jax.sharding import PartitionSpec as P

PHI = 4096
CELLS = 128
CYCLE_BLOCKS = PHI // CELLS
F32 = jnp.float32
BF16 = jnp.bfloat16
LAST_LAST = (((1,), (1,)), ((), ()))


def iota(shape, axis):
    return lax.broadcasted_iota(jnp.int32, shape, axis)


def vmem(count):
    return [pl.BlockSpec(memory_space=pltpu.VMEM)] * count


def smem(count):
    return [pl.BlockSpec(memory_space=pltpu.SMEM)] * count


def hbm(count):
    return [pl.BlockSpec(memory_space=pltpu.HBM)] * count


def sine_turns(z):
    square = z * z
    value = 39.53670603 * square - 76.54978229
    value = value * square + 81.60100407
    value = value * square - 41.34165503
    value = value * square + 6.28318516
    return value * z


def cosine_steps(steps):
    centred = ((steps + PHI // 2) & (PHI - 1)) - PHI // 2
    return sine_turns(0.25 - jnp.abs(centred).astype(F32) * (1.0 / PHI))


def every(ref, first, count, step):
    if ref.shape[1] == CELLS:
        return ref[pl.ds(first, count, stride=step), :]
    return jnp.concatenate([ref[first + i * step][None] for i in range(count)], axis=0)


def put_every(ref, first, step, values):
    if ref.shape[1] == CELLS:
        ref[pl.ds(first, values.shape[0], stride=step), :] = values
    else:
        for i in range(values.shape[0]):
            ref[first + i * step, :] = values[i]


def bring(sources, places, semaphores, first):
    copies = [
        pltpu.make_async_copy(source, place, semaphores.at[first + i])
        for i, (source, place) in enumerate(zip(sources, places))
    ]
    for copy in copies:
        copy.start()
    return copies


def own_block(orders, cycles):
    shape = (orders, orders * cycles)
    return iota(shape, 1) // cycles == iota(shape, 0)


def modes_kernel(sky_hbm, beam_hbm, wigner_hbm, later_hbm, out, later, sky, beam, wigner, arrivals):
    chunks, orders, sky_orders, cycles, width = wigner.shape
    small = bring((sky_hbm, beam_hbm), (sky, beam), arrivals, 0)
    spans = [pl.ds(i * width, width) for i in range(chunks)]
    large = bring([wigner_hbm.at[:, :, :, span] for span in spans], [wigner.at[i] for i in range(chunks)], arrivals, 2)
    places = [
        place if place.shape == source.shape else place.at[0 : source.shape[0]]
        for source, place in zip(later_hbm, later)
    ]
    others = bring(later_hbm, places, arrivals, 2 + chunks)
    for copy in small:
        copy.wait()
    beam_real, beam_imag = beam[:, 0, :], beam[:, 1, :]
    diagonal = own_block(orders, cycles)
    products = []
    for m in range(sky_orders):
        sky_real, sky_imag = sky[m, 0:1, :], sky[m, 1:2, :]
        first = sky_real * beam_real - sky_imag * beam_imag
        second = sky_real * beam_imag + sky_imag * beam_real
        products.append(jnp.concatenate([first, second], axis=0).astype(BF16))
    sums = [0.0] * sky_orders
    for i in range(chunks):
        large[i].wait()
        for m in range(sky_orders):
            table = wigner[i, :, m].reshape(orders * cycles, width)
            left = products[m][:, i * width : (i + 1) * width]
            sums[m] += lax.dot_general(table, left, LAST_LAST, preferred_element_type=F32)
    rows = [None] * (2 * sky_orders)
    for m in range(sky_orders):
        modes = sums[m].T
        for c in range(2):
            part = jnp.where(diagonal, modes[c * orders : (c + 1) * orders], 0.0)
            rows[c * sky_orders + m] = jnp.sum(part, axis=0, keepdims=True)
    block = jnp.concatenate(rows + rows, axis=0).astype(BF16)
    for d in range(out.shape[0]):
        out[d] = block
    for copy in others:
        copy.wait()


def tables_kernel(
    blocks_local, sky_devices,
    order_vmem, owners_vmem, locals_vmem, angles, offsets, fractions, beam_hbm, wigner_hbm,
    phi, turn, own, pieces_hbm, pieces, beam, departures, order_map, owners, locals_, arrivals,
    step_real, step_imag, powers,
):
    copies = bring((order_vmem, owners_vmem, locals_vmem), (order_map, owners, locals_), arrivals, 0)
    me = lax.axis_index("beam")
    extra = bring((beam_hbm,), (beam,), arrivals, 3)[0]
    beams, beam_orders, width = pieces.shape[0], beam.shape[0], pieces.shape[4]
    spans = [pl.ds(pl.multiple_of((me ^ j) * width, width), width) for j in range(beams)]
    arriving = bring(
        [wigner_hbm.at[:, :, :, span] for span in spans],
        [pieces.at[j, 0:beam_orders] for j in range(beams)],
        departures, 0,
    )
    orders = order_map.shape[0]
    blocks = angles.shape[0]
    half = turn.shape[0] // blocks // 2
    own_half = own.shape[0] // blocks // 2

    part = angles[...] * (0.5 / math.pi)
    part = part - jnp.round(part)
    folded = jnp.where(part > 0.25, 0.5 - part, jnp.where(part < -0.25, -0.5 - part, part))
    real, imag = sine_turns(0.25 - jnp.abs(part)), sine_turns(folded)
    for i in range(4):
        if i:
            real, imag = real * real - imag * imag, 2.0 * real * imag
        powers[2 * i, 0:blocks], powers[2 * i + 1, 0:blocks] = real, imag

    copies[0].wait()
    order = jnp.zeros((orders, CELLS), jnp.int32)
    row = iota((orders, CELLS), 0)
    lane = iota((orders, CELLS), 1)
    for m in range(orders):
        place = m % (orders // sky_devices) * sky_devices + m // (orders // sky_devices)
        order = jnp.where(row == place, order_map[m], order)

    def phase(steps):
        return cosine_steps(steps), cosine_steps(steps + PHI // 4)

    scaling = 1.0 / math.sqrt(orders)
    cell_real, cell_imag = phase(order * lane)
    cell_real, cell_imag = cell_real * scaling, cell_imag * scaling
    next_real, next_imag = phase(order)
    next_real = next_real - 1.0
    first_real, first_imag = phase(((order * CELLS) & (PHI - 1)) * lane)
    for j in range(CYCLE_BLOCKS):
        step_real[j] = jnp.broadcast_to(first_real[:, j : j + 1], (orders, CELLS))
        step_imag[j] = jnp.broadcast_to(first_imag[:, j : j + 1], (orders, CELLS))
    for copy in copies[1:]:
        copy.wait()

    def block_phases(s):
        place = (owners[s] * blocks_local + locals_[s]) & (CYCLE_BLOCKS - 1)
        offset = offsets[pl.ds(s, orders, stride=0), :]
        fraction = fractions[pl.ds(s, orders, stride=0), :]
        real = jnp.take_along_axis(cell_real, offset, axis=1, mode="promise_in_bounds")
        imag = jnp.take_along_axis(cell_imag, offset, axis=1, mode="promise_in_bounds")
        base_real, base_imag = step_real[place], step_imag[place]
        left_real = real * base_real - imag * base_imag
        left_imag = real * base_imag + imag * base_real
        mix_real = 1.0 + fraction * next_real
        mix_imag = fraction * next_imag
        both = jnp.concatenate(
            [left_real * mix_real - left_imag * mix_imag, left_real * mix_imag + left_imag * mix_real],
            axis=0,
        )
        start = pl.multiple_of(s * 2 * orders, 2 * orders)
        phi[pl.ds(start, 2 * orders), :] = both.astype(BF16)

    scale = 1.0 / math.sqrt(2 * half)
    power = iota((8, CELLS), 0)

    def block_turns(s):
        steps = [powers[i, pl.ds(s, 8, stride=0), :] for i in range(8)]
        one_real, one_imag = steps[:2]
        step = steps[6:]
        odd = power & 1 == 1
        real, imag = jnp.where(odd, one_real * scale, scale), jnp.where(odd, one_imag * scale, 0.0)
        for bit in (2, 4):
            taken = power & bit == bit
            by_real, by_imag = jnp.where(taken, steps[bit], 1.0), jnp.where(taken, steps[bit + 1], 0.0)
            real, imag = real * by_real - imag * by_imag, real * by_imag + imag * by_real
        evens, odds = [], []
        for j in range(half // 8):
            if j:
                real, imag = real * step[0] - imag * step[1], real * step[1] + imag * step[0]
            evens.append(real)
            odds.append(real * one_imag + imag * one_real)
        return evens + odds

    extra.wait()
    sky_orders, cycles = pieces.shape[2:4]
    for j, span in enumerate(spans):
        terms = []
        for c in range(2):
            values = beam[:, c, span]
            high = values.astype(BF16)
            terms += [high, (values - high.astype(F32)).astype(BF16)]
        filling = sky_orders * cycles - 4 * beam_orders
        if filling:
            terms.append(jnp.zeros((filling, width), BF16))
        pieces[j, beam_orders] = jnp.concatenate(terms, axis=0).reshape(sky_orders, cycles, width)
    some = max(2, CELLS // (2 * half))
    shape = (some * 2 * own_half, some * 2 * half)
    own_row, turn_row = iota(shape, 0), iota(shape, 1)
    kept = own_row % (2 * own_half)
    source = kept // own_half * half + me * own_half + kept % own_half
    chosen = turn_row == own_row // (2 * own_half) * (2 * half) + source
    chosen = jnp.where(chosen, 1.0, 0.0).astype(BF16)
    run = 16

    def one_run(group):
        for j in range(0, run, some):
            first = group * run + j
            rows = []
            for i in range(some):
                block_phases(first + i)
                rows += block_turns(first + i)
            rows = jnp.concatenate(rows, axis=0).astype(BF16)
            turn[pl.ds(pl.multiple_of(first * 2 * half, shape[1]), shape[1]), :] = rows
            mine = jnp.dot(chosen, rows, preferred_element_type=F32)
            own[pl.ds(pl.multiple_of(first * 2 * own_half, shape[0]), shape[0]), :] = mine.astype(BF16)

    runs = blocks // run
    early = max(1, runs // 4)
    pl.loop(0, early)(one_run)
    for copy in arriving:
        copy.wait()
    leaving = bring([pieces.at[j] for j in range(beams)], pieces_hbm, departures, beams)
    pl.loop(early, runs)(one_run)
    for copy in leaving:
        copy.wait()


def samples_kernel(
    blocks_local, rows, owners_vmem, locals_vmem, count, noise, arrived, phi, turn, own,
    out, owners, locals_, arrivals, widened,
    stacked, modes_rows, modes, partial, filtered, totals, ordered, shares,
):
    copies = bring((owners_vmem, locals_vmem), (owners, locals_), arrivals, 0)
    widened[...] = arrived[...].astype(F32)
    lanes = shares.shape[1]
    parts = shares.shape[0]
    beams = arrived.shape[0] // parts
    sky_devices = parts // rows
    blocks = partial.shape[0] // 8
    total = turn.shape[0] // blocks
    orders = total // beams
    cycles = lanes // orders
    together = len(totals)
    unroll = 32

    steps = max(1, blocks // (together * unroll))

    def cycle_of(s):
        return (owners[s] * blocks_local + locals_[s]) // CYCLE_BLOCKS

    width = together * parts
    for b in range(beams):
        for row in range(rows):
            some = every(widened, b * parts + row, sky_devices, rows)
            for j in range(together):
                start = j * parts + row * sky_devices
                stacked[b, start : start + sky_devices, :] = some
        modes_rows[b * lanes : (b + 1) * lanes, :] = stacked[b].T
    lane_group = iota((total, width), 1) // parts
    for r in range(cycles):
        halves = [
            modes_rows[pl.ds(r + parity * cycles, total // 2, stride=2 * cycles), :]
            for parity in range(2)
        ]
        values = jnp.concatenate(halves, axis=0)
        for j in range(together):
            modes[r, j] = jnp.where(lane_group == j, values, 0.0).astype(BF16)
    for copy in copies:
        copy.wait()

    def gather(first):
        left = jnp.concatenate([modes[cycle_of(first + j), j] for j in range(together)], axis=0)
        table = phi[pl.ds(pl.multiple_of(first * parts, width), width), :]
        cells = jnp.dot(left, table, preferred_element_type=F32)
        rotation = turn[pl.ds(pl.multiple_of(first * total, together * total), together * total), :]
        turned = (cells * rotation.astype(F32)).reshape(together, total // 8, 8, CELLS)
        kept = jnp.sum(turned, axis=1).reshape(together * 8, CELLS)
        partial[pl.ds(pl.multiple_of(first * 8, together * 8), together * 8), :] = kept

    @pl.loop(0, steps)
    def _(step):
        for i in range(unroll):
            gather((step * unroll + i) * together)

    signal = partial[pl.ds(0, blocks, stride=8), :]
    for i in range(1, 8):
        signal = signal + partial[pl.ds(i, blocks, stride=8), :]
    valid = iota((blocks, CELLS), 0) * CELLS + iota((blocks, CELLS), 1) < count[0:1, :]
    signal = jnp.where(valid, signal, 0.0)
    clean = lax.dot_general(
        signal.astype(BF16), noise[...].astype(BF16), LAST_LAST, preferred_element_type=F32
    )
    filtered[0:blocks] = jnp.where(valid, clean, 0.0)

    for one in totals:
        one[...] = jnp.zeros_like(one)
    half = orders // 2

    def spread(first):
        rotation = own[pl.ds(pl.multiple_of(first * orders, 16), together * orders), :].astype(F32)
        weighted = [
            rotation[j * orders : (j + 1) * orders] * filtered[pl.ds(first + j, orders, stride=0), :]
            for j in range(together)
        ]
        weighted = jnp.concatenate(weighted, axis=0).astype(BF16)
        table = phi[pl.ds(pl.multiple_of(first * parts, width), width), :]
        terms = lax.dot_general(weighted, table, LAST_LAST, preferred_element_type=F32)
        for j in range(together):
            row = pl.multiple_of(cycle_of(first + j) * orders, orders)
            here = totals[j]
            here[pl.ds(row, orders), :] += terms[j * orders : (j + 1) * orders]

    @pl.loop(0, steps)
    def _(step):
        for i in range(unroll):
            spread((step * unroll + i) * together)

    gathered = totals[0][...]
    which = iota(gathered.shape, 1) // parts
    for j in range(1, together):
        gathered = jnp.where(which == j, totals[j][...], gathered)
    totals[0][...] = gathered
    for k in range(orders):
        place = k // 2 + (k % 2) * half
        ordered[k * cycles : (k + 1) * cycles, :] = totals[0][pl.ds(place, cycles, stride=orders), :]
    turned = ordered[...].T
    summed = turned[0:parts]
    for j in range(1, together):
        summed = summed + turned[j * parts : (j + 1) * parts]
    for row in range(rows):
        put_every(shares, row, rows, summed[row * sky_devices : (row + 1) * sky_devices])
    block = shares[...].astype(BF16)
    for b in range(beams):
        out[b] = block


def gradient_kernel(arrived, pieces, out, modes):
    me = lax.axis_index("beam")
    parts, sky_orders, cycles, width = pieces[0].shape
    orders = parts - 1
    diagonal = own_block(orders, cycles)
    for b in range(len(pieces)):
        terms = arrived[b].astype(F32)
        while terms.shape[0] > 2 * sky_orders:
            middle = terms.shape[0] // 2
            terms = terms[:middle] + terms[middle:]
        modes[b] = terms.astype(BF16).astype(F32)
    first, second = [0.0] * sky_orders, [0.0] * sky_orders
    for j, piece in enumerate(pieces):
        terms = piece[orders].reshape(sky_orders * cycles, width).astype(F32)
        beam_real, beam_imag = [
            terms[2 * c * orders : (2 * c + 1) * orders] + terms[(2 * c + 1) * orders : (2 * c + 2) * orders]
            for c in range(2)
        ]
        these = modes[me ^ j]
        for m in range(sky_orders):
            spreads = []
            for c in range(2):
                row = these[c * sky_orders + m : c * sky_orders + m + 1]
                spreads.append(jnp.where(diagonal, row, 0.0))
            left = jnp.concatenate(spreads, axis=0).astype(BF16)
            table = piece[0:orders, m].reshape(orders * cycles, width)
            harmonics = jnp.dot(left, table, preferred_element_type=F32)
            real, imag = harmonics[:orders], harmonics[orders:]
            first[m] += real * beam_real + imag * beam_imag
            second[m] += imag * beam_real - real * beam_imag
    for m in range(sky_orders):
        out[m, 0:1, :] = jnp.sum(first[m], axis=0, keepdims=True)
        out[m, 1:2, :] = jnp.sum(second[m], axis=0, keepdims=True)


def exchange(pieces, axis):
    count = lax.axis_size(axis)
    return [pieces[0]] + [
        lax.ppermute(pieces[j], axis, [(i, i ^ j) for i in range(count)]) for j in range(1, count)
    ]


def local(
    sky_harmonics,
    beam_harmonics,
    wigner,
    order_map,
    block_owner,
    block_local,
    cell_offset,
    cell_fraction,
    beam_angle,
    sample_count,
    noise_weight,
):
    beams, sky_devices = lax.axis_size("beam"), lax.axis_size("ma")
    orders, sky_orders, cycles, degrees = wigner.shape
    total = orders * beams
    all_sky = sky_orders * sky_devices
    parts = 2 * all_sky
    blocks = block_local.shape[0]
    blocks_local = cycles // sky_devices * CYCLE_BLOCKS
    width = degrees // beams
    lanes = orders * cycles
    rows = 2 * sky_orders
    together = max(1, CELLS // parts)
    owners = block_owner.reshape(blocks)
    limit = pltpu.CompilerParams(vmem_limit_bytes=32 * 1024 * 1024)
    integers = [
        pltpu.SMEM((blocks,), jnp.int32),
        pltpu.SMEM((blocks,), jnp.int32),
    ]

    def pinned(*arrays):
        return [pltpu.with_memory_space_constraint(array, pltpu.HBM) for array in arrays]

    later = (
        order_map, owners, block_local,
        beam_angle.reshape(blocks, CELLS),
        cell_offset.reshape(blocks, CELLS),
        cell_fraction.reshape(blocks, CELLS),
        noise_weight,
    )
    sent, (order_map, owners, places, angles, offsets, fractions, noise) = pl.pallas_call(
        modes_kernel,
        out_shape=[
            jax.ShapeDtypeStruct((beams * sky_devices // 2, 2 * rows, lanes), BF16),
            [
                pltpu.VMEM((blocks + all_sky, CELLS) if place in (4, 5) else array.shape, array.dtype)
                for place, array in enumerate(later)
            ],
        ],
        in_specs=[*hbm(3), hbm(len(later))],
        out_specs=[vmem(1)[0], vmem(len(later))],
        scratch_shapes=[
            pltpu.VMEM(sky_harmonics.shape, F32),
            pltpu.VMEM(beam_harmonics.shape, F32),
            pltpu.VMEM((beams, orders, sky_orders, cycles, width), BF16),
            pltpu.SemaphoreType.DMA((2 + beams + len(later),)),
        ],
        compiler_params=limit,
        name="modes",
    )(*pinned(sky_harmonics, beam_harmonics, wigner), pinned(*later))
    sent = sent.reshape(beams * sky_devices, rows, lanes)
    arrived = lax.all_to_all(sent, ("beam", "ma"), split_axis=0, concat_axis=0, tiled=True)

    samples = pltpu.VMEM((blocks, CELLS), F32)
    piece = (orders + 1, sky_orders, cycles, width)
    phi, turn, own, pieces = pl.pallas_call(
        functools.partial(tables_kernel, blocks_local, sky_devices),
        out_shape=[
            pltpu.VMEM((blocks * parts, CELLS), BF16),
            pltpu.VMEM((blocks * total, CELLS), BF16),
            pltpu.VMEM((blocks * orders, CELLS), BF16),
            [pltpu.HBM(piece, BF16)] * beams,
        ],
        in_specs=vmem(6) + hbm(2),
        out_specs=[*vmem(3), hbm(beams)],
        scratch_shapes=[
            pltpu.VMEM((beams, *piece), BF16),
            pltpu.VMEM(beam_harmonics.shape, F32),
            pltpu.SemaphoreType.DMA((2 * beams,)),
            pltpu.SMEM((all_sky,), jnp.int32),
            *integers,
            pltpu.SemaphoreType.DMA((4,)),
            pltpu.VMEM((CYCLE_BLOCKS, all_sky, CELLS), F32),
            pltpu.VMEM((CYCLE_BLOCKS, all_sky, CELLS), F32),
            pltpu.VMEM((8, blocks + 8, CELLS), F32),
        ],
        compiler_params=limit,
        cost_estimate=pl.CostEstimate(flops=100_000_000, bytes_accessed=4_000_000, transcendentals=0),
        name="tables",
    )(
        order_map, owners, places, angles, offsets, fractions,
        *pinned(beam_harmonics, wigner),
    )
    pieces = exchange(pieces, "beam")

    grads = pl.pallas_call(
        functools.partial(samples_kernel, blocks_local, rows),
        out_shape=jax.ShapeDtypeStruct((beams, parts, lanes), BF16),
        in_specs=vmem(8),
        out_specs=vmem(1)[0],
        scratch_shapes=[
            *integers,
            pltpu.SemaphoreType.DMA((2,)),
            pltpu.VMEM((beams * parts, lanes), F32),
            pltpu.VMEM((beams, together * parts, lanes), F32),
            pltpu.VMEM((beams * lanes, together * parts), F32),
            pltpu.VMEM((cycles, together, total, together * parts), BF16),
            pltpu.VMEM((blocks * 8, CELLS), F32),
            pltpu.VMEM((blocks + orders, CELLS), F32),
            [pltpu.VMEM((lanes, together * parts), F32) for _ in range(together)],
            pltpu.VMEM((lanes, together * parts), F32),
            pltpu.VMEM((parts, lanes), F32),
        ],
        compiler_params=limit,
        cost_estimate=pl.CostEstimate(flops=40_000_000_000, bytes_accessed=100_000_000, transcendentals=0),
        name="samples",
    )(
        owners, places, jnp.broadcast_to(sample_count[None, :], (8, CELLS)), noise,
        arrived.reshape(beams * parts, lanes), phi, turn, own,
    )
    grads = grads.reshape(beams * sky_devices, rows, lanes)
    grads = lax.all_to_all(grads, ("beam", "ma"), split_axis=0, concat_axis=0, tiled=True)
    return pl.pallas_call(
        gradient_kernel,
        out_shape=jax.ShapeDtypeStruct((sky_orders, 2, width), F32),
        in_specs=[vmem(1)[0], vmem(beams)],
        out_specs=vmem(1)[0],
        scratch_shapes=[pltpu.VMEM((beams, rows, lanes), F32)],
        compiler_params=limit,
        name="gradient",
    )(grads.reshape(beams, parts, lanes), pieces)


def solution(mesh):
    return jax.shard_map(
        local,
        mesh=mesh,
        in_specs=(
            P("ma", None, None),
            P("beam", None, None),
            P("beam", "ma", None, None),
            P(),
            P("ma", None),
            P("ma"),
            P("ma"),
            P("ma"),
            P("ma"),
            P("ma"),
            P(),
        ),
        out_specs=P("ma", None, "beam"),
        check_vma=False,
    )
```

```python
import functools
import math

import jax
import jax.numpy as jnp
from jax import lax
from jax.experimental import pallas as pl
from jax.experimental.pallas import tpu as pltpu
from jax.sharding import PartitionSpec as P

PHI = 4096
CELLS = 128
CYCLE_BLOCKS = PHI // CELLS
F32 = jnp.float32
BF16 = jnp.bfloat16
LAST_LAST = (((1,), (1,)), ((), ()))


def iota(shape, axis):
    return lax.broadcasted_iota(jnp.int32, shape, axis)


def vmem(count):
    return [pl.BlockSpec(memory_space=pltpu.VMEM)] * count


def smem(count):
    return [pl.BlockSpec(memory_space=pltpu.SMEM)] * count


def hbm(count):
    return [pl.BlockSpec(memory_space=pltpu.HBM)] * count


def sine_turns(z):
    square = z * z
    value = 39.53670603 * square - 76.54978229
    value = value * square + 81.60100407
    value = value * square - 41.34165503
    value = value * square + 6.28318516
    return value * z


def cosine_steps(steps):
    centred = ((steps + PHI // 2) & (PHI - 1)) - PHI // 2
    return sine_turns(0.25 - jnp.abs(centred).astype(F32) * (1.0 / PHI))


def every(ref, first, count, step):
    if ref.shape[1] == CELLS:
        return ref[pl.ds(first, count, stride=step), :]
    return jnp.concatenate([ref[first + i * step][None] for i in range(count)], axis=0)


def put_every(ref, first, step, values):
    if ref.shape[1] == CELLS:
        ref[pl.ds(first, values.shape[0], stride=step), :] = values
    else:
        for i in range(values.shape[0]):
            ref[first + i * step, :] = values[i]


def bring(sources, places, semaphores, first):
    copies = [
        pltpu.make_async_copy(source, place, semaphores.at[first + i])
        for i, (source, place) in enumerate(zip(sources, places))
    ]
    for copy in copies:
        copy.start()
    return copies


def own_block(orders, cycles):
    shape = (orders, orders * cycles)
    return iota(shape, 1) // cycles == iota(shape, 0)


def modes_kernel(sky_hbm, beam_hbm, wigner_hbm, later_hbm, out, later, sky, beam, wigner, arrivals):
    chunks, orders, sky_orders, cycles, width = wigner.shape
    small = bring((sky_hbm, beam_hbm), (sky, beam), arrivals, 0)
    spans = [pl.ds(i * width, width) for i in range(chunks)]
    large = bring([wigner_hbm.at[:, :, :, span] for span in spans], [wigner.at[i] for i in range(chunks)], arrivals, 2)
    places = [
        place if place.shape == source.shape else place.at[0 : source.shape[0]]
        for source, place in zip(later_hbm, later)
    ]
    others = bring(later_hbm, places, arrivals, 2 + chunks)
    for copy in small:
        copy.wait()
    beam_real, beam_imag = beam[:, 0, :], beam[:, 1, :]
    diagonal = own_block(orders, cycles)
    products = []
    for m in range(sky_orders):
        sky_real, sky_imag = sky[m, 0:1, :], sky[m, 1:2, :]
        first = sky_real * beam_real - sky_imag * beam_imag
        second = sky_real * beam_imag + sky_imag * beam_real
        products.append(jnp.concatenate([first, second], axis=0).astype(BF16))
    sums = [0.0] * sky_orders
    for i in range(chunks):
        large[i].wait()
        for m in range(sky_orders):
            table = wigner[i, :, m].reshape(orders * cycles, width)
            left = products[m][:, i * width : (i + 1) * width]
            sums[m] += lax.dot_general(table, left, LAST_LAST, preferred_element_type=F32)
    rows = [None] * (2 * sky_orders)
    for m in range(sky_orders):
        modes = sums[m].T
        for c in range(2):
            part = jnp.where(diagonal, modes[c * orders : (c + 1) * orders], 0.0)
            rows[c * sky_orders + m] = jnp.sum(part, axis=0, keepdims=True)
    block = jnp.concatenate(rows + rows, axis=0).astype(BF16)
    for d in range(out.shape[0]):
        out[d] = block
    for copy in others:
        copy.wait()


def tables_kernel(
    blocks_local, sky_devices,
    order_vmem, owners_vmem, locals_vmem, angles, offsets, fractions, beam_hbm, wigner_hbm,
    phi, turn, own, pieces_hbm, pieces, beam, departures, order_map, owners, locals_, arrivals,
    step_real, step_imag, powers,
):
    copies = bring((order_vmem, owners_vmem, locals_vmem), (order_map, owners, locals_), arrivals, 0)
    me = lax.axis_index("beam")
    extra = bring((beam_hbm,), (beam,), arrivals, 3)[0]
    beams, beam_orders, width = pieces.shape[0], beam.shape[0], pieces.shape[4]
    spans = [pl.ds(pl.multiple_of((me ^ j) * width, width), width) for j in range(beams)]
    arriving = [
        pltpu.make_async_copy(wigner_hbm.at[:, :, :, span], pieces.at[j, 0:beam_orders], departures.at[j])
        for j, span in enumerate(spans)
    ]
    for j in [*range(1, beams), 0]:
        arriving[j].start()
    orders = order_map.shape[0]
    blocks = angles.shape[0]
    half = turn.shape[0] // blocks // 2
    own_half = own.shape[0] // blocks // 2

    part = angles[...] * (0.5 / math.pi)
    part = part - jnp.round(part)
    folded = jnp.where(part > 0.25, 0.5 - part, jnp.where(part < -0.25, -0.5 - part, part))
    real, imag = sine_turns(0.25 - jnp.abs(part)), sine_turns(folded)
    for i in range(4):
        if i:
            real, imag = real * real - imag * imag, 2.0 * real * imag
        powers[2 * i, 0:blocks], powers[2 * i + 1, 0:blocks] = real, imag

    copies[0].wait()
    order = jnp.zeros((orders, CELLS), jnp.int32)
    row = iota((orders, CELLS), 0)
    lane = iota((orders, CELLS), 1)
    for m in range(orders):
        place = m % (orders // sky_devices) * sky_devices + m // (orders // sky_devices)
        order = jnp.where(row == place, order_map[m], order)

    def phase(steps):
        return cosine_steps(steps), cosine_steps(steps + PHI // 4)

    scaling = 1.0 / math.sqrt(orders)
    cell_real, cell_imag = phase(order * lane)
    cell_real, cell_imag = cell_real * scaling, cell_imag * scaling
    next_real, next_imag = phase(order)
    next_real = next_real - 1.0
    first_real, first_imag = phase(((order * CELLS) & (PHI - 1)) * lane)
    for j in range(CYCLE_BLOCKS):
        step_real[j] = jnp.broadcast_to(first_real[:, j : j + 1], (orders, CELLS))
        step_imag[j] = jnp.broadcast_to(first_imag[:, j : j + 1], (orders, CELLS))
    for copy in copies[1:]:
        copy.wait()

    def block_phases(s):
        place = (owners[s] * blocks_local + locals_[s]) & (CYCLE_BLOCKS - 1)
        offset = offsets[pl.ds(s, orders, stride=0), :]
        fraction = fractions[pl.ds(s, orders, stride=0), :]
        real = jnp.take_along_axis(cell_real, offset, axis=1, mode="promise_in_bounds")
        imag = jnp.take_along_axis(cell_imag, offset, axis=1, mode="promise_in_bounds")
        base_real, base_imag = step_real[place], step_imag[place]
        left_real = real * base_real - imag * base_imag
        left_imag = real * base_imag + imag * base_real
        mix_real = 1.0 + fraction * next_real
        mix_imag = fraction * next_imag
        both = jnp.concatenate(
            [left_real * mix_real - left_imag * mix_imag, left_real * mix_imag + left_imag * mix_real],
            axis=0,
        )
        start = pl.multiple_of(s * 2 * orders, 2 * orders)
        phi[pl.ds(start, 2 * orders), :] = both.astype(BF16)

    scale = 1.0 / math.sqrt(2 * half)
    power = iota((8, CELLS), 0)

    def block_turns(s):
        steps = [powers[i, pl.ds(s, 8, stride=0), :] for i in range(8)]
        one_real, one_imag = steps[:2]
        step = steps[6:]
        odd = power & 1 == 1
        real, imag = jnp.where(odd, one_real * scale, scale), jnp.where(odd, one_imag * scale, 0.0)
        for bit in (2, 4):
            taken = power & bit == bit
            by_real, by_imag = jnp.where(taken, steps[bit], 1.0), jnp.where(taken, steps[bit + 1], 0.0)
            real, imag = real * by_real - imag * by_imag, real * by_imag + imag * by_real
        evens, odds = [], []
        for j in range(half // 8):
            if j:
                real, imag = real * step[0] - imag * step[1], real * step[1] + imag * step[0]
            evens.append(real)
            odds.append(real * one_imag + imag * one_real)
        return evens + odds

    some = max(2, CELLS // (2 * half))
    shape = (some * 2 * own_half, some * 2 * half)
    own_row, turn_row = iota(shape, 0), iota(shape, 1)
    kept = own_row % (2 * own_half)
    source = kept // own_half * half + me * own_half + kept % own_half
    chosen = turn_row == own_row // (2 * own_half) * (2 * half) + source
    chosen = jnp.where(chosen, 1.0, 0.0).astype(BF16)
    run = 16

    def one_run(group):
        for j in range(0, run, some):
            first = group * run + j
            rows = []
            for i in range(some):
                block_phases(first + i)
                rows += block_turns(first + i)
            rows = jnp.concatenate(rows, axis=0).astype(BF16)
            turn[pl.ds(pl.multiple_of(first * 2 * half, shape[1]), shape[1]), :] = rows
            mine = jnp.dot(chosen, rows, preferred_element_type=F32)
            own[pl.ds(pl.multiple_of(first * 2 * own_half, shape[0]), shape[0]), :] = mine.astype(BF16)

    def beam_terms():
        extra.wait()
        sky_orders, cycles = pieces.shape[2:4]
        for j, span in enumerate(spans):
            terms = []
            for c in range(2):
                values = beam[:, c, span]
                high = values.astype(BF16)
                terms += [high, (values - high.astype(F32)).astype(BF16)]
            filling = sky_orders * cycles - 4 * beam_orders
            if filling:
                terms.append(jnp.zeros((filling, width), BF16))
            pieces[j, beam_orders] = jnp.concatenate(terms, axis=0).reshape(sky_orders, cycles, width)

    runs = blocks // run
    turns = [*range(1, beams), 0]

    def leaving(j):
        return pltpu.make_async_copy(pieces.at[j], pieces_hbm[j], departures.at[beams + j])

    @pl.loop(0, runs)
    def _(group):
        one_run(group)
        pl.when(group == 0)(beam_terms)
        for i, j in enumerate(turns):

            @pl.when(group == i * (runs // 2) // beams)
            def _(j=j):
                arriving[j].wait()
                leaving(j).start()

    for j in range(beams):
        leaving(j).wait()


def samples_kernel(
    blocks_local, rows, owners_vmem, locals_vmem, count, noise, arrived, phi, turn, own,
    out, owners, locals_, arrivals, widened,
    stacked, modes_rows, modes, partial, filtered, totals, ordered, shares,
):
    copies = bring((owners_vmem, locals_vmem), (owners, locals_), arrivals, 0)
    widened[...] = arrived[...].astype(F32)
    lanes = shares.shape[1]
    parts = shares.shape[0]
    beams = arrived.shape[0] // parts
    sky_devices = parts // rows
    blocks = partial.shape[0] // 8
    total = turn.shape[0] // blocks
    orders = total // beams
    cycles = lanes // orders
    together = len(totals)
    unroll = 32

    steps = max(1, blocks // (together * unroll))

    def cycle_of(s):
        return (owners[s] * blocks_local + locals_[s]) // CYCLE_BLOCKS

    width = together * parts
    for b in range(beams):
        for row in range(rows):
            some = every(widened, b * parts + row, sky_devices, rows)
            for j in range(together):
                start = j * parts + row * sky_devices
                stacked[b, start : start + sky_devices, :] = some
        modes_rows[b * lanes : (b + 1) * lanes, :] = stacked[b].T
    lane_group = iota((total, width), 1) // parts
    for r in range(cycles):
        halves = [
            modes_rows[pl.ds(r + parity * cycles, total // 2, stride=2 * cycles), :]
            for parity in range(2)
        ]
        values = jnp.concatenate(halves, axis=0)
        for j in range(together):
            modes[r, j] = jnp.where(lane_group == j, values, 0.0).astype(BF16)
    for copy in copies:
        copy.wait()

    def gather(first):
        left = jnp.concatenate([modes[cycle_of(first + j), j] for j in range(together)], axis=0)
        table = phi[pl.ds(pl.multiple_of(first * parts, width), width), :]
        cells = jnp.dot(left, table, preferred_element_type=F32)
        rotation = turn[pl.ds(pl.multiple_of(first * total, together * total), together * total), :]
        turned = (cells * rotation.astype(F32)).reshape(together, total // 8, 8, CELLS)
        kept = jnp.sum(turned, axis=1).reshape(together * 8, CELLS)
        partial[pl.ds(pl.multiple_of(first * 8, together * 8), together * 8), :] = kept

    @pl.loop(0, steps)
    def _(step):
        for i in range(unroll):
            gather((step * unroll + i) * together)

    signal = partial[pl.ds(0, blocks, stride=8), :]
    for i in range(1, 8):
        signal = signal + partial[pl.ds(i, blocks, stride=8), :]
    valid = iota((blocks, CELLS), 0) * CELLS + iota((blocks, CELLS), 1) < count[0:1, :]
    signal = jnp.where(valid, signal, 0.0)
    clean = lax.dot_general(
        signal.astype(BF16), noise[...].astype(BF16), LAST_LAST, preferred_element_type=F32
    )
    filtered[0:blocks] = jnp.where(valid, clean, 0.0)

    for one in totals:
        one[...] = jnp.zeros_like(one)
    half = orders // 2

    def spread(first):
        rotation = own[pl.ds(pl.multiple_of(first * orders, 16), together * orders), :].astype(F32)
        weighted = [
            rotation[j * orders : (j + 1) * orders] * filtered[pl.ds(first + j, orders, stride=0), :]
            for j in range(together)
        ]
        weighted = jnp.concatenate(weighted, axis=0).astype(BF16)
        table = phi[pl.ds(pl.multiple_of(first * parts, width), width), :]
        terms = lax.dot_general(weighted, table, LAST_LAST, preferred_element_type=F32)
        for j in range(together):
            row = pl.multiple_of(cycle_of(first + j) * orders, orders)
            here = totals[j]
            here[pl.ds(row, orders), :] += terms[j * orders : (j + 1) * orders]

    @pl.loop(0, steps)
    def _(step):
        for i in range(unroll):
            spread((step * unroll + i) * together)

    gathered = totals[0][...]
    which = iota(gathered.shape, 1) // parts
    for j in range(1, together):
        gathered = jnp.where(which == j, totals[j][...], gathered)
    totals[0][...] = gathered
    for k in range(orders):
        place = k // 2 + (k % 2) * half
        ordered[k * cycles : (k + 1) * cycles, :] = totals[0][pl.ds(place, cycles, stride=orders), :]
    turned = ordered[...].T
    summed = turned[0:parts]
    for j in range(1, together):
        summed = summed + turned[j * parts : (j + 1) * parts]
    for row in range(rows):
        put_every(shares, row, rows, summed[row * sky_devices : (row + 1) * sky_devices])
    block = shares[...].astype(BF16)
    for b in range(beams):
        out[b] = block


def gradient_kernel(arrived, pieces, out, modes):
    me = lax.axis_index("beam")
    parts, sky_orders, cycles, width = pieces[0].shape
    orders = parts - 1
    diagonal = own_block(orders, cycles)
    for b in range(len(pieces)):
        terms = arrived[b].astype(F32)
        while terms.shape[0] > 2 * sky_orders:
            middle = terms.shape[0] // 2
            terms = terms[:middle] + terms[middle:]
        modes[b] = terms.astype(BF16).astype(F32)
    first, second = [0.0] * sky_orders, [0.0] * sky_orders
    for j, piece in enumerate(pieces):
        terms = piece[orders].reshape(sky_orders * cycles, width).astype(F32)
        beam_real, beam_imag = [
            terms[2 * c * orders : (2 * c + 1) * orders] + terms[(2 * c + 1) * orders : (2 * c + 2) * orders]
            for c in range(2)
        ]
        these = modes[me ^ j]
        for m in range(sky_orders):
            spreads = []
            for c in range(2):
                row = these[c * sky_orders + m : c * sky_orders + m + 1]
                spreads.append(jnp.where(diagonal, row, 0.0))
            left = jnp.concatenate(spreads, axis=0).astype(BF16)
            table = piece[0:orders, m].reshape(orders * cycles, width)
            harmonics = jnp.dot(left, table, preferred_element_type=F32)
            real, imag = harmonics[:orders], harmonics[orders:]
            first[m] += real * beam_real + imag * beam_imag
            second[m] += imag * beam_real - real * beam_imag
    for m in range(sky_orders):
        out[m, 0:1, :] = jnp.sum(first[m], axis=0, keepdims=True)
        out[m, 1:2, :] = jnp.sum(second[m], axis=0, keepdims=True)


def exchange(pieces, axis):
    count = lax.axis_size(axis)
    return [pieces[0]] + [
        lax.ppermute(pieces[j], axis, [(i, i ^ j) for i in range(count)]) for j in range(1, count)
    ]


def local(
    sky_harmonics,
    beam_harmonics,
    wigner,
    order_map,
    block_owner,
    block_local,
    cell_offset,
    cell_fraction,
    beam_angle,
    sample_count,
    noise_weight,
):
    beams, sky_devices = lax.axis_size("beam"), lax.axis_size("ma")
    orders, sky_orders, cycles, degrees = wigner.shape
    total = orders * beams
    all_sky = sky_orders * sky_devices
    parts = 2 * all_sky
    blocks = block_local.shape[0]
    blocks_local = cycles // sky_devices * CYCLE_BLOCKS
    width = degrees // beams
    lanes = orders * cycles
    rows = 2 * sky_orders
    together = max(1, CELLS // parts)
    owners = block_owner.reshape(blocks)
    limit = pltpu.CompilerParams(vmem_limit_bytes=32 * 1024 * 1024)
    integers = [
        pltpu.SMEM((blocks,), jnp.int32),
        pltpu.SMEM((blocks,), jnp.int32),
    ]

    def pinned(*arrays):
        return [pltpu.with_memory_space_constraint(array, pltpu.HBM) for array in arrays]

    later = (
        order_map, owners, block_local,
        beam_angle.reshape(blocks, CELLS),
        cell_offset.reshape(blocks, CELLS),
        cell_fraction.reshape(blocks, CELLS),
        noise_weight,
    )
    sent, (order_map, owners, places, angles, offsets, fractions, noise) = pl.pallas_call(
        modes_kernel,
        out_shape=[
            jax.ShapeDtypeStruct((beams * sky_devices // 2, 2 * rows, lanes), BF16),
            [
                pltpu.VMEM((blocks + all_sky, CELLS) if place in (4, 5) else array.shape, array.dtype)
                for place, array in enumerate(later)
            ],
        ],
        in_specs=[*hbm(3), hbm(len(later))],
        out_specs=[vmem(1)[0], vmem(len(later))],
        scratch_shapes=[
            pltpu.VMEM(sky_harmonics.shape, F32),
            pltpu.VMEM(beam_harmonics.shape, F32),
            pltpu.VMEM((beams, orders, sky_orders, cycles, width), BF16),
            pltpu.SemaphoreType.DMA((2 + beams + len(later),)),
        ],
        compiler_params=limit,
        name="modes",
    )(*pinned(sky_harmonics, beam_harmonics, wigner), pinned(*later))
    sent = sent.reshape(beams * sky_devices, rows, lanes)
    arrived = lax.all_to_all(sent, ("beam", "ma"), split_axis=0, concat_axis=0, tiled=True)

    samples = pltpu.VMEM((blocks, CELLS), F32)
    piece = (orders + 1, sky_orders, cycles, width)
    phi, turn, own, pieces = pl.pallas_call(
        functools.partial(tables_kernel, blocks_local, sky_devices),
        out_shape=[
            pltpu.VMEM((blocks * parts, CELLS), BF16),
            pltpu.VMEM((blocks * total, CELLS), BF16),
            pltpu.VMEM((blocks * orders, CELLS), BF16),
            [pltpu.HBM(piece, BF16)] * beams,
        ],
        in_specs=vmem(6) + hbm(2),
        out_specs=[*vmem(3), hbm(beams)],
        scratch_shapes=[
            pltpu.VMEM((beams, *piece), BF16),
            pltpu.VMEM(beam_harmonics.shape, F32),
            pltpu.SemaphoreType.DMA((2 * beams,)),
            pltpu.SMEM((all_sky,), jnp.int32),
            *integers,
            pltpu.SemaphoreType.DMA((4,)),
            pltpu.VMEM((CYCLE_BLOCKS, all_sky, CELLS), F32),
            pltpu.VMEM((CYCLE_BLOCKS, all_sky, CELLS), F32),
            pltpu.VMEM((8, blocks + 8, CELLS), F32),
        ],
        compiler_params=limit,
        cost_estimate=pl.CostEstimate(flops=100_000_000, bytes_accessed=4_000_000, transcendentals=0),
        name="tables",
    )(
        order_map, owners, places, angles, offsets, fractions,
        *pinned(beam_harmonics, wigner),
    )
    pieces = exchange(pieces, "beam")

    grads = pl.pallas_call(
        functools.partial(samples_kernel, blocks_local, rows),
        out_shape=jax.ShapeDtypeStruct((beams, parts, lanes), BF16),
        in_specs=vmem(8),
        out_specs=vmem(1)[0],
        scratch_shapes=[
            *integers,
            pltpu.SemaphoreType.DMA((2,)),
            pltpu.VMEM((beams * parts, lanes), F32),
            pltpu.VMEM((beams, together * parts, lanes), F32),
            pltpu.VMEM((beams * lanes, together * parts), F32),
            pltpu.VMEM((cycles, together, total, together * parts), BF16),
            pltpu.VMEM((blocks * 8, CELLS), F32),
            pltpu.VMEM((blocks + orders, CELLS), F32),
            [pltpu.VMEM((lanes, together * parts), F32) for _ in range(together)],
            pltpu.VMEM((lanes, together * parts), F32),
            pltpu.VMEM((parts, lanes), F32),
        ],
        compiler_params=limit,
        cost_estimate=pl.CostEstimate(flops=40_000_000_000, bytes_accessed=100_000_000, transcendentals=0),
        name="samples",
    )(
        owners, places, jnp.broadcast_to(sample_count[None, :], (8, CELLS)), noise,
        arrived.reshape(beams * parts, lanes), phi, turn, own,
    )
    grads = grads.reshape(beams * sky_devices, rows, lanes)
    grads = lax.all_to_all(grads, ("beam", "ma"), split_axis=0, concat_axis=0, tiled=True)
    return pl.pallas_call(
        gradient_kernel,
        out_shape=jax.ShapeDtypeStruct((sky_orders, 2, width), F32),
        in_specs=[vmem(1)[0], vmem(beams)],
        out_specs=vmem(1)[0],
        scratch_shapes=[pltpu.VMEM((beams, rows, lanes), F32)],
        compiler_params=limit,
        name="gradient",
    )(grads.reshape(beams, parts, lanes), pieces)


def solution(mesh):
    return jax.shard_map(
        local,
        mesh=mesh,
        in_specs=(
            P("ma", None, None),
            P("beam", None, None),
            P("beam", "ma", None, None),
            P(),
            P("ma", None),
            P("ma"),
            P("ma"),
            P("ma"),
            P("ma"),
            P("ma"),
            P(),
        ),
        out_specs=P("ma", None, "beam"),
        check_vma=False,
    )
```

```python
import functools
import math

import jax
import jax.numpy as jnp
from jax import lax
from jax.experimental import pallas as pl
from jax.experimental.pallas import tpu as pltpu
from jax.sharding import PartitionSpec as P

PHI = 4096
CELLS = 128
CYCLE_BLOCKS = PHI // CELLS
F32 = jnp.float32
BF16 = jnp.bfloat16
LAST_LAST = (((1,), (1,)), ((), ()))


def iota(shape, axis):
    return lax.broadcasted_iota(jnp.int32, shape, axis)


def vmem(count):
    return [pl.BlockSpec(memory_space=pltpu.VMEM)] * count


def smem(count):
    return [pl.BlockSpec(memory_space=pltpu.SMEM)] * count


def hbm(count):
    return [pl.BlockSpec(memory_space=pltpu.HBM)] * count


def sine_turns(z):
    square = z * z
    value = 39.53670603 * square - 76.54978229
    value = value * square + 81.60100407
    value = value * square - 41.34165503
    value = value * square + 6.28318516
    return value * z


def cosine_steps(steps):
    centred = ((steps + PHI // 2) & (PHI - 1)) - PHI // 2
    return sine_turns(0.25 - jnp.abs(centred).astype(F32) * (1.0 / PHI))


def every(ref, first, count, step):
    if ref.shape[1] == CELLS:
        return ref[pl.ds(first, count, stride=step), :]
    return jnp.concatenate([ref[first + i * step][None] for i in range(count)], axis=0)


def put_every(ref, first, step, values):
    if ref.shape[1] == CELLS:
        ref[pl.ds(first, values.shape[0], stride=step), :] = values
    else:
        for i in range(values.shape[0]):
            ref[first + i * step, :] = values[i]


def bring(sources, places, semaphores, first):
    copies = [
        pltpu.make_async_copy(source, place, semaphores.at[first + i])
        for i, (source, place) in enumerate(zip(sources, places))
    ]
    for copy in copies:
        copy.start()
    return copies


def own_block(orders, cycles):
    shape = (orders, orders * cycles)
    return iota(shape, 1) // cycles == iota(shape, 0)


def modes_kernel(sky_hbm, beam_hbm, wigner_hbm, later_hbm, out, later, sky, beam, wigner, arrivals):
    chunks, orders, sky_orders, cycles, width = wigner.shape
    small = bring((sky_hbm, beam_hbm), (sky, beam), arrivals, 0)
    spans = [pl.ds(i * width, width) for i in range(chunks)]
    large = bring([wigner_hbm.at[:, :, :, span] for span in spans], [wigner.at[i] for i in range(chunks)], arrivals, 2)
    places = [
        place if place.shape == source.shape else place.at[0 : source.shape[0]]
        for source, place in zip(later_hbm, later)
    ]
    others = bring(later_hbm, places, arrivals, 2 + chunks)
    for copy in small:
        copy.wait()
    beam_real, beam_imag = beam[:, 0, :], beam[:, 1, :]
    diagonal = own_block(orders, cycles)
    products = []
    for m in range(sky_orders):
        sky_real, sky_imag = sky[m, 0:1, :], sky[m, 1:2, :]
        first = sky_real * beam_real - sky_imag * beam_imag
        second = sky_real * beam_imag + sky_imag * beam_real
        products.append(jnp.concatenate([first, second], axis=0).astype(BF16))
    sums = [0.0] * sky_orders
    for i in range(chunks):
        large[i].wait()
        for m in range(sky_orders):
            table = wigner[i, :, m].reshape(orders * cycles, width)
            left = products[m][:, i * width : (i + 1) * width]
            sums[m] += lax.dot_general(table, left, LAST_LAST, preferred_element_type=F32)
    rows = [None] * (2 * sky_orders)
    for m in range(sky_orders):
        modes = sums[m].T
        for c in range(2):
            part = jnp.where(diagonal, modes[c * orders : (c + 1) * orders], 0.0)
            rows[c * sky_orders + m] = jnp.sum(part, axis=0, keepdims=True)
    block = jnp.concatenate(rows + rows, axis=0).astype(BF16)
    for d in range(out.shape[0]):
        out[d] = block
    for copy in others:
        copy.wait()


def tables_kernel(
    blocks_local, sky_devices,
    order_vmem, owners_vmem, locals_vmem, angles, offsets, fractions, beam_hbm, wigner_hbm,
    phi, turn, own, pieces_hbm, pieces, beam, departures, order_map, owners, locals_, arrivals,
    step_real, step_imag, powers,
):
    copies = bring((order_vmem, owners_vmem, locals_vmem), (order_map, owners, locals_), arrivals, 0)
    me = lax.axis_index("beam")
    extra = bring((beam_hbm,), (beam,), arrivals, 3)[0]
    beams, beam_orders, width = pieces.shape[0], beam.shape[0], pieces.shape[4]
    spans = [pl.ds(pl.multiple_of((me ^ j) * width, width), width) for j in range(beams)]
    arriving = [
        pltpu.make_async_copy(wigner_hbm.at[:, :, :, span], pieces.at[j, 0:beam_orders], departures.at[j])
        for j, span in enumerate(spans)
    ]
    for j in [*range(1, beams), 0]:
        arriving[j].start()
    orders = order_map.shape[0]
    blocks = angles.shape[0]
    half = turn.shape[0] // blocks // 2
    own_half = own.shape[0] // blocks // 2

    part = angles[...] * (0.5 / math.pi)
    part = part - jnp.round(part)
    folded = jnp.where(part > 0.25, 0.5 - part, jnp.where(part < -0.25, -0.5 - part, part))
    real, imag = sine_turns(0.25 - jnp.abs(part)), sine_turns(folded)
    for i in range(4):
        if i:
            real, imag = real * real - imag * imag, 2.0 * real * imag
        powers[2 * i, 0:blocks], powers[2 * i + 1, 0:blocks] = real, imag

    copies[0].wait()
    order = jnp.zeros((orders, CELLS), jnp.int32)
    row = iota((orders, CELLS), 0)
    lane = iota((orders, CELLS), 1)
    for m in range(orders):
        place = m % (orders // sky_devices) * sky_devices + m // (orders // sky_devices)
        order = jnp.where(row == place, order_map[m], order)

    def phase(steps):
        return cosine_steps(steps), cosine_steps(steps + PHI // 4)

    scaling = 1.0 / math.sqrt(orders)
    cell_real, cell_imag = phase(order * lane)
    cell_real, cell_imag = cell_real * scaling, cell_imag * scaling
    next_real, next_imag = phase(order)
    next_real = next_real - 1.0
    first_real, first_imag = phase(((order * CELLS) & (PHI - 1)) * lane)
    for j in range(CYCLE_BLOCKS):
        step_real[j] = jnp.broadcast_to(first_real[:, j : j + 1], (orders, CELLS))
        step_imag[j] = jnp.broadcast_to(first_imag[:, j : j + 1], (orders, CELLS))
    for copy in copies[1:]:
        copy.wait()

    def block_phases(s):
        place = (owners[s] * blocks_local + locals_[s]) & (CYCLE_BLOCKS - 1)
        offset = offsets[pl.ds(s, orders, stride=0), :]
        fraction = fractions[pl.ds(s, orders, stride=0), :]
        real = jnp.take_along_axis(cell_real, offset, axis=1, mode="promise_in_bounds")
        imag = jnp.take_along_axis(cell_imag, offset, axis=1, mode="promise_in_bounds")
        base_real, base_imag = step_real[place], step_imag[place]
        left_real = real * base_real - imag * base_imag
        left_imag = real * base_imag + imag * base_real
        mix_real = 1.0 + fraction * next_real
        mix_imag = fraction * next_imag
        both = jnp.concatenate(
            [left_real * mix_real - left_imag * mix_imag, left_real * mix_imag + left_imag * mix_real],
            axis=0,
        )
        start = pl.multiple_of(s * 2 * orders, 2 * orders)
        phi[pl.ds(start, 2 * orders), :] = both.astype(BF16)

    scale = 1.0 / math.sqrt(2 * half)
    power = iota((8, CELLS), 0)

    def block_turns(s):
        steps = [powers[i, pl.ds(s, 8, stride=0), :] for i in range(8)]
        one_real, one_imag = steps[:2]
        step = steps[6:]
        odd = power & 1 == 1
        real, imag = jnp.where(odd, one_real * scale, scale), jnp.where(odd, one_imag * scale, 0.0)
        for bit in (2, 4):
            taken = power & bit == bit
            by_real, by_imag = jnp.where(taken, steps[bit], 1.0), jnp.where(taken, steps[bit + 1], 0.0)
            real, imag = real * by_real - imag * by_imag, real * by_imag + imag * by_real
        evens, odds = [], []
        for j in range(half // 8):
            if j:
                real, imag = real * step[0] - imag * step[1], real * step[1] + imag * step[0]
            evens.append(real)
            odds.append(real * one_imag + imag * one_real)
        return evens + odds

    some = max(2, CELLS // (2 * half))
    shape = (some * 2 * own_half, some * 2 * half)
    own_row, turn_row = iota(shape, 0), iota(shape, 1)
    kept = own_row % (2 * own_half)
    source = kept // own_half * half + me * own_half + kept % own_half
    chosen = turn_row == own_row // (2 * own_half) * (2 * half) + source
    chosen = jnp.where(chosen, 1.0, 0.0).astype(BF16)
    run = 32

    def one_run(group):
        for j in range(0, run, some):
            first = group * run + j
            rows = []
            for i in range(some):
                block_phases(first + i)
                rows += block_turns(first + i)
            rows = jnp.concatenate(rows, axis=0).astype(BF16)
            turn[pl.ds(pl.multiple_of(first * 2 * half, shape[1]), shape[1]), :] = rows
            mine = jnp.dot(chosen, rows, preferred_element_type=F32)
            own[pl.ds(pl.multiple_of(first * 2 * own_half, shape[0]), shape[0]), :] = mine.astype(BF16)

    def beam_terms():
        extra.wait()
        sky_orders, cycles = pieces.shape[2:4]
        for j, span in enumerate(spans):
            terms = []
            for c in range(2):
                values = beam[:, c, span]
                high = values.astype(BF16)
                terms += [high, (values - high.astype(F32)).astype(BF16)]
            filling = sky_orders * cycles - 4 * beam_orders
            if filling:
                terms.append(jnp.zeros((filling, width), BF16))
            pieces[j, beam_orders] = jnp.concatenate(terms, axis=0).reshape(sky_orders, cycles, width)

    runs = blocks // run
    turns = [*range(1, beams), 0]

    def leaving(j):
        return pltpu.make_async_copy(pieces.at[j], pieces_hbm[j], departures.at[beams + j])

    @pl.loop(0, runs)
    def _(group):
        one_run(group)
        pl.when(group == 0)(beam_terms)
        for i, j in enumerate(turns):

            @pl.when(group == i * (runs // 2) // beams)
            def _(j=j):
                arriving[j].wait()
                leaving(j).start()

    for j in range(beams):
        leaving(j).wait()


def samples_kernel(
    blocks_local, rows, owners_vmem, locals_vmem, count, noise, arrived, phi, turn, own,
    out, owners, locals_, arrivals, widened,
    stacked, modes_rows, modes, partial, filtered, totals, ordered, shares,
):
    copies = bring((owners_vmem, locals_vmem), (owners, locals_), arrivals, 0)
    widened[...] = arrived[...].astype(F32)
    lanes = shares.shape[1]
    parts = shares.shape[0]
    beams = arrived.shape[0] // parts
    sky_devices = parts // rows
    blocks = partial.shape[0] // 8
    total = turn.shape[0] // blocks
    orders = total // beams
    cycles = lanes // orders
    together = len(totals)
    unroll = 32

    steps = max(1, blocks // (together * unroll))

    def cycle_of(s):
        return (owners[s] * blocks_local + locals_[s]) // CYCLE_BLOCKS

    width = together * parts
    for b in range(beams):
        for row in range(rows):
            some = every(widened, b * parts + row, sky_devices, rows)
            for j in range(together):
                start = j * parts + row * sky_devices
                stacked[b, start : start + sky_devices, :] = some
        modes_rows[b * lanes : (b + 1) * lanes, :] = stacked[b].T
    lane_group = iota((total, width), 1) // parts
    for r in range(cycles):
        halves = [
            modes_rows[pl.ds(r + parity * cycles, total // 2, stride=2 * cycles), :]
            for parity in range(2)
        ]
        values = jnp.concatenate(halves, axis=0)
        for j in range(together):
            modes[r, j] = jnp.where(lane_group == j, values, 0.0).astype(BF16)
    for copy in copies:
        copy.wait()

    def gather(first):
        left = jnp.concatenate([modes[cycle_of(first + j), j] for j in range(together)], axis=0)
        table = phi[pl.ds(pl.multiple_of(first * parts, width), width), :]
        cells = jnp.dot(left, table, preferred_element_type=F32)
        rotation = turn[pl.ds(pl.multiple_of(first * total, together * total), together * total), :]
        turned = (cells * rotation.astype(F32)).reshape(together, total // 8, 8, CELLS)
        kept = jnp.sum(turned, axis=1).reshape(together * 8, CELLS)
        partial[pl.ds(pl.multiple_of(first * 8, together * 8), together * 8), :] = kept

    @pl.loop(0, steps)
    def _(step):
        for i in range(unroll):
            gather((step * unroll + i) * together)

    signal = partial[pl.ds(0, blocks, stride=8), :]
    for i in range(1, 8):
        signal = signal + partial[pl.ds(i, blocks, stride=8), :]
    valid = iota((blocks, CELLS), 0) * CELLS + iota((blocks, CELLS), 1) < count[0:1, :]
    signal = jnp.where(valid, signal, 0.0)
    clean = lax.dot_general(
        signal.astype(BF16), noise[...].astype(BF16), LAST_LAST, preferred_element_type=F32
    )
    filtered[0:blocks] = jnp.where(valid, clean, 0.0)

    for one in totals:
        one[...] = jnp.zeros_like(one)
    half = orders // 2

    def spread(first):
        rotation = own[pl.ds(pl.multiple_of(first * orders, 16), together * orders), :].astype(F32)
        weighted = [
            rotation[j * orders : (j + 1) * orders] * filtered[pl.ds(first + j, orders, stride=0), :]
            for j in range(together)
        ]
        weighted = jnp.concatenate(weighted, axis=0).astype(BF16)
        table = phi[pl.ds(pl.multiple_of(first * parts, width), width), :]
        terms = lax.dot_general(weighted, table, LAST_LAST, preferred_element_type=F32)
        for j in range(together):
            row = pl.multiple_of(cycle_of(first + j) * orders, orders)
            here = totals[j]
            here[pl.ds(row, orders), :] += terms[j * orders : (j + 1) * orders]

    @pl.loop(0, steps)
    def _(step):
        for i in range(unroll):
            spread((step * unroll + i) * together)

    gathered = totals[0][...]
    which = iota(gathered.shape, 1) // parts
    for j in range(1, together):
        gathered = jnp.where(which == j, totals[j][...], gathered)
    totals[0][...] = gathered
    for k in range(orders):
        place = k // 2 + (k % 2) * half
        ordered[k * cycles : (k + 1) * cycles, :] = totals[0][pl.ds(place, cycles, stride=orders), :]
    turned = ordered[...].T
    summed = turned[0:parts]
    for j in range(1, together):
        summed = summed + turned[j * parts : (j + 1) * parts]
    for row in range(rows):
        put_every(shares, row, rows, summed[row * sky_devices : (row + 1) * sky_devices])
    block = shares[...].astype(BF16)
    for b in range(beams):
        out[b] = block


def gradient_kernel(arrived, pieces, out, modes):
    me = lax.axis_index("beam")
    parts, sky_orders, cycles, width = pieces[0].shape
    orders = parts - 1
    diagonal = own_block(orders, cycles)
    for b in range(len(pieces)):
        terms = arrived[b].astype(F32)
        while terms.shape[0] > 2 * sky_orders:
            middle = terms.shape[0] // 2
            terms = terms[:middle] + terms[middle:]
        modes[b] = terms.astype(BF16).astype(F32)
    first, second = [0.0] * sky_orders, [0.0] * sky_orders
    for j, piece in enumerate(pieces):
        terms = piece[orders].reshape(sky_orders * cycles, width).astype(F32)
        beam_real, beam_imag = [
            terms[2 * c * orders : (2 * c + 1) * orders] + terms[(2 * c + 1) * orders : (2 * c + 2) * orders]
            for c in range(2)
        ]
        these = modes[me ^ j]
        for m in range(sky_orders):
            spreads = []
            for c in range(2):
                row = these[c * sky_orders + m : c * sky_orders + m + 1]
                spreads.append(jnp.where(diagonal, row, 0.0))
            left = jnp.concatenate(spreads, axis=0).astype(BF16)
            table = piece[0:orders, m].reshape(orders * cycles, width)
            harmonics = jnp.dot(left, table, preferred_element_type=F32)
            real, imag = harmonics[:orders], harmonics[orders:]
            first[m] += real * beam_real + imag * beam_imag
            second[m] += imag * beam_real - real * beam_imag
    for m in range(sky_orders):
        out[m, 0:1, :] = jnp.sum(first[m], axis=0, keepdims=True)
        out[m, 1:2, :] = jnp.sum(second[m], axis=0, keepdims=True)


def exchange(pieces, axis):
    count = lax.axis_size(axis)
    return [pieces[0]] + [
        lax.ppermute(pieces[j], axis, [(i, i ^ j) for i in range(count)]) for j in range(1, count)
    ]


def local(
    sky_harmonics,
    beam_harmonics,
    wigner,
    order_map,
    block_owner,
    block_local,
    cell_offset,
    cell_fraction,
    beam_angle,
    sample_count,
    noise_weight,
):
    beams, sky_devices = lax.axis_size("beam"), lax.axis_size("ma")
    orders, sky_orders, cycles, degrees = wigner.shape
    total = orders * beams
    all_sky = sky_orders * sky_devices
    parts = 2 * all_sky
    blocks = block_local.shape[0]
    blocks_local = cycles // sky_devices * CYCLE_BLOCKS
    width = degrees // beams
    lanes = orders * cycles
    rows = 2 * sky_orders
    together = max(1, CELLS // parts)
    owners = block_owner.reshape(blocks)
    limit = pltpu.CompilerParams(vmem_limit_bytes=32 * 1024 * 1024)
    integers = [
        pltpu.SMEM((blocks,), jnp.int32),
        pltpu.SMEM((blocks,), jnp.int32),
    ]

    def pinned(*arrays):
        return [pltpu.with_memory_space_constraint(array, pltpu.HBM) for array in arrays]

    later = (
        order_map, owners, block_local,
        beam_angle.reshape(blocks, CELLS),
        cell_offset.reshape(blocks, CELLS),
        cell_fraction.reshape(blocks, CELLS),
        noise_weight,
    )
    sent, (order_map, owners, places, angles, offsets, fractions, noise) = pl.pallas_call(
        modes_kernel,
        out_shape=[
            jax.ShapeDtypeStruct((beams * sky_devices // 2, 2 * rows, lanes), BF16),
            [
                pltpu.VMEM((blocks + all_sky, CELLS) if place in (4, 5) else array.shape, array.dtype)
                for place, array in enumerate(later)
            ],
        ],
        in_specs=[*hbm(3), hbm(len(later))],
        out_specs=[vmem(1)[0], vmem(len(later))],
        scratch_shapes=[
            pltpu.VMEM(sky_harmonics.shape, F32),
            pltpu.VMEM(beam_harmonics.shape, F32),
            pltpu.VMEM((beams, orders, sky_orders, cycles, width), BF16),
            pltpu.SemaphoreType.DMA((2 + beams + len(later),)),
        ],
        compiler_params=limit,
        name="modes",
    )(*pinned(sky_harmonics, beam_harmonics, wigner), pinned(*later))
    sent = sent.reshape(beams * sky_devices, rows, lanes)
    arrived = lax.all_to_all(sent, ("beam", "ma"), split_axis=0, concat_axis=0, tiled=True)

    samples = pltpu.VMEM((blocks, CELLS), F32)
    piece = (orders + 1, sky_orders, cycles, width)
    phi, turn, own, pieces = pl.pallas_call(
        functools.partial(tables_kernel, blocks_local, sky_devices),
        out_shape=[
            pltpu.VMEM((blocks * parts, CELLS), BF16),
            pltpu.VMEM((blocks * total, CELLS), BF16),
            pltpu.VMEM((blocks * orders, CELLS), BF16),
            [pltpu.HBM(piece, BF16)] * beams,
        ],
        in_specs=vmem(6) + hbm(2),
        out_specs=[*vmem(3), hbm(beams)],
        scratch_shapes=[
            pltpu.VMEM((beams, *piece), BF16),
            pltpu.VMEM(beam_harmonics.shape, F32),
            pltpu.SemaphoreType.DMA((2 * beams,)),
            pltpu.SMEM((all_sky,), jnp.int32),
            *integers,
            pltpu.SemaphoreType.DMA((4,)),
            pltpu.VMEM((CYCLE_BLOCKS, all_sky, CELLS), F32),
            pltpu.VMEM((CYCLE_BLOCKS, all_sky, CELLS), F32),
            pltpu.VMEM((8, blocks + 8, CELLS), F32),
        ],
        compiler_params=limit,
        cost_estimate=pl.CostEstimate(flops=100_000_000, bytes_accessed=4_000_000, transcendentals=0),
        name="tables",
    )(
        order_map, owners, places, angles, offsets, fractions,
        *pinned(beam_harmonics, wigner),
    )
    pieces = exchange(pieces, "beam")

    grads = pl.pallas_call(
        functools.partial(samples_kernel, blocks_local, rows),
        out_shape=jax.ShapeDtypeStruct((beams, parts, lanes), BF16),
        in_specs=vmem(8),
        out_specs=vmem(1)[0],
        scratch_shapes=[
            *integers,
            pltpu.SemaphoreType.DMA((2,)),
            pltpu.VMEM((beams * parts, lanes), F32),
            pltpu.VMEM((beams, together * parts, lanes), F32),
            pltpu.VMEM((beams * lanes, together * parts), F32),
            pltpu.VMEM((cycles, together, total, together * parts), BF16),
            pltpu.VMEM((blocks * 8, CELLS), F32),
            pltpu.VMEM((blocks + orders, CELLS), F32),
            [pltpu.VMEM((lanes, together * parts), F32) for _ in range(together)],
            pltpu.VMEM((lanes, together * parts), F32),
            pltpu.VMEM((parts, lanes), F32),
        ],
        compiler_params=limit,
        cost_estimate=pl.CostEstimate(flops=40_000_000_000, bytes_accessed=100_000_000, transcendentals=0),
        name="samples",
    )(
        owners, places, jnp.broadcast_to(sample_count[None, :], (8, CELLS)), noise,
        arrived.reshape(beams * parts, lanes), phi, turn, own,
    )
    grads = grads.reshape(beams * sky_devices, rows, lanes)
    grads = lax.all_to_all(grads, ("beam", "ma"), split_axis=0, concat_axis=0, tiled=True)
    return pl.pallas_call(
        gradient_kernel,
        out_shape=jax.ShapeDtypeStruct((sky_orders, 2, width), F32),
        in_specs=[vmem(1)[0], vmem(beams)],
        out_specs=vmem(1)[0],
        scratch_shapes=[pltpu.VMEM((beams, rows, lanes), F32)],
        compiler_params=limit,
        name="gradient",
    )(grads.reshape(beams, parts, lanes), pieces)


def solution(mesh):
    return jax.shard_map(
        local,
        mesh=mesh,
        in_specs=(
            P("ma", None, None),
            P("beam", None, None),
            P("beam", "ma", None, None),
            P(),
            P("ma", None),
            P("ma"),
            P("ma"),
            P("ma"),
            P("ma"),
            P("ma"),
            P(),
        ),
        out_specs=P("ma", None, "beam"),
        check_vma=False,
    )
```

```python
import functools
import math

import jax
import jax.numpy as jnp
from jax import lax
from jax.experimental import pallas as pl
from jax.experimental.pallas import tpu as pltpu
from jax.sharding import PartitionSpec as P

PHI = 4096
CELLS = 128
CYCLE_BLOCKS = PHI // CELLS
F32 = jnp.float32
BF16 = jnp.bfloat16
LAST_LAST = (((1,), (1,)), ((), ()))


def iota(shape, axis):
    return lax.broadcasted_iota(jnp.int32, shape, axis)


def vmem(count):
    return [pl.BlockSpec(memory_space=pltpu.VMEM)] * count


def smem(count):
    return [pl.BlockSpec(memory_space=pltpu.SMEM)] * count


def hbm(count):
    return [pl.BlockSpec(memory_space=pltpu.HBM)] * count


def sine_turns(z):
    square = z * z
    value = 39.53670603 * square - 76.54978229
    value = value * square + 81.60100407
    value = value * square - 41.34165503
    value = value * square + 6.28318516
    return value * z


def cosine_steps(steps):
    centred = ((steps + PHI // 2) & (PHI - 1)) - PHI // 2
    return sine_turns(0.25 - jnp.abs(centred).astype(F32) * (1.0 / PHI))


def every(ref, first, count, step):
    if ref.shape[1] == CELLS:
        return ref[pl.ds(first, count, stride=step), :]
    return jnp.concatenate([ref[first + i * step][None] for i in range(count)], axis=0)


def put_every(ref, first, step, values):
    if ref.shape[1] == CELLS:
        ref[pl.ds(first, values.shape[0], stride=step), :] = values
    else:
        for i in range(values.shape[0]):
            ref[first + i * step, :] = values[i]


def bring(sources, places, semaphores, first):
    copies = [
        pltpu.make_async_copy(source, place, semaphores.at[first + i])
        for i, (source, place) in enumerate(zip(sources, places))
    ]
    for copy in copies:
        copy.start()
    return copies


def own_block(orders, cycles):
    shape = (orders, orders * cycles)
    return iota(shape, 1) // cycles == iota(shape, 0)


def modes_kernel(sky_hbm, beam_hbm, wigner_hbm, later_hbm, out, later, sky, beam, wigner, arrivals):
    chunks, orders, sky_orders, cycles, width = wigner.shape
    small = bring((sky_hbm, beam_hbm), (sky, beam), arrivals, 0)
    spans = [pl.ds(i * width, width) for i in range(chunks)]
    large = bring([wigner_hbm.at[:, :, :, span] for span in spans], [wigner.at[i] for i in range(chunks)], arrivals, 2)
    places = [
        place if place.shape == source.shape else place.at[0 : source.shape[0]]
        for source, place in zip(later_hbm, later)
    ]
    others = bring(later_hbm, places, arrivals, 2 + chunks)
    for copy in small:
        copy.wait()
    beam_real, beam_imag = beam[:, 0, :], beam[:, 1, :]
    diagonal = own_block(orders, cycles)
    products = []
    for m in range(sky_orders):
        sky_real, sky_imag = sky[m, 0:1, :], sky[m, 1:2, :]
        first = sky_real * beam_real - sky_imag * beam_imag
        second = sky_real * beam_imag + sky_imag * beam_real
        products.append(jnp.concatenate([first, second], axis=0).astype(BF16))
    sums = [0.0] * sky_orders
    for i in range(chunks):
        large[i].wait()
        for m in range(sky_orders):
            table = wigner[i, :, m].reshape(orders * cycles, width)
            left = products[m][:, i * width : (i + 1) * width]
            sums[m] += lax.dot_general(table, left, LAST_LAST, preferred_element_type=F32)
    rows = [None] * (2 * sky_orders)
    for m in range(sky_orders):
        modes = sums[m].T
        for c in range(2):
            part = jnp.where(diagonal, modes[c * orders : (c + 1) * orders], 0.0)
            rows[c * sky_orders + m] = jnp.sum(part, axis=0, keepdims=True)
    block = jnp.concatenate(rows + rows, axis=0).astype(BF16)
    for d in range(out.shape[0]):
        out[d] = block
    for copy in others:
        copy.wait()


def tables_kernel(
    blocks_local, sky_devices,
    order_vmem, owners_vmem, locals_vmem, angles, offsets, fractions, beam_hbm, wigner_hbm,
    phi, turn, own, pieces_hbm, pieces, beam, departures, order_map, owners, locals_, arrivals,
    step_real, step_imag, powers,
):
    copies = bring((order_vmem, owners_vmem, locals_vmem), (order_map, owners, locals_), arrivals, 0)
    me = lax.axis_index("beam")
    extra = bring((beam_hbm,), (beam,), arrivals, 3)[0]
    beams, beam_orders, width = pieces.shape[0], beam.shape[0], pieces.shape[4]
    spans = [pl.ds(pl.multiple_of((me ^ j) * width, width), width) for j in range(beams)]
    arriving = [
        pltpu.make_async_copy(wigner_hbm.at[:, :, :, span], pieces.at[j, 0:beam_orders], departures.at[j])
        for j, span in enumerate(spans)
    ]
    for j in [*range(1, beams), 0]:
        arriving[j].start()
    orders = order_map.shape[0]
    blocks = angles.shape[0]
    half = turn.shape[0] // blocks // 2
    own_half = own.shape[0] // blocks // 2

    part = angles[...] * (0.5 / math.pi)
    part = part - jnp.round(part)
    folded = jnp.where(part > 0.25, 0.5 - part, jnp.where(part < -0.25, -0.5 - part, part))
    real, imag = sine_turns(0.25 - jnp.abs(part)), sine_turns(folded)
    for i in range(4):
        if i:
            real, imag = real * real - imag * imag, 2.0 * real * imag
        powers[2 * i, 0:blocks], powers[2 * i + 1, 0:blocks] = real, imag

    copies[0].wait()
    order = jnp.zeros((orders, CELLS), jnp.int32)
    row = iota((orders, CELLS), 0)
    lane = iota((orders, CELLS), 1)
    for m in range(orders):
        place = m % (orders // sky_devices) * sky_devices + m // (orders // sky_devices)
        order = jnp.where(row == place, order_map[m], order)

    def phase(steps):
        return cosine_steps(steps), cosine_steps(steps + PHI // 4)

    scaling = 1.0 / math.sqrt(orders)
    cell_real, cell_imag = phase(order * lane)
    cell_real, cell_imag = cell_real * scaling, cell_imag * scaling
    next_real, next_imag = phase(order)
    next_real = next_real - 1.0
    first_real, first_imag = phase(((order * CELLS) & (PHI - 1)) * lane)
    for j in range(CYCLE_BLOCKS):
        step_real[j] = jnp.broadcast_to(first_real[:, j : j + 1], (orders, CELLS))
        step_imag[j] = jnp.broadcast_to(first_imag[:, j : j + 1], (orders, CELLS))
    for copy in copies[1:]:
        copy.wait()

    def block_phases(s):
        place = (owners[s] * blocks_local + locals_[s]) & (CYCLE_BLOCKS - 1)
        offset = offsets[pl.ds(s, orders, stride=0), :]
        fraction = fractions[pl.ds(s, orders, stride=0), :]
        real = jnp.take_along_axis(cell_real, offset, axis=1, mode="promise_in_bounds")
        imag = jnp.take_along_axis(cell_imag, offset, axis=1, mode="promise_in_bounds")
        base_real, base_imag = step_real[place], step_imag[place]
        left_real = real * base_real - imag * base_imag
        left_imag = real * base_imag + imag * base_real
        mix_real = 1.0 + fraction * next_real
        mix_imag = fraction * next_imag
        both = jnp.concatenate(
            [left_real * mix_real - left_imag * mix_imag, left_real * mix_imag + left_imag * mix_real],
            axis=0,
        )
        start = pl.multiple_of(s * 2 * orders, 2 * orders)
        phi[pl.ds(start, 2 * orders), :] = both.astype(BF16)

    scale = 1.0 / math.sqrt(2 * half)
    power = iota((8, CELLS), 0)

    def block_turns(s):
        steps = [powers[i, pl.ds(s, 8, stride=0), :] for i in range(8)]
        one_real, one_imag = steps[:2]
        step = steps[6:]
        odd = power & 1 == 1
        real, imag = jnp.where(odd, one_real * scale, scale), jnp.where(odd, one_imag * scale, 0.0)
        for bit in (2, 4):
            taken = power & bit == bit
            by_real, by_imag = jnp.where(taken, steps[bit], 1.0), jnp.where(taken, steps[bit + 1], 0.0)
            real, imag = real * by_real - imag * by_imag, real * by_imag + imag * by_real
        evens, odds = [], []
        for j in range(half // 8):
            if j:
                real, imag = real * step[0] - imag * step[1], real * step[1] + imag * step[0]
            evens.append(real)
            odds.append(real * one_imag + imag * one_real)
        return evens + odds

    some = max(2, CELLS // (2 * half))
    shape = (some * 2 * own_half, some * 2 * half)
    own_row, turn_row = iota(shape, 0), iota(shape, 1)
    kept = own_row % (2 * own_half)
    source = kept // own_half * half + me * own_half + kept % own_half
    chosen = turn_row == own_row // (2 * own_half) * (2 * half) + source
    chosen = jnp.where(chosen, 1.0, 0.0).astype(BF16)
    run = 32

    def one_run(group):
        for j in range(0, run, some):
            first = group * run + j
            rows = []
            for i in range(some):
                block_phases(first + i)
                rows += block_turns(first + i)
            rows = jnp.concatenate(rows, axis=0).astype(BF16)
            turn[pl.ds(pl.multiple_of(first * 2 * half, shape[1]), shape[1]), :] = rows
            mine = jnp.dot(chosen, rows, preferred_element_type=F32)
            own[pl.ds(pl.multiple_of(first * 2 * own_half, shape[0]), shape[0]), :] = mine.astype(BF16)

    def beam_terms():
        extra.wait()
        sky_orders, cycles = pieces.shape[2:4]
        for j, span in enumerate(spans):
            terms = []
            for c in range(2):
                values = beam[:, c, span]
                high = values.astype(BF16)
                terms += [high, (values - high.astype(F32)).astype(BF16)]
            filling = sky_orders * cycles - 4 * beam_orders
            if filling:
                terms.append(jnp.zeros((filling, width), BF16))
            pieces[j, beam_orders] = jnp.concatenate(terms, axis=0).reshape(sky_orders, cycles, width)

    runs = blocks // run
    turns = [*range(1, beams), 0]

    def leaving(j):
        return pltpu.make_async_copy(pieces.at[j], pieces_hbm[j], departures.at[beams + j])

    @pl.loop(0, runs)
    def _(group):
        one_run(group)
        pl.when(group == 0)(beam_terms)
        for i, j in enumerate(turns):

            @pl.when(group == i * (runs // 2) // beams)
            def _(j=j):
                arriving[j].wait()
                leaving(j).start()

    for j in range(beams):
        leaving(j).wait()


def samples_kernel(
    blocks_local, rows, owners_vmem, locals_vmem, count, noise, arrived, phi, turn, own,
    out, owners, locals_, arrivals, widened,
    stacked, modes_rows, modes, partial, filtered, totals, ordered, shares,
):
    copies = bring((owners_vmem, locals_vmem), (owners, locals_), arrivals, 0)
    widened[...] = arrived[...].astype(F32)
    lanes = shares.shape[1]
    parts = shares.shape[0]
    beams = arrived.shape[0] // parts
    sky_devices = parts // rows
    blocks = partial.shape[0] // 8
    total = turn.shape[0] // blocks
    orders = total // beams
    cycles = lanes // orders
    together = len(totals)
    unroll = 32

    steps = max(1, blocks // (together * unroll))

    def cycle_of(s):
        return (owners[s] * blocks_local + locals_[s]) // CYCLE_BLOCKS

    width = together * parts
    for b in range(beams):
        for row in range(rows):
            some = every(widened, b * parts + row, sky_devices, rows)
            for j in range(together):
                start = j * parts + row * sky_devices
                stacked[b, start : start + sky_devices, :] = some
        modes_rows[b * lanes : (b + 1) * lanes, :] = stacked[b].T
    lane_group = iota((total, width), 1) // parts
    for r in range(cycles):
        halves = [
            modes_rows[pl.ds(r + parity * cycles, total // 2, stride=2 * cycles), :]
            for parity in range(2)
        ]
        values = jnp.concatenate(halves, axis=0)
        for j in range(together):
            modes[r, j] = jnp.where(lane_group == j, values, 0.0).astype(BF16)
    for copy in copies:
        copy.wait()

    def gather(first):
        left = jnp.concatenate([modes[cycle_of(first + j), j] for j in range(together)], axis=0)
        table = phi[pl.ds(pl.multiple_of(first * parts, width), width), :]
        cells = jnp.dot(left, table, preferred_element_type=F32)
        rotation = turn[pl.ds(pl.multiple_of(first * total, together * total), together * total), :]
        turned = (cells * rotation.astype(F32)).reshape(together, total // 8, 8, CELLS)
        kept = jnp.sum(turned, axis=1).reshape(together * 8, CELLS)
        partial[pl.ds(pl.multiple_of(first * 8, together * 8), together * 8), :] = kept

    @pl.loop(0, steps)
    def _(step):
        for i in range(unroll):
            gather((step * unroll + i) * together)

    signal = partial[pl.ds(0, blocks, stride=8), :]
    for i in range(1, 8):
        signal = signal + partial[pl.ds(i, blocks, stride=8), :]
    valid = iota((blocks, CELLS), 0) * CELLS + iota((blocks, CELLS), 1) < count[0:1, :]
    signal = jnp.where(valid, signal, 0.0)
    clean = lax.dot_general(
        signal.astype(BF16), noise[...].astype(BF16), LAST_LAST, preferred_element_type=F32
    )
    filtered[0:blocks] = jnp.where(valid, clean, 0.0)

    for one in totals:
        one[...] = jnp.zeros_like(one)
    half = orders // 2

    def spread(first):
        rotation = own[pl.ds(pl.multiple_of(first * orders, 16), together * orders), :].astype(F32)
        weighted = [
            rotation[j * orders : (j + 1) * orders] * filtered[pl.ds(first + j, orders, stride=0), :]
            for j in range(together)
        ]
        weighted = jnp.concatenate(weighted, axis=0).astype(BF16)
        table = phi[pl.ds(pl.multiple_of(first * parts, width), width), :]
        terms = lax.dot_general(weighted, table, LAST_LAST, preferred_element_type=F32)
        for j in range(together):
            row = pl.multiple_of(cycle_of(first + j) * orders, orders)
            here = totals[j]
            here[pl.ds(row, orders), :] += terms[j * orders : (j + 1) * orders]

    @pl.loop(0, steps)
    def _(step):
        for i in range(unroll):
            spread((step * unroll + i) * together)

    gathered = totals[0][...]
    which = iota(gathered.shape, 1) // parts
    for j in range(1, together):
        gathered = jnp.where(which == j, totals[j][...], gathered)
    totals[0][...] = gathered
    for k in range(orders):
        place = k // 2 + (k % 2) * half
        ordered[k * cycles : (k + 1) * cycles, :] = totals[0][pl.ds(place, cycles, stride=orders), :]
    turned = ordered[...].T
    summed = turned[0:parts]
    for j in range(1, together):
        summed = summed + turned[j * parts : (j + 1) * parts]
    for row in range(rows):
        put_every(shares, row, rows, summed[row * sky_devices : (row + 1) * sky_devices])
    block = shares[...].astype(BF16)
    for b in range(beams):
        out[b] = block


def gradient_kernel(arrived, pieces, out, modes):
    me = lax.axis_index("beam")
    parts, sky_orders, cycles, width = pieces[0].shape
    orders = parts - 1
    diagonal = own_block(orders, cycles)
    for b in range(len(pieces)):
        terms = arrived[b].astype(F32)
        while terms.shape[0] > 2 * sky_orders:
            middle = terms.shape[0] // 2
            terms = terms[:middle] + terms[middle:]
        modes[b] = terms.astype(BF16).astype(F32)
    first, second = [0.0] * sky_orders, [0.0] * sky_orders
    for j, piece in enumerate(pieces):
        terms = piece[orders].reshape(sky_orders * cycles, width).astype(F32)
        beam_real, beam_imag = [
            terms[2 * c * orders : (2 * c + 1) * orders] + terms[(2 * c + 1) * orders : (2 * c + 2) * orders]
            for c in range(2)
        ]
        these = modes[me ^ j]
        for m in range(sky_orders):
            spreads = []
            for c in range(2):
                row = these[c * sky_orders + m : c * sky_orders + m + 1]
                spreads.append(jnp.where(diagonal, row, 0.0))
            left = jnp.concatenate(spreads, axis=0).astype(BF16)
            table = piece[0:orders, m].reshape(orders * cycles, width)
            harmonics = jnp.dot(left, table, preferred_element_type=F32)
            real, imag = harmonics[:orders], harmonics[orders:]
            first[m] += real * beam_real + imag * beam_imag
            second[m] += imag * beam_real - real * beam_imag
    for m in range(sky_orders):
        out[m, 0:1, :] = jnp.sum(first[m], axis=0, keepdims=True)
        out[m, 1:2, :] = jnp.sum(second[m], axis=0, keepdims=True)


def exchange(pieces, axis):
    count = lax.axis_size(axis)
    moved = {j: lax.ppermute(pieces[j], axis, [(i, i ^ j) for i in range(count)]) for j in range(count - 1, 0, -1)}
    return [pieces[0]] + [moved[j] for j in range(1, count)]


def local(
    sky_harmonics,
    beam_harmonics,
    wigner,
    order_map,
    block_owner,
    block_local,
    cell_offset,
    cell_fraction,
    beam_angle,
    sample_count,
    noise_weight,
):
    beams, sky_devices = lax.axis_size("beam"), lax.axis_size("ma")
    orders, sky_orders, cycles, degrees = wigner.shape
    total = orders * beams
    all_sky = sky_orders * sky_devices
    parts = 2 * all_sky
    blocks = block_local.shape[0]
    blocks_local = cycles // sky_devices * CYCLE_BLOCKS
    width = degrees // beams
    lanes = orders * cycles
    rows = 2 * sky_orders
    together = max(1, CELLS // parts)
    owners = block_owner.reshape(blocks)
    limit = pltpu.CompilerParams(vmem_limit_bytes=32 * 1024 * 1024)
    integers = [
        pltpu.SMEM((blocks,), jnp.int32),
        pltpu.SMEM((blocks,), jnp.int32),
    ]

    def pinned(*arrays):
        return [pltpu.with_memory_space_constraint(array, pltpu.HBM) for array in arrays]

    later = (
        order_map, owners, block_local,
        beam_angle.reshape(blocks, CELLS),
        cell_offset.reshape(blocks, CELLS),
        cell_fraction.reshape(blocks, CELLS),
        noise_weight,
    )
    sent, (order_map, owners, places, angles, offsets, fractions, noise) = pl.pallas_call(
        modes_kernel,
        out_shape=[
            jax.ShapeDtypeStruct((beams * sky_devices // 2, 2 * rows, lanes), BF16),
            [
                pltpu.VMEM((blocks + all_sky, CELLS) if place in (4, 5) else array.shape, array.dtype)
                for place, array in enumerate(later)
            ],
        ],
        in_specs=[*hbm(3), hbm(len(later))],
        out_specs=[vmem(1)[0], vmem(len(later))],
        scratch_shapes=[
            pltpu.VMEM(sky_harmonics.shape, F32),
            pltpu.VMEM(beam_harmonics.shape, F32),
            pltpu.VMEM((beams, orders, sky_orders, cycles, width), BF16),
            pltpu.SemaphoreType.DMA((2 + beams + len(later),)),
        ],
        compiler_params=limit,
        name="modes",
    )(*pinned(sky_harmonics, beam_harmonics, wigner), pinned(*later))
    sent = sent.reshape(beams * sky_devices, rows, lanes)
    arrived = lax.all_to_all(sent, ("beam", "ma"), split_axis=0, concat_axis=0, tiled=True)

    samples = pltpu.VMEM((blocks, CELLS), F32)
    piece = (orders + 1, sky_orders, cycles, width)
    phi, turn, own, pieces = pl.pallas_call(
        functools.partial(tables_kernel, blocks_local, sky_devices),
        out_shape=[
            pltpu.VMEM((blocks * parts, CELLS), BF16),
            pltpu.VMEM((blocks * total, CELLS), BF16),
            pltpu.VMEM((blocks * orders, CELLS), BF16),
            [pltpu.HBM(piece, BF16)] * beams,
        ],
        in_specs=vmem(6) + hbm(2),
        out_specs=[*vmem(3), hbm(beams)],
        scratch_shapes=[
            pltpu.VMEM((beams, *piece), BF16),
            pltpu.VMEM(beam_harmonics.shape, F32),
            pltpu.SemaphoreType.DMA((2 * beams,)),
            pltpu.SMEM((all_sky,), jnp.int32),
            *integers,
            pltpu.SemaphoreType.DMA((4,)),
            pltpu.VMEM((CYCLE_BLOCKS, all_sky, CELLS), F32),
            pltpu.VMEM((CYCLE_BLOCKS, all_sky, CELLS), F32),
            pltpu.VMEM((8, blocks + 8, CELLS), F32),
        ],
        compiler_params=limit,
        cost_estimate=pl.CostEstimate(flops=100_000_000, bytes_accessed=4_000_000, transcendentals=0),
        name="tables",
    )(
        order_map, owners, places, angles, offsets, fractions,
        *pinned(beam_harmonics, wigner),
    )
    pieces = exchange(pieces, "beam")

    grads = pl.pallas_call(
        functools.partial(samples_kernel, blocks_local, rows),
        out_shape=jax.ShapeDtypeStruct((beams, parts, lanes), BF16),
        in_specs=vmem(8),
        out_specs=vmem(1)[0],
        scratch_shapes=[
            *integers,
            pltpu.SemaphoreType.DMA((2,)),
            pltpu.VMEM((beams * parts, lanes), F32),
            pltpu.VMEM((beams, together * parts, lanes), F32),
            pltpu.VMEM((beams * lanes, together * parts), F32),
            pltpu.VMEM((cycles, together, total, together * parts), BF16),
            pltpu.VMEM((blocks * 8, CELLS), F32),
            pltpu.VMEM((blocks + orders, CELLS), F32),
            [pltpu.VMEM((lanes, together * parts), F32) for _ in range(together)],
            pltpu.VMEM((lanes, together * parts), F32),
            pltpu.VMEM((parts, lanes), F32),
        ],
        compiler_params=limit,
        cost_estimate=pl.CostEstimate(flops=40_000_000_000, bytes_accessed=100_000_000, transcendentals=0),
        name="samples",
    )(
        owners, places, jnp.broadcast_to(sample_count[None, :], (8, CELLS)), noise,
        arrived.reshape(beams * parts, lanes), phi, turn, own,
    )
    grads = grads.reshape(beams * sky_devices, rows, lanes)
    grads = lax.all_to_all(grads, ("beam", "ma"), split_axis=0, concat_axis=0, tiled=True)
    return pl.pallas_call(
        gradient_kernel,
        out_shape=jax.ShapeDtypeStruct((sky_orders, 2, width), F32),
        in_specs=[vmem(1)[0], vmem(beams)],
        out_specs=vmem(1)[0],
        scratch_shapes=[pltpu.VMEM((beams, rows, lanes), F32)],
        compiler_params=limit,
        name="gradient",
    )(grads.reshape(beams, parts, lanes), pieces)


def solution(mesh):
    return jax.shard_map(
        local,
        mesh=mesh,
        in_specs=(
            P("ma", None, None),
            P("beam", None, None),
            P("beam", "ma", None, None),
            P(),
            P("ma", None),
            P("ma"),
            P("ma"),
            P("ma"),
            P("ma"),
            P("ma"),
            P(),
        ),
        out_specs=P("ma", None, "beam"),
        check_vma=False,
    )
```

```python
import functools
import math

import jax
import jax.numpy as jnp
from jax import lax
from jax.experimental import pallas as pl
from jax.experimental.pallas import tpu as pltpu
from jax.sharding import PartitionSpec as P

PHI = 4096
CELLS = 128
CYCLE_BLOCKS = PHI // CELLS
F32 = jnp.float32
BF16 = jnp.bfloat16
LAST_LAST = (((1,), (1,)), ((), ()))


def iota(shape, axis):
    return lax.broadcasted_iota(jnp.int32, shape, axis)


def vmem(count):
    return [pl.BlockSpec(memory_space=pltpu.VMEM)] * count


def smem(count):
    return [pl.BlockSpec(memory_space=pltpu.SMEM)] * count


def hbm(count):
    return [pl.BlockSpec(memory_space=pltpu.HBM)] * count


def sine_turns(z):
    square = z * z
    value = 39.53670603 * square - 76.54978229
    value = value * square + 81.60100407
    value = value * square - 41.34165503
    value = value * square + 6.28318516
    return value * z


def cosine_steps(steps):
    centred = ((steps + PHI // 2) & (PHI - 1)) - PHI // 2
    return sine_turns(0.25 - jnp.abs(centred).astype(F32) * (1.0 / PHI))


def every(ref, first, count, step):
    if ref.shape[1] == CELLS:
        return ref[pl.ds(first, count, stride=step), :]
    return jnp.concatenate([ref[first + i * step][None] for i in range(count)], axis=0)


def put_every(ref, first, step, values):
    if ref.shape[1] == CELLS:
        ref[pl.ds(first, values.shape[0], stride=step), :] = values
    else:
        for i in range(values.shape[0]):
            ref[first + i * step, :] = values[i]


def bring(sources, places, semaphores, first):
    copies = [
        pltpu.make_async_copy(source, place, semaphores.at[first + i])
        for i, (source, place) in enumerate(zip(sources, places))
    ]
    for copy in copies:
        copy.start()
    return copies


def own_block(orders, cycles):
    shape = (orders, orders * cycles)
    return iota(shape, 1) // cycles == iota(shape, 0)


def modes_kernel(sky_hbm, beam_hbm, wigner_hbm, later_hbm, out, later, sky, beam, wigner, arrivals):
    chunks, orders, sky_orders, cycles, width = wigner.shape
    spans = [pl.ds(i * width, width) for i in range(chunks)]
    large = bring([wigner_hbm.at[:, :, :, span] for span in spans], [wigner.at[i] for i in range(chunks)], arrivals, 2)
    small = bring((sky_hbm, beam_hbm), (sky, beam), arrivals, 0)
    places = [
        place if place.shape == source.shape else place.at[0 : source.shape[0]]
        for source, place in zip(later_hbm, later)
    ]
    others = bring(later_hbm, places, arrivals, 2 + chunks)
    for copy in small:
        copy.wait()
    beam_real, beam_imag = beam[:, 0, :], beam[:, 1, :]
    diagonal = own_block(orders, cycles)
    products = []
    for m in range(sky_orders):
        sky_real, sky_imag = sky[m, 0:1, :], sky[m, 1:2, :]
        first = sky_real * beam_real - sky_imag * beam_imag
        second = sky_real * beam_imag + sky_imag * beam_real
        products.append(jnp.concatenate([first, second], axis=0).astype(BF16))
    sums = [0.0] * sky_orders
    for i in range(chunks):
        large[i].wait()
        for m in range(sky_orders):
            table = wigner[i, :, m].reshape(orders * cycles, width)
            left = products[m][:, i * width : (i + 1) * width]
            sums[m] += lax.dot_general(table, left, LAST_LAST, preferred_element_type=F32)
    rows = [None] * (2 * sky_orders)
    for m in range(sky_orders):
        modes = sums[m].T
        for c in range(2):
            part = jnp.where(diagonal, modes[c * orders : (c + 1) * orders], 0.0)
            rows[c * sky_orders + m] = jnp.sum(part, axis=0, keepdims=True)
    block = jnp.concatenate(rows + rows, axis=0).astype(BF16)
    for d in range(out.shape[0]):
        out[d] = block
    for copy in others:
        copy.wait()


def tables_kernel(
    blocks_local, sky_devices,
    order_vmem, owners_vmem, locals_vmem, angles, offsets, fractions, beam_hbm, wigner_hbm,
    phi, turn, own, pieces_hbm, pieces, beam, departures, order_map, owners, locals_, arrivals,
    step_real, step_imag, powers,
):
    copies = bring((order_vmem, owners_vmem, locals_vmem), (order_map, owners, locals_), arrivals, 0)
    me = lax.axis_index("beam")
    extra = bring((beam_hbm,), (beam,), arrivals, 3)[0]
    beams, beam_orders, width = pieces.shape[0], beam.shape[0], pieces.shape[4]
    spans = [pl.ds(pl.multiple_of((me ^ j) * width, width), width) for j in range(beams)]
    arriving = [
        pltpu.make_async_copy(wigner_hbm.at[:, :, :, span], pieces.at[j, 0:beam_orders], departures.at[j])
        for j, span in enumerate(spans)
    ]
    for j in [*range(1, beams), 0]:
        arriving[j].start()
    orders = order_map.shape[0]
    blocks = angles.shape[0]
    half = turn.shape[0] // blocks // 2
    own_half = own.shape[0] // blocks // 2

    part = angles[...] * (0.5 / math.pi)
    part = part - jnp.round(part)
    folded = jnp.where(part > 0.25, 0.5 - part, jnp.where(part < -0.25, -0.5 - part, part))
    real, imag = sine_turns(0.25 - jnp.abs(part)), sine_turns(folded)
    for i in range(4):
        if i:
            real, imag = real * real - imag * imag, 2.0 * real * imag
        powers[2 * i, 0:blocks], powers[2 * i + 1, 0:blocks] = real, imag

    copies[0].wait()
    order = jnp.zeros((orders, CELLS), jnp.int32)
    row = iota((orders, CELLS), 0)
    lane = iota((orders, CELLS), 1)
    for m in range(orders):
        place = m % (orders // sky_devices) * sky_devices + m // (orders // sky_devices)
        order = jnp.where(row == place, order_map[m], order)

    def phase(steps):
        return cosine_steps(steps), cosine_steps(steps + PHI // 4)

    scaling = 1.0 / math.sqrt(orders)
    cell_real, cell_imag = phase(order * lane)
    cell_real, cell_imag = cell_real * scaling, cell_imag * scaling
    next_real, next_imag = phase(order)
    next_real = next_real - 1.0
    first_real, first_imag = phase(((order * CELLS) & (PHI - 1)) * lane)
    for j in range(CYCLE_BLOCKS):
        step_real[j] = jnp.broadcast_to(first_real[:, j : j + 1], (orders, CELLS))
        step_imag[j] = jnp.broadcast_to(first_imag[:, j : j + 1], (orders, CELLS))
    for copy in copies[1:]:
        copy.wait()

    def block_phases(s):
        place = (owners[s] * blocks_local + locals_[s]) & (CYCLE_BLOCKS - 1)
        offset = offsets[pl.ds(s, orders, stride=0), :]
        fraction = fractions[pl.ds(s, orders, stride=0), :]
        real = jnp.take_along_axis(cell_real, offset, axis=1, mode="promise_in_bounds")
        imag = jnp.take_along_axis(cell_imag, offset, axis=1, mode="promise_in_bounds")
        base_real, base_imag = step_real[place], step_imag[place]
        left_real = real * base_real - imag * base_imag
        left_imag = real * base_imag + imag * base_real
        mix_real = 1.0 + fraction * next_real
        mix_imag = fraction * next_imag
        both = jnp.concatenate(
            [left_real * mix_real - left_imag * mix_imag, left_real * mix_imag + left_imag * mix_real],
            axis=0,
        )
        start = pl.multiple_of(s * 2 * orders, 2 * orders)
        phi[pl.ds(start, 2 * orders), :] = both.astype(BF16)

    scale = 1.0 / math.sqrt(2 * half)
    power = iota((8, CELLS), 0)

    def block_turns(s):
        steps = [powers[i, pl.ds(s, 8, stride=0), :] for i in range(8)]
        one_real, one_imag = steps[:2]
        step = steps[6:]
        odd = power & 1 == 1
        real, imag = jnp.where(odd, one_real * scale, scale), jnp.where(odd, one_imag * scale, 0.0)
        for bit in (2, 4):
            taken = power & bit == bit
            by_real, by_imag = jnp.where(taken, steps[bit], 1.0), jnp.where(taken, steps[bit + 1], 0.0)
            real, imag = real * by_real - imag * by_imag, real * by_imag + imag * by_real
        evens, odds = [], []
        for j in range(half // 8):
            if j:
                real, imag = real * step[0] - imag * step[1], real * step[1] + imag * step[0]
            evens.append(real)
            odds.append(real * one_imag + imag * one_real)
        return evens + odds

    some = max(2, CELLS // (2 * half))
    shape = (some * 2 * own_half, some * 2 * half)
    own_row, turn_row = iota(shape, 0), iota(shape, 1)
    kept = own_row % (2 * own_half)
    source = kept // own_half * half + me * own_half + kept % own_half
    chosen = turn_row == own_row // (2 * own_half) * (2 * half) + source
    chosen = jnp.where(chosen, 1.0, 0.0).astype(BF16)
    run = 32

    def one_run(group):
        for j in range(0, run, some):
            first = group * run + j
            rows = []
            for i in range(some):
                block_phases(first + i)
                rows += block_turns(first + i)
            rows = jnp.concatenate(rows, axis=0).astype(BF16)
            turn[pl.ds(pl.multiple_of(first * 2 * half, shape[1]), shape[1]), :] = rows
            mine = jnp.dot(chosen, rows, preferred_element_type=F32)
            own[pl.ds(pl.multiple_of(first * 2 * own_half, shape[0]), shape[0]), :] = mine.astype(BF16)

    def beam_terms():
        extra.wait()
        sky_orders, cycles = pieces.shape[2:4]
        for j, span in enumerate(spans):
            terms = []
            for c in range(2):
                values = beam[:, c, span]
                high = values.astype(BF16)
                terms += [high, (values - high.astype(F32)).astype(BF16)]
            filling = sky_orders * cycles - 4 * beam_orders
            if filling:
                terms.append(jnp.zeros((filling, width), BF16))
            pieces[j, beam_orders] = jnp.concatenate(terms, axis=0).reshape(sky_orders, cycles, width)

    runs = blocks // run
    turns = [*range(1, beams), 0]

    def leaving(j):
        return pltpu.make_async_copy(pieces.at[j], pieces_hbm[j], departures.at[beams + j])

    @pl.loop(0, runs)
    def _(group):
        one_run(group)
        pl.when(group == 0)(beam_terms)
        for i, j in enumerate(turns):

            @pl.when(group == i * (runs // 2) // beams)
            def _(j=j):
                arriving[j].wait()
                leaving(j).start()

    for j in range(beams):
        leaving(j).wait()


def samples_kernel(
    blocks_local, rows, owners_vmem, locals_vmem, count, noise, arrived, phi, turn, own,
    out, owners, locals_, arrivals, widened,
    stacked, modes_rows, modes, partial, filtered, totals, ordered, shares,
):
    copies = bring((owners_vmem, locals_vmem), (owners, locals_), arrivals, 0)
    widened[...] = arrived[...].astype(F32)
    lanes = shares.shape[1]
    parts = shares.shape[0]
    beams = arrived.shape[0] // parts
    sky_devices = parts // rows
    blocks = partial.shape[0] // 8
    total = turn.shape[0] // blocks
    orders = total // beams
    cycles = lanes // orders
    together = len(totals)
    unroll = 32

    steps = max(1, blocks // (together * unroll))

    def cycle_of(s):
        return (owners[s] * blocks_local + locals_[s]) // CYCLE_BLOCKS

    width = together * parts
    for b in range(beams):
        for row in range(rows):
            some = every(widened, b * parts + row, sky_devices, rows)
            for j in range(together):
                start = j * parts + row * sky_devices
                stacked[b, start : start + sky_devices, :] = some
        modes_rows[b * lanes : (b + 1) * lanes, :] = stacked[b].T
    lane_group = iota((total, width), 1) // parts
    for r in range(cycles):
        halves = [
            modes_rows[pl.ds(r + parity * cycles, total // 2, stride=2 * cycles), :]
            for parity in range(2)
        ]
        values = jnp.concatenate(halves, axis=0)
        for j in range(together):
            modes[r, j] = jnp.where(lane_group == j, values, 0.0).astype(BF16)
    for copy in copies:
        copy.wait()

    def gather(first):
        left = jnp.concatenate([modes[cycle_of(first + j), j] for j in range(together)], axis=0)
        table = phi[pl.ds(pl.multiple_of(first * parts, width), width), :]
        cells = jnp.dot(left, table, preferred_element_type=F32)
        rotation = turn[pl.ds(pl.multiple_of(first * total, together * total), together * total), :]
        turned = (cells * rotation.astype(F32)).reshape(together, total // 8, 8, CELLS)
        kept = jnp.sum(turned, axis=1).reshape(together * 8, CELLS)
        partial[pl.ds(pl.multiple_of(first * 8, together * 8), together * 8), :] = kept

    @pl.loop(0, steps)
    def _(step):
        for i in range(unroll):
            gather((step * unroll + i) * together)

    signal = partial[pl.ds(0, blocks, stride=8), :]
    for i in range(1, 8):
        signal = signal + partial[pl.ds(i, blocks, stride=8), :]
    valid = iota((blocks, CELLS), 0) * CELLS + iota((blocks, CELLS), 1) < count[0:1, :]
    signal = jnp.where(valid, signal, 0.0)
    clean = lax.dot_general(
        signal.astype(BF16), noise[...].astype(BF16), LAST_LAST, preferred_element_type=F32
    )
    filtered[0:blocks] = jnp.where(valid, clean, 0.0)

    for one in totals:
        one[...] = jnp.zeros_like(one)
    half = orders // 2

    def spread(first):
        rotation = own[pl.ds(pl.multiple_of(first * orders, 16), together * orders), :].astype(F32)
        weighted = [
            rotation[j * orders : (j + 1) * orders] * filtered[pl.ds(first + j, orders, stride=0), :]
            for j in range(together)
        ]
        weighted = jnp.concatenate(weighted, axis=0).astype(BF16)
        table = phi[pl.ds(pl.multiple_of(first * parts, width), width), :]
        terms = lax.dot_general(weighted, table, LAST_LAST, preferred_element_type=F32)
        for j in range(together):
            row = pl.multiple_of(cycle_of(first + j) * orders, orders)
            here = totals[j]
            here[pl.ds(row, orders), :] += terms[j * orders : (j + 1) * orders]

    @pl.loop(0, steps)
    def _(step):
        for i in range(unroll):
            spread((step * unroll + i) * together)

    gathered = totals[0][...]
    which = iota(gathered.shape, 1) // parts
    for j in range(1, together):
        gathered = jnp.where(which == j, totals[j][...], gathered)
    totals[0][...] = gathered
    for k in range(orders):
        place = k // 2 + (k % 2) * half
        ordered[k * cycles : (k + 1) * cycles, :] = totals[0][pl.ds(place, cycles, stride=orders), :]
    turned = ordered[...].T
    summed = turned[0:parts]
    for j in range(1, together):
        summed = summed + turned[j * parts : (j + 1) * parts]
    for row in range(rows):
        put_every(shares, row, rows, summed[row * sky_devices : (row + 1) * sky_devices])
    block = shares[...].astype(BF16)
    for b in range(beams):
        out[b] = block


def gradient_kernel(arrived, pieces, out, modes):
    me = lax.axis_index("beam")
    parts, sky_orders, cycles, width = pieces[0].shape
    orders = parts - 1
    diagonal = own_block(orders, cycles)
    for b in range(len(pieces)):
        terms = arrived[b].astype(F32)
        while terms.shape[0] > 2 * sky_orders:
            middle = terms.shape[0] // 2
            terms = terms[:middle] + terms[middle:]
        modes[b] = terms.astype(BF16).astype(F32)
    first, second = [0.0] * sky_orders, [0.0] * sky_orders
    for j, piece in enumerate(pieces):
        terms = piece[orders].reshape(sky_orders * cycles, width).astype(F32)
        beam_real, beam_imag = [
            terms[2 * c * orders : (2 * c + 1) * orders] + terms[(2 * c + 1) * orders : (2 * c + 2) * orders]
            for c in range(2)
        ]
        these = modes[me ^ j]
        for m in range(sky_orders):
            spreads = []
            for c in range(2):
                row = these[c * sky_orders + m : c * sky_orders + m + 1]
                spreads.append(jnp.where(diagonal, row, 0.0))
            left = jnp.concatenate(spreads, axis=0).astype(BF16)
            table = piece[0:orders, m].reshape(orders * cycles, width)
            harmonics = jnp.dot(left, table, preferred_element_type=F32)
            real, imag = harmonics[:orders], harmonics[orders:]
            first[m] += real * beam_real + imag * beam_imag
            second[m] += imag * beam_real - real * beam_imag
    for m in range(sky_orders):
        out[m, 0:1, :] = jnp.sum(first[m], axis=0, keepdims=True)
        out[m, 1:2, :] = jnp.sum(second[m], axis=0, keepdims=True)


def exchange(pieces, axis):
    count = lax.axis_size(axis)
    moved = {j: lax.ppermute(pieces[j], axis, [(i, i ^ j) for i in range(count)]) for j in range(count - 1, 0, -1)}
    return [pieces[0]] + [moved[j] for j in range(1, count)]


def local(
    sky_harmonics,
    beam_harmonics,
    wigner,
    order_map,
    block_owner,
    block_local,
    cell_offset,
    cell_fraction,
    beam_angle,
    sample_count,
    noise_weight,
):
    beams, sky_devices = lax.axis_size("beam"), lax.axis_size("ma")
    orders, sky_orders, cycles, degrees = wigner.shape
    total = orders * beams
    all_sky = sky_orders * sky_devices
    parts = 2 * all_sky
    blocks = block_local.shape[0]
    blocks_local = cycles // sky_devices * CYCLE_BLOCKS
    width = degrees // beams
    lanes = orders * cycles
    rows = 2 * sky_orders
    together = max(1, CELLS // parts)
    owners = block_owner.reshape(blocks)
    limit = pltpu.CompilerParams(vmem_limit_bytes=32 * 1024 * 1024)
    integers = [
        pltpu.SMEM((blocks,), jnp.int32),
        pltpu.SMEM((blocks,), jnp.int32),
    ]

    def pinned(*arrays):
        return [pltpu.with_memory_space_constraint(array, pltpu.HBM) for array in arrays]

    later = (
        order_map, owners, block_local,
        beam_angle.reshape(blocks, CELLS),
        cell_offset.reshape(blocks, CELLS),
        cell_fraction.reshape(blocks, CELLS),
        noise_weight,
    )
    sent, (order_map, owners, places, angles, offsets, fractions, noise) = pl.pallas_call(
        modes_kernel,
        out_shape=[
            jax.ShapeDtypeStruct((beams * sky_devices // 2, 2 * rows, lanes), BF16),
            [
                pltpu.VMEM((blocks + all_sky, CELLS) if place in (4, 5) else array.shape, array.dtype)
                for place, array in enumerate(later)
            ],
        ],
        in_specs=[*hbm(3), hbm(len(later))],
        out_specs=[vmem(1)[0], vmem(len(later))],
        scratch_shapes=[
            pltpu.VMEM(sky_harmonics.shape, F32),
            pltpu.VMEM(beam_harmonics.shape, F32),
            pltpu.VMEM((beams, orders, sky_orders, cycles, width), BF16),
            pltpu.SemaphoreType.DMA((2 + beams + len(later),)),
        ],
        compiler_params=limit,
        name="modes",
    )(*pinned(sky_harmonics, beam_harmonics, wigner), pinned(*later))
    sent = sent.reshape(beams * sky_devices, rows, lanes)
    arrived = lax.all_to_all(sent, ("beam", "ma"), split_axis=0, concat_axis=0, tiled=True)

    samples = pltpu.VMEM((blocks, CELLS), F32)
    piece = (orders + 1, sky_orders, cycles, width)
    phi, turn, own, pieces = pl.pallas_call(
        functools.partial(tables_kernel, blocks_local, sky_devices),
        out_shape=[
            pltpu.VMEM((blocks * parts, CELLS), BF16),
            pltpu.VMEM((blocks * total, CELLS), BF16),
            pltpu.VMEM((blocks * orders, CELLS), BF16),
            [pltpu.HBM(piece, BF16)] * beams,
        ],
        in_specs=vmem(6) + hbm(2),
        out_specs=[*vmem(3), hbm(beams)],
        scratch_shapes=[
            pltpu.VMEM((beams, *piece), BF16),
            pltpu.VMEM(beam_harmonics.shape, F32),
            pltpu.SemaphoreType.DMA((2 * beams,)),
            pltpu.SMEM((all_sky,), jnp.int32),
            *integers,
            pltpu.SemaphoreType.DMA((4,)),
            pltpu.VMEM((CYCLE_BLOCKS, all_sky, CELLS), F32),
            pltpu.VMEM((CYCLE_BLOCKS, all_sky, CELLS), F32),
            pltpu.VMEM((8, blocks + 8, CELLS), F32),
        ],
        compiler_params=limit,
        cost_estimate=pl.CostEstimate(flops=100_000_000, bytes_accessed=4_000_000, transcendentals=0),
        name="tables",
    )(
        order_map, owners, places, angles, offsets, fractions,
        *pinned(beam_harmonics, wigner),
    )
    pieces = exchange(pieces, "beam")

    grads = pl.pallas_call(
        functools.partial(samples_kernel, blocks_local, rows),
        out_shape=jax.ShapeDtypeStruct((beams, parts, lanes), BF16),
        in_specs=vmem(8),
        out_specs=vmem(1)[0],
        scratch_shapes=[
            *integers,
            pltpu.SemaphoreType.DMA((2,)),
            pltpu.VMEM((beams * parts, lanes), F32),
            pltpu.VMEM((beams, together * parts, lanes), F32),
            pltpu.VMEM((beams * lanes, together * parts), F32),
            pltpu.VMEM((cycles, together, total, together * parts), BF16),
            pltpu.VMEM((blocks * 8, CELLS), F32),
            pltpu.VMEM((blocks + orders, CELLS), F32),
            [pltpu.VMEM((lanes, together * parts), F32) for _ in range(together)],
            pltpu.VMEM((lanes, together * parts), F32),
            pltpu.VMEM((parts, lanes), F32),
        ],
        compiler_params=limit,
        cost_estimate=pl.CostEstimate(flops=40_000_000_000, bytes_accessed=100_000_000, transcendentals=0),
        name="samples",
    )(
        owners, places, jnp.broadcast_to(sample_count[None, :], (8, CELLS)), noise,
        arrived.reshape(beams * parts, lanes), phi, turn, own,
    )
    grads = grads.reshape(beams * sky_devices, rows, lanes)
    grads = lax.all_to_all(grads, ("beam", "ma"), split_axis=0, concat_axis=0, tiled=True)
    return pl.pallas_call(
        gradient_kernel,
        out_shape=jax.ShapeDtypeStruct((sky_orders, 2, width), F32),
        in_specs=[vmem(1)[0], vmem(beams)],
        out_specs=vmem(1)[0],
        scratch_shapes=[pltpu.VMEM((beams, rows, lanes), F32)],
        compiler_params=limit,
        name="gradient",
    )(grads.reshape(beams, parts, lanes), pieces)


def solution(mesh):
    return jax.shard_map(
        local,
        mesh=mesh,
        in_specs=(
            P("ma", None, None),
            P("beam", None, None),
            P("beam", "ma", None, None),
            P(),
            P("ma", None),
            P("ma"),
            P("ma"),
            P("ma"),
            P("ma"),
            P("ma"),
            P(),
        ),
        out_specs=P("ma", None, "beam"),
        check_vma=False,
    )
```
